32 devices in a mesh: gx: 4 (over z), gy: 2 (over y), gz: 4 (over x, core).
Axes of the slice: x: 2, y: 2, z: 4, core: 2. Of those that a mesh axis runs over, the one named last changes fastest.
Arguments:
- saved_heat_state: float32 [32, 32, 512], P('gx', 'gy', 'gz'), may hold values from 0 to 1
- forward_motion: float32 [3, 32, 32, 512], P(None, 'gx', 'gy', 'gz'), may hold values from -1 to 1
- dual_heat_after: float32 [32, 32, 512], P('gx', 'gy', 'gz'), may hold values from -1 to 6
- rheology_class: int32 [32, 32, 512], P('gx', 'gy', 'gz'), may hold values from 0 to 7, as said below
- class_base_stiffness: float32 [8], replicated, may hold values from 0.01 to 100
Outputs:
- adj_temp_prev: float32 [32, 32, 512], P('gx', 'gy', 'gz')
- adj_velocity: float32 [3, 32, 32, 512], P(None, 'gx', 'gy', 'gz')
- adj_pressure: float32 [32, 32, 512], P('gx', 'gy', 'gz')
The draws below stay inside these ranges and needn't reach their ends.
Inputs may be any that keep to these rules, and one draw needn't show every extreme that they name: `rheology_class`: each cell's viscosity class.
All inputs are finite; a program needn't handle non-finite values.
Results may differ from the reference program's by a relative error of at most 0.0003.
Values sent between devices are 32-bit elements; how exact they have to be, the bound alone decides.
No kernel may reach another device: no remote copies, remote signals or barrier semaphores. Data moves between devices by JAX's collectives and lax.ppermute only.
A program may use at most 128 MiB of HBM per device.

```python
import math
import jax
import jax.numpy as jnp

RECOMPUTE = 2
SCHUR_ITERS = 4
COARSE_SWEEPS = 3
LAYERS = 8
GRID_WIDTH = 32
GRID_BREADTH = 32
GRID_HEIGHT = 512


def draw_saved_heat_state(key, part):
    extent = (GRID_WIDTH, GRID_BREADTH, GRID_HEIGHT)
    uniform_draw = jax.random.uniform(jax.random.fold_in(key, 11), extent, jnp.float32)
    return uniform_draw


def draw_dual_heat_after(key, part):
    extent = (GRID_WIDTH, GRID_BREADTH, GRID_HEIGHT)
    depth_share = jnp.arange(GRID_HEIGHT, dtype=jnp.float32) / GRID_HEIGHT
    rough_part = jnp.clip(jax.random.normal(jax.random.fold_in(key, 22), extent, jnp.float32), -2.5, 2.5)
    offset_part = 1.5 + 2.0 * depth_share
    return offset_part[None, None, :] + rough_part


def draw_rheology_class(key, part):
    extent = (GRID_WIDTH, GRID_BREADTH, GRID_HEIGHT)
    class_order = jax.random.permutation(jax.random.fold_in(key, 31), LAYERS).astype(jnp.int32)
    jitter = jax.random.randint(jax.random.fold_in(key, 32), extent, 0, GRID_HEIGHT // LAYERS, dtype=jnp.int32)
    depth_index = jnp.arange(GRID_HEIGHT, dtype=jnp.int32)[None, None, :]
    depth_band = jnp.minimum((depth_index + jitter) * LAYERS // GRID_HEIGHT, LAYERS - 1)
    return jnp.take(class_order, depth_band).astype(jnp.int32)


def shard_levels(rng, shape, split, smallest, top_value):
    factor_of, own = 1.0, jax.random.fold_in(rng, 6)
    for dim, blocks in split:
        draws = jnp.exp(jax.random.uniform(jax.random.fold_in(own, dim), (blocks,), jnp.float32, smallest / len(split), top_value / len(split)))
        factor_of = factor_of * jnp.repeat(draws, shape[dim] // blocks).reshape([-1 if axis == dim else 1 for axis in range(len(shape))])
    return factor_of


def setup_inputs(seed: int = 0) -> dict:
    streams_of = jax.random.split(jax.random.key(seed), 6)
    saved_heat_state = draw_saved_heat_state(jax.random.fold_in(streams_of[5], 71), 0)
    forward_motion = jnp.clip(jax.random.uniform(streams_of[1], (3, GRID_WIDTH, GRID_BREADTH, GRID_HEIGHT), jnp.float32, -1.0, 1.0) * shard_levels(streams_of[1], (3, GRID_WIDTH, GRID_BREADTH, GRID_HEIGHT), ((1, 4), (2, 2), (3, 4)), -0.4, 0.0), -1.0, 1.0)
    dual_heat_after = draw_dual_heat_after(jax.random.fold_in(streams_of[5], 71), 0)
    rheology_class = draw_rheology_class(jax.random.fold_in(streams_of[5], 71), 0)
    class_base_stiffness = jnp.clip(jnp.exp(jax.random.uniform(streams_of[4], (LAYERS,), jnp.float32, math.log(0.01), math.log(100.0))), 0.01, 100.0)
    return dict(saved_heat_state=saved_heat_state, forward_motion=forward_motion, dual_heat_after=dual_heat_after, rheology_class=rheology_class, class_base_stiffness=class_base_stiffness)


INCREMENT_DT = 0.2
DIFFUSIVITY = 0.3
ACTIVATION_ENERGY = 2.3
JACOBI_WEIGHT = 0.7
SCHUR_WEIGHT = 0.5
RAYLEIGH = 1.0


def widen_boxes(field):
    return jnp.pad(field, [(0, 0)] * (field.ndim - 3) + [(1, 1)] * 3)


def neighbours(bordered_array):
    centre = bordered_array[..., 1:-1, 1:-1, 1:-1]
    beside_all = [bordered_array[..., 2:, 1:-1, 1:-1], bordered_array[..., :-2, 1:-1, 1:-1],
              bordered_array[..., 1:-1, 2:, 1:-1], bordered_array[..., 1:-1, :-2, 1:-1],
              bordered_array[..., 1:-1, 1:-1, 2:], bordered_array[..., 1:-1, 1:-1, :-2]]
    return centre, beside_all


def march_backward(bordered_array, shallower_adjacent, deeper_adjacent):
    centre, beside_all = neighbours(bordered_array)
    drift = 0.0
    for dim_index in range(3):
        drift = drift + shallower_adjacent[dim_index] * (centre - beside_all[2 * dim_index + 1]) + deeper_adjacent[dim_index] * (beside_all[2 * dim_index] - centre)
    spread = sum(beside_all) - 6.0 * centre
    return centre - INCREMENT_DT * drift + INCREMENT_DT * DIFFUSIVITY * spread


def motion_source(bordered_heat, forward_motion, dual_heat_after):
    centre, beside_all = neighbours(bordered_heat)
    device_pieces = [jnp.where(forward_motion[dim_index] > 0, centre - beside_all[2 * dim_index + 1], beside_all[2 * dim_index] - centre) for dim_index in range(3)]
    return -INCREMENT_DT * dual_heat_after[None] * jnp.stack(device_pieces)


def advect_dual_heat(pos_padded, neg_padded, lam_padded):
    centre, beside_all = neighbours(lam_padded)
    result = centre + INCREMENT_DT * DIFFUSIVITY * (sum(beside_all) - 6.0 * centre)
    for dim_index in range(3):
        pos_centre, pos_around = neighbours(pos_padded[dim_index])
        neg_centre, neg_around = neighbours(neg_padded[dim_index])
        result = result - INCREMENT_DT * (pos_centre - pos_around[2 * dim_index] + neg_around[2 * dim_index + 1] - neg_centre)
    return result


def coefficients(bordered_array, factor):
    centre, beside_all = neighbours(bordered_array)
    return [factor * (0.5 * (centre + other)) for other in beside_all]


def apply_operator(face_coef, bordered_array):
    centre, beside_all = neighbours(bordered_array)
    return sum(coef * (centre - other) for coef, other in zip(face_coef, beside_all))


def gradient(bordered_array):
    centre, beside_all = neighbours(bordered_array)
    return jnp.stack([0.5 * (beside_all[2 * dim_index] - beside_all[2 * dim_index + 1]) for dim_index in range(3)])


def divergence(bordered_array):
    centre, beside_all = neighbours(bordered_array)
    return sum(0.5 * (beside_all[2 * dim_index][dim_index] - beside_all[2 * dim_index + 1][dim_index]) for dim_index in range(3))


def restrict(field):
    leading = field.shape[:-3]
    cells_x, cells_y, cells_z = field.shape[-3:]
    blocks = field.reshape(leading + (cells_x // 2, 2, cells_y // 2, 2, cells_z // 2, 2))
    return blocks.mean(axis=(-5, -3, -1))


def prolong(field):
    return jnp.repeat(jnp.repeat(jnp.repeat(field, 2, axis=-3), 2, axis=-2), 2, axis=-1)


def evaluate_viscosity(rheology_class, class_base_stiffness):
    base = jnp.zeros(rheology_class.shape, jnp.float32)
    for layer_index in range(LAYERS):
        base = base + jnp.where(rheology_class == layer_index, class_base_stiffness[layer_index], 0.0)
    return base


def reference(saved_heat_state, forward_motion, dual_heat_after, rheology_class, class_base_stiffness):
    shallower_adjacent = jnp.maximum(forward_motion, 0.0)
    deeper_adjacent = jnp.minimum(forward_motion, 0.0)
    heat_state = saved_heat_state
    for repeat_index in range(RECOMPUTE):
        heat_state = march_backward(widen_boxes(heat_state), shallower_adjacent, deeper_adjacent)
    local_viscosity = evaluate_viscosity(rheology_class, class_base_stiffness) * jnp.exp(-ACTIVATION_ENERGY * heat_state)
    driving_source = motion_source(widen_boxes(heat_state), forward_motion, dual_heat_after)
    advected_result = advect_dual_heat(widen_boxes(shallower_adjacent * dual_heat_after[None]), widen_boxes(deeper_adjacent * dual_heat_after[None]), widen_boxes(dual_heat_after))
    face_coef = coefficients(widen_boxes(local_viscosity), 1.0)
    diagonal = sum(face_coef)
    coarse_coef = coefficients(widen_boxes(restrict(local_viscosity)), 0.25)
    coarse_diag = sum(coarse_coef)
    total_cells = GRID_WIDTH * GRID_BREADTH * GRID_HEIGHT
    velocity = jnp.zeros(forward_motion.shape, jnp.float32)
    mean_stress = jnp.zeros(saved_heat_state.shape, jnp.float32)
    for iteration in range(SCHUR_ITERS):
        if iteration == 0:
            residual = driving_source
        else:
            residual = driving_source - apply_operator(face_coef, widen_boxes(velocity)) - gradient(widen_boxes(mean_stress))
        correction = JACOBI_WEIGHT * residual / diagonal
        residual_two = residual - apply_operator(face_coef, widen_boxes(correction))
        coarse_res = restrict(residual_two)
        coarse_corr = JACOBI_WEIGHT * coarse_res / coarse_diag
        for sweep in range(COARSE_SWEEPS - 1):
            coarse_corr = coarse_corr + JACOBI_WEIGHT * (coarse_res - apply_operator(coarse_coef, widen_boxes(coarse_corr))) / coarse_diag
        correction = correction + prolong(coarse_corr)
        correction = correction + JACOBI_WEIGHT * (residual - apply_operator(face_coef, widen_boxes(correction))) / diagonal
        velocity = velocity + correction
        mean_stress = mean_stress - SCHUR_WEIGHT * local_viscosity * divergence(widen_boxes(velocity))
        mean_stress = mean_stress - jnp.sum(mean_stress) / total_cells
    adj_temp_prev = advected_result + RAYLEIGH * velocity[2]
    return (adj_temp_prev, velocity, mean_stress)
```

```python
import functools

import jax
import jax.numpy as jnp
from jax import lax
from jax.experimental import pallas as pl
from jax.experimental.pallas import tpu as pltpu
from jax.sharding import PartitionSpec as P

RECOMPUTE = 2
SCHUR_ITERS = 4
COARSE_SWEEPS = 3
LAYERS = 8


INCREMENT_DT = 0.2
DIFFUSIVITY = 0.3
ACTIVATION_ENERGY = 2.3
JACOBI_WEIGHT = 0.7
SCHUR_WEIGHT = 0.5
RAYLEIGH = 1.0


def extended(block, sides, width):
    for axis, dim in sides:
        count = lax.axis_size(axis)
        forward = [(i, i + 1) for i in range(count - 1)]
        backward = [(target, source) for source, target in forward]
        low = lax.ppermute(
            lax.slice_in_dim(block, block.shape[dim] - width, None, axis=dim), axis, forward
        )
        high = lax.ppermute(lax.slice_in_dim(block, 0, width, axis=dim), axis, backward)
        block = jnp.concatenate([low, block, high], axis=dim)
    return block


def neighbours(bordered_array):
    centre = bordered_array[..., 1:-1, 1:-1, 1:-1]
    beside_all = [
        bordered_array[..., 2:, 1:-1, 1:-1],
        bordered_array[..., :-2, 1:-1, 1:-1],
        bordered_array[..., 1:-1, 2:, 1:-1],
        bordered_array[..., 1:-1, :-2, 1:-1],
        bordered_array[..., 1:-1, 1:-1, 2:],
        bordered_array[..., 1:-1, 1:-1, :-2],
    ]
    return (centre, beside_all)


def finest_halo_cells(field):
    return extended(field, (("gx", 1), ("gy", 2), ("gz", 3)), 1)


def deep_halo(field):
    return extended(field, (("gx", 1), ("gy", 2), ("gz", 3)), 2)


def coarse_halo(field):
    return extended(field, (("gx", 1), ("gy", 2), ("gz", 3)), 1)


def march_backward(bordered_array, shallower_adjacent, deeper_adjacent):
    centre, beside_all = neighbours(bordered_array)
    drift = 0.0
    for dim_index in range(3):
        drift = (
            drift
            + shallower_adjacent[dim_index] * (centre - beside_all[2 * dim_index + 1])
            + deeper_adjacent[dim_index] * (beside_all[2 * dim_index] - centre)
        )
    spread = sum(beside_all) - 6.0 * centre
    return centre - INCREMENT_DT * drift + INCREMENT_DT * DIFFUSIVITY * spread


def motion_source(bordered_heat, forward_motion, dual_heat_after):
    centre, beside_all = neighbours(bordered_heat)
    device_pieces = [
        jnp.where(
            forward_motion[dim_index] > 0,
            centre - beside_all[2 * dim_index + 1],
            beside_all[2 * dim_index] - centre,
        )
        for dim_index in range(3)
    ]
    return -INCREMENT_DT * dual_heat_after[None] * jnp.stack(device_pieces)


def advect_dual_heat(pos_padded, neg_padded, lam_padded):
    centre, beside_all = neighbours(lam_padded)
    result = centre + INCREMENT_DT * DIFFUSIVITY * (sum(beside_all) - 6.0 * centre)
    for dim_index in range(3):
        pos_centre, pos_around = neighbours(pos_padded[dim_index])
        neg_centre, neg_around = neighbours(neg_padded[dim_index])
        result = result - INCREMENT_DT * (
            pos_centre - pos_around[2 * dim_index] + neg_around[2 * dim_index + 1] - neg_centre
        )
    return result


def coefficients(bordered_array, factor):
    centre, beside_all = neighbours(bordered_array)
    return [factor * (0.5 * (centre + other)) for other in beside_all]


def apply_operator(face_coef, bordered_array):
    centre, beside_all = neighbours(bordered_array)
    return sum((coef * (centre - other) for coef, other in zip(face_coef, beside_all)))


def gradient(bordered_array):
    centre, beside_all = neighbours(bordered_array)
    return jnp.stack(
        [
            0.5 * (beside_all[2 * dim_index] - beside_all[2 * dim_index + 1])
            for dim_index in range(3)
        ]
    )


def divergence(bordered_array):
    centre, beside_all = neighbours(bordered_array)
    return sum(
        (
            0.5 * (beside_all[2 * dim_index][dim_index] - beside_all[2 * dim_index + 1][dim_index])
            for dim_index in range(3)
        )
    )


def restrict(field):
    leading = field.shape[:-3]
    cells_x, cells_y, cells_z = field.shape[-3:]
    blocks = field.reshape(leading + (cells_x // 2, 2, cells_y // 2, 2, cells_z // 2, 2))
    return blocks.mean(axis=(-5, -3, -1))


def prolong(field):
    return jnp.repeat(jnp.repeat(jnp.repeat(field, 2, axis=-3), 2, axis=-2), 2, axis=-1)


def evaluate_viscosity(rheology_class, class_base_stiffness):
    base = jnp.zeros(rheology_class.shape, jnp.float32)
    for layer_index in range(LAYERS):
        base = base + jnp.where(
            rheology_class == layer_index, class_base_stiffness[layer_index], 0.0
        )
    return base


def inside_mask(extent_first, extent_second, extent_vertical):
    index_x = (
        lax.axis_index("gx") * extent_first + jnp.arange(extent_first + 2, dtype=jnp.int32) - 1
    )
    index_y = (
        lax.axis_index("gy") * extent_second + jnp.arange(extent_second + 2, dtype=jnp.int32) - 1
    )
    index_z = (
        lax.axis_index("gz") * extent_vertical
        + jnp.arange(extent_vertical + 2, dtype=jnp.int32)
        - 1
    )
    inside_x = (index_x >= 0) & (index_x < extent_first * lax.axis_size("gx"))
    inside_y = (index_y >= 0) & (index_y < extent_second * lax.axis_size("gy"))
    inside_z = (index_z >= 0) & (index_z < extent_vertical * lax.axis_size("gz"))
    return inside_x[:, None, None] & inside_y[None, :, None] & inside_z[None, None, :]


def coarse_solve(coarse_res, coarse_coef, coarse_diag, pad_field):
    coarse_corr = JACOBI_WEIGHT * coarse_res / coarse_diag
    for sweep in range(COARSE_SWEEPS - 1):
        coarse_corr = (
            coarse_corr
            + JACOBI_WEIGHT
            * (coarse_res - apply_operator(coarse_coef, pad_field(coarse_corr)))
            / coarse_diag
        )
    return coarse_corr


def shards(saved_heat_state, forward_motion, dual_heat_after, rheology_class, class_base_stiffness):
    extent_first, extent_second, extent_vertical = saved_heat_state.shape
    shallower_adjacent = jnp.maximum(forward_motion, 0.0)
    deeper_adjacent = jnp.minimum(forward_motion, 0.0)
    heat_state = saved_heat_state
    for repeat_index in range(RECOMPUTE):
        heat_state = march_backward(
            finest_halo_cells(heat_state[None])[0], shallower_adjacent, deeper_adjacent
        )
    local_viscosity = evaluate_viscosity(rheology_class, class_base_stiffness) * jnp.exp(
        -ACTIVATION_ENERGY * heat_state
    )
    stacked = jnp.concatenate(
        [
            heat_state[None],
            dual_heat_after[None],
            shallower_adjacent * dual_heat_after[None],
            deeper_adjacent * dual_heat_after[None],
            local_viscosity[None],
        ],
        0,
    )
    bordered_array = finest_halo_cells(stacked)
    driving_source = motion_source(bordered_array[0], forward_motion, dual_heat_after)
    advected_result = advect_dual_heat(bordered_array[2:5], bordered_array[5:8], bordered_array[1])
    face_coef = coefficients(bordered_array[8], 1.0)
    diagonal = sum(face_coef)
    coarse_visc = restrict(local_viscosity)
    coarse_coef = coefficients(coarse_halo(coarse_visc[None])[0], 0.25)
    coarse_diag = sum(coarse_coef)
    deep_static = deep_halo(jnp.concatenate([local_viscosity[None], driving_source], 0))
    cycle_coef = coefficients(deep_static[0], 1.0)
    cycle_source = deep_static[1:4, 1:-1, 1:-1, 1:-1]
    inside = inside_mask(extent_first, extent_second, extent_vertical)
    safe_diag = jnp.where(inside, sum(cycle_coef), 1.0)
    total_cells = (
        extent_first
        * extent_second
        * extent_vertical
        * lax.axis_size("gx")
        * lax.axis_size("gy")
        * lax.axis_size("gz")
    )
    velocity = jnp.zeros(forward_motion.shape, jnp.float32)
    mean_stress = jnp.zeros(saved_heat_state.shape, jnp.float32)
    for iteration in range(SCHUR_ITERS):
        if iteration == 0:
            cycle_resid = cycle_source
        else:
            flow_press = deep_halo(jnp.concatenate([velocity, mean_stress[None]], 0))
            cycle_resid = (
                cycle_source - apply_operator(cycle_coef, flow_press[0:3]) - gradient(flow_press[3])
            )
        cycle_corr = jnp.where(inside, JACOBI_WEIGHT * cycle_resid / safe_diag, 0.0)
        residual = cycle_resid[:, 1:-1, 1:-1, 1:-1]
        correction = cycle_corr[:, 1:-1, 1:-1, 1:-1]
        residual_two = residual - apply_operator(face_coef, cycle_corr)
        coarse_res = restrict(residual_two)
        coarse_corr = coarse_solve(coarse_res, coarse_coef, coarse_diag, coarse_halo)
        correction = correction + prolong(coarse_corr)
        correction = (
            correction
            + JACOBI_WEIGHT
            * (residual - apply_operator(face_coef, finest_halo_cells(correction)))
            / diagonal
        )
        velocity = velocity + correction
        spread_flow = divergence(finest_halo_cells(velocity))
        mean_stress = mean_stress - SCHUR_WEIGHT * local_viscosity * spread_flow
        mean_stress = mean_stress - lax.psum(jnp.sum(mean_stress), ("gx", "gy", "gz")) / total_cells
    adj_temp_prev = advected_result + RAYLEIGH * velocity[2]
    return (adj_temp_prev, velocity, mean_stress)


SUB = 8
LANES = 128
FIELDS = 6
EDGE = 2
PHASE = 8
VMEM_LIMIT = 48 * 1024 * 1024


def slab_plan_fits(mesh, shape):
    sizes = mesh.shape
    group = sizes["gx"] * sizes["gy"]
    block = (shape[0] // sizes["gx"], shape[1] // sizes["gy"], shape[2] // sizes["gz"])
    return (
        group == SUB
        and block[0] == SUB
        and block[0] * block[1] == LANES
        and block[1] * group == LANES
        and block[2] == LANES
        and block[2] == group * 2 * PHASE
    )


class Slabs:
    def __init__(self, mesh, shape):
        self.nx, self.ny, self.nz = mesh.shape["gx"], mesh.shape["gy"], mesh.shape["gz"]
        self.group = self.nx * self.ny
        self.width, self.breadth, self.height = shape
        self.block_x, self.block_y, self.block_z = (
            shape[0] // self.nx,
            shape[1] // self.ny,
            shape[2] // self.nz,
        )
        self.slab = self.block_z // self.group
        self.halo = self.slab + EDGE
        self.layers = self.slab + 2 * self.halo
        self.cells = self.width * self.breadth * self.height
        self.place = []
        for ix in range(self.nx):
            for iy in range(self.ny):
                step = ix if iy % 2 == 0 else self.nx - 1 - ix
                self.place.append(iy * self.nx + step)
        self.holder = [self.place.index(j) for j in range(self.group)]

    def device(self, slab):
        return self.holder[slab % self.group] * self.nz + slab // self.group

    def shifts(self, distance):
        count = self.group * self.nz
        return [
            (self.device(p), self.device(p + distance))
            for p in range(count)
            if 0 <= p + distance < count
        ]

    def index(self):
        ix, iy = lax.axis_index("gx"), lax.axis_index("gy")
        step = jnp.where(iy % 2 == 0, ix, self.nx - 1 - ix)
        return lax.axis_index("gz") * self.group + iy * self.nx + step


def tile_iota():
    s = lax.broadcasted_iota(jnp.int32, (1, SUB, LANES), 1)
    l = lax.broadcasted_iota(jnp.int32, (1, SUB, LANES), 2)
    return s, l


def swap_granules(tiles, granule):
    lane = lax.broadcasted_iota(jnp.int32, (SUB, LANES), 1) // granule
    for bit in (1, 2, 4):
        low = (lane & bit) == 0
        new = list(tiles)
        for a in range(SUB):
            if a & bit:
                continue
            b = a | bit
            new[a] = jnp.where(low, tiles[a], pltpu.roll(tiles[b], granule * bit, 1))
            new[b] = jnp.where(low, pltpu.roll(tiles[a], LANES - granule * bit, 1), tiles[b])
        tiles = new
    return tiles


class Tiles:
    def __init__(self, breadth):
        self.breadth = breadth
        self.s, self.l = tile_iota()
        self.x = (self.l // breadth) * SUB + self.s
        self.y = self.l % breadth
        self.width = SUB * (LANES // breadth)

    def xs(self, f, d):
        t = pltpu.roll(f, (-d) % SUB, 1)
        u = pltpu.roll(t, (-self.breadth if d > 0 else self.breadth) % LANES, 2)
        crosses = (self.s >= SUB - d) if d > 0 else (self.s < -d)
        return jnp.where(crosses, u, t)

    def ys(self, f, d):
        return pltpu.roll(f, (-d) % LANES, 2)

    def masks(self, d, value):
        keep = (
            self.x < self.width - d,
            self.x >= d,
            self.y < self.breadth - d,
            self.y >= d,
        )
        return [jnp.where(k, jnp.float32(value), jnp.float32(0.0)) for k in keep]

    def four(self, f, d):
        return [self.xs(f, d), self.xs(f, -d), self.ys(f, d), self.ys(f, -d)]

    def block_sum(self, f):
        f = f + jnp.where(self.l % 2 == 0, pltpu.roll(f, LANES - 1, 2), pltpu.roll(f, 1, 2))
        return f + jnp.where(self.s % 2 == 0, pltpu.roll(f, SUB - 1, 1), pltpu.roll(f, 1, 1))


def get(ref, i, n, *lead):
    return ref[(*lead, pl.ds(pl.multiple_of(i * SUB, SUB), n * SUB), slice(None))].reshape(
        n, SUB, LANES
    )


def put(ref, i, value, *lead):
    n = value.shape[0]
    ref[(*lead, pl.ds(pl.multiple_of(i * SUB, SUB), n * SUB), slice(None))] = value.reshape(
        n * SUB, LANES
    )


def sweep(lo, hi, n, body):
    assert (hi - lo) % n == 0
    lax.fori_loop(0, (hi - lo) // n, lambda t, _: (body(lo + t * n), 0)[1], 0)


def pack_kernel(geo, heat, flow, dual, kind, out):
    b, e = geo.slab, EDGE
    flat = [heat[...], flow[0], flow[1], flow[2], dual[...], kind[...].astype(jnp.float32)]
    turned = [f.reshape(LANES, LANES).T for f in flat]
    for j in range(geo.group):
        q = geo.holder[j]
        for f in range(FIELDS):
            out[q, f * b : (f + 1) * b, :] = turned[f][j * b : (j + 1) * b]
        tail = FIELDS * b
        first = jnp.concatenate([turned[f][j * b : j * b + e] for f in range(4)], 0)
        last = jnp.concatenate([turned[f][(j + 1) * b - e : (j + 1) * b] for f in range(4)], 0)
        out[q, tail : tail + SUB, :] = first
        out[q, tail + SUB : tail + 2 * SUB, :] = last


STATIC_FINE = ("s0", "s1", "s2", "visc", "w", "diag", "cxp", "cxm", "cyp", "cym", "cz")
STATIC_COARSE = ("kxp", "kxm", "kyp", "kym", "kzp", "kzm")


def iterate(geo, st, v, p, res, cor, cor2, cc0, cc1, seqs, lo, hi, first):
    tl = Tiles(geo.breadth)
    half = tl.masks(1, 0.5)
    comps = [3 * q + k for q in seqs for k in range(3)]
    keep = 1.0 - JACOBI_WEIGHT

    def faces(i, n):
        c = [get(st[name], i, n) for name in ("cxp", "cxm", "cyp", "cym")]
        return c, get(st["cz"], i, n), get(st["cz"], i - 1, n)

    def around(coef, ref, i, n, *lead):
        (c, up, down) = coef
        f = get(ref, i, n, *lead)
        total = up * get(ref, i + 1, n, *lead) + down * get(ref, i - 1, n, *lead)
        for a, b in zip(c, tl.four(f, 1)):
            total = total + a * b
        return f, total

    def residual(i):
        n = 4
        coef = None if first else faces(i, n)
        w = get(st["w"], i, n)
        for q in seqs:
            if not (first and q == 0):
                pq = get(p, i, n, q)
                xp, xm, yp, ym = tl.four(pq, 1)
                slope = [
                    half[0] * xp - half[1] * xm,
                    half[2] * yp - half[3] * ym,
                    0.5 * (get(p, i + 1, n, q) - get(p, i - 1, n, q)),
                ]
            for k in range(3):
                value = get(st["s%d" % k], i, n) if q == 0 else None
                if not (first and q == 0):
                    value = -slope[k] if value is None else value - slope[k]
                if not first:
                    f, total = around(coef, v, i, n, 3 * q + k)
                    value = value - (get(st["diag"], i, n) * f - total)
                put(res, i, value, 3 * q + k)
                put(cor, i, w * value, 3 * q + k)

    sweep(lo - 8, hi + 8, 4, residual)

    def restricted(i):
        m = 1
        pair = i // 2
        coef = faces(i, 2 * m)
        for c in comps:
            _, total = around(coef, cor, i, 2 * m, c)
            left = keep * get(res, i, 2 * m, c) + total
            left = tl.block_sum(left.reshape(m, 2, SUB, LANES).sum(1))
            put(cc0, pair, get(st["wc"], pair, m) * 0.125 * left, c)

    sweep(lo - 6, hi + 6, 2, restricted)

    def coarse_step(src, c, pair, m):
        f = get(src, pair, m, c)
        value = get(cc0, pair, m, c) + keep * f
        value = value + get(st["kzp"], pair, m) * get(src, pair + 1, m, c)
        value = value + get(st["kzm"], pair, m) * get(src, pair - 1, m, c)
        for name, b in zip(("kxp", "kxm", "kyp", "kym"), tl.four(f, 2)):
            value = value + get(st[name], pair, m) * b
        return value

    def sweep_one(pair):
        for c in comps:
            put(cc1, pair, coarse_step(cc0, c, pair, 2), c)

    sweep((lo - 4) // 2, (hi + 4) // 2, 2, sweep_one)

    def sweep_two(pair):
        for c in comps:
            value = coarse_step(cc1, c, pair, 2)
            fine = jnp.broadcast_to(value[:, None], (2, 2, SUB, LANES)).reshape(4, SUB, LANES)
            put(cor2, 2 * pair, get(cor, 2 * pair, 4, c) + fine, c)

    sweep((lo - 2) // 2, (hi + 2) // 2, 2, sweep_two)

    def velocity(i):
        n = 4
        coef = faces(i, n)
        w = get(st["w"], i, n)
        for c in comps:
            f, total = around(coef, cor2, i, n, c)
            value = get(cor, i, n, c) + keep * f + w * total
            if not first:
                value = get(v, i, n, c) + value
            put(v, i, value, c)

    sweep(lo - 2, hi + 2, 4, velocity)

    def pressure(i):
        n = 4
        visc = SCHUR_WEIGHT * get(st["visc"], i, n)
        for q in seqs:
            a, b = get(v, i, n, 3 * q), get(v, i, n, 3 * q + 1)
            div = half[0] * tl.xs(a, 1) - half[1] * tl.xs(a, -1)
            div = div + half[2] * tl.ys(b, 1) - half[3] * tl.ys(b, -1)
            div = div + 0.5 * (get(v, i + 1, n, 3 * q + 2) - get(v, i - 1, n, 3 * q + 2))
            if first and q == 0:
                put(p, i, -(visc * div), q)
            else:
                put(p, i, get(p, i, n, q) - visc * div, q)

    sweep(lo, hi, 4, pressure)


def slab_total(geo, p, q):
    own = get(p, geo.halo, geo.slab, q)
    return jnp.sum(jnp.sum(own, axis=0), axis=(0, 1), keepdims=True)


def in_lanes(values, rows):
    lane = lax.broadcasted_iota(jnp.int32, (rows, LANES), 1)
    out = jnp.zeros((rows, LANES), jnp.float32)
    for k, value in values:
        out = jnp.where(lane == k, value, out)
    return out


def first_kernel(geo, stiffness, own, low, high, low_edge, high_edge, *refs):
    names = STATIC_FINE + STATIC_COARSE + ("wc",)
    st = dict(zip(names, refs[: len(names)]))
    moved, state, message_down, message_up, response, sums, raw, spare, heat, vc, *work = refs[
        len(names) :
    ]
    v, p, res, cor, cor2, cc0, cc1 = work
    tl = Tiles(geo.breadth)
    b, h, n_layers = geo.slab, geo.halo, geo.layers
    granule = geo.block_y

    for source, base in ((low, EDGE), (own, h), (high, h + b)):

        def place(t, _, source=source, base=base):
            f, d = t // (b // SUB), (t % (b // SUB)) * SUB
            row = pl.multiple_of(f * b + d, SUB)
            tiles = [source[q, pl.ds(row, SUB), :] for q in range(geo.group)]
            start = (f * n_layers + base + d) * SUB
            for s, tile in enumerate(swap_granules(tiles, granule)):
                raw[pl.ds(start + s, SUB, stride=SUB), :] = tile
            return 0

        lax.fori_loop(0, FIELDS * (b // SUB), place, 0)
    for source, base in ((low_edge, 0), (high_edge, n_layers - EDGE)):
        tiles = [source[q] for q in range(geo.group)]
        for s, tile in enumerate(swap_granules(tiles, granule)):
            spare[pl.ds(s, SUB, stride=SUB), :] = tile
        for f in range(4):
            start = (f * n_layers + base) * SUB
            raw[start : start + EDGE * SUB, :] = spare[f * EDGE * SUB : (f + 1) * EDGE * SUB, :]

    def field(f, i, n):
        return get(raw, f * n_layers + i, n)

    first_layer = geo.index() * b - h

    def inside(i, n):
        layer = first_layer + i + lax.broadcasted_iota(jnp.int32, (n, 1, 1), 0)
        return (layer >= 0) & (layer < geo.height)

    one = tl.masks(1, 1.0)

    def masked_four(f):
        return [m * g for m, g in zip(one, tl.four(f, 1))]

    def advance(old, new):
        def body(i):
            n = 2
            f = old(i, n)
            beside = masked_four(f) + [old(i + 1, n), old(i - 1, n)]
            drift = 0.0
            for k in range(3):
                flow = field(1 + k, i, n)
                drift = drift + jnp.maximum(flow, 0.0) * (f - beside[2 * k + 1])
                drift = drift + jnp.minimum(flow, 0.0) * (beside[2 * k] - f)
            spread = sum(beside) - 6.0 * f
            value = f - INCREMENT_DT * drift + INCREMENT_DT * DIFFUSIVITY * spread
            put(heat, i, jnp.where(inside(i, n), value, 0.0), new)

        return body

    sweep(1, n_layers - 1, 2, advance(lambda i, n: field(0, i, n), 0))
    sweep(2, n_layers - 2, 2, advance(lambda i, n: get(heat, i, n, 0), 1))

    def viscosity(i):
        n = 2
        kind = field(5, i, n)
        base = jnp.zeros(kind.shape, jnp.float32)
        for layer in range(LAYERS):
            base = base + jnp.where(kind == float(layer), stiffness[layer], 0.0)
        value = base * jnp.exp(-ACTIVATION_ENERGY * get(heat, i, n, 1))
        value = jnp.where(inside(i, n), value, 0.0)
        put(st["visc"], i, value)
        put(vc, i // 2, 0.125 * tl.block_sum(value[0:1] + value[1:2]))

    sweep(2, n_layers - 2, 2, viscosity)

    def statics(i):
        n = 2
        c = get(st["visc"], i, n)
        beside = masked_four(c) + [get(st["visc"], i + 1, n), get(st["visc"], i - 1, n)]
        face = [0.5 * (c + o) for o in beside]
        diag = sum(face)
        for name, m, f in zip(("cxp", "cxm", "cyp", "cym"), one, face):
            put(st[name], i, m * f)
        put(st["cz"], i, face[4])
        put(st["diag"], i, diag)
        put(st["w"], i, jnp.where(inside(i, n), JACOBI_WEIGHT / diag, 0.0))
        f = get(heat, i, n, 1)
        beside = masked_four(f) + [get(heat, i + 1, n, 1), get(heat, i - 1, n, 1)]
        dual = -INCREMENT_DT * field(4, i, n)
        for k in range(3):
            flow = field(1 + k, i, n)
            step = jnp.where(flow > 0, f - beside[2 * k + 1], beside[2 * k] - f)
            put(st["s%d" % k], i, dual * step)

    sweep(2, n_layers - 2, 2, statics)

    two = tl.masks(2, 1.0)

    def coarse_statics(pair):
        n = 1
        c = get(vc, pair, n)
        beside = [m * g for m, g in zip(two, tl.four(c, 2))]
        beside = beside + [get(vc, pair + 1, n), get(vc, pair - 1, n)]
        face = [0.25 * (0.5 * (c + o)) for o in beside]
        wc = JACOBI_WEIGHT / sum(face)
        wc = jnp.where(inside(2 * pair, 1), wc, 0.0)
        put(st["wc"], pair, wc)
        for name, m, f in zip(STATIC_COARSE, two + [1.0, 1.0], face):
            put(st[name], pair, wc * (m * f))

    sweep(1, n_layers // 2 - 1, 1, coarse_statics)

    def transport(i):
        n = 2
        dual = field(4, i, n)
        up, down = field(4, i + 1, n), field(4, i - 1, n)
        value = dual + INCREMENT_DT * DIFFUSIVITY * (
            sum(masked_four(dual)) + up + down - 6.0 * dual
        )
        for k in range(3):
            a = jnp.maximum(field(1 + k, i, n), 0.0) * dual
            c = jnp.minimum(field(1 + k, i, n), 0.0) * dual
            if k == 0:
                ahead, behind = one[0] * tl.xs(a, 1), one[1] * tl.xs(c, -1)
            elif k == 1:
                ahead, behind = one[2] * tl.ys(a, 1), one[3] * tl.ys(c, -1)
            else:
                ahead = jnp.maximum(field(3, i + 1, n), 0.0) * up
                behind = jnp.minimum(field(3, i - 1, n), 0.0) * down
            value = value - INCREMENT_DT * (a - ahead + behind - c)
        put(moved, i - h, value)

    sweep(h, h + b, 2, transport)

    def unit(i):
        put(p, i, jnp.broadcast_to(jnp.where(inside(i, 4), 1.0, 0.0), (4, SUB, LANES)), 1)

    sweep(0, n_layers, 4, unit)

    work = (v, p, res, cor, cor2, cc0, cc1)
    iterate(geo, st, *work, (0, 1), h - PHASE, h + b + PHASE, True)
    totals = [slab_total(geo, p, 0), slab_total(geo, p, 1)]
    for k in range(3):
        put(response, 0, get(v, h, b, 3 + k), k)
    put(response, 0, get(p, h, b, 1), 3)
    iterate(geo, st, *work, (0, 1), h, h + b, False)
    totals += [slab_total(geo, p, 0), slab_total(geo, p, 1)]
    sums[...] = in_lanes(enumerate(totals), SUB)
    for q in range(2):
        for k in range(4):
            value = get(v, h, b, 3 * q + k) if k < 3 else get(p, h, b, q)
            put(state, 0, value, 4 * q + k)
            if q == 0:
                put(message_down, k * b, value)
                put(message_up, k * b, value)
            else:
                put(message_down, 4 * b + k * PHASE, value[:PHASE])
                put(message_up, 4 * b + k * PHASE, value[b - PHASE :])


def second_kernel(geo, *refs):
    names = STATIC_FINE + STATIC_COARSE + ("wc",)
    st = dict(zip(names, refs[: len(names)]))
    state, low, high, earlier, final, sums, v, p, res, cor, cor2, cc0, cc1 = refs[len(names) :]
    b, h = geo.slab, geo.halo
    for q in range(2):
        for k in range(4):
            ref, lead = (v, 3 * q + k) if k < 3 else (p, q)
            put(ref, h, get(state, 0, b, 4 * q + k), lead)
            thick = b if q == 0 else PHASE
            at = k * b if q == 0 else 4 * b + k * PHASE
            put(ref, h - thick, get(low, at, thick), lead)
            put(ref, h + b, get(high, at, thick), lead)
    work = (v, p, res, cor, cor2, cc0, cc1)
    iterate(geo, st, *work, (0,), h - PHASE, h + b + PHASE, False)
    totals = [(4, slab_total(geo, p, 0))]
    iterate(geo, st, *work, (0, 1), h, h + b, False)
    totals += [(5, slab_total(geo, p, 0)), (6, slab_total(geo, p, 1))]
    row = in_lanes(totals, SUB) + earlier[...]
    for r in range(0, sums.shape[0], SUB):
        sums[r : r + SUB, :] = row
    for q in range(2):
        for k in range(3):
            put(final, 0, get(v, h, b, 3 * q + k), 4 * q + k)
        put(final, 0, get(p, h, b, q), 4 * q + 3)


def means(geo, sums):
    row = jnp.sum(sums, axis=0, keepdims=True) / geo.cells
    lane = lax.broadcasted_iota(jnp.int32, row.shape, 1)

    def at(k):
        return jnp.sum(jnp.where(lane == k, row, 0.0), axis=1, keepdims=True)

    s1, r1, s2, r2, s3, s4, r3 = [at(k) for k in range(7)]
    m1 = s1
    m2 = s2 - m1 * r1
    m3 = s3 - m1 * r2 - m2 * r1
    m4 = s4 - m1 * r3 - m2 * r2 - m3 * r1
    return m1, m2, m3, m4


def combine_kernel(geo, sums, final, state, response, moved, out, mixed):
    b = geo.slab
    m1, m2, m3, m4 = means(geo, sums[...])
    for k in range(4):
        value = final[k] - m1 * final[4 + k] - m2 * state[4 + k] - m3 * response[k]
        mixed[k] = value - m4 if k == 3 else value
    mixed[4] = moved[...] + mixed[2]

    def place(t, _):
        f, d = t // (b // SUB), (t % (b // SUB)) * SUB
        tiles = [mixed[f, pl.ds(d * SUB + s, SUB, stride=SUB), :] for s in range(SUB)]
        for q, tile in enumerate(swap_granules(tiles, geo.block_y)):
            out[q, pl.ds(pl.multiple_of(f * b + d, SUB), SUB), :] = tile
        return 0

    lax.fori_loop(0, 5 * (b // SUB), place, 0)


def unpack_kernel(geo, chunks, heat, flow, pressure):
    b = geo.slab
    shape = (geo.block_x, geo.block_y, geo.block_z)
    for f in range(5):
        rows = [chunks[geo.holder[j], f * b : (f + 1) * b, :] for j in range(geo.group)]
        block = jnp.concatenate(rows, 0).T.reshape(shape)
        if f < 3:
            flow[f] = block
        elif f == 3:
            pressure[...] = block
        else:
            heat[...] = block


def call(kernel, out, scratch, *args, smem=()):
    f32 = jnp.float32
    specs = [
        pl.BlockSpec(memory_space=pltpu.SMEM if i in smem else pltpu.VMEM)
        for i in range(len(args))
    ]
    return pl.pallas_call(
        kernel,
        out_shape=[jax.ShapeDtypeStruct(s, f32) for s in out],
        in_specs=specs,
        out_specs=[pl.BlockSpec(memory_space=pltpu.VMEM) for _ in out],
        scratch_shapes=[pltpu.VMEM(s, f32) for s in scratch],
        compiler_params=pltpu.CompilerParams(vmem_limit_bytes=VMEM_LIMIT),
    )(*args)


def slab_shards(geo, heat, flow, dual, kind, stiffness):
    b, n_layers, group = geo.slab, geo.layers, geo.group
    rows = FIELDS * b
    (chunks,) = call(
        functools.partial(pack_kernel, geo),
        [(group, rows + 2 * SUB, LANES)],
        [],
        heat,
        flow,
        dual,
        kind,
    )
    own = lax.all_to_all(chunks, ("gx", "gy"), 0, 0, tiled=True)
    axes = ("gx", "gy", "gz")
    low = lax.ppermute(own, axes, geo.shifts(1))
    high = lax.ppermute(own, axes, geo.shifts(-1))
    high_edge = lax.ppermute(own[:, rows : rows + SUB], axes, geo.shifts(-2))
    low_edge = lax.ppermute(own[:, rows + SUB :], axes, geo.shifts(2))

    fine, coarse = (n_layers * SUB, LANES), (n_layers // 2 * SUB, LANES)
    n_fine, n_coarse = len(STATIC_FINE), len(STATIC_COARSE) + 1
    slab = (b * SUB, LANES)
    message = ((4 * b + 4 * PHASE) * SUB, LANES)
    work = [(6, *fine), (2, *fine)] + [(6, *fine)] * 3 + [(6, *coarse)] * 2
    *static, moved, state, down, up, response, sums = call(
        functools.partial(first_kernel, geo),
        [fine] * n_fine
        + [coarse] * n_coarse
        + [slab, (8, *slab), message, message, (4, *slab), (SUB, LANES)],
        [(FIELDS * n_layers * SUB, LANES), (SUB * SUB, LANES), (2, *fine), coarse] + work,
        stiffness,
        own,
        low,
        high,
        low_edge,
        high_edge,
        smem=(0,),
    )
    from_low = lax.ppermute(up, axes, geo.shifts(1))
    from_high = lax.ppermute(down, axes, geo.shifts(-1))
    devices = group * geo.nz
    final, sums = call(
        functools.partial(second_kernel, geo),
        [(8, *slab), (devices, LANES)],
        work,
        *static,
        state,
        from_low,
        from_high,
        sums,
    )
    sums = lax.all_to_all(sums, axes, 0, 0, tiled=True)
    (chunks,) = call(
        functools.partial(combine_kernel, geo),
        [(group, 5 * b, LANES)],
        [(5, *slab)],
        sums,
        final,
        state,
        response,
        moved,
    )
    chunks = lax.all_to_all(chunks, ("gx", "gy"), 0, 0, tiled=True)
    block = (geo.block_x, geo.block_y, geo.block_z)
    return tuple(
        call(
            functools.partial(unpack_kernel, geo),
            [block, (3, *block), block],
            [],
            chunks,
        )
    )


def solution(mesh):
    in_specs = (
        P("gx", "gy", "gz"),
        P(None, "gx", "gy", "gz"),
        P("gx", "gy", "gz"),
        P("gx", "gy", "gz"),
        P(),
    )
    out_specs = (P("gx", "gy", "gz"), P(None, "gx", "gy", "gz"), P("gx", "gy", "gz"))

    def program(saved_heat_state, *others):
        shape = saved_heat_state.shape
        plan = shards
        if slab_plan_fits(mesh, shape):
            plan = functools.partial(slab_shards, Slabs(mesh, shape))
        return jax.shard_map(
            plan, mesh=mesh, in_specs=in_specs, out_specs=out_specs, check_vma=False
        )(saved_heat_state, *others)

    return program
```

```python
import functools

import jax
import jax.numpy as jnp
from jax import lax
from jax.experimental import pallas as pl
from jax.experimental.pallas import tpu as pltpu
from jax.sharding import PartitionSpec as P

RECOMPUTE = 2
SCHUR_ITERS = 4
COARSE_SWEEPS = 3
LAYERS = 8


INCREMENT_DT = 0.2
DIFFUSIVITY = 0.3
ACTIVATION_ENERGY = 2.3
JACOBI_WEIGHT = 0.7
SCHUR_WEIGHT = 0.5
RAYLEIGH = 1.0


def extended(block, sides, width):
    for axis, dim in sides:
        count = lax.axis_size(axis)
        forward = [(i, i + 1) for i in range(count - 1)]
        backward = [(target, source) for source, target in forward]
        low = lax.ppermute(
            lax.slice_in_dim(block, block.shape[dim] - width, None, axis=dim), axis, forward
        )
        high = lax.ppermute(lax.slice_in_dim(block, 0, width, axis=dim), axis, backward)
        block = jnp.concatenate([low, block, high], axis=dim)
    return block


def neighbours(bordered_array):
    centre = bordered_array[..., 1:-1, 1:-1, 1:-1]
    beside_all = [
        bordered_array[..., 2:, 1:-1, 1:-1],
        bordered_array[..., :-2, 1:-1, 1:-1],
        bordered_array[..., 1:-1, 2:, 1:-1],
        bordered_array[..., 1:-1, :-2, 1:-1],
        bordered_array[..., 1:-1, 1:-1, 2:],
        bordered_array[..., 1:-1, 1:-1, :-2],
    ]
    return (centre, beside_all)


def finest_halo_cells(field):
    return extended(field, (("gx", 1), ("gy", 2), ("gz", 3)), 1)


def deep_halo(field):
    return extended(field, (("gx", 1), ("gy", 2), ("gz", 3)), 2)


def coarse_halo(field):
    return extended(field, (("gx", 1), ("gy", 2), ("gz", 3)), 1)


def march_backward(bordered_array, shallower_adjacent, deeper_adjacent):
    centre, beside_all = neighbours(bordered_array)
    drift = 0.0
    for dim_index in range(3):
        drift = (
            drift
            + shallower_adjacent[dim_index] * (centre - beside_all[2 * dim_index + 1])
            + deeper_adjacent[dim_index] * (beside_all[2 * dim_index] - centre)
        )
    spread = sum(beside_all) - 6.0 * centre
    return centre - INCREMENT_DT * drift + INCREMENT_DT * DIFFUSIVITY * spread


def motion_source(bordered_heat, forward_motion, dual_heat_after):
    centre, beside_all = neighbours(bordered_heat)
    device_pieces = [
        jnp.where(
            forward_motion[dim_index] > 0,
            centre - beside_all[2 * dim_index + 1],
            beside_all[2 * dim_index] - centre,
        )
        for dim_index in range(3)
    ]
    return -INCREMENT_DT * dual_heat_after[None] * jnp.stack(device_pieces)


def advect_dual_heat(pos_padded, neg_padded, lam_padded):
    centre, beside_all = neighbours(lam_padded)
    result = centre + INCREMENT_DT * DIFFUSIVITY * (sum(beside_all) - 6.0 * centre)
    for dim_index in range(3):
        pos_centre, pos_around = neighbours(pos_padded[dim_index])
        neg_centre, neg_around = neighbours(neg_padded[dim_index])
        result = result - INCREMENT_DT * (
            pos_centre - pos_around[2 * dim_index] + neg_around[2 * dim_index + 1] - neg_centre
        )
    return result


def coefficients(bordered_array, factor):
    centre, beside_all = neighbours(bordered_array)
    return [factor * (0.5 * (centre + other)) for other in beside_all]


def apply_operator(face_coef, bordered_array):
    centre, beside_all = neighbours(bordered_array)
    return sum((coef * (centre - other) for coef, other in zip(face_coef, beside_all)))


def gradient(bordered_array):
    centre, beside_all = neighbours(bordered_array)
    return jnp.stack(
        [
            0.5 * (beside_all[2 * dim_index] - beside_all[2 * dim_index + 1])
            for dim_index in range(3)
        ]
    )


def divergence(bordered_array):
    centre, beside_all = neighbours(bordered_array)
    return sum(
        (
            0.5 * (beside_all[2 * dim_index][dim_index] - beside_all[2 * dim_index + 1][dim_index])
            for dim_index in range(3)
        )
    )


def restrict(field):
    leading = field.shape[:-3]
    cells_x, cells_y, cells_z = field.shape[-3:]
    blocks = field.reshape(leading + (cells_x // 2, 2, cells_y // 2, 2, cells_z // 2, 2))
    return blocks.mean(axis=(-5, -3, -1))


def prolong(field):
    return jnp.repeat(jnp.repeat(jnp.repeat(field, 2, axis=-3), 2, axis=-2), 2, axis=-1)


def evaluate_viscosity(rheology_class, class_base_stiffness):
    base = jnp.zeros(rheology_class.shape, jnp.float32)
    for layer_index in range(LAYERS):
        base = base + jnp.where(
            rheology_class == layer_index, class_base_stiffness[layer_index], 0.0
        )
    return base


def inside_mask(extent_first, extent_second, extent_vertical):
    index_x = (
        lax.axis_index("gx") * extent_first + jnp.arange(extent_first + 2, dtype=jnp.int32) - 1
    )
    index_y = (
        lax.axis_index("gy") * extent_second + jnp.arange(extent_second + 2, dtype=jnp.int32) - 1
    )
    index_z = (
        lax.axis_index("gz") * extent_vertical
        + jnp.arange(extent_vertical + 2, dtype=jnp.int32)
        - 1
    )
    inside_x = (index_x >= 0) & (index_x < extent_first * lax.axis_size("gx"))
    inside_y = (index_y >= 0) & (index_y < extent_second * lax.axis_size("gy"))
    inside_z = (index_z >= 0) & (index_z < extent_vertical * lax.axis_size("gz"))
    return inside_x[:, None, None] & inside_y[None, :, None] & inside_z[None, None, :]


def coarse_solve(coarse_res, coarse_coef, coarse_diag, pad_field):
    coarse_corr = JACOBI_WEIGHT * coarse_res / coarse_diag
    for sweep in range(COARSE_SWEEPS - 1):
        coarse_corr = (
            coarse_corr
            + JACOBI_WEIGHT
            * (coarse_res - apply_operator(coarse_coef, pad_field(coarse_corr)))
            / coarse_diag
        )
    return coarse_corr


def shards(saved_heat_state, forward_motion, dual_heat_after, rheology_class, class_base_stiffness):
    extent_first, extent_second, extent_vertical = saved_heat_state.shape
    shallower_adjacent = jnp.maximum(forward_motion, 0.0)
    deeper_adjacent = jnp.minimum(forward_motion, 0.0)
    heat_state = saved_heat_state
    for repeat_index in range(RECOMPUTE):
        heat_state = march_backward(
            finest_halo_cells(heat_state[None])[0], shallower_adjacent, deeper_adjacent
        )
    local_viscosity = evaluate_viscosity(rheology_class, class_base_stiffness) * jnp.exp(
        -ACTIVATION_ENERGY * heat_state
    )
    stacked = jnp.concatenate(
        [
            heat_state[None],
            dual_heat_after[None],
            shallower_adjacent * dual_heat_after[None],
            deeper_adjacent * dual_heat_after[None],
            local_viscosity[None],
        ],
        0,
    )
    bordered_array = finest_halo_cells(stacked)
    driving_source = motion_source(bordered_array[0], forward_motion, dual_heat_after)
    advected_result = advect_dual_heat(bordered_array[2:5], bordered_array[5:8], bordered_array[1])
    face_coef = coefficients(bordered_array[8], 1.0)
    diagonal = sum(face_coef)
    coarse_visc = restrict(local_viscosity)
    coarse_coef = coefficients(coarse_halo(coarse_visc[None])[0], 0.25)
    coarse_diag = sum(coarse_coef)
    deep_static = deep_halo(jnp.concatenate([local_viscosity[None], driving_source], 0))
    cycle_coef = coefficients(deep_static[0], 1.0)
    cycle_source = deep_static[1:4, 1:-1, 1:-1, 1:-1]
    inside = inside_mask(extent_first, extent_second, extent_vertical)
    safe_diag = jnp.where(inside, sum(cycle_coef), 1.0)
    total_cells = (
        extent_first
        * extent_second
        * extent_vertical
        * lax.axis_size("gx")
        * lax.axis_size("gy")
        * lax.axis_size("gz")
    )
    velocity = jnp.zeros(forward_motion.shape, jnp.float32)
    mean_stress = jnp.zeros(saved_heat_state.shape, jnp.float32)
    for iteration in range(SCHUR_ITERS):
        if iteration == 0:
            cycle_resid = cycle_source
        else:
            flow_press = deep_halo(jnp.concatenate([velocity, mean_stress[None]], 0))
            cycle_resid = (
                cycle_source - apply_operator(cycle_coef, flow_press[0:3]) - gradient(flow_press[3])
            )
        cycle_corr = jnp.where(inside, JACOBI_WEIGHT * cycle_resid / safe_diag, 0.0)
        residual = cycle_resid[:, 1:-1, 1:-1, 1:-1]
        correction = cycle_corr[:, 1:-1, 1:-1, 1:-1]
        residual_two = residual - apply_operator(face_coef, cycle_corr)
        coarse_res = restrict(residual_two)
        coarse_corr = coarse_solve(coarse_res, coarse_coef, coarse_diag, coarse_halo)
        correction = correction + prolong(coarse_corr)
        correction = (
            correction
            + JACOBI_WEIGHT
            * (residual - apply_operator(face_coef, finest_halo_cells(correction)))
            / diagonal
        )
        velocity = velocity + correction
        spread_flow = divergence(finest_halo_cells(velocity))
        mean_stress = mean_stress - SCHUR_WEIGHT * local_viscosity * spread_flow
        mean_stress = mean_stress - lax.psum(jnp.sum(mean_stress), ("gx", "gy", "gz")) / total_cells
    adj_temp_prev = advected_result + RAYLEIGH * velocity[2]
    return (adj_temp_prev, velocity, mean_stress)


SUB = 8
LANES = 128
FIELDS = 6
BACK = 9
EDGE = 2
PHASE = 8
VMEM_LIMIT = 48 * 1024 * 1024


def slab_plan_fits(mesh, shape):
    sizes = mesh.shape
    group = sizes["gx"] * sizes["gy"]
    block = (shape[0] // sizes["gx"], shape[1] // sizes["gy"], shape[2] // sizes["gz"])
    return (
        group == SUB
        and block[0] == SUB
        and block[0] * block[1] == LANES
        and block[1] * group == LANES
        and block[2] == LANES
        and block[2] == group * 2 * PHASE
    )


class Slabs:
    def __init__(self, mesh, shape):
        self.nx, self.ny, self.nz = mesh.shape["gx"], mesh.shape["gy"], mesh.shape["gz"]
        self.group = self.nx * self.ny
        self.width, self.breadth, self.height = shape
        self.block_x, self.block_y, self.block_z = (
            shape[0] // self.nx,
            shape[1] // self.ny,
            shape[2] // self.nz,
        )
        self.slab = self.block_z // self.group
        self.halo = self.slab + EDGE
        self.layers = self.slab + 2 * self.halo
        self.cells = self.width * self.breadth * self.height
        self.place = []
        for ix in range(self.nx):
            for iy in range(self.ny):
                step = ix if iy % 2 == 0 else self.nx - 1 - ix
                self.place.append(iy * self.nx + step)
        self.holder = [self.place.index(j) for j in range(self.group)]

    def device(self, slab):
        return self.holder[slab % self.group] * self.nz + slab // self.group

    def shifts(self, distance):
        count = self.group * self.nz
        return [
            (self.device(p), self.device(p + distance))
            for p in range(count)
            if 0 <= p + distance < count
        ]

    def index(self):
        ix, iy = lax.axis_index("gx"), lax.axis_index("gy")
        step = jnp.where(iy % 2 == 0, ix, self.nx - 1 - ix)
        return lax.axis_index("gz") * self.group + iy * self.nx + step


def tile_iota():
    s = lax.broadcasted_iota(jnp.int32, (1, SUB, LANES), 1)
    l = lax.broadcasted_iota(jnp.int32, (1, SUB, LANES), 2)
    return s, l


def swap_granules(tiles, granule):
    lane = lax.broadcasted_iota(jnp.int32, (SUB, LANES), 1) // granule
    for bit in (1, 2, 4):
        low = (lane & bit) == 0
        new = list(tiles)
        for a in range(SUB):
            if a & bit:
                continue
            b = a | bit
            new[a] = jnp.where(low, tiles[a], pltpu.roll(tiles[b], granule * bit, 1))
            new[b] = jnp.where(low, pltpu.roll(tiles[a], LANES - granule * bit, 1), tiles[b])
        tiles = new
    return tiles


class Tiles:
    def __init__(self, breadth):
        self.breadth = breadth
        self.s, self.l = tile_iota()
        self.x = (self.l // breadth) * SUB + self.s
        self.y = self.l % breadth
        self.width = SUB * (LANES // breadth)

    def xs(self, f, d):
        t = pltpu.roll(f, (-d) % SUB, 1)
        u = pltpu.roll(t, (-self.breadth if d > 0 else self.breadth) % LANES, 2)
        crosses = (self.s >= SUB - d) if d > 0 else (self.s < -d)
        return jnp.where(crosses, u, t)

    def ys(self, f, d):
        return pltpu.roll(f, (-d) % LANES, 2)

    def masks(self, d, value):
        keep = (
            self.x < self.width - d,
            self.x >= d,
            self.y < self.breadth - d,
            self.y >= d,
        )
        return [jnp.where(k, jnp.float32(value), jnp.float32(0.0)) for k in keep]

    def four(self, f, d):
        return [self.xs(f, d), self.xs(f, -d), self.ys(f, d), self.ys(f, -d)]

    def block_sum(self, f):
        f = f + jnp.where(self.l % 2 == 0, pltpu.roll(f, LANES - 1, 2), pltpu.roll(f, 1, 2))
        return f + jnp.where(self.s % 2 == 0, pltpu.roll(f, SUB - 1, 1), pltpu.roll(f, 1, 1))


def get(ref, i, n, *lead):
    return ref[(*lead, pl.ds(pl.multiple_of(i * SUB, SUB), n * SUB), slice(None))].reshape(
        n, SUB, LANES
    )


def put(ref, i, value, *lead):
    n = value.shape[0]
    ref[(*lead, pl.ds(pl.multiple_of(i * SUB, SUB), n * SUB), slice(None))] = value.reshape(
        n * SUB, LANES
    )


def sweep(lo, hi, n, body, most=4):
    count = (hi - lo) // n
    assert count * n == hi - lo
    unroll = max(u for u in range(1, most + 1) if count % u == 0)

    def step(t, _):
        todo = []
        for u in range(unroll):
            todo += body(lo + (t * unroll + u) * n)
        for ref, i, value, *lead in todo:
            put(ref, i, value, *lead)
        return 0

    lax.fori_loop(0, count // unroll, step, 0)


def regroup(source, target, granule, count, most=3):
    unroll = max(u for u in range(1, most + 1) if count % u == 0)

    def step(t, _):
        groups = [source(t * unroll + u) for u in range(unroll)]
        groups = [swap_granules(tiles, granule) for tiles in groups]
        for u in range(unroll):
            target(t * unroll + u, groups[u])
        return 0

    lax.fori_loop(0, count // unroll, step, 0)


def pack_kernel(geo, heat_in, flow_in, dual_in, kind_in, out, heat, flow, dual, kind, sems):
    b, e = geo.slab, EDGE
    pairs = ((heat_in, heat), (flow_in, flow), (dual_in, dual), (kind_in, kind))
    copies = [
        pltpu.make_async_copy(source, target, sems.at[k])
        for k, (source, target) in enumerate(pairs)
    ]
    for copy in copies:
        copy.start()
    for copy in copies:
        copy.wait()
    flat = [heat[...], flow[0], flow[1], flow[2], dual[...], kind[...].astype(jnp.float32)]
    turned = [f.reshape(LANES, LANES).T for f in flat]
    for j in range(geo.group):
        q = geo.holder[j]
        for f in range(FIELDS):
            out[q, f * b : (f + 1) * b, :] = turned[f][j * b : (j + 1) * b]
        tail = FIELDS * b
        first = jnp.concatenate([turned[f][j * b : j * b + e] for f in range(4)], 0)
        last = jnp.concatenate([turned[f][(j + 1) * b - e : (j + 1) * b] for f in range(4)], 0)
        out[q, tail : tail + SUB, :] = first
        out[q, tail + SUB : tail + 2 * SUB, :] = last


STATIC_FINE = ("s0", "s1", "s2", "visc", "w", "diag", "cxp", "cxm", "cyp", "cym", "cz")
STATIC_COARSE = ("kxp", "kxm", "kyp", "kym", "kzp", "kzm")


def iterate(geo, st, v, p, res, cor, cor2, cc0, cc1, seqs, lo, hi, first):
    tl = Tiles(geo.breadth)
    half = tl.masks(1, 0.5)
    comps = [3 * q + k for q in seqs for k in range(3)]
    keep = 1.0 - JACOBI_WEIGHT

    def faces(i, n):
        c = [get(st[name], i, n) for name in ("cxp", "cxm", "cyp", "cym")]
        return c, get(st["cz"], i, n), get(st["cz"], i - 1, n)

    def around(coef, ref, i, n, *lead):
        (c, up, down) = coef
        f = get(ref, i, n, *lead)
        total = up * get(ref, i + 1, n, *lead) + down * get(ref, i - 1, n, *lead)
        for a, b in zip(c, tl.four(f, 1)):
            total = total + a * b
        return f, total

    def residual(i):
        n, todo = 2, []
        coef = None if first else faces(i, n)
        w = get(st["w"], i, n)
        diag = None if first else get(st["diag"], i, n)
        for q in seqs:
            if not (first and q == 0):
                pq = get(p, i, n, q)
                xp, xm, yp, ym = tl.four(pq, 1)
                slope = [
                    half[0] * xp - half[1] * xm,
                    half[2] * yp - half[3] * ym,
                    0.5 * (get(p, i + 1, n, q) - get(p, i - 1, n, q)),
                ]
            for k in range(3):
                value = get(st["s%d" % k], i, n) if q == 0 else None
                if not (first and q == 0):
                    value = -slope[k] if value is None else value - slope[k]
                if not first:
                    f, total = around(coef, v, i, n, 3 * q + k)
                    value = value - (diag * f - total)
                todo += [(res, i, value, 3 * q + k), (cor, i, w * value, 3 * q + k)]
        return todo

    sweep(lo - 8, hi + 8, 2, residual)

    def restricted(i):
        pair, todo = i // 2, []
        coef = faces(i, 2)
        wc = 0.125 * get(st["wc"], pair, 1)
        for c in comps:
            _, total = around(coef, cor, i, 2, c)
            left = keep * get(res, i, 2, c) + total
            todo.append((cc0, pair, wc * tl.block_sum(left[0:1] + left[1:2]), c))
        return todo

    sweep(lo - 6, hi + 6, 2, restricted)

    def coarse_step(src, c, pair, n):
        f = get(src, pair, n, c)
        value = get(cc0, pair, n, c) + keep * f
        value = value + get(st["kzp"], pair, n) * get(src, pair + 1, n, c)
        value = value + get(st["kzm"], pair, n) * get(src, pair - 1, n, c)
        for name, b in zip(("kxp", "kxm", "kyp", "kym"), tl.four(f, 2)):
            value = value + get(st[name], pair, n) * b
        return value

    def sweep_one(pair):
        return [(cc1, pair, coarse_step(cc0, c, pair, 2), c) for c in comps]

    sweep((lo - 4) // 2, (hi + 4) // 2, 2, sweep_one)

    def sweep_two(pair):
        todo = []
        for c in comps:
            value = coarse_step(cc1, c, pair, 2)
            fine = jnp.broadcast_to(value[:, None], (2, 2, SUB, LANES)).reshape(4, SUB, LANES)
            todo.append((cor2, 2 * pair, get(cor, 2 * pair, 4, c) + fine, c))
        return todo

    sweep((lo - 2) // 2, (hi + 2) // 2, 2, sweep_two)

    def velocity(i):
        n, todo = 2, []
        coef = faces(i, n)
        w = get(st["w"], i, n)
        for c in comps:
            f, total = around(coef, cor2, i, n, c)
            value = get(cor, i, n, c) + keep * f + w * total
            if not first:
                value = get(v, i, n, c) + value
            todo.append((v, i, value, c))
        return todo

    sweep(lo - 2, hi + 2, 2, velocity)

    def pressure(i):
        n, todo = 2, []
        visc = SCHUR_WEIGHT * get(st["visc"], i, n)
        for q in seqs:
            a, b = get(v, i, n, 3 * q), get(v, i, n, 3 * q + 1)
            div = half[0] * tl.xs(a, 1) - half[1] * tl.xs(a, -1)
            div = div + half[2] * tl.ys(b, 1) - half[3] * tl.ys(b, -1)
            div = div + 0.5 * (get(v, i + 1, n, 3 * q + 2) - get(v, i - 1, n, 3 * q + 2))
            value = -(visc * div)
            todo.append((p, i, value if first and q == 0 else get(p, i, n, q) + value, q))
        return todo

    sweep(lo, hi, 2, pressure)


def slab_total(geo, p, q):
    own = get(p, geo.halo, geo.slab, q)
    return jnp.sum(jnp.sum(own, axis=0), axis=(0, 1), keepdims=True)


def in_lanes(values, rows):
    lane = lax.broadcasted_iota(jnp.int32, (rows, LANES), 1)
    out = jnp.zeros((rows, LANES), jnp.float32)
    for k, value in values:
        out = jnp.where(lane == k, value, out)
    return out


def first_kernel(geo, stiffness, own, low, high, low_edge, high_edge, *refs):
    names = STATIC_FINE + STATIC_COARSE + ("wc",)
    st = dict(zip(names, refs[: len(names)]))
    moved, state, message_down, message_up, response, sums, raw, spare, heat, vc, *work = refs[
        len(names) :
    ]
    v, p, res, cor, cor2, cc0, cc1 = work
    tl = Tiles(geo.breadth)
    b, h, n_layers = geo.slab, geo.halo, geo.layers
    granule = geo.block_y

    for source, base in ((low, EDGE), (own, h), (high, h + b)):

        def load(t, source=source):
            row = pl.multiple_of(t * SUB, SUB)
            return [source[q, pl.ds(row, SUB), :] for q in range(geo.group)]

        def store(t, tiles, base=base):
            f, d = t // (b // SUB), (t % (b // SUB)) * SUB
            start = (f * n_layers + base + d) * SUB
            for s, tile in enumerate(tiles):
                raw[pl.ds(start + s, SUB, stride=SUB), :] = tile

        regroup(load, store, granule, FIELDS * (b // SUB))
    for source, base in ((low_edge, 0), (high_edge, n_layers - EDGE)):
        tiles = [source[q] for q in range(geo.group)]
        for s, tile in enumerate(swap_granules(tiles, granule)):
            spare[pl.ds(s, SUB, stride=SUB), :] = tile
        for f in range(4):
            start = (f * n_layers + base) * SUB
            raw[start : start + EDGE * SUB, :] = spare[f * EDGE * SUB : (f + 1) * EDGE * SUB, :]

    def field(f, i, n):
        return get(raw, f * n_layers + i, n)

    first_layer = geo.index() * b - h

    def inside(i, n):
        layer = first_layer + i + lax.broadcasted_iota(jnp.int32, (n, 1, 1), 0)
        return (layer >= 0) & (layer < geo.height)

    one = tl.masks(1, 1.0)

    def masked_four(f):
        return [m * g for m, g in zip(one, tl.four(f, 1))]

    def advance(old, new):
        def body(i):
            n = 2
            f = old(i, n)
            beside = masked_four(f) + [old(i + 1, n), old(i - 1, n)]
            drift = 0.0
            for k in range(3):
                flow = field(1 + k, i, n)
                drift = drift + jnp.maximum(flow, 0.0) * (f - beside[2 * k + 1])
                drift = drift + jnp.minimum(flow, 0.0) * (beside[2 * k] - f)
            spread = sum(beside) - 6.0 * f
            value = f - INCREMENT_DT * drift + INCREMENT_DT * DIFFUSIVITY * spread
            return [(heat, i, jnp.where(inside(i, n), value, 0.0), new)]

        return body

    sweep(1, n_layers - 1, 2, advance(lambda i, n: field(0, i, n), 0), 5)
    sweep(2, n_layers - 2, 2, advance(lambda i, n: get(heat, i, n, 0), 1))

    def viscosity(i):
        n = 2
        kind = field(5, i, n)
        base = jnp.zeros(kind.shape, jnp.float32)
        for layer in range(LAYERS):
            base = base + jnp.where(kind == float(layer), stiffness[layer], 0.0)
        value = base * jnp.exp(-ACTIVATION_ENERGY * get(heat, i, n, 1))
        value = jnp.where(inside(i, n), value, 0.0)
        coarse = 0.125 * tl.block_sum(value[0:1] + value[1:2])
        return [(st["visc"], i, value), (vc, i // 2, coarse)]

    sweep(2, n_layers - 2, 2, viscosity)

    def statics(i):
        n = 2
        c = get(st["visc"], i, n)
        beside = masked_four(c) + [get(st["visc"], i + 1, n), get(st["visc"], i - 1, n)]
        face = [0.5 * (c + o) for o in beside]
        diag = sum(face)
        todo = [
            (st[name], i, m * f)
            for name, m, f in zip(("cxp", "cxm", "cyp", "cym"), one, face)
        ]
        todo += [(st["cz"], i, face[4]), (st["diag"], i, diag)]
        todo.append((st["w"], i, jnp.where(inside(i, n), JACOBI_WEIGHT / diag, 0.0)))
        f = get(heat, i, n, 1)
        beside = masked_four(f) + [get(heat, i + 1, n, 1), get(heat, i - 1, n, 1)]
        dual = -INCREMENT_DT * field(4, i, n)
        for k in range(3):
            flow = field(1 + k, i, n)
            step = jnp.where(flow > 0, f - beside[2 * k + 1], beside[2 * k] - f)
            todo.append((st["s%d" % k], i, dual * step))
        return todo

    sweep(2, n_layers - 2, 2, statics)

    two = tl.masks(2, 1.0)

    def coarse_statics(pair):
        n = 1
        c = get(vc, pair, n)
        beside = [m * g for m, g in zip(two, tl.four(c, 2))]
        beside = beside + [get(vc, pair + 1, n), get(vc, pair - 1, n)]
        face = [0.25 * (0.5 * (c + o)) for o in beside]
        wc = JACOBI_WEIGHT / sum(face)
        wc = jnp.where(inside(2 * pair, 1), wc, 0.0)
        return [(st["wc"], pair, wc)] + [
            (st[name], pair, wc * (m * f))
            for name, m, f in zip(STATIC_COARSE, two + [1.0, 1.0], face)
        ]

    sweep(1, n_layers // 2 - 1, 1, coarse_statics)

    def transport(i):
        n = 2
        dual = field(4, i, n)
        up, down = field(4, i + 1, n), field(4, i - 1, n)
        value = dual + INCREMENT_DT * DIFFUSIVITY * (
            sum(masked_four(dual)) + up + down - 6.0 * dual
        )
        for k in range(3):
            a = jnp.maximum(field(1 + k, i, n), 0.0) * dual
            c = jnp.minimum(field(1 + k, i, n), 0.0) * dual
            if k == 0:
                ahead, behind = one[0] * tl.xs(a, 1), one[1] * tl.xs(c, -1)
            elif k == 1:
                ahead, behind = one[2] * tl.ys(a, 1), one[3] * tl.ys(c, -1)
            else:
                ahead = jnp.maximum(field(3, i + 1, n), 0.0) * up
                behind = jnp.minimum(field(3, i - 1, n), 0.0) * down
            value = value - INCREMENT_DT * (a - ahead + behind - c)
        return [(moved, i - h, value)]

    sweep(h, h + b, 2, transport)

    def unit(i):
        return [(p, i, jnp.broadcast_to(jnp.where(inside(i, 4), 1.0, 0.0), (4, SUB, LANES)), 1)]

    sweep(0, n_layers, 4, unit)

    work = (v, p, res, cor, cor2, cc0, cc1)
    iterate(geo, st, *work, (0, 1), h - PHASE, h + b + PHASE, True)
    totals = [slab_total(geo, p, 0), slab_total(geo, p, 1)]
    for k in range(3):
        put(response, 0, get(v, h, b, 3 + k), k)
    put(response, 0, get(p, h, b, 1), 3)
    iterate(geo, st, *work, (0, 1), h, h + b, False)
    totals += [slab_total(geo, p, 0), slab_total(geo, p, 1)]
    sums[...] = in_lanes(enumerate(totals), 1)
    for q in range(2):
        for k in range(4):
            value = get(v, h, b, 3 * q + k) if k < 3 else get(p, h, b, q)
            put(state, 0, value, 4 * q + k)
            if q == 0:
                put(message_down, k * b, value)
                put(message_up, k * b, value)
            else:
                put(message_down, 4 * b + k * PHASE, value[:PHASE])
                put(message_up, 4 * b + k * PHASE, value[b - PHASE :])


def second_kernel(geo, *refs):
    names = STATIC_FINE + STATIC_COARSE + ("wc",)
    st = dict(zip(names, refs[: len(names)]))
    state, low, high, earlier, response, moved, out, sums, mixed, *work = refs[len(names) :]
    v, p, res, cor, cor2, cc0, cc1 = work
    b, h = geo.slab, geo.halo
    for q in range(2):
        for k in range(4):
            ref, lead = (v, 3 * q + k) if k < 3 else (p, q)
            put(ref, h, get(state, 0, b, 4 * q + k), lead)
            thick = b if q == 0 else PHASE
            at = k * b if q == 0 else 4 * b + k * PHASE
            put(ref, h - thick, get(low, at, thick), lead)
            put(ref, h + b, get(high, at, thick), lead)
    iterate(geo, st, *work, (0,), h - PHASE, h + b + PHASE, False)
    totals = [(4, slab_total(geo, p, 0))]
    iterate(geo, st, *work, (0, 1), h, h + b, False)
    totals += [(5, slab_total(geo, p, 0)), (6, slab_total(geo, p, 1))]
    sums[...] = in_lanes(totals, 1)

    m1, m2 = means(geo, earlier[...])[:2]
    for k in range(4):
        last = [get(p, h, b, q) if k == 3 else get(v, h, b, 3 * q + k) for q in range(2)]
        value = last[0] - m1 * last[1] - m2 * get(state, 0, b, 4 + k)
        put(mixed, k * b, value)
        put(mixed, (4 + k) * b, get(response, 0, b, k))
    put(mixed, 8 * b, get(moved, 0, b))

    def load(t):
        return [mixed[pl.ds(t * SUB * SUB + s, SUB, stride=SUB), :] for s in range(SUB)]

    def store(t, tiles):
        for q, tile in enumerate(tiles):
            out[q, pl.ds(pl.multiple_of(t * SUB, SUB), SUB), :] = tile

    regroup(load, store, geo.block_y, BACK * (b // SUB))


def means(geo, sums):
    row = jnp.sum(sums, axis=0, keepdims=True) / geo.cells
    lane = lax.broadcasted_iota(jnp.int32, row.shape, 1)

    def at(k):
        return jnp.sum(jnp.where(lane == k, row, 0.0), axis=1, keepdims=True)

    s1, r1, s2, r2, s3, s4, r3 = [at(k) for k in range(7)]
    m1 = s1
    m2 = s2 - m1 * r1
    m3 = s3 - m1 * r2 - m2 * r1
    m4 = s4 - m1 * r3 - m2 * r2 - m3 * r1
    return m1, m2, m3, m4


def unpack_kernel(geo, chunks, earlier, later, heat, flow, pressure):
    b = geo.slab
    shape = (geo.block_x, geo.block_y, geo.block_z)
    m3, m4 = means(geo, earlier[...] + later[...])[2:]

    def block(f):
        rows = [chunks[geo.holder[j], f * b : (f + 1) * b, :] for j in range(geo.group)]
        return jnp.concatenate(rows, 0)

    for k in range(4):
        value = block(k) - m3 * block(4 + k)
        if k == 3:
            pressure[...] = (value - m4).T.reshape(shape)
        else:
            flow[k] = value.T.reshape(shape)
        if k == 2:
            heat[...] = (block(8) + value).T.reshape(shape)


def call(kernel, out, scratch, *args, smem=(), hbm=()):
    f32 = jnp.float32
    specs = [
        pl.BlockSpec(
            memory_space=pltpu.SMEM if i in smem else pltpu.HBM if i in hbm else pltpu.VMEM
        )
        for i in range(len(args))
    ]
    return pl.pallas_call(
        kernel,
        out_shape=[jax.ShapeDtypeStruct(s, f32) for s in out],
        in_specs=specs,
        out_specs=[pl.BlockSpec(memory_space=pltpu.VMEM) for _ in out],
        scratch_shapes=[pltpu.VMEM(s, f32) if isinstance(s, tuple) else s for s in scratch],
        compiler_params=pltpu.CompilerParams(vmem_limit_bytes=VMEM_LIMIT),
    )(*args)


def slab_shards(geo, heat, flow, dual, kind, stiffness):
    b, n_layers, group = geo.slab, geo.layers, geo.group
    rows = FIELDS * b
    inputs = (heat, flow, dual, kind)
    (chunks,) = call(
        functools.partial(pack_kernel, geo),
        [(group, rows + 2 * SUB, LANES)],
        [pltpu.VMEM(a.shape, a.dtype) for a in inputs] + [pltpu.SemaphoreType.DMA((4,))],
        *inputs,
        hbm=range(4),
    )
    own = lax.all_to_all(chunks, ("gx", "gy"), 0, 0, tiled=True)
    axes = ("gx", "gy", "gz")
    low = lax.ppermute(own, axes, geo.shifts(1))
    high = lax.ppermute(own, axes, geo.shifts(-1))
    high_edge = lax.ppermute(own[:, rows : rows + SUB], axes, geo.shifts(-2))
    low_edge = lax.ppermute(own[:, rows + SUB :], axes, geo.shifts(2))

    fine, coarse = (n_layers * SUB, LANES), (n_layers // 2 * SUB, LANES)
    n_fine, n_coarse = len(STATIC_FINE), len(STATIC_COARSE) + 1
    slab = (b * SUB, LANES)
    message = ((4 * b + 4 * PHASE) * SUB, LANES)
    work = [(6, *fine), (2, *fine)] + [(6, *fine)] * 3 + [(6, *coarse)] * 2
    *static, moved, state, down, up, response, sums = call(
        functools.partial(first_kernel, geo),
        [fine] * n_fine
        + [coarse] * n_coarse
        + [slab, (8, *slab), message, message, (4, *slab), (1, LANES)],
        [(FIELDS * n_layers * SUB, LANES), (SUB * SUB, LANES), (2, *fine), coarse] + work,
        stiffness,
        own,
        low,
        high,
        low_edge,
        high_edge,
        smem=(0,),
    )
    earlier = lax.all_gather(sums, axes, axis=0, tiled=True)
    from_low = lax.ppermute(up, axes, geo.shifts(1))
    from_high = lax.ppermute(down, axes, geo.shifts(-1))
    chunks, sums = call(
        functools.partial(second_kernel, geo),
        [(group, BACK * b, LANES), (1, LANES)],
        [(BACK * b * SUB, LANES)] + work,
        *static,
        state,
        from_low,
        from_high,
        earlier,
        response,
        moved,
    )
    later = lax.all_gather(sums, axes, axis=0, tiled=True)
    chunks = lax.all_to_all(chunks, ("gx", "gy"), 0, 0, tiled=True)
    block = (geo.block_x, geo.block_y, geo.block_z)
    return tuple(
        call(
            functools.partial(unpack_kernel, geo),
            [block, (3, *block), block],
            [],
            chunks,
            earlier,
            later,
        )
    )


def solution(mesh):
    in_specs = (
        P("gx", "gy", "gz"),
        P(None, "gx", "gy", "gz"),
        P("gx", "gy", "gz"),
        P("gx", "gy", "gz"),
        P(),
    )
    out_specs = (P("gx", "gy", "gz"), P(None, "gx", "gy", "gz"), P("gx", "gy", "gz"))

    def program(saved_heat_state, *others):
        shape = saved_heat_state.shape
        plan = shards
        if slab_plan_fits(mesh, shape):
            plan = functools.partial(slab_shards, Slabs(mesh, shape))
        return jax.shard_map(
            plan, mesh=mesh, in_specs=in_specs, out_specs=out_specs, check_vma=False
        )(saved_heat_state, *others)

    return program
```

```python
import functools

import jax
import jax.numpy as jnp
from jax import lax
from jax.experimental import pallas as pl
from jax.experimental.pallas import tpu as pltpu
from jax.sharding import PartitionSpec as P

RECOMPUTE = 2
SCHUR_ITERS = 4
COARSE_SWEEPS = 3
LAYERS = 8


INCREMENT_DT = 0.2
DIFFUSIVITY = 0.3
ACTIVATION_ENERGY = 2.3
JACOBI_WEIGHT = 0.7
SCHUR_WEIGHT = 0.5
RAYLEIGH = 1.0


def extended(block, sides, width):
    for axis, dim in sides:
        count = lax.axis_size(axis)
        forward = [(i, i + 1) for i in range(count - 1)]
        backward = [(target, source) for source, target in forward]
        low = lax.ppermute(
            lax.slice_in_dim(block, block.shape[dim] - width, None, axis=dim), axis, forward
        )
        high = lax.ppermute(lax.slice_in_dim(block, 0, width, axis=dim), axis, backward)
        block = jnp.concatenate([low, block, high], axis=dim)
    return block


def neighbours(bordered_array):
    centre = bordered_array[..., 1:-1, 1:-1, 1:-1]
    beside_all = [
        bordered_array[..., 2:, 1:-1, 1:-1],
        bordered_array[..., :-2, 1:-1, 1:-1],
        bordered_array[..., 1:-1, 2:, 1:-1],
        bordered_array[..., 1:-1, :-2, 1:-1],
        bordered_array[..., 1:-1, 1:-1, 2:],
        bordered_array[..., 1:-1, 1:-1, :-2],
    ]
    return (centre, beside_all)


def finest_halo_cells(field):
    return extended(field, (("gx", 1), ("gy", 2), ("gz", 3)), 1)


def deep_halo(field):
    return extended(field, (("gx", 1), ("gy", 2), ("gz", 3)), 2)


def coarse_halo(field):
    return extended(field, (("gx", 1), ("gy", 2), ("gz", 3)), 1)


def march_backward(bordered_array, shallower_adjacent, deeper_adjacent):
    centre, beside_all = neighbours(bordered_array)
    drift = 0.0
    for dim_index in range(3):
        drift = (
            drift
            + shallower_adjacent[dim_index] * (centre - beside_all[2 * dim_index + 1])
            + deeper_adjacent[dim_index] * (beside_all[2 * dim_index] - centre)
        )
    spread = sum(beside_all) - 6.0 * centre
    return centre - INCREMENT_DT * drift + INCREMENT_DT * DIFFUSIVITY * spread


def motion_source(bordered_heat, forward_motion, dual_heat_after):
    centre, beside_all = neighbours(bordered_heat)
    device_pieces = [
        jnp.where(
            forward_motion[dim_index] > 0,
            centre - beside_all[2 * dim_index + 1],
            beside_all[2 * dim_index] - centre,
        )
        for dim_index in range(3)
    ]
    return -INCREMENT_DT * dual_heat_after[None] * jnp.stack(device_pieces)


def advect_dual_heat(pos_padded, neg_padded, lam_padded):
    centre, beside_all = neighbours(lam_padded)
    result = centre + INCREMENT_DT * DIFFUSIVITY * (sum(beside_all) - 6.0 * centre)
    for dim_index in range(3):
        pos_centre, pos_around = neighbours(pos_padded[dim_index])
        neg_centre, neg_around = neighbours(neg_padded[dim_index])
        result = result - INCREMENT_DT * (
            pos_centre - pos_around[2 * dim_index] + neg_around[2 * dim_index + 1] - neg_centre
        )
    return result


def coefficients(bordered_array, factor):
    centre, beside_all = neighbours(bordered_array)
    return [factor * (0.5 * (centre + other)) for other in beside_all]


def apply_operator(face_coef, bordered_array):
    centre, beside_all = neighbours(bordered_array)
    return sum((coef * (centre - other) for coef, other in zip(face_coef, beside_all)))


def gradient(bordered_array):
    centre, beside_all = neighbours(bordered_array)
    return jnp.stack(
        [
            0.5 * (beside_all[2 * dim_index] - beside_all[2 * dim_index + 1])
            for dim_index in range(3)
        ]
    )


def divergence(bordered_array):
    centre, beside_all = neighbours(bordered_array)
    return sum(
        (
            0.5 * (beside_all[2 * dim_index][dim_index] - beside_all[2 * dim_index + 1][dim_index])
            for dim_index in range(3)
        )
    )


def restrict(field):
    leading = field.shape[:-3]
    cells_x, cells_y, cells_z = field.shape[-3:]
    blocks = field.reshape(leading + (cells_x // 2, 2, cells_y // 2, 2, cells_z // 2, 2))
    return blocks.mean(axis=(-5, -3, -1))


def prolong(field):
    return jnp.repeat(jnp.repeat(jnp.repeat(field, 2, axis=-3), 2, axis=-2), 2, axis=-1)


def evaluate_viscosity(rheology_class, class_base_stiffness):
    base = jnp.zeros(rheology_class.shape, jnp.float32)
    for layer_index in range(LAYERS):
        base = base + jnp.where(
            rheology_class == layer_index, class_base_stiffness[layer_index], 0.0
        )
    return base


def inside_mask(extent_first, extent_second, extent_vertical):
    index_x = (
        lax.axis_index("gx") * extent_first + jnp.arange(extent_first + 2, dtype=jnp.int32) - 1
    )
    index_y = (
        lax.axis_index("gy") * extent_second + jnp.arange(extent_second + 2, dtype=jnp.int32) - 1
    )
    index_z = (
        lax.axis_index("gz") * extent_vertical
        + jnp.arange(extent_vertical + 2, dtype=jnp.int32)
        - 1
    )
    inside_x = (index_x >= 0) & (index_x < extent_first * lax.axis_size("gx"))
    inside_y = (index_y >= 0) & (index_y < extent_second * lax.axis_size("gy"))
    inside_z = (index_z >= 0) & (index_z < extent_vertical * lax.axis_size("gz"))
    return inside_x[:, None, None] & inside_y[None, :, None] & inside_z[None, None, :]


def coarse_solve(coarse_res, coarse_coef, coarse_diag, pad_field):
    coarse_corr = JACOBI_WEIGHT * coarse_res / coarse_diag
    for sweep in range(COARSE_SWEEPS - 1):
        coarse_corr = (
            coarse_corr
            + JACOBI_WEIGHT
            * (coarse_res - apply_operator(coarse_coef, pad_field(coarse_corr)))
            / coarse_diag
        )
    return coarse_corr


def shards(saved_heat_state, forward_motion, dual_heat_after, rheology_class, class_base_stiffness):
    extent_first, extent_second, extent_vertical = saved_heat_state.shape
    shallower_adjacent = jnp.maximum(forward_motion, 0.0)
    deeper_adjacent = jnp.minimum(forward_motion, 0.0)
    heat_state = saved_heat_state
    for repeat_index in range(RECOMPUTE):
        heat_state = march_backward(
            finest_halo_cells(heat_state[None])[0], shallower_adjacent, deeper_adjacent
        )
    local_viscosity = evaluate_viscosity(rheology_class, class_base_stiffness) * jnp.exp(
        -ACTIVATION_ENERGY * heat_state
    )
    stacked = jnp.concatenate(
        [
            heat_state[None],
            dual_heat_after[None],
            shallower_adjacent * dual_heat_after[None],
            deeper_adjacent * dual_heat_after[None],
            local_viscosity[None],
        ],
        0,
    )
    bordered_array = finest_halo_cells(stacked)
    driving_source = motion_source(bordered_array[0], forward_motion, dual_heat_after)
    advected_result = advect_dual_heat(bordered_array[2:5], bordered_array[5:8], bordered_array[1])
    face_coef = coefficients(bordered_array[8], 1.0)
    diagonal = sum(face_coef)
    coarse_visc = restrict(local_viscosity)
    coarse_coef = coefficients(coarse_halo(coarse_visc[None])[0], 0.25)
    coarse_diag = sum(coarse_coef)
    deep_static = deep_halo(jnp.concatenate([local_viscosity[None], driving_source], 0))
    cycle_coef = coefficients(deep_static[0], 1.0)
    cycle_source = deep_static[1:4, 1:-1, 1:-1, 1:-1]
    inside = inside_mask(extent_first, extent_second, extent_vertical)
    safe_diag = jnp.where(inside, sum(cycle_coef), 1.0)
    total_cells = (
        extent_first
        * extent_second
        * extent_vertical
        * lax.axis_size("gx")
        * lax.axis_size("gy")
        * lax.axis_size("gz")
    )
    velocity = jnp.zeros(forward_motion.shape, jnp.float32)
    mean_stress = jnp.zeros(saved_heat_state.shape, jnp.float32)
    for iteration in range(SCHUR_ITERS):
        if iteration == 0:
            cycle_resid = cycle_source
        else:
            flow_press = deep_halo(jnp.concatenate([velocity, mean_stress[None]], 0))
            cycle_resid = (
                cycle_source - apply_operator(cycle_coef, flow_press[0:3]) - gradient(flow_press[3])
            )
        cycle_corr = jnp.where(inside, JACOBI_WEIGHT * cycle_resid / safe_diag, 0.0)
        residual = cycle_resid[:, 1:-1, 1:-1, 1:-1]
        correction = cycle_corr[:, 1:-1, 1:-1, 1:-1]
        residual_two = residual - apply_operator(face_coef, cycle_corr)
        coarse_res = restrict(residual_two)
        coarse_corr = coarse_solve(coarse_res, coarse_coef, coarse_diag, coarse_halo)
        correction = correction + prolong(coarse_corr)
        correction = (
            correction
            + JACOBI_WEIGHT
            * (residual - apply_operator(face_coef, finest_halo_cells(correction)))
            / diagonal
        )
        velocity = velocity + correction
        spread_flow = divergence(finest_halo_cells(velocity))
        mean_stress = mean_stress - SCHUR_WEIGHT * local_viscosity * spread_flow
        mean_stress = mean_stress - lax.psum(jnp.sum(mean_stress), ("gx", "gy", "gz")) / total_cells
    adj_temp_prev = advected_result + RAYLEIGH * velocity[2]
    return (adj_temp_prev, velocity, mean_stress)


SUB = 8
LANES = 128
FIELDS = 6
BACK = 9
EDGE = 2
PHASE = 8
VMEM_LIMIT = 48 * 1024 * 1024


def slab_plan_fits(mesh, shape):
    sizes = mesh.shape
    group = sizes["gx"] * sizes["gy"]
    block = (shape[0] // sizes["gx"], shape[1] // sizes["gy"], shape[2] // sizes["gz"])
    return (
        group == SUB
        and block[0] == SUB
        and block[0] * block[1] == LANES
        and block[1] * group == LANES
        and block[2] == LANES
        and block[2] == group * 2 * PHASE
    )


class Slabs:
    def __init__(self, mesh, shape):
        self.nx, self.ny, self.nz = mesh.shape["gx"], mesh.shape["gy"], mesh.shape["gz"]
        self.group = self.nx * self.ny
        self.width, self.breadth, self.height = shape
        self.block_x, self.block_y, self.block_z = (
            shape[0] // self.nx,
            shape[1] // self.ny,
            shape[2] // self.nz,
        )
        self.slab = self.block_z // self.group
        self.halo = self.slab + EDGE
        self.layers = self.slab + 2 * self.halo
        self.cells = self.width * self.breadth * self.height
        self.place = []
        for ix in range(self.nx):
            for iy in range(self.ny):
                step = ix if iy % 2 == 0 else self.nx - 1 - ix
                self.place.append(iy * self.nx + step)
        self.holder = [self.place.index(j) for j in range(self.group)]

    def device(self, slab):
        return self.holder[slab % self.group] * self.nz + slab // self.group

    def shifts(self, distance):
        count = self.group * self.nz
        return [
            (self.device(p), self.device(p + distance))
            for p in range(count)
            if 0 <= p + distance < count
        ]

    def index(self):
        ix, iy = lax.axis_index("gx"), lax.axis_index("gy")
        step = jnp.where(iy % 2 == 0, ix, self.nx - 1 - ix)
        return lax.axis_index("gz") * self.group + iy * self.nx + step


def tile_iota():
    s = lax.broadcasted_iota(jnp.int32, (1, SUB, LANES), 1)
    l = lax.broadcasted_iota(jnp.int32, (1, SUB, LANES), 2)
    return s, l


def swap_granules(tiles, granule):
    lane = lax.broadcasted_iota(jnp.int32, (SUB, LANES), 1) // granule
    for bit in (1, 2, 4):
        low = (lane & bit) == 0
        new = list(tiles)
        for a in range(SUB):
            if a & bit:
                continue
            b = a | bit
            new[a] = jnp.where(low, tiles[a], pltpu.roll(tiles[b], granule * bit, 1))
            new[b] = jnp.where(low, pltpu.roll(tiles[a], LANES - granule * bit, 1), tiles[b])
        tiles = new
    return tiles


class Tiles:
    def __init__(self, breadth):
        self.breadth = breadth
        self.s, self.l = tile_iota()
        self.x = (self.l // breadth) * SUB + self.s
        self.y = self.l % breadth
        self.width = SUB * (LANES // breadth)

    def xs(self, f, d):
        t = pltpu.roll(f, (-d) % SUB, 1)
        u = pltpu.roll(t, (-self.breadth if d > 0 else self.breadth) % LANES, 2)
        crosses = (self.s >= SUB - d) if d > 0 else (self.s < -d)
        return jnp.where(crosses, u, t)

    def ys(self, f, d):
        return pltpu.roll(f, (-d) % LANES, 2)

    def masks(self, d, value):
        keep = (
            self.x < self.width - d,
            self.x >= d,
            self.y < self.breadth - d,
            self.y >= d,
        )
        return [jnp.where(k, jnp.float32(value), jnp.float32(0.0)) for k in keep]

    def four(self, f, d):
        return [self.xs(f, d), self.xs(f, -d), self.ys(f, d), self.ys(f, -d)]

    def block_sum(self, f):
        f = f + jnp.where(self.l % 2 == 0, pltpu.roll(f, LANES - 1, 2), pltpu.roll(f, 1, 2))
        return f + jnp.where(self.s % 2 == 0, pltpu.roll(f, SUB - 1, 1), pltpu.roll(f, 1, 1))


def get(ref, i, n, *lead):
    return ref[(*lead, pl.ds(pl.multiple_of(i * SUB, SUB), n * SUB), slice(None))].reshape(
        n, SUB, LANES
    )


def put(ref, i, value, *lead):
    n = value.shape[0]
    ref[(*lead, pl.ds(pl.multiple_of(i * SUB, SUB), n * SUB), slice(None))] = value.reshape(
        n * SUB, LANES
    )


def sweep(lo, hi, n, body, most=4):
    count = (hi - lo) // n
    assert count * n == hi - lo
    unroll = max(u for u in range(1, most + 1) if count % u == 0)

    def step(t, _):
        todo = []
        for u in range(unroll):
            todo += body(lo + (t * unroll + u) * n)
        for ref, i, value, *lead in todo:
            put(ref, i, value, *lead)
        return 0

    lax.fori_loop(0, count // unroll, step, 0)


def regroup(source, target, granule, count, most=3):
    unroll = max(u for u in range(1, most + 1) if count % u == 0)

    def step(t, _):
        groups = [source(t * unroll + u) for u in range(unroll)]
        groups = [swap_granules(tiles, granule) for tiles in groups]
        for u in range(unroll):
            target(t * unroll + u, groups[u])
        return 0

    lax.fori_loop(0, count // unroll, step, 0)


def pack_kernel(geo, heat_in, flow_in, dual_in, kind_in, out, heat, flow, dual, kind, sems):
    b, e = geo.slab, EDGE
    pairs = ((heat_in, heat), (flow_in, flow), (dual_in, dual), (kind_in, kind))
    copies = [
        pltpu.make_async_copy(source, target, sems.at[k])
        for k, (source, target) in enumerate(pairs)
    ]
    for copy in copies:
        copy.start()
    for copy in copies:
        copy.wait()
    flat = [heat[...], flow[0], flow[1], flow[2], dual[...], kind[...].astype(jnp.float32)]
    turned = [f.reshape(LANES, LANES).T for f in flat]
    for j in range(geo.group):
        q = geo.holder[j]
        for f in range(FIELDS):
            out[q, f * b : (f + 1) * b, :] = turned[f][j * b : (j + 1) * b]
        tail = FIELDS * b
        first = jnp.concatenate([turned[f][j * b : j * b + e] for f in range(4)], 0)
        last = jnp.concatenate([turned[f][(j + 1) * b - e : (j + 1) * b] for f in range(4)], 0)
        out[q, tail : tail + SUB, :] = first
        out[q, tail + SUB : tail + 2 * SUB, :] = last


STATIC_FINE = ("s0", "s1", "s2", "visc", "w", "diag", "cxp", "cxm", "cyp", "cym", "cz")
STATIC_COARSE = ("kxp", "kxm", "kyp", "kym", "kzp", "kzm")


def iterate(geo, st, v, p, res, cor, cor2, cc0, cc1, seqs, lo, hi, first):
    tl = Tiles(geo.breadth)
    half = tl.masks(1, 0.5)
    comps = [3 * q + k for q in seqs for k in range(3)]
    keep = 1.0 - JACOBI_WEIGHT

    def faces(i, n):
        c = [get(st[name], i, n) for name in ("cxp", "cxm", "cyp", "cym")]
        return c, get(st["cz"], i, n), get(st["cz"], i - 1, n)

    def around(coef, ref, i, n, *lead):
        (c, up, down) = coef
        f = get(ref, i, n, *lead)
        total = up * get(ref, i + 1, n, *lead) + down * get(ref, i - 1, n, *lead)
        for a, b in zip(c, tl.four(f, 1)):
            total = total + a * b
        return f, total

    def residual(i):
        n, todo = 2, []
        coef = None if first else faces(i, n)
        w = get(st["w"], i, n)
        diag = None if first else get(st["diag"], i, n)
        for q in seqs:
            if not (first and q == 0):
                pq = get(p, i, n, q)
                xp, xm, yp, ym = tl.four(pq, 1)
                slope = [
                    half[0] * xp - half[1] * xm,
                    half[2] * yp - half[3] * ym,
                    0.5 * (get(p, i + 1, n, q) - get(p, i - 1, n, q)),
                ]
            for k in range(3):
                value = get(st["s%d" % k], i, n) if q == 0 else None
                if not (first and q == 0):
                    value = -slope[k] if value is None else value - slope[k]
                if not first:
                    f, total = around(coef, v, i, n, 3 * q + k)
                    value = value - (diag * f - total)
                todo += [(res, i, value, 3 * q + k), (cor, i, w * value, 3 * q + k)]
        return todo

    sweep(lo - 8, hi + 8, 2, residual)

    def restricted(i):
        pair, todo = i // 2, []
        coef = faces(i, 2)
        wc = 0.125 * get(st["wc"], pair, 1)
        for c in comps:
            _, total = around(coef, cor, i, 2, c)
            left = keep * get(res, i, 2, c) + total
            todo.append((cc0, pair, wc * tl.block_sum(left[0:1] + left[1:2]), c))
        return todo

    sweep(lo - 6, hi + 6, 2, restricted)

    def coarse_step(src, c, pair, n):
        f = get(src, pair, n, c)
        value = get(cc0, pair, n, c) + keep * f
        value = value + get(st["kzp"], pair, n) * get(src, pair + 1, n, c)
        value = value + get(st["kzm"], pair, n) * get(src, pair - 1, n, c)
        for name, b in zip(("kxp", "kxm", "kyp", "kym"), tl.four(f, 2)):
            value = value + get(st[name], pair, n) * b
        return value

    def sweep_one(pair):
        return [(cc1, pair, coarse_step(cc0, c, pair, 2), c) for c in comps]

    sweep((lo - 4) // 2, (hi + 4) // 2, 2, sweep_one)

    def sweep_two(pair):
        todo = []
        for c in comps:
            value = coarse_step(cc1, c, pair, 2)
            fine = jnp.broadcast_to(value[:, None], (2, 2, SUB, LANES)).reshape(4, SUB, LANES)
            todo.append((cor2, 2 * pair, get(cor, 2 * pair, 4, c) + fine, c))
        return todo

    sweep((lo - 2) // 2, (hi + 2) // 2, 2, sweep_two)

    def velocity(i):
        n, todo = 2, []
        coef = faces(i, n)
        w = get(st["w"], i, n)
        for c in comps:
            f, total = around(coef, cor2, i, n, c)
            value = get(cor, i, n, c) + keep * f + w * total
            if not first:
                value = get(v, i, n, c) + value
            todo.append((v, i, value, c))
        return todo

    sweep(lo - 2, hi + 2, 2, velocity)

    def pressure(i):
        n, todo = 2, []
        visc = SCHUR_WEIGHT * get(st["visc"], i, n)
        for q in seqs:
            a, b = get(v, i, n, 3 * q), get(v, i, n, 3 * q + 1)
            div = half[0] * tl.xs(a, 1) - half[1] * tl.xs(a, -1)
            div = div + half[2] * tl.ys(b, 1) - half[3] * tl.ys(b, -1)
            div = div + 0.5 * (get(v, i + 1, n, 3 * q + 2) - get(v, i - 1, n, 3 * q + 2))
            value = -(visc * div)
            todo.append((p, i, value if first and q == 0 else get(p, i, n, q) + value, q))
        return todo

    sweep(lo, hi, 2, pressure)


def slab_total(geo, p, q):
    own = get(p, geo.halo, geo.slab, q)
    return jnp.sum(jnp.sum(own, axis=0), axis=(0, 1), keepdims=True)


def in_lanes(values, rows):
    lane = lax.broadcasted_iota(jnp.int32, (rows, LANES), 1)
    out = jnp.zeros((rows, LANES), jnp.float32)
    for k, value in values:
        out = jnp.where(lane == k, value, out)
    return out


def first_kernel(geo, stiffness, own, low, high, low_edge, high_edge, *refs):
    names = STATIC_FINE + STATIC_COARSE + ("wc",)
    st = dict(zip(names, refs[: len(names)]))
    moved, state, message_down, message_up, response, sums, raw, spare, heat, vc, *work = refs[
        len(names) :
    ]
    v, p, res, cor, cor2, cc0, cc1 = work
    tl = Tiles(geo.breadth)
    b, h, n_layers = geo.slab, geo.halo, geo.layers
    granule = geo.block_y

    for source, base in ((low, EDGE), (own, h), (high, h + b)):

        def load(t, source=source):
            row = pl.multiple_of(t * SUB, SUB)
            return [source[q, pl.ds(row, SUB), :] for q in range(geo.group)]

        def store(t, tiles, base=base):
            f, d = t // (b // SUB), (t % (b // SUB)) * SUB
            start = (f * n_layers + base + d) * SUB
            for s, tile in enumerate(tiles):
                raw[pl.ds(start + s, SUB, stride=SUB), :] = tile

        regroup(load, store, granule, FIELDS * (b // SUB))
    for source, base in ((low_edge, 0), (high_edge, n_layers - EDGE)):
        tiles = [source[q] for q in range(geo.group)]
        for s, tile in enumerate(swap_granules(tiles, granule)):
            spare[pl.ds(s, SUB, stride=SUB), :] = tile
        for f in range(4):
            start = (f * n_layers + base) * SUB
            raw[start : start + EDGE * SUB, :] = spare[f * EDGE * SUB : (f + 1) * EDGE * SUB, :]

    def field(f, i, n):
        return get(raw, f * n_layers + i, n)

    first_layer = geo.index() * b - h

    def inside(i, n):
        layer = first_layer + i + lax.broadcasted_iota(jnp.int32, (n, 1, 1), 0)
        return (layer >= 0) & (layer < geo.height)

    one = tl.masks(1, 1.0)

    def masked_four(f):
        return [m * g for m, g in zip(one, tl.four(f, 1))]

    def advance(old, new):
        def body(i):
            n = 2
            f = old(i, n)
            beside = masked_four(f) + [old(i + 1, n), old(i - 1, n)]
            drift = 0.0
            for k in range(3):
                flow = field(1 + k, i, n)
                drift = drift + jnp.maximum(flow, 0.0) * (f - beside[2 * k + 1])
                drift = drift + jnp.minimum(flow, 0.0) * (beside[2 * k] - f)
            spread = sum(beside) - 6.0 * f
            value = f - INCREMENT_DT * drift + INCREMENT_DT * DIFFUSIVITY * spread
            return [(heat, i, jnp.where(inside(i, n), value, 0.0), new)]

        return body

    sweep(1, n_layers - 1, 2, advance(lambda i, n: field(0, i, n), 0), 5)
    sweep(2, n_layers - 2, 2, advance(lambda i, n: get(heat, i, n, 0), 1))

    def viscosity(i):
        n = 2
        kind = field(5, i, n)
        base = jnp.zeros(kind.shape, jnp.float32)
        for layer in range(LAYERS):
            base = base + jnp.where(kind == float(layer), stiffness[layer], 0.0)
        value = base * jnp.exp(-ACTIVATION_ENERGY * get(heat, i, n, 1))
        value = jnp.where(inside(i, n), value, 0.0)
        coarse = 0.125 * tl.block_sum(value[0:1] + value[1:2])
        return [(st["visc"], i, value), (vc, i // 2, coarse)]

    sweep(2, n_layers - 2, 2, viscosity)

    def statics(i):
        n = 2
        c = get(st["visc"], i, n)
        beside = masked_four(c) + [get(st["visc"], i + 1, n), get(st["visc"], i - 1, n)]
        face = [0.5 * (c + o) for o in beside]
        diag = sum(face)
        todo = [
            (st[name], i, m * f)
            for name, m, f in zip(("cxp", "cxm", "cyp", "cym"), one, face)
        ]
        todo += [(st["cz"], i, face[4]), (st["diag"], i, diag)]
        todo.append((st["w"], i, jnp.where(inside(i, n), JACOBI_WEIGHT / diag, 0.0)))
        f = get(heat, i, n, 1)
        beside = masked_four(f) + [get(heat, i + 1, n, 1), get(heat, i - 1, n, 1)]
        dual = -INCREMENT_DT * field(4, i, n)
        for k in range(3):
            flow = field(1 + k, i, n)
            step = jnp.where(flow > 0, f - beside[2 * k + 1], beside[2 * k] - f)
            todo.append((st["s%d" % k], i, dual * step))
        return todo

    sweep(2, n_layers - 2, 2, statics)

    two = tl.masks(2, 1.0)

    def coarse_statics(pair):
        n = 1
        c = get(vc, pair, n)
        beside = [m * g for m, g in zip(two, tl.four(c, 2))]
        beside = beside + [get(vc, pair + 1, n), get(vc, pair - 1, n)]
        face = [0.25 * (0.5 * (c + o)) for o in beside]
        wc = JACOBI_WEIGHT / sum(face)
        wc = jnp.where(inside(2 * pair, 1), wc, 0.0)
        return [(st["wc"], pair, wc)] + [
            (st[name], pair, wc * (m * f))
            for name, m, f in zip(STATIC_COARSE, two + [1.0, 1.0], face)
        ]

    sweep(1, n_layers // 2 - 1, 1, coarse_statics)

    def transport(i):
        n = 2
        dual = field(4, i, n)
        up, down = field(4, i + 1, n), field(4, i - 1, n)
        value = dual + INCREMENT_DT * DIFFUSIVITY * (
            sum(masked_four(dual)) + up + down - 6.0 * dual
        )
        for k in range(3):
            a = jnp.maximum(field(1 + k, i, n), 0.0) * dual
            c = jnp.minimum(field(1 + k, i, n), 0.0) * dual
            if k == 0:
                ahead, behind = one[0] * tl.xs(a, 1), one[1] * tl.xs(c, -1)
            elif k == 1:
                ahead, behind = one[2] * tl.ys(a, 1), one[3] * tl.ys(c, -1)
            else:
                ahead = jnp.maximum(field(3, i + 1, n), 0.0) * up
                behind = jnp.minimum(field(3, i - 1, n), 0.0) * down
            value = value - INCREMENT_DT * (a - ahead + behind - c)
        return [(moved, i - h, value)]

    sweep(h, h + b, 2, transport)

    def unit(i):
        return [(p, i, jnp.broadcast_to(jnp.where(inside(i, 4), 1.0, 0.0), (4, SUB, LANES)), 1)]

    sweep(0, n_layers, 4, unit)

    work = (v, p, res, cor, cor2, cc0, cc1)
    iterate(geo, st, *work, (0, 1), h - PHASE, h + b + PHASE, True)
    totals = [slab_total(geo, p, 0), slab_total(geo, p, 1)]
    for k in range(3):
        put(response, 0, get(v, h, b, 3 + k), k)
    put(response, 0, get(p, h, b, 1), 3)
    iterate(geo, st, *work, (0, 1), h, h + b, False)
    totals += [slab_total(geo, p, 0), slab_total(geo, p, 1)]
    sums[...] = in_lanes(enumerate(totals), sums.shape[0])
    for q in range(2):
        for k in range(4):
            value = get(v, h, b, 3 * q + k) if k < 3 else get(p, h, b, q)
            put(state, 0, value, 4 * q + k)
            if q == 0:
                put(message_down, k * b, value)
                put(message_up, k * b, value)
            else:
                put(message_down, 4 * b + k * PHASE, value[:PHASE])
                put(message_up, 4 * b + k * PHASE, value[b - PHASE :])


def second_kernel(geo, *refs):
    names = STATIC_FINE + STATIC_COARSE + ("wc",)
    st = dict(zip(names, refs[: len(names)]))
    state, low, high, earlier, response, moved, out, sums, mixed, *work = refs[len(names) :]
    v, p, res, cor, cor2, cc0, cc1 = work
    b, h = geo.slab, geo.halo
    for q in range(2):
        for k in range(4):
            ref, lead = (v, 3 * q + k) if k < 3 else (p, q)
            put(ref, h, get(state, 0, b, 4 * q + k), lead)
            thick = b if q == 0 else PHASE
            at = k * b if q == 0 else 4 * b + k * PHASE
            put(ref, h - thick, get(low, at, thick), lead)
            put(ref, h + b, get(high, at, thick), lead)
    iterate(geo, st, *work, (0,), h - PHASE, h + b + PHASE, False)
    totals = [(4, slab_total(geo, p, 0))]
    iterate(geo, st, *work, (0, 1), h, h + b, False)
    totals += [(5, slab_total(geo, p, 0)), (6, slab_total(geo, p, 1))]
    sums[...] = in_lanes(totals, sums.shape[0])

    m1, m2 = means(geo, earlier[...])[:2]
    for k in range(4):
        last = [get(p, h, b, q) if k == 3 else get(v, h, b, 3 * q + k) for q in range(2)]
        value = last[0] - m1 * last[1] - m2 * get(state, 0, b, 4 + k)
        put(mixed, k * b, value)
        put(mixed, (4 + k) * b, get(response, 0, b, k))
    put(mixed, 8 * b, get(moved, 0, b))

    def load(t):
        return [mixed[pl.ds(t * SUB * SUB + s, SUB, stride=SUB), :] for s in range(SUB)]

    def store(t, tiles):
        for q, tile in enumerate(tiles):
            out[q, pl.ds(pl.multiple_of(t * SUB, SUB), SUB), :] = tile

    regroup(load, store, geo.block_y, BACK * (b // SUB))


def means(geo, sums):
    row = jnp.sum(sums, axis=0, keepdims=True) / geo.cells
    lane = lax.broadcasted_iota(jnp.int32, row.shape, 1)

    def at(k):
        return jnp.sum(jnp.where(lane == k, row, 0.0), axis=1, keepdims=True)

    s1, r1, s2, r2, s3, s4, r3 = [at(k) for k in range(7)]
    m1 = s1
    m2 = s2 - m1 * r1
    m3 = s3 - m1 * r2 - m2 * r1
    m4 = s4 - m1 * r3 - m2 * r2 - m3 * r1
    return m1, m2, m3, m4


def unpack_kernel(geo, chunks, earlier, later, heat, flow, pressure):
    b = geo.slab
    shape = (geo.block_x, geo.block_y, geo.block_z)
    m3, m4 = means(geo, earlier[...] + later[...])[2:]

    def block(f):
        rows = [chunks[geo.holder[j], f * b : (f + 1) * b, :] for j in range(geo.group)]
        return jnp.concatenate(rows, 0)

    for k in range(4):
        value = block(k) - m3 * block(4 + k)
        if k == 3:
            pressure[...] = (value - m4).T.reshape(shape)
        else:
            flow[k] = value.T.reshape(shape)
        if k == 2:
            heat[...] = (block(8) + value).T.reshape(shape)


def call(kernel, out, scratch, *args, smem=(), hbm=()):
    f32 = jnp.float32
    specs = [
        pl.BlockSpec(
            memory_space=pltpu.SMEM if i in smem else pltpu.HBM if i in hbm else pltpu.VMEM
        )
        for i in range(len(args))
    ]
    return pl.pallas_call(
        kernel,
        out_shape=[jax.ShapeDtypeStruct(s, f32) for s in out],
        in_specs=specs,
        out_specs=[pl.BlockSpec(memory_space=pltpu.VMEM) for _ in out],
        scratch_shapes=[pltpu.VMEM(s, f32) if isinstance(s, tuple) else s for s in scratch],
        compiler_params=pltpu.CompilerParams(vmem_limit_bytes=VMEM_LIMIT),
    )(*args)


def slab_shards(geo, heat, flow, dual, kind, stiffness):
    b, n_layers, group = geo.slab, geo.layers, geo.group
    rows = FIELDS * b
    inputs = (heat, flow, dual, kind)
    (chunks,) = call(
        functools.partial(pack_kernel, geo),
        [(group, rows + 2 * SUB, LANES)],
        [pltpu.VMEM(a.shape, a.dtype) for a in inputs] + [pltpu.SemaphoreType.DMA((4,))],
        *inputs,
        hbm=range(4),
    )
    own = lax.all_to_all(chunks, ("gx", "gy"), 0, 0, tiled=True)
    axes = ("gx", "gy", "gz")
    low = lax.ppermute(own, axes, geo.shifts(1))
    high = lax.ppermute(own, axes, geo.shifts(-1))
    high_edge = lax.ppermute(own[:, rows : rows + SUB], axes, geo.shifts(-2))
    low_edge = lax.ppermute(own[:, rows + SUB :], axes, geo.shifts(2))

    fine, coarse = (n_layers * SUB, LANES), (n_layers // 2 * SUB, LANES)
    devices = group * geo.nz
    n_fine, n_coarse = len(STATIC_FINE), len(STATIC_COARSE) + 1
    slab = (b * SUB, LANES)
    message = ((4 * b + 4 * PHASE) * SUB, LANES)
    work = [(6, *fine), (2, *fine)] + [(6, *fine)] * 3 + [(6, *coarse)] * 2
    *static, moved, state, down, up, response, sums = call(
        functools.partial(first_kernel, geo),
        [fine] * n_fine
        + [coarse] * n_coarse
        + [slab, (8, *slab), message, message, (4, *slab), (devices, LANES)],
        [(FIELDS * n_layers * SUB, LANES), (SUB * SUB, LANES), (2, *fine), coarse] + work,
        stiffness,
        own,
        low,
        high,
        low_edge,
        high_edge,
        smem=(0,),
    )
    earlier = lax.all_to_all(sums, axes, 0, 0, tiled=True)
    from_low = lax.ppermute(up, axes, geo.shifts(1))
    from_high = lax.ppermute(down, axes, geo.shifts(-1))
    chunks, sums = call(
        functools.partial(second_kernel, geo),
        [(group, BACK * b, LANES), (devices, LANES)],
        [(BACK * b * SUB, LANES)] + work,
        *static,
        state,
        from_low,
        from_high,
        earlier,
        response,
        moved,
    )
    later = lax.all_to_all(sums, axes, 0, 0, tiled=True)
    chunks = lax.all_to_all(chunks, ("gx", "gy"), 0, 0, tiled=True)
    block = (geo.block_x, geo.block_y, geo.block_z)
    return tuple(
        call(
            functools.partial(unpack_kernel, geo),
            [block, (3, *block), block],
            [],
            chunks,
            earlier,
            later,
        )
    )


def solution(mesh):
    in_specs = (
        P("gx", "gy", "gz"),
        P(None, "gx", "gy", "gz"),
        P("gx", "gy", "gz"),
        P("gx", "gy", "gz"),
        P(),
    )
    out_specs = (P("gx", "gy", "gz"), P(None, "gx", "gy", "gz"), P("gx", "gy", "gz"))

    def program(saved_heat_state, *others):
        shape = saved_heat_state.shape
        plan = shards
        if slab_plan_fits(mesh, shape):
            plan = functools.partial(slab_shards, Slabs(mesh, shape))
        return jax.shard_map(
            plan, mesh=mesh, in_specs=in_specs, out_specs=out_specs, check_vma=False
        )(saved_heat_state, *others)

    return program
```

```python
import functools

import jax
import jax.numpy as jnp
from jax import lax
from jax.experimental import pallas as pl
from jax.experimental.pallas import tpu as pltpu
from jax.sharding import PartitionSpec as P

RECOMPUTE = 2
SCHUR_ITERS = 4
COARSE_SWEEPS = 3
LAYERS = 8


INCREMENT_DT = 0.2
DIFFUSIVITY = 0.3
ACTIVATION_ENERGY = 2.3
JACOBI_WEIGHT = 0.7
SCHUR_WEIGHT = 0.5
RAYLEIGH = 1.0


def extended(block, sides, width):
    for axis, dim in sides:
        count = lax.axis_size(axis)
        forward = [(i, i + 1) for i in range(count - 1)]
        backward = [(target, source) for source, target in forward]
        low = lax.ppermute(
            lax.slice_in_dim(block, block.shape[dim] - width, None, axis=dim), axis, forward
        )
        high = lax.ppermute(lax.slice_in_dim(block, 0, width, axis=dim), axis, backward)
        block = jnp.concatenate([low, block, high], axis=dim)
    return block


def neighbours(bordered_array):
    centre = bordered_array[..., 1:-1, 1:-1, 1:-1]
    beside_all = [
        bordered_array[..., 2:, 1:-1, 1:-1],
        bordered_array[..., :-2, 1:-1, 1:-1],
        bordered_array[..., 1:-1, 2:, 1:-1],
        bordered_array[..., 1:-1, :-2, 1:-1],
        bordered_array[..., 1:-1, 1:-1, 2:],
        bordered_array[..., 1:-1, 1:-1, :-2],
    ]
    return (centre, beside_all)


def finest_halo_cells(field):
    return extended(field, (("gx", 1), ("gy", 2), ("gz", 3)), 1)


def deep_halo(field):
    return extended(field, (("gx", 1), ("gy", 2), ("gz", 3)), 2)


def coarse_halo(field):
    return extended(field, (("gx", 1), ("gy", 2), ("gz", 3)), 1)


def march_backward(bordered_array, shallower_adjacent, deeper_adjacent):
    centre, beside_all = neighbours(bordered_array)
    drift = 0.0
    for dim_index in range(3):
        drift = (
            drift
            + shallower_adjacent[dim_index] * (centre - beside_all[2 * dim_index + 1])
            + deeper_adjacent[dim_index] * (beside_all[2 * dim_index] - centre)
        )
    spread = sum(beside_all) - 6.0 * centre
    return centre - INCREMENT_DT * drift + INCREMENT_DT * DIFFUSIVITY * spread


def motion_source(bordered_heat, forward_motion, dual_heat_after):
    centre, beside_all = neighbours(bordered_heat)
    device_pieces = [
        jnp.where(
            forward_motion[dim_index] > 0,
            centre - beside_all[2 * dim_index + 1],
            beside_all[2 * dim_index] - centre,
        )
        for dim_index in range(3)
    ]
    return -INCREMENT_DT * dual_heat_after[None] * jnp.stack(device_pieces)


def advect_dual_heat(pos_padded, neg_padded, lam_padded):
    centre, beside_all = neighbours(lam_padded)
    result = centre + INCREMENT_DT * DIFFUSIVITY * (sum(beside_all) - 6.0 * centre)
    for dim_index in range(3):
        pos_centre, pos_around = neighbours(pos_padded[dim_index])
        neg_centre, neg_around = neighbours(neg_padded[dim_index])
        result = result - INCREMENT_DT * (
            pos_centre - pos_around[2 * dim_index] + neg_around[2 * dim_index + 1] - neg_centre
        )
    return result


def coefficients(bordered_array, factor):
    centre, beside_all = neighbours(bordered_array)
    return [factor * (0.5 * (centre + other)) for other in beside_all]


def apply_operator(face_coef, bordered_array):
    centre, beside_all = neighbours(bordered_array)
    return sum((coef * (centre - other) for coef, other in zip(face_coef, beside_all)))


def gradient(bordered_array):
    centre, beside_all = neighbours(bordered_array)
    return jnp.stack(
        [
            0.5 * (beside_all[2 * dim_index] - beside_all[2 * dim_index + 1])
            for dim_index in range(3)
        ]
    )


def divergence(bordered_array):
    centre, beside_all = neighbours(bordered_array)
    return sum(
        (
            0.5 * (beside_all[2 * dim_index][dim_index] - beside_all[2 * dim_index + 1][dim_index])
            for dim_index in range(3)
        )
    )


def restrict(field):
    leading = field.shape[:-3]
    cells_x, cells_y, cells_z = field.shape[-3:]
    blocks = field.reshape(leading + (cells_x // 2, 2, cells_y // 2, 2, cells_z // 2, 2))
    return blocks.mean(axis=(-5, -3, -1))


def prolong(field):
    return jnp.repeat(jnp.repeat(jnp.repeat(field, 2, axis=-3), 2, axis=-2), 2, axis=-1)


def evaluate_viscosity(rheology_class, class_base_stiffness):
    base = jnp.zeros(rheology_class.shape, jnp.float32)
    for layer_index in range(LAYERS):
        base = base + jnp.where(
            rheology_class == layer_index, class_base_stiffness[layer_index], 0.0
        )
    return base


def inside_mask(extent_first, extent_second, extent_vertical):
    index_x = (
        lax.axis_index("gx") * extent_first + jnp.arange(extent_first + 2, dtype=jnp.int32) - 1
    )
    index_y = (
        lax.axis_index("gy") * extent_second + jnp.arange(extent_second + 2, dtype=jnp.int32) - 1
    )
    index_z = (
        lax.axis_index("gz") * extent_vertical
        + jnp.arange(extent_vertical + 2, dtype=jnp.int32)
        - 1
    )
    inside_x = (index_x >= 0) & (index_x < extent_first * lax.axis_size("gx"))
    inside_y = (index_y >= 0) & (index_y < extent_second * lax.axis_size("gy"))
    inside_z = (index_z >= 0) & (index_z < extent_vertical * lax.axis_size("gz"))
    return inside_x[:, None, None] & inside_y[None, :, None] & inside_z[None, None, :]


def coarse_solve(coarse_res, coarse_coef, coarse_diag, pad_field):
    coarse_corr = JACOBI_WEIGHT * coarse_res / coarse_diag
    for sweep in range(COARSE_SWEEPS - 1):
        coarse_corr = (
            coarse_corr
            + JACOBI_WEIGHT
            * (coarse_res - apply_operator(coarse_coef, pad_field(coarse_corr)))
            / coarse_diag
        )
    return coarse_corr


def shards(saved_heat_state, forward_motion, dual_heat_after, rheology_class, class_base_stiffness):
    extent_first, extent_second, extent_vertical = saved_heat_state.shape
    shallower_adjacent = jnp.maximum(forward_motion, 0.0)
    deeper_adjacent = jnp.minimum(forward_motion, 0.0)
    heat_state = saved_heat_state
    for repeat_index in range(RECOMPUTE):
        heat_state = march_backward(
            finest_halo_cells(heat_state[None])[0], shallower_adjacent, deeper_adjacent
        )
    local_viscosity = evaluate_viscosity(rheology_class, class_base_stiffness) * jnp.exp(
        -ACTIVATION_ENERGY * heat_state
    )
    stacked = jnp.concatenate(
        [
            heat_state[None],
            dual_heat_after[None],
            shallower_adjacent * dual_heat_after[None],
            deeper_adjacent * dual_heat_after[None],
            local_viscosity[None],
        ],
        0,
    )
    bordered_array = finest_halo_cells(stacked)
    driving_source = motion_source(bordered_array[0], forward_motion, dual_heat_after)
    advected_result = advect_dual_heat(bordered_array[2:5], bordered_array[5:8], bordered_array[1])
    face_coef = coefficients(bordered_array[8], 1.0)
    diagonal = sum(face_coef)
    coarse_visc = restrict(local_viscosity)
    coarse_coef = coefficients(coarse_halo(coarse_visc[None])[0], 0.25)
    coarse_diag = sum(coarse_coef)
    deep_static = deep_halo(jnp.concatenate([local_viscosity[None], driving_source], 0))
    cycle_coef = coefficients(deep_static[0], 1.0)
    cycle_source = deep_static[1:4, 1:-1, 1:-1, 1:-1]
    inside = inside_mask(extent_first, extent_second, extent_vertical)
    safe_diag = jnp.where(inside, sum(cycle_coef), 1.0)
    total_cells = (
        extent_first
        * extent_second
        * extent_vertical
        * lax.axis_size("gx")
        * lax.axis_size("gy")
        * lax.axis_size("gz")
    )
    velocity = jnp.zeros(forward_motion.shape, jnp.float32)
    mean_stress = jnp.zeros(saved_heat_state.shape, jnp.float32)
    for iteration in range(SCHUR_ITERS):
        if iteration == 0:
            cycle_resid = cycle_source
        else:
            flow_press = deep_halo(jnp.concatenate([velocity, mean_stress[None]], 0))
            cycle_resid = (
                cycle_source - apply_operator(cycle_coef, flow_press[0:3]) - gradient(flow_press[3])
            )
        cycle_corr = jnp.where(inside, JACOBI_WEIGHT * cycle_resid / safe_diag, 0.0)
        residual = cycle_resid[:, 1:-1, 1:-1, 1:-1]
        correction = cycle_corr[:, 1:-1, 1:-1, 1:-1]
        residual_two = residual - apply_operator(face_coef, cycle_corr)
        coarse_res = restrict(residual_two)
        coarse_corr = coarse_solve(coarse_res, coarse_coef, coarse_diag, coarse_halo)
        correction = correction + prolong(coarse_corr)
        correction = (
            correction
            + JACOBI_WEIGHT
            * (residual - apply_operator(face_coef, finest_halo_cells(correction)))
            / diagonal
        )
        velocity = velocity + correction
        spread_flow = divergence(finest_halo_cells(velocity))
        mean_stress = mean_stress - SCHUR_WEIGHT * local_viscosity * spread_flow
        mean_stress = mean_stress - lax.psum(jnp.sum(mean_stress), ("gx", "gy", "gz")) / total_cells
    adj_temp_prev = advected_result + RAYLEIGH * velocity[2]
    return (adj_temp_prev, velocity, mean_stress)


SUB = 8
LANES = 128
FIELDS = 6
BACK = 5
EDGE = 2
PHASE = 8
VMEM_LIMIT = 48 * 1024 * 1024


def slab_plan_fits(mesh, shape):
    sizes = mesh.shape
    group = sizes["gx"] * sizes["gy"]
    block = (shape[0] // sizes["gx"], shape[1] // sizes["gy"], shape[2] // sizes["gz"])
    return (
        group == SUB
        and block[0] == SUB
        and block[0] * block[1] == LANES
        and block[1] * group == LANES
        and block[2] == LANES
        and block[2] == group * 2 * PHASE
    )


class Slabs:
    def __init__(self, mesh, shape):
        self.nx, self.ny, self.nz = mesh.shape["gx"], mesh.shape["gy"], mesh.shape["gz"]
        self.group = self.nx * self.ny
        self.width, self.breadth, self.height = shape
        self.block_x, self.block_y, self.block_z = (
            shape[0] // self.nx,
            shape[1] // self.ny,
            shape[2] // self.nz,
        )
        self.slab = self.block_z // self.group
        self.halo = self.slab + EDGE
        self.layers = self.slab + 2 * self.halo
        self.cells = self.width * self.breadth * self.height
        self.place = []
        for ix in range(self.nx):
            for iy in range(self.ny):
                step = ix if iy % 2 == 0 else self.nx - 1 - ix
                self.place.append(iy * self.nx + step)
        self.holder = [self.place.index(j) for j in range(self.group)]

    def device(self, slab):
        return self.holder[slab % self.group] * self.nz + slab // self.group

    def shifts(self, distance):
        count = self.group * self.nz
        return [
            (self.device(p), self.device(p + distance))
            for p in range(count)
            if 0 <= p + distance < count
        ]

    def index(self):
        ix, iy = lax.axis_index("gx"), lax.axis_index("gy")
        step = jnp.where(iy % 2 == 0, ix, self.nx - 1 - ix)
        return lax.axis_index("gz") * self.group + iy * self.nx + step


def tile_iota():
    s = lax.broadcasted_iota(jnp.int32, (1, SUB, LANES), 1)
    l = lax.broadcasted_iota(jnp.int32, (1, SUB, LANES), 2)
    return s, l


def swap_granules(tiles, granule):
    lane = lax.broadcasted_iota(jnp.int32, (SUB, LANES), 1) // granule
    for bit in (1, 2, 4):
        low = (lane & bit) == 0
        new = list(tiles)
        for a in range(SUB):
            if a & bit:
                continue
            b = a | bit
            new[a] = jnp.where(low, tiles[a], pltpu.roll(tiles[b], granule * bit, 1))
            new[b] = jnp.where(low, pltpu.roll(tiles[a], LANES - granule * bit, 1), tiles[b])
        tiles = new
    return tiles


class Tiles:
    def __init__(self, breadth):
        self.breadth = breadth
        self.s, self.l = tile_iota()
        self.x = (self.l // breadth) * SUB + self.s
        self.y = self.l % breadth
        self.width = SUB * (LANES // breadth)

    def xs(self, f, d):
        t = pltpu.roll(f, (-d) % SUB, 1)
        u = pltpu.roll(t, (-self.breadth if d > 0 else self.breadth) % LANES, 2)
        crosses = (self.s >= SUB - d) if d > 0 else (self.s < -d)
        return jnp.where(crosses, u, t)

    def ys(self, f, d):
        return pltpu.roll(f, (-d) % LANES, 2)

    def masks(self, d, value):
        keep = (
            self.x < self.width - d,
            self.x >= d,
            self.y < self.breadth - d,
            self.y >= d,
        )
        return [jnp.where(k, jnp.float32(value), jnp.float32(0.0)) for k in keep]

    def four(self, f, d):
        return [self.xs(f, d), self.xs(f, -d), self.ys(f, d), self.ys(f, -d)]

    def block_sum(self, f):
        f = f + jnp.where(self.l % 2 == 0, pltpu.roll(f, LANES - 1, 2), pltpu.roll(f, 1, 2))
        return f + jnp.where(self.s % 2 == 0, pltpu.roll(f, SUB - 1, 1), pltpu.roll(f, 1, 1))


def get(ref, i, n, *lead):
    return ref[(*lead, pl.ds(pl.multiple_of(i * SUB, SUB), n * SUB), slice(None))].reshape(
        n, SUB, LANES
    )


def put(ref, i, value, *lead):
    n = value.shape[0]
    ref[(*lead, pl.ds(pl.multiple_of(i * SUB, SUB), n * SUB), slice(None))] = value.reshape(
        n * SUB, LANES
    )


def sweep(lo, hi, n, body, most=4):
    count = (hi - lo) // n
    assert count * n == hi - lo
    unroll = max(u for u in range(1, most + 1) if count % u == 0)

    def step(t, _):
        todo = []
        for u in range(unroll):
            todo += body(lo + (t * unroll + u) * n)
        for ref, i, value, *lead in todo:
            put(ref, i, value, *lead)
        return 0

    lax.fori_loop(0, count // unroll, step, 0)


def regroup(source, target, granule, count, most=3):
    unroll = max(u for u in range(1, most + 1) if count % u == 0)

    def step(t, _):
        groups = [source(t * unroll + u) for u in range(unroll)]
        groups = [swap_granules(tiles, granule) for tiles in groups]
        for u in range(unroll):
            target(t * unroll + u, groups[u])
        return 0

    lax.fori_loop(0, count // unroll, step, 0)


def pack_kernel(geo, heat_in, flow_in, dual_in, kind_in, out, heat, flow, dual, kind, sems):
    b, e = geo.slab, EDGE
    pairs = ((heat_in, heat), (flow_in, flow), (dual_in, dual), (kind_in, kind))
    copies = [
        pltpu.make_async_copy(source, target, sems.at[k])
        for k, (source, target) in enumerate(pairs)
    ]
    for copy in copies:
        copy.start()
    for copy in copies:
        copy.wait()
    flat = [heat[...], flow[0], flow[1], flow[2], dual[...], kind[...].astype(jnp.float32)]
    turned = [f.reshape(LANES, LANES).T for f in flat]
    for j in range(geo.group):
        q = geo.holder[j]
        for f in range(FIELDS):
            out[q, f * b : (f + 1) * b, :] = turned[f][j * b : (j + 1) * b]
        tail = FIELDS * b
        first = jnp.concatenate([turned[f][j * b : j * b + e] for f in range(4)], 0)
        last = jnp.concatenate([turned[f][(j + 1) * b - e : (j + 1) * b] for f in range(4)], 0)
        out[q, tail : tail + SUB, :] = first
        out[q, tail + SUB : tail + 2 * SUB, :] = last


STATIC_FINE = ("s0", "s1", "s2", "visc", "w", "diag", "cxp", "cxm", "cyp", "cym", "cz")
STATIC_COARSE = ("kxp", "kxm", "kyp", "kym", "kzp", "kzm")


FORWARD, ADJOINT, RESPONSE = range(3)


def inside(geo, i, n):
    layer = geo.index() * geo.slab - geo.halo + i
    layer = layer + lax.broadcasted_iota(jnp.int32, (n, 1, 1), 0)
    return (layer >= 0) & (layer < geo.height)


def iterate(geo, st, v, p, res, cor, cor2, cc0, cc1, seqs, lo, hi, first=(), mean=None):
    tl = Tiles(geo.breadth)
    half = tl.masks(1, 0.5)
    comps = [3 * q + k for q in seqs for k in range(3)]
    keep = 1.0 - JACOBI_WEIGHT

    def faces(i, n):
        c = [get(st[name], i, n) for name in ("cxp", "cxm", "cyp", "cym")]
        return c, get(st["cz"], i, n), get(st["cz"], i - 1, n)

    def around(coef, ref, i, n, *lead):
        (c, up, down) = coef
        f = get(ref, i, n, *lead)
        total = up * get(ref, i + 1, n, *lead) + down * get(ref, i - 1, n, *lead)
        for a, b in zip(c, tl.four(f, 1)):
            total = total + a * b
        return f, total

    def spread(i, n, q):
        if q != ADJOINT:
            return get(p, i, n, q)
        value = SCHUR_WEIGHT * get(st["visc"], i, n)
        return value if q in first else value * get(p, i, n, q)

    def residual(i):
        n, todo = 2, []
        apply = FORWARD in seqs and FORWARD not in first
        coef = faces(i, n) if apply else None
        diag = get(st["diag"], i, n) if apply else None
        w = get(st["w"], i, n)
        for q in seqs:
            slope = None
            if not (q == FORWARD and q in first):
                xp, xm, yp, ym = tl.four(spread(i, n, q), 1)
                slope = [
                    half[0] * xp - half[1] * xm,
                    half[2] * yp - half[3] * ym,
                    0.5 * (spread(i + 1, n, q) - spread(i - 1, n, q)),
                ]
            for k in range(3):
                c = 3 * q + k
                if q == FORWARD:
                    value = get(st["s%d" % k], i, n)
                    if slope is not None:
                        f, total = around(coef, v, i, n, c)
                        value = value - slope[k] - (diag * f - total)
                elif q == RESPONSE:
                    value = -slope[k]
                else:
                    value = slope[k] if q in first else get(cor, i, n, c) + slope[k]
                todo += [(res, i, value, c), (cor, i, w * value, c)]
        return todo

    sweep(lo - 8, hi + 8, 2, residual)

    def restricted(i):
        pair, todo = i // 2, []
        coef = faces(i, 2)
        wc = 0.125 * get(st["wc"], pair, 1)
        for c in comps:
            _, total = around(coef, cor, i, 2, c)
            left = keep * get(res, i, 2, c) + total
            todo.append((cc0, pair, wc * tl.block_sum(left[0:1] + left[1:2]), c))
        return todo

    sweep(lo - 6, hi + 6, 2, restricted)

    def coarse_step(src, c, pair, n):
        f = get(src, pair, n, c)
        value = get(cc0, pair, n, c) + keep * f
        value = value + get(st["kzp"], pair, n) * get(src, pair + 1, n, c)
        value = value + get(st["kzm"], pair, n) * get(src, pair - 1, n, c)
        for name, b in zip(("kxp", "kxm", "kyp", "kym"), tl.four(f, 2)):
            value = value + get(st[name], pair, n) * b
        return value

    def sweep_one(pair):
        return [(cc1, pair, coarse_step(cc0, c, pair, 2), c) for c in comps]

    sweep((lo - 4) // 2, (hi + 4) // 2, 2, sweep_one)

    def sweep_two(pair):
        todo = []
        for c in comps:
            value = coarse_step(cc1, c, pair, 2)
            fine = jnp.broadcast_to(value[:, None], (2, 2, SUB, LANES)).reshape(4, SUB, LANES)
            todo.append((cor2, 2 * pair, get(cor, 2 * pair, 4, c) + fine, c))
        return todo

    sweep((lo - 2) // 2, (hi + 2) // 2, 2, sweep_two)

    def velocity(i):
        n, todo = 2, []
        coef = faces(i, n)
        w = get(st["w"], i, n)
        for c in comps:
            f, total = around(coef, cor2, i, n, c)
            value = get(cor, i, n, c) + keep * f + w * total
            if c // 3 == FORWARD and FORWARD not in first:
                value = get(v, i, n, c) + value
            todo.append((v, i, value, c))
        return todo

    sweep(lo - 2, hi + 2, 2, velocity)

    def pressure(i):
        n, todo = 2, []
        visc = SCHUR_WEIGHT * get(st["visc"], i, n)
        coef = faces(i, n) if ADJOINT in seqs else None
        for q in seqs:
            a, b = get(v, i, n, 3 * q), get(v, i, n, 3 * q + 1)
            div = half[0] * tl.xs(a, 1) - half[1] * tl.xs(a, -1)
            div = div + half[2] * tl.ys(b, 1) - half[3] * tl.ys(b, -1)
            div = div + 0.5 * (get(v, i + 1, n, 3 * q + 2) - get(v, i - 1, n, 3 * q + 2))
            if q == ADJOINT:
                todo.append((p, i, get(p, i, n, q) + div, q))
                for c in range(3 * q, 3 * q + 3):
                    f, total = around(coef, v, i, n, c)
                    value = get(res, i, n, c) - (get(st["diag"], i, n) * f - total)
                    todo.append((cor, i, value, c))
                continue
            value = -(visc * div)
            if not (q == FORWARD and q in first):
                value = get(p, i, n, q) + value
            if mean is not None:
                value = value - jnp.where(inside(geo, i, n), mean, 0.0)
            todo.append((p, i, value, q))
        return todo

    sweep(lo, hi, 2, pressure)


def total(value):
    return jnp.sum(jnp.sum(value, axis=0), axis=(0, 1), keepdims=True)


def product(geo, left, right):
    value = 0.0
    for a, b in zip(left, right):
        value = value + get(a[0], a[1], geo.slab, *a[2:]) * get(b[0], b[1], geo.slab, *b[2:])
    return total(value)


def in_lanes(values, rows):
    lane = lax.broadcasted_iota(jnp.int32, (rows, LANES), 1)
    out = jnp.zeros((rows, LANES), jnp.float32)
    for k, value in values:
        out = jnp.where(lane == k, value, out)
    return out


def first_kernel(geo, stiffness, own, low, high, low_edge, high_edge, *refs):
    names = STATIC_FINE + STATIC_COARSE + ("wc",)
    st = dict(zip(names, refs[: len(names)]))
    moved, state, sums, raw, spare, heat, vc, kept, *work = refs[len(names) :]
    v, p, res, cor, cor2, cc0, cc1 = work
    tl = Tiles(geo.breadth)
    b, h, n_layers = geo.slab, geo.halo, geo.layers
    granule = geo.block_y

    for source, base in ((low, EDGE), (own, h), (high, h + b)):

        def load(t, source=source):
            row = pl.multiple_of(t * SUB, SUB)
            return [source[q, pl.ds(row, SUB), :] for q in range(geo.group)]

        def store(t, tiles, base=base):
            f, d = t // (b // SUB), (t % (b // SUB)) * SUB
            start = (f * n_layers + base + d) * SUB
            for s, tile in enumerate(tiles):
                raw[pl.ds(start + s, SUB, stride=SUB), :] = tile

        regroup(load, store, granule, FIELDS * (b // SUB))
    for source, base in ((low_edge, 0), (high_edge, n_layers - EDGE)):
        tiles = [source[q] for q in range(geo.group)]
        for s, tile in enumerate(swap_granules(tiles, granule)):
            spare[pl.ds(s, SUB, stride=SUB), :] = tile
        for f in range(4):
            start = (f * n_layers + base) * SUB
            raw[start : start + EDGE * SUB, :] = spare[f * EDGE * SUB : (f + 1) * EDGE * SUB, :]

    def field(f, i, n):
        return get(raw, f * n_layers + i, n)

    one = tl.masks(1, 1.0)

    def masked_four(f):
        return [m * g for m, g in zip(one, tl.four(f, 1))]

    def advance(old, new):
        def body(i):
            n = 2
            f = old(i, n)
            beside = masked_four(f) + [old(i + 1, n), old(i - 1, n)]
            drift = 0.0
            for k in range(3):
                flow = field(1 + k, i, n)
                drift = drift + jnp.maximum(flow, 0.0) * (f - beside[2 * k + 1])
                drift = drift + jnp.minimum(flow, 0.0) * (beside[2 * k] - f)
            spread = sum(beside) - 6.0 * f
            value = f - INCREMENT_DT * drift + INCREMENT_DT * DIFFUSIVITY * spread
            return [(heat, i, jnp.where(inside(geo, i, n), value, 0.0), new)]

        return body

    sweep(1, n_layers - 1, 2, advance(lambda i, n: field(0, i, n), 0), 5)
    sweep(2, n_layers - 2, 2, advance(lambda i, n: get(heat, i, n, 0), 1))

    def viscosity(i):
        n = 2
        kind = field(5, i, n)
        base = jnp.zeros(kind.shape, jnp.float32)
        for layer in range(LAYERS):
            base = base + jnp.where(kind == float(layer), stiffness[layer], 0.0)
        value = base * jnp.exp(-ACTIVATION_ENERGY * get(heat, i, n, 1))
        value = jnp.where(inside(geo, i, n), value, 0.0)
        coarse = 0.125 * tl.block_sum(value[0:1] + value[1:2])
        return [(st["visc"], i, value), (vc, i // 2, coarse)]

    sweep(2, n_layers - 2, 2, viscosity)

    def statics(i):
        n = 2
        c = get(st["visc"], i, n)
        beside = masked_four(c) + [get(st["visc"], i + 1, n), get(st["visc"], i - 1, n)]
        face = [0.5 * (c + o) for o in beside]
        diag = sum(face)
        todo = [
            (st[name], i, m * f)
            for name, m, f in zip(("cxp", "cxm", "cyp", "cym"), one, face)
        ]
        todo += [(st["cz"], i, face[4]), (st["diag"], i, diag)]
        todo.append((st["w"], i, jnp.where(inside(geo, i, n), JACOBI_WEIGHT / diag, 0.0)))
        f = get(heat, i, n, 1)
        beside = masked_four(f) + [get(heat, i + 1, n, 1), get(heat, i - 1, n, 1)]
        dual = -INCREMENT_DT * field(4, i, n)
        for k in range(3):
            flow = field(1 + k, i, n)
            step = jnp.where(flow > 0, f - beside[2 * k + 1], beside[2 * k] - f)
            todo.append((st["s%d" % k], i, dual * step))
        return todo

    sweep(2, n_layers - 2, 2, statics)

    two = tl.masks(2, 1.0)

    def coarse_statics(pair):
        n = 1
        c = get(vc, pair, n)
        beside = [m * g for m, g in zip(two, tl.four(c, 2))]
        beside = beside + [get(vc, pair + 1, n), get(vc, pair - 1, n)]
        face = [0.25 * (0.5 * (c + o)) for o in beside]
        wc = JACOBI_WEIGHT / sum(face)
        wc = jnp.where(inside(geo, 2 * pair, 1), wc, 0.0)
        return [(st["wc"], pair, wc)] + [
            (st[name], pair, wc * (m * f))
            for name, m, f in zip(STATIC_COARSE, two + [1.0, 1.0], face)
        ]

    sweep(1, n_layers // 2 - 1, 1, coarse_statics)

    def transport(i):
        n = 2
        dual = field(4, i, n)
        up, down = field(4, i + 1, n), field(4, i - 1, n)
        value = dual + INCREMENT_DT * DIFFUSIVITY * (
            sum(masked_four(dual)) + up + down - 6.0 * dual
        )
        for k in range(3):
            a = jnp.maximum(field(1 + k, i, n), 0.0) * dual
            c = jnp.minimum(field(1 + k, i, n), 0.0) * dual
            if k == 0:
                ahead, behind = one[0] * tl.xs(a, 1), one[1] * tl.xs(c, -1)
            elif k == 1:
                ahead, behind = one[2] * tl.ys(a, 1), one[3] * tl.ys(c, -1)
            else:
                ahead = jnp.maximum(field(3, i + 1, n), 0.0) * up
                behind = jnp.minimum(field(3, i - 1, n), 0.0) * down
            value = value - INCREMENT_DT * (a - ahead + behind - c)
        return [(moved, i - h, value)]

    sweep(h, h + b, 2, transport)

    def unit(i):
        value = jnp.where(inside(geo, i, 4), 1.0, 0.0)
        value = jnp.broadcast_to(value, (4, SUB, LANES))
        return [(p, i, value, ADJOINT), (p, i, value, RESPONSE)]

    sweep(0, n_layers, 4, unit)

    work = (v, p, res, cor, cor2, cc0, cc1)
    both = (FORWARD, ADJOINT)
    iterate(geo, st, *work, both, h - PHASE, h + b + PHASE, both)

    def fields(q):
        three = cor if q == ADJOINT else v
        return [(three, h, 3 * q + k) for k in range(3)] + [(p, h, q)]

    def count(q):
        return total(get(p, h, b, q))

    sums_of = [count(FORWARD), count(ADJOINT), product(geo, fields(ADJOINT), fields(FORWARD))]
    for k, (ref, layer, lead) in enumerate(fields(ADJOINT)):
        put(kept, 0, get(ref, layer, b, lead), k)
    iterate(geo, st, *work, (FORWARD, ADJOINT, RESPONSE), h, h + b, (RESPONSE,))
    earlier = [(kept, 0, k) for k in range(4)]
    sums_of += [count(FORWARD), count(ADJOINT), product(geo, earlier, fields(FORWARD))]
    sums_of += [product(geo, fields(ADJOINT), fields(q)) for q in (FORWARD, RESPONSE)]
    sums[...] = in_lanes(enumerate(sums_of), sums.shape[0])
    for at, q in enumerate((FORWARD, RESPONSE)):
        for k, (ref, layer, lead) in enumerate(fields(q)):
            put(state, 0, get(ref, layer, b, lead), 4 * at + k)


def means(geo, sums):
    row = jnp.sum(sums, axis=0, keepdims=True) / geo.cells
    lane = lax.broadcasted_iota(jnp.int32, row.shape, 1)

    def at(k):
        return jnp.sum(jnp.where(lane == k, row, 0.0), axis=1, keepdims=True)

    p1, q1, l1_x1, p2, q2, l1_x2, l2_x2, l2_r1 = [at(k) for k in range(8)]
    m1 = p1
    m2 = p2 - m1 * q1
    m3 = l1_x2 - m1 * q2 - m2 * q1 + p1
    m4 = l2_x2 - m1 * l2_r1 - m2 * q2 + l1_x1 - m3 * q1 + p1
    return m1, m2, m3, m4


def second_kernel(geo, *refs):
    names = STATIC_FINE + STATIC_COARSE + ("wc",)
    st = dict(zip(names, refs[: len(names)]))
    state, low, high, sums, moved, out, mixed, *work = refs[len(names) :]
    v, p, res, cor, cor2, cc0, cc1 = work
    b, h = geo.slab, geo.halo
    m1, m2, m3, m4 = means(geo, sums[...])
    for source, base in ((low, h - b), (state, h), (high, h + b)):
        for k in range(4):
            value = get(source, 0, b, k) - m1 * get(source, 0, b, 4 + k)
            if k < 3:
                put(v, base, value, k)
            else:
                put(p, base, value - jnp.where(inside(geo, base, b), m2, 0.0), 0)
    iterate(geo, st, *work, (FORWARD,), h - PHASE, h + b + PHASE, mean=m3)
    iterate(geo, st, *work, (FORWARD,), h, h + b, mean=m4)
    for k in range(3):
        put(mixed, k * b, get(v, h, b, k))
    put(mixed, 3 * b, get(p, h, b, 0))
    put(mixed, 4 * b, get(moved, 0, b) + get(v, h, b, 2))

    def load(t):
        return [mixed[pl.ds(t * SUB * SUB + s, SUB, stride=SUB), :] for s in range(SUB)]

    def store(t, tiles):
        for q, tile in enumerate(tiles):
            out[q, pl.ds(pl.multiple_of(t * SUB, SUB), SUB), :] = tile

    regroup(load, store, geo.block_y, BACK * (b // SUB))


def unpack_kernel(geo, chunks, heat, flow, pressure):
    b = geo.slab
    shape = (geo.block_x, geo.block_y, geo.block_z)
    for f in range(BACK):
        rows = [chunks[geo.holder[j], f * b : (f + 1) * b, :] for j in range(geo.group)]
        block = jnp.concatenate(rows, 0).T.reshape(shape)
        if f < 3:
            flow[f] = block
        elif f == 3:
            pressure[...] = block
        else:
            heat[...] = block


def call(kernel, out, scratch, *args, smem=(), hbm=()):
    f32 = jnp.float32
    specs = [
        pl.BlockSpec(
            memory_space=pltpu.SMEM if i in smem else pltpu.HBM if i in hbm else pltpu.VMEM
        )
        for i in range(len(args))
    ]
    return pl.pallas_call(
        kernel,
        out_shape=[jax.ShapeDtypeStruct(s, f32) for s in out],
        in_specs=specs,
        out_specs=[pl.BlockSpec(memory_space=pltpu.VMEM) for _ in out],
        scratch_shapes=[pltpu.VMEM(s, f32) if isinstance(s, tuple) else s for s in scratch],
        compiler_params=pltpu.CompilerParams(vmem_limit_bytes=VMEM_LIMIT),
    )(*args)


def slab_shards(geo, heat, flow, dual, kind, stiffness):
    b, n_layers, group = geo.slab, geo.layers, geo.group
    rows = FIELDS * b
    inputs = (heat, flow, dual, kind)
    (chunks,) = call(
        functools.partial(pack_kernel, geo),
        [(group, rows + 2 * SUB, LANES)],
        [pltpu.VMEM(a.shape, a.dtype) for a in inputs] + [pltpu.SemaphoreType.DMA((4,))],
        *inputs,
        hbm=range(4),
    )
    own = lax.all_to_all(chunks, ("gx", "gy"), 0, 0, tiled=True)
    axes = ("gx", "gy", "gz")
    low = lax.ppermute(own, axes, geo.shifts(1))
    high = lax.ppermute(own, axes, geo.shifts(-1))
    high_edge = lax.ppermute(own[:, rows : rows + SUB], axes, geo.shifts(-2))
    low_edge = lax.ppermute(own[:, rows + SUB :], axes, geo.shifts(2))

    fine, coarse = (n_layers * SUB, LANES), (n_layers // 2 * SUB, LANES)
    devices = group * geo.nz
    n_fine, n_coarse = len(STATIC_FINE), len(STATIC_COARSE) + 1
    slab = (b * SUB, LANES)

    def work(n):
        fields = [(3 * n, *fine), (n, *fine)] + [(3 * n, *fine)] * 3
        return fields + [(3 * n, *coarse)] * 2

    *static, moved, state, sums = call(
        functools.partial(first_kernel, geo),
        [fine] * n_fine + [coarse] * n_coarse + [slab, (8, *slab), (devices, LANES)],
        [(FIELDS * n_layers * SUB, LANES), (SUB * SUB, LANES), (2, *fine), coarse, (4, *slab)]
        + work(3),
        stiffness,
        own,
        low,
        high,
        low_edge,
        high_edge,
        smem=(0,),
    )
    sums = lax.all_to_all(sums, axes, 0, 0, tiled=True)
    from_low = lax.ppermute(state, axes, geo.shifts(1))
    from_high = lax.ppermute(state, axes, geo.shifts(-1))
    (chunks,) = call(
        functools.partial(second_kernel, geo),
        [(group, BACK * b, LANES)],
        [(BACK * b * SUB, LANES)] + work(1),
        *static,
        state,
        from_low,
        from_high,
        sums,
        moved,
    )
    chunks = lax.all_to_all(chunks, ("gx", "gy"), 0, 0, tiled=True)
    block = (geo.block_x, geo.block_y, geo.block_z)
    return tuple(
        call(functools.partial(unpack_kernel, geo), [block, (3, *block), block], [], chunks)
    )


def solution(mesh):
    in_specs = (
        P("gx", "gy", "gz"),
        P(None, "gx", "gy", "gz"),
        P("gx", "gy", "gz"),
        P("gx", "gy", "gz"),
        P(),
    )
    out_specs = (P("gx", "gy", "gz"), P(None, "gx", "gy", "gz"), P("gx", "gy", "gz"))

    def program(saved_heat_state, *others):
        shape = saved_heat_state.shape
        plan = shards
        if slab_plan_fits(mesh, shape):
            plan = functools.partial(slab_shards, Slabs(mesh, shape))
        return jax.shard_map(
            plan, mesh=mesh, in_specs=in_specs, out_specs=out_specs, check_vma=False
        )(saved_heat_state, *others)

    return program
```

```python
import functools

import jax
import jax.numpy as jnp
from jax import lax
from jax.experimental import pallas as pl
from jax.experimental.pallas import tpu as pltpu
from jax.sharding import PartitionSpec as P

RECOMPUTE = 2
SCHUR_ITERS = 4
COARSE_SWEEPS = 3
LAYERS = 8


INCREMENT_DT = 0.2
DIFFUSIVITY = 0.3
ACTIVATION_ENERGY = 2.3
JACOBI_WEIGHT = 0.7
SCHUR_WEIGHT = 0.5
RAYLEIGH = 1.0


def extended(block, sides, width):
    for axis, dim in sides:
        count = lax.axis_size(axis)
        forward = [(i, i + 1) for i in range(count - 1)]
        backward = [(target, source) for source, target in forward]
        low = lax.ppermute(
            lax.slice_in_dim(block, block.shape[dim] - width, None, axis=dim), axis, forward
        )
        high = lax.ppermute(lax.slice_in_dim(block, 0, width, axis=dim), axis, backward)
        block = jnp.concatenate([low, block, high], axis=dim)
    return block


def neighbours(bordered_array):
    centre = bordered_array[..., 1:-1, 1:-1, 1:-1]
    beside_all = [
        bordered_array[..., 2:, 1:-1, 1:-1],
        bordered_array[..., :-2, 1:-1, 1:-1],
        bordered_array[..., 1:-1, 2:, 1:-1],
        bordered_array[..., 1:-1, :-2, 1:-1],
        bordered_array[..., 1:-1, 1:-1, 2:],
        bordered_array[..., 1:-1, 1:-1, :-2],
    ]
    return (centre, beside_all)


def finest_halo_cells(field):
    return extended(field, (("gx", 1), ("gy", 2), ("gz", 3)), 1)


def deep_halo(field):
    return extended(field, (("gx", 1), ("gy", 2), ("gz", 3)), 2)


def coarse_halo(field):
    return extended(field, (("gx", 1), ("gy", 2), ("gz", 3)), 1)


def march_backward(bordered_array, shallower_adjacent, deeper_adjacent):
    centre, beside_all = neighbours(bordered_array)
    drift = 0.0
    for dim_index in range(3):
        drift = (
            drift
            + shallower_adjacent[dim_index] * (centre - beside_all[2 * dim_index + 1])
            + deeper_adjacent[dim_index] * (beside_all[2 * dim_index] - centre)
        )
    spread = sum(beside_all) - 6.0 * centre
    return centre - INCREMENT_DT * drift + INCREMENT_DT * DIFFUSIVITY * spread


def motion_source(bordered_heat, forward_motion, dual_heat_after):
    centre, beside_all = neighbours(bordered_heat)
    device_pieces = [
        jnp.where(
            forward_motion[dim_index] > 0,
            centre - beside_all[2 * dim_index + 1],
            beside_all[2 * dim_index] - centre,
        )
        for dim_index in range(3)
    ]
    return -INCREMENT_DT * dual_heat_after[None] * jnp.stack(device_pieces)


def advect_dual_heat(pos_padded, neg_padded, lam_padded):
    centre, beside_all = neighbours(lam_padded)
    result = centre + INCREMENT_DT * DIFFUSIVITY * (sum(beside_all) - 6.0 * centre)
    for dim_index in range(3):
        pos_centre, pos_around = neighbours(pos_padded[dim_index])
        neg_centre, neg_around = neighbours(neg_padded[dim_index])
        result = result - INCREMENT_DT * (
            pos_centre - pos_around[2 * dim_index] + neg_around[2 * dim_index + 1] - neg_centre
        )
    return result


def coefficients(bordered_array, factor):
    centre, beside_all = neighbours(bordered_array)
    return [factor * (0.5 * (centre + other)) for other in beside_all]


def apply_operator(face_coef, bordered_array):
    centre, beside_all = neighbours(bordered_array)
    return sum((coef * (centre - other) for coef, other in zip(face_coef, beside_all)))


def gradient(bordered_array):
    centre, beside_all = neighbours(bordered_array)
    return jnp.stack(
        [
            0.5 * (beside_all[2 * dim_index] - beside_all[2 * dim_index + 1])
            for dim_index in range(3)
        ]
    )


def divergence(bordered_array):
    centre, beside_all = neighbours(bordered_array)
    return sum(
        (
            0.5 * (beside_all[2 * dim_index][dim_index] - beside_all[2 * dim_index + 1][dim_index])
            for dim_index in range(3)
        )
    )


def restrict(field):
    leading = field.shape[:-3]
    cells_x, cells_y, cells_z = field.shape[-3:]
    blocks = field.reshape(leading + (cells_x // 2, 2, cells_y // 2, 2, cells_z // 2, 2))
    return blocks.mean(axis=(-5, -3, -1))


def prolong(field):
    return jnp.repeat(jnp.repeat(jnp.repeat(field, 2, axis=-3), 2, axis=-2), 2, axis=-1)


def evaluate_viscosity(rheology_class, class_base_stiffness):
    base = jnp.zeros(rheology_class.shape, jnp.float32)
    for layer_index in range(LAYERS):
        base = base + jnp.where(
            rheology_class == layer_index, class_base_stiffness[layer_index], 0.0
        )
    return base


def inside_mask(extent_first, extent_second, extent_vertical):
    index_x = (
        lax.axis_index("gx") * extent_first + jnp.arange(extent_first + 2, dtype=jnp.int32) - 1
    )
    index_y = (
        lax.axis_index("gy") * extent_second + jnp.arange(extent_second + 2, dtype=jnp.int32) - 1
    )
    index_z = (
        lax.axis_index("gz") * extent_vertical
        + jnp.arange(extent_vertical + 2, dtype=jnp.int32)
        - 1
    )
    inside_x = (index_x >= 0) & (index_x < extent_first * lax.axis_size("gx"))
    inside_y = (index_y >= 0) & (index_y < extent_second * lax.axis_size("gy"))
    inside_z = (index_z >= 0) & (index_z < extent_vertical * lax.axis_size("gz"))
    return inside_x[:, None, None] & inside_y[None, :, None] & inside_z[None, None, :]


def coarse_solve(coarse_res, coarse_coef, coarse_diag, pad_field):
    coarse_corr = JACOBI_WEIGHT * coarse_res / coarse_diag
    for sweep in range(COARSE_SWEEPS - 1):
        coarse_corr = (
            coarse_corr
            + JACOBI_WEIGHT
            * (coarse_res - apply_operator(coarse_coef, pad_field(coarse_corr)))
            / coarse_diag
        )
    return coarse_corr


def shards(saved_heat_state, forward_motion, dual_heat_after, rheology_class, class_base_stiffness):
    extent_first, extent_second, extent_vertical = saved_heat_state.shape
    shallower_adjacent = jnp.maximum(forward_motion, 0.0)
    deeper_adjacent = jnp.minimum(forward_motion, 0.0)
    heat_state = saved_heat_state
    for repeat_index in range(RECOMPUTE):
        heat_state = march_backward(
            finest_halo_cells(heat_state[None])[0], shallower_adjacent, deeper_adjacent
        )
    local_viscosity = evaluate_viscosity(rheology_class, class_base_stiffness) * jnp.exp(
        -ACTIVATION_ENERGY * heat_state
    )
    stacked = jnp.concatenate(
        [
            heat_state[None],
            dual_heat_after[None],
            shallower_adjacent * dual_heat_after[None],
            deeper_adjacent * dual_heat_after[None],
            local_viscosity[None],
        ],
        0,
    )
    bordered_array = finest_halo_cells(stacked)
    driving_source = motion_source(bordered_array[0], forward_motion, dual_heat_after)
    advected_result = advect_dual_heat(bordered_array[2:5], bordered_array[5:8], bordered_array[1])
    face_coef = coefficients(bordered_array[8], 1.0)
    diagonal = sum(face_coef)
    coarse_visc = restrict(local_viscosity)
    coarse_coef = coefficients(coarse_halo(coarse_visc[None])[0], 0.25)
    coarse_diag = sum(coarse_coef)
    deep_static = deep_halo(jnp.concatenate([local_viscosity[None], driving_source], 0))
    cycle_coef = coefficients(deep_static[0], 1.0)
    cycle_source = deep_static[1:4, 1:-1, 1:-1, 1:-1]
    inside = inside_mask(extent_first, extent_second, extent_vertical)
    safe_diag = jnp.where(inside, sum(cycle_coef), 1.0)
    total_cells = (
        extent_first
        * extent_second
        * extent_vertical
        * lax.axis_size("gx")
        * lax.axis_size("gy")
        * lax.axis_size("gz")
    )
    velocity = jnp.zeros(forward_motion.shape, jnp.float32)
    mean_stress = jnp.zeros(saved_heat_state.shape, jnp.float32)
    for iteration in range(SCHUR_ITERS):
        if iteration == 0:
            cycle_resid = cycle_source
        else:
            flow_press = deep_halo(jnp.concatenate([velocity, mean_stress[None]], 0))
            cycle_resid = (
                cycle_source - apply_operator(cycle_coef, flow_press[0:3]) - gradient(flow_press[3])
            )
        cycle_corr = jnp.where(inside, JACOBI_WEIGHT * cycle_resid / safe_diag, 0.0)
        residual = cycle_resid[:, 1:-1, 1:-1, 1:-1]
        correction = cycle_corr[:, 1:-1, 1:-1, 1:-1]
        residual_two = residual - apply_operator(face_coef, cycle_corr)
        coarse_res = restrict(residual_two)
        coarse_corr = coarse_solve(coarse_res, coarse_coef, coarse_diag, coarse_halo)
        correction = correction + prolong(coarse_corr)
        correction = (
            correction
            + JACOBI_WEIGHT
            * (residual - apply_operator(face_coef, finest_halo_cells(correction)))
            / diagonal
        )
        velocity = velocity + correction
        spread_flow = divergence(finest_halo_cells(velocity))
        mean_stress = mean_stress - SCHUR_WEIGHT * local_viscosity * spread_flow
        mean_stress = mean_stress - lax.psum(jnp.sum(mean_stress), ("gx", "gy", "gz")) / total_cells
    adj_temp_prev = advected_result + RAYLEIGH * velocity[2]
    return (adj_temp_prev, velocity, mean_stress)


SUB = 8
LANES = 128
FIELDS = 6
BACK = 5
EDGE = 2
PHASE = 8
HELD = 16
VMEM_LIMIT = 48 * 1024 * 1024
FORWARD, ADJOINT, RESPONSE = range(3)


def slab_plan_fits(mesh, shape):
    sizes = mesh.shape
    group = sizes["gx"] * sizes["gy"]
    block = (shape[0] // sizes["gx"], shape[1] // sizes["gy"], shape[2] // sizes["gz"])
    return (
        group == SUB
        and block[0] == SUB
        and block[0] * block[1] == LANES
        and block[1] * group == LANES
        and block[2] == LANES
        and block[2] == group * 2 * PHASE
    )


class Slabs:
    def __init__(self, mesh, shape):
        self.nx, self.ny, self.nz = mesh.shape["gx"], mesh.shape["gy"], mesh.shape["gz"]
        self.group = self.nx * self.ny
        self.width, self.breadth, self.height = shape
        self.block = (shape[0] // self.nx, shape[1] // self.ny, shape[2] // self.nz)
        self.slab = self.block[2] // self.group
        self.margin = self.slab + SUB
        self.rows = self.slab + 2 * self.margin
        self.cells = self.width * self.breadth * self.height
        self.place = []
        for ix in range(self.nx):
            for iy in range(self.ny):
                step = ix if iy % 2 == 0 else self.nx - 1 - ix
                self.place.append(iy * self.nx + step)
        self.holder = [self.place.index(j) for j in range(self.group)]

    def device(self, slab):
        return self.holder[slab % self.group] * self.nz + slab // self.group

    def shifts(self, distance):
        count = self.group * self.nz
        return [
            (self.device(p), self.device(p + distance))
            for p in range(count)
            if 0 <= p + distance < count
        ]

    def index(self):
        ix, iy = lax.axis_index("gx"), lax.axis_index("gy")
        step = jnp.where(iy % 2 == 0, ix, self.nx - 1 - ix)
        return lax.axis_index("gz") * self.group + iy * self.nx + step

    def inside(self, z, n=SUB):
        layer = self.index() * self.slab - self.margin + z
        layer = layer + lax.broadcasted_iota(jnp.int32, (n, LANES), 0)
        return (layer >= 0) & (layer < self.height)


def swap_granules(tiles, granule):
    lane = lax.broadcasted_iota(jnp.int32, (SUB, LANES), 1) // granule
    for bit in (1, 2, 4):
        low = (lane & bit) == 0
        new = list(tiles)
        for a in range(SUB):
            if a & bit:
                continue
            b = a | bit
            new[a] = jnp.where(low, tiles[a], pltpu.roll(tiles[b], granule * bit, 1))
            new[b] = jnp.where(low, pltpu.roll(tiles[a], LANES - granule * bit, 1), tiles[b])
        tiles = new
    return tiles


class Tiles:
    def __init__(self, geo):
        self.breadth = geo.breadth
        self.row = lax.broadcasted_iota(jnp.int32, (SUB, LANES), 0)
        self.lane = lax.broadcasted_iota(jnp.int32, (SUB, LANES), 1)
        self.y = self.lane % self.breadth

    def x(self, load, x, count, step):
        j = x + step
        if 0 <= j < count:
            return load(j)
        if step > 0:
            turned = pltpu.roll(load(0), LANES - self.breadth, 1)
            return jnp.where(self.lane < LANES - self.breadth, turned, 0.0)
        turned = pltpu.roll(load(count - 1), self.breadth, 1)
        return jnp.where(self.lane >= self.breadth, turned, 0.0)

    def ys(self, f, d):
        return pltpu.roll(f, LANES - d, 1), pltpu.roll(f, d, 1)

    def y_masks(self, d, value):
        up, down = self.y < self.breadth - d, self.y >= d
        value = jnp.float32(value)
        return jnp.where(up, value, 0.0), jnp.where(down, value, 0.0)

    def pair_sum(self, f):
        f = f + jnp.where(self.lane % 2 == 0, pltpu.roll(f, LANES - 1, 1), pltpu.roll(f, 1, 1))
        return f + jnp.where(self.row % 2 == 0, pltpu.roll(f, SUB - 1, 0), pltpu.roll(f, 1, 0))


def get(ref, z, *index):
    return ref[(*index, pl.ds(z, SUB), slice(None))]


def sweep(lo, hi, body):
    assert (hi - lo) % SUB == 0

    def step(t, _):
        late = []

        def store(ref, value, z, *index):
            ref[(*index, pl.ds(z, SUB), slice(None))] = value

        def put(*item):
            late.append(item)
            if len(late) > HELD:
                store(*late.pop(0))

        body(pl.multiple_of(t * SUB, SUB) + lo, put)
        for item in late:
            store(*item)
        return 0

    lax.fori_loop(0, (hi - lo) // SUB, step, 0)


def pack_kernel(geo, heat_in, flow_in, dual_in, kind_in, out, heat, flow, dual, kind, sems):
    b, e = geo.slab, EDGE
    pairs = ((heat_in, heat), (flow_in, flow), (dual_in, dual), (kind_in, kind))
    copies = [
        pltpu.make_async_copy(source, target, sems.at[k])
        for k, (source, target) in enumerate(pairs)
    ]
    for copy in copies:
        copy.start()
    for copy in copies:
        copy.wait()
    flat = [heat[...], flow[0], flow[1], flow[2], dual[...], kind[...].astype(jnp.float32)]
    turned = [f.reshape(LANES, LANES).T for f in flat]
    for j in range(geo.group):
        q = geo.holder[j]
        for f in range(FIELDS):
            out[q, f * b : (f + 1) * b, :] = turned[f][j * b : (j + 1) * b]
        tail = FIELDS * b
        first = jnp.concatenate([turned[f][j * b : j * b + e] for f in range(4)], 0)
        last = jnp.concatenate([turned[f][(j + 1) * b - e : (j + 1) * b] for f in range(4)], 0)
        out[q, tail : tail + SUB, :] = first
        out[q, tail + SUB : tail + 2 * SUB, :] = last


STATIC_FINE = ("s0", "s1", "s2", "visc", "w", "diag", "cxp", "cxm", "cyp", "cym", "cz")
STATIC_COARSE = ("kxp", "kxm", "kyp", "kym", "kzp", "kzm", "wc")
STATIC = STATIC_FINE + STATIC_COARSE


def iterate(geo, st, work, seqs, lo, hi, first=(), mean=None):
    v, p, res, cor, cor2, cc0, cc1 = work
    tl = Tiles(geo)
    half_up, half_down = tl.y_masks(1, 0.5)
    keep = 1.0 - JACOBI_WEIGHT
    slots = [(q, 3 * s + k) for s, q in enumerate(seqs) for k in range(3)]
    transposed = 2

    def faces(x, z):
        c = [get(st[name], z, x) for name in ("cxp", "cxm", "cyp", "cym", "cz")]
        return c + [get(st["cz"], z - 1, x)]

    def beside(ref, c, x, z):
        f = get(ref, z, c, x)
        load = lambda j: get(ref, z, c, j)
        near = [tl.x(load, x, SUB, 1), tl.x(load, x, SUB, -1), *tl.ys(f, 1)]
        return f, near + [get(ref, z + 1, c, x), get(ref, z - 1, c, x)]

    def around(coef, ref, c, x, z):
        f, near = beside(ref, c, x, z)
        return f, sum(a * b for a, b in zip(coef, near))

    def residual(z, put):
        for x in range(SUB):
            w = get(st["w"], z, x)
            if FORWARD in seqs and FORWARD not in first:
                coef, diag = faces(x, z), get(st["diag"], z, x)
            for s, q in enumerate(seqs):
                start = q == FORWARD and q in first
                if not start:
                    _, near = beside(p, transposed if q == ADJOINT else s, x, z)
                    slope = [
                        0.5 * (near[0] - near[1]),
                        half_up * near[2] - half_down * near[3],
                        0.5 * (near[4] - near[5]),
                    ]
                for k in range(3):
                    c = 3 * s + k
                    if q == FORWARD:
                        value = get(st["s%d" % k], z, x)
                        if not start:
                            f, total = around(coef, v, c, x, z)
                            value = value - slope[k] - (diag * f - total)
                    elif q == RESPONSE:
                        value = -slope[k]
                    else:
                        value = slope[k] if q in first else get(cor, z, c, x) + slope[k]
                    put(res, value, z, c, x)
                    put(cor, w * value, z, c, x)

    sweep(lo - 8, hi + 8, residual)

    def restricted(z, put):
        for pair in range(SUB // 2):
            coefs = [faces(2 * pair + side, z) for side in range(2)]
            wc = 0.125 * get(st["wc"], z, pair)
            for _, c in slots:
                left = 0.0
                for side in range(2):
                    _, total = around(coefs[side], cor, c, 2 * pair + side, z)
                    left = left + (keep * get(res, z, c, 2 * pair + side) + total)
                put(cc0, wc * tl.pair_sum(left), z, c, pair)

    sweep(lo - 8, hi + 8, restricted)

    def coarse_step(ref, c, pair, z):
        f = get(ref, z, c, pair)
        load = lambda j: get(ref, z, c, j)
        near = [tl.x(load, pair, SUB // 2, 1), tl.x(load, pair, SUB // 2, -1), *tl.ys(f, 2)]
        near += [get(ref, z + 2, c, pair), get(ref, z - 2, c, pair)]
        value = get(cc0, z, c, pair) + keep * f
        for name, b in zip(STATIC_COARSE, near):
            value = value + get(st[name], z, pair) * b
        return value

    def sweep_one(z, put):
        for pair in range(SUB // 2):
            for _, c in slots:
                put(cc1, coarse_step(cc0, c, pair, z), z, c, pair)

    sweep(lo - 4, hi + 4, sweep_one)

    def sweep_two(z, put):
        for pair in range(SUB // 2):
            for _, c in slots:
                value = coarse_step(cc1, c, pair, z)
                for x in (2 * pair, 2 * pair + 1):
                    put(cor2, get(cor, z, c, x) + value, z, c, x)

    sweep(lo - 4, hi + 4, sweep_two)

    def velocity(z, put):
        for x in range(SUB):
            coef, w = faces(x, z), get(st["w"], z, x)
            for q, c in slots:
                f, total = around(coef, cor2, c, x, z)
                value = get(cor, z, c, x) + keep * f + w * total
                if q == FORWARD and q not in first:
                    value = get(v, z, c, x) + value
                put(v, value, z, c, x)

    sweep(lo - 4, hi + 4, velocity)

    def pressure(z, put):
        for x in range(SUB):
            visc = SCHUR_WEIGHT * get(st["visc"], z, x)
            for s, q in enumerate(seqs):
                load = lambda j: get(v, z, 3 * s, j)
                div = 0.5 * (tl.x(load, x, SUB, 1) - tl.x(load, x, SUB, -1))
                up, down = tl.ys(get(v, z, 3 * s + 1, x), 1)
                div = div + (half_up * up - half_down * down)
                div = div + 0.5 * (get(v, z + 1, 3 * s + 2, x) - get(v, z - 1, 3 * s + 2, x))
                if q == ADJOINT:
                    value = get(p, z, s, x) + div
                    put(p, value, z, s, x)
                    put(p, visc * value, z, transposed, x)
                    coef, diag = faces(x, z), get(st["diag"], z, x)
                    for c in range(3 * s, 3 * s + 3):
                        f, total = around(coef, v, c, x, z)
                        put(cor, get(res, z, c, x) - (diag * f - total), z, c, x)
                    continue
                value = -(visc * div)
                if not (q == FORWARD and q in first):
                    value = get(p, z, s, x) + value
                if mean is not None:
                    value = value - jnp.where(geo.inside(z), mean, 0.0)
                put(p, value, z, s, x)

    sweep(lo, hi, pressure)


def whole_sum(value):
    return jnp.sum(jnp.sum(value, axis=0), axis=(0, 1), keepdims=True)


def product(left, right):
    value = 0.0
    for a, b in zip(left, right):
        value = value + a[...] * b[...]
    return whole_sum(value)


def in_lanes(values, rows):
    lane = lax.broadcasted_iota(jnp.int32, (rows, LANES), 1)
    out = jnp.zeros((rows, LANES), jnp.float32)
    for k, value in values:
        out = jnp.where(lane == k, value, out)
    return out


def setup_kernel(geo, stiffness, own, low, high, low_edge, high_edge, *refs):
    st = dict(zip(STATIC, refs))
    moved, duals, response, sums, raw, heat, vc, *work = refs[len(STATIC) :]
    v, p, res, cor, cor2, cc0, cc1 = work
    tl = Tiles(geo)
    b, m, n_rows = geo.slab, geo.margin, geo.rows
    granule = geo.block[1]

    for source, base in ((low, m - b), (own, m), (high, m + b)):

        def place(t, _, source=source, base=base):
            groups = []
            for u in range(b // SUB):
                row = pl.multiple_of(t * b, b) + u * SUB
                groups.append([source[q, pl.ds(row, SUB), :] for q in range(geo.group)])
            for u, tiles in enumerate(groups):
                for x, tile in enumerate(swap_granules(tiles, granule)):
                    raw[t, x, base + u * SUB : base + (u + 1) * SUB, :] = tile
            return 0

        lax.fori_loop(0, FIELDS, place, 0)
    for source, base in ((low_edge, m - b - EDGE), (high_edge, m + 2 * b)):
        tiles = [source[q] for q in range(geo.group)]
        for x, tile in enumerate(swap_granules(tiles, granule)):
            for f in range(4):
                raw[f, x, base : base + EDGE, :] = tile[f * EDGE : (f + 1) * EDGE]

    one_up, one_down = tl.y_masks(1, 1.0)

    def beside(load, x, z):
        f = load(z, x)
        up, down = tl.ys(f, 1)
        near = [tl.x(lambda j: load(z, j), x, SUB, s) for s in (1, -1)]
        return f, near + [one_up * up, one_down * down, load(z + 1, x), load(z - 1, x)]

    def field(f):
        return lambda z, x: get(raw, z, f, x)

    def advance(old, new):
        def body(z, put):
            inside = geo.inside(z)
            for x in range(SUB):
                f, near = beside(old, x, z)
                drift = 0.0
                for k in range(3):
                    flow = get(raw, z, 1 + k, x)
                    drift = drift + jnp.maximum(flow, 0.0) * (f - near[2 * k + 1])
                    drift = drift + jnp.minimum(flow, 0.0) * (near[2 * k] - f)
                spread = sum(near) - 6.0 * f
                value = f - INCREMENT_DT * drift + INCREMENT_DT * DIFFUSIVITY * spread
                put(heat, jnp.where(inside, value, 0.0), z, new, x)

        return body

    def warm(new):
        return lambda z, x: get(heat, z, new, x)

    sweep(m - b - 4, m + 2 * b + 4, advance(field(0), 0))
    sweep(m - b, m + 2 * b, advance(warm(0), 1))

    def viscosity(z, put):
        inside = geo.inside(z)
        for pair in range(SUB // 2):
            coarse = 0.0
            for x in (2 * pair, 2 * pair + 1):
                kind = get(raw, z, 5, x)
                base = jnp.zeros(kind.shape, jnp.float32)
                for layer in range(LAYERS):
                    base = base + jnp.where(kind == float(layer), stiffness[layer], 0.0)
                value = base * jnp.exp(-ACTIVATION_ENERGY * get(heat, z, 1, x))
                value = jnp.where(inside, value, 0.0)
                put(st["visc"], value, z, x)
                coarse = coarse + value
            put(vc, 0.125 * tl.pair_sum(coarse), z, pair)

    sweep(m - b, m + 2 * b, viscosity)

    def statics(z, put):
        inside = geo.inside(z)
        for x in range(SUB):
            c, near = beside(lambda z, x: get(st["visc"], z, x), x, z)
            face = [0.5 * (c + o) for o in near]
            diag = sum(face)
            face[2], face[3] = one_up * face[2], one_down * face[3]
            for name, f in zip(("cxp", "cxm", "cyp", "cym", "cz"), face):
                put(st[name], f, z, x)
            put(st["diag"], diag, z, x)
            put(st["w"], jnp.where(inside, JACOBI_WEIGHT / diag, 0.0), z, x)
            f, near = beside(warm(1), x, z)
            dual = -INCREMENT_DT * get(raw, z, 4, x)
            for k in range(3):
                flow = get(raw, z, 1 + k, x)
                step = jnp.where(flow > 0, f - near[2 * k + 1], near[2 * k] - f)
                put(st["s%d" % k], dual * step, z, x)

    sweep(m - b, m + 2 * b, statics)

    two_up, two_down = tl.y_masks(2, 1.0)

    def coarse_statics(z, put):
        inside = geo.inside(z)
        for pair in range(SUB // 2):
            c = get(vc, z, pair)
            load = lambda j: get(vc, z, j)
            up, down = tl.ys(c, 2)
            near = [tl.x(load, pair, SUB // 2, s) for s in (1, -1)]
            near += [two_up * up, two_down * down, get(vc, z + 2, pair), get(vc, z - 2, pair)]
            face = [0.25 * (0.5 * (c + o)) for o in near]
            wc = jnp.where(inside, JACOBI_WEIGHT / sum(face), 0.0)
            face[2], face[3] = two_up * face[2], two_down * face[3]
            for name, f in zip(STATIC_COARSE, face):
                put(st[name], wc * f, z, pair)
            put(st["wc"], wc, z, pair)

    sweep(m - b, m + 2 * b, coarse_statics)

    def transport(z, put):
        for x in range(SUB):
            dual, near = beside(field(4), x, z)
            value = dual + INCREMENT_DT * DIFFUSIVITY * (sum(near) - 6.0 * dual)
            for k in range(3):
                flow, sides = beside(field(1 + k), x, z)
                a = jnp.maximum(flow, 0.0) * dual
                c = jnp.minimum(flow, 0.0) * dual
                ahead = jnp.maximum(sides[2 * k], 0.0) * near[2 * k]
                behind = jnp.minimum(sides[2 * k + 1], 0.0) * near[2 * k + 1]
                value = value - INCREMENT_DT * (a - ahead + behind - c)
            put(moved, value, z - m, x)

    sweep(m, m + b, transport)

    def unit(z, put):
        value = jnp.where(geo.inside(z), 1.0, 0.0)
        for x in range(SUB):
            put(p, value, z, 0, x)
            put(p, value, z, 1, x)
            put(p, SCHUR_WEIGHT * get(st["visc"], z, x), z, 2, x)

    sweep(0, n_rows, unit)

    mine = slice(m, m + b)
    iterate(geo, st, work, (ADJOINT,), m - PHASE, m + b + PHASE, (ADJOINT,))
    for k in range(3):
        duals[k] = cor[k, :, mine, :]
    duals[3] = p[0, :, mine, :]
    iterate(geo, st, work, (ADJOINT, RESPONSE), m, m + b, (RESPONSE,))
    for k in range(3):
        duals[4 + k] = cor[k, :, mine, :]
        response[k] = v[3 + k, :, mine, :]
    duals[7] = p[0, :, mine, :]
    response[3] = p[1, :, mine, :]
    sums_of = [
        (1, whole_sum(duals[3])),
        (4, whole_sum(duals[7])),
        (7, product([duals.at[4 + k] for k in range(4)], [response.at[k] for k in range(4)])),
    ]
    sums[...] = in_lanes(sums_of, 1)


def first_kernel(geo, *refs):
    st = dict(zip(STATIC, refs))
    duals, part, state, sums, *work = refs[len(STATIC) :]
    v, p = work[:2]
    b, m = geo.slab, geo.margin
    mine = slice(m, m + b)

    def fields():
        return [v.at[k, :, mine, :] for k in range(3)] + [p.at[0, :, mine, :]]

    near, far = [duals.at[k] for k in range(4)], [duals.at[4 + k] for k in range(4)]
    iterate(geo, st, work, (FORWARD,), m - PHASE, m + b + PHASE, (FORWARD,))
    sums_of = [(0, whole_sum(p[0, :, mine, :])), (2, product(near, fields()))]
    iterate(geo, st, work, (FORWARD,), m, m + b)
    sums_of += [(3, whole_sum(p[0, :, mine, :]))]
    sums_of += [(5, product(near, fields())), (6, product(far, fields()))]
    sums[...] = in_lanes(sums_of, sums.shape[0]) + part[...]
    for k, ref in enumerate(fields()):
        state[k] = ref[...]


def means(geo, sums):
    row = jnp.sum(sums, axis=0, keepdims=True) / geo.cells
    lane = lax.broadcasted_iota(jnp.int32, row.shape, 1)

    def at(k):
        return jnp.sum(jnp.where(lane == k, row, 0.0), axis=1, keepdims=True)

    p1, q1, l1_x1, p2, q2, l1_x2, l2_x2, l2_r1 = [at(k) for k in range(8)]
    m1 = p1
    m2 = p2 - m1 * q1
    m3 = l1_x2 - m1 * q2 - m2 * q1 + p1
    m4 = l2_x2 - m1 * l2_r1 - m2 * q2 + l1_x1 - m3 * q1 + p1
    return m1, m2, m3, m4


def second_kernel(geo, *refs):
    st = dict(zip(STATIC, refs))
    own, low, high, own_r, low_r, high_r, sums, moved, out, *work = refs[len(STATIC) :]
    v, p = work[:2]
    b, m = geo.slab, geo.margin
    m1, m2, m3, m4 = means(geo, sums[...])
    for source, turn, base in ((low, low_r, m - b), (own, own_r, m), (high, high_r, m + b)):
        rows = slice(base, base + b)
        for k in range(3):
            v[k, :, rows, :] = source[k] - m1 * turn[k]
        shift = jnp.where(geo.inside(base, b), m2, 0.0)
        p[0, :, rows, :] = source[3] - m1 * turn[3] - shift[None]
    iterate(geo, st, work, (FORWARD,), m - PHASE, m + b + PHASE, mean=m3)
    iterate(geo, st, work, (FORWARD,), m, m + b, mean=m4)
    for u in range(0, b, SUB):
        at = slice(m + u, m + u + SUB)
        columns = range(SUB)
        fields = [[v[k, x, at, :] for x in columns] for k in range(3)]
        fields.append([p[0, x, at, :] for x in columns])
        fields.append([moved[x, u : u + SUB, :] + fields[2][x] for x in columns])
        for f, tiles in enumerate(fields):
            for q, tile in enumerate(swap_granules(tiles, geo.block[1])):
                out[q, f * b + u : f * b + u + SUB, :] = tile


def unpack_kernel(geo, chunks, heat, flow, pressure):
    b = geo.slab
    for f in range(BACK):
        rows = [chunks[geo.holder[j], f * b : (f + 1) * b, :] for j in range(geo.group)]
        block = jnp.concatenate(rows, 0).T.reshape(geo.block)
        if f < 3:
            flow[f] = block
        elif f == 3:
            pressure[...] = block
        else:
            heat[...] = block


def call(kernel, out, scratch, *args, smem=(), hbm=()):
    f32 = jnp.float32
    specs = [
        pl.BlockSpec(
            memory_space=pltpu.SMEM if i in smem else pltpu.HBM if i in hbm else pltpu.VMEM
        )
        for i in range(len(args))
    ]
    return pl.pallas_call(
        kernel,
        out_shape=[jax.ShapeDtypeStruct(s, f32) for s in out],
        in_specs=specs,
        out_specs=[pl.BlockSpec(memory_space=pltpu.VMEM) for _ in out],
        scratch_shapes=[pltpu.VMEM(s, f32) if isinstance(s, tuple) else s for s in scratch],
        compiler_params=pltpu.CompilerParams(vmem_limit_bytes=VMEM_LIMIT),
    )(*args)


def slab_shards(geo, heat, flow, dual, kind, stiffness):
    b, group = geo.slab, geo.group
    rows = FIELDS * b
    inputs = (heat, flow, dual, kind)
    (chunks,) = call(
        functools.partial(pack_kernel, geo),
        [(group, rows + 2 * SUB, LANES)],
        [pltpu.VMEM(a.shape, a.dtype) for a in inputs] + [pltpu.SemaphoreType.DMA((4,))],
        *inputs,
        hbm=range(4),
    )
    own = lax.all_to_all(chunks, ("gx", "gy"), 0, 0, tiled=True)
    axes = ("gx", "gy", "gz")
    low = lax.ppermute(own, axes, geo.shifts(1))
    high = lax.ppermute(own, axes, geo.shifts(-1))
    high_edge = lax.ppermute(own[:, rows : rows + SUB], axes, geo.shifts(-2))
    low_edge = lax.ppermute(own[:, rows + SUB :], axes, geo.shifts(2))

    fine, coarse = (SUB, geo.rows, LANES), (SUB // 2, geo.rows, LANES)
    slab = (SUB, b, LANES)

    def work(n, more=0):
        fields = [(3 * n, *fine), (n + more, *fine)] + [(3 * n, *fine)] * 3
        return fields + [(3 * n, *coarse)] * 2

    *static, moved, duals, response, part = call(
        functools.partial(setup_kernel, geo),
        [fine] * len(STATIC_FINE)
        + [coarse] * len(STATIC_COARSE)
        + [slab, (8, *slab), (4, *slab), (1, LANES)],
        [(FIELDS, *fine), (2, *fine), coarse] + work(2, 1),
        stiffness,
        own,
        low,
        high,
        low_edge,
        high_edge,
        smem=(0,),
    )
    low_response = lax.ppermute(response, axes, geo.shifts(1))
    high_response = lax.ppermute(response, axes, geo.shifts(-1))
    state, sums = call(
        functools.partial(first_kernel, geo),
        [(4, *slab), (group * geo.nz, LANES)],
        work(1),
        *static,
        duals,
        part,
    )
    sums = lax.all_to_all(sums, axes, 0, 0, tiled=True)
    low_state = lax.ppermute(state, axes, geo.shifts(1))
    high_state = lax.ppermute(state, axes, geo.shifts(-1))
    (chunks,) = call(
        functools.partial(second_kernel, geo),
        [(group, BACK * b, LANES)],
        work(1),
        *static,
        state,
        low_state,
        high_state,
        response,
        low_response,
        high_response,
        sums,
        moved,
    )
    chunks = lax.all_to_all(chunks, ("gx", "gy"), 0, 0, tiled=True)
    return tuple(
        call(
            functools.partial(unpack_kernel, geo),
            [geo.block, (3, *geo.block), geo.block],
            [],
            chunks,
        )
    )


def solution(mesh):
    in_specs = (
        P("gx", "gy", "gz"),
        P(None, "gx", "gy", "gz"),
        P("gx", "gy", "gz"),
        P("gx", "gy", "gz"),
        P(),
    )
    out_specs = (P("gx", "gy", "gz"), P(None, "gx", "gy", "gz"), P("gx", "gy", "gz"))

    def program(saved_heat_state, *others):
        shape = saved_heat_state.shape
        plan = shards
        if slab_plan_fits(mesh, shape):
            plan = functools.partial(slab_shards, Slabs(mesh, shape))
        return jax.shard_map(
            plan, mesh=mesh, in_specs=in_specs, out_specs=out_specs, check_vma=False
        )(saved_heat_state, *others)

    return program
```

```python
import functools

import jax
import jax.numpy as jnp
from jax import lax
from jax.experimental import pallas as pl
from jax.experimental.pallas import tpu as pltpu
from jax.sharding import PartitionSpec as P

RECOMPUTE = 2
SCHUR_ITERS = 4
COARSE_SWEEPS = 3
LAYERS = 8


INCREMENT_DT = 0.2
DIFFUSIVITY = 0.3
ACTIVATION_ENERGY = 2.3
JACOBI_WEIGHT = 0.7
SCHUR_WEIGHT = 0.5
RAYLEIGH = 1.0


def extended(block, sides, width):
    for axis, dim in sides:
        count = lax.axis_size(axis)
        forward = [(i, i + 1) for i in range(count - 1)]
        backward = [(target, source) for source, target in forward]
        low = lax.ppermute(
            lax.slice_in_dim(block, block.shape[dim] - width, None, axis=dim), axis, forward
        )
        high = lax.ppermute(lax.slice_in_dim(block, 0, width, axis=dim), axis, backward)
        block = jnp.concatenate([low, block, high], axis=dim)
    return block


def neighbours(bordered_array):
    centre = bordered_array[..., 1:-1, 1:-1, 1:-1]
    beside_all = [
        bordered_array[..., 2:, 1:-1, 1:-1],
        bordered_array[..., :-2, 1:-1, 1:-1],
        bordered_array[..., 1:-1, 2:, 1:-1],
        bordered_array[..., 1:-1, :-2, 1:-1],
        bordered_array[..., 1:-1, 1:-1, 2:],
        bordered_array[..., 1:-1, 1:-1, :-2],
    ]
    return (centre, beside_all)


def finest_halo_cells(field):
    return extended(field, (("gx", 1), ("gy", 2), ("gz", 3)), 1)


def deep_halo(field):
    return extended(field, (("gx", 1), ("gy", 2), ("gz", 3)), 2)


def coarse_halo(field):
    return extended(field, (("gx", 1), ("gy", 2), ("gz", 3)), 1)


def march_backward(bordered_array, shallower_adjacent, deeper_adjacent):
    centre, beside_all = neighbours(bordered_array)
    drift = 0.0
    for dim_index in range(3):
        drift = (
            drift
            + shallower_adjacent[dim_index] * (centre - beside_all[2 * dim_index + 1])
            + deeper_adjacent[dim_index] * (beside_all[2 * dim_index] - centre)
        )
    spread = sum(beside_all) - 6.0 * centre
    return centre - INCREMENT_DT * drift + INCREMENT_DT * DIFFUSIVITY * spread


def motion_source(bordered_heat, forward_motion, dual_heat_after):
    centre, beside_all = neighbours(bordered_heat)
    device_pieces = [
        jnp.where(
            forward_motion[dim_index] > 0,
            centre - beside_all[2 * dim_index + 1],
            beside_all[2 * dim_index] - centre,
        )
        for dim_index in range(3)
    ]
    return -INCREMENT_DT * dual_heat_after[None] * jnp.stack(device_pieces)


def advect_dual_heat(pos_padded, neg_padded, lam_padded):
    centre, beside_all = neighbours(lam_padded)
    result = centre + INCREMENT_DT * DIFFUSIVITY * (sum(beside_all) - 6.0 * centre)
    for dim_index in range(3):
        pos_centre, pos_around = neighbours(pos_padded[dim_index])
        neg_centre, neg_around = neighbours(neg_padded[dim_index])
        result = result - INCREMENT_DT * (
            pos_centre - pos_around[2 * dim_index] + neg_around[2 * dim_index + 1] - neg_centre
        )
    return result


def coefficients(bordered_array, factor):
    centre, beside_all = neighbours(bordered_array)
    return [factor * (0.5 * (centre + other)) for other in beside_all]


def apply_operator(face_coef, bordered_array):
    centre, beside_all = neighbours(bordered_array)
    return sum((coef * (centre - other) for coef, other in zip(face_coef, beside_all)))


def gradient(bordered_array):
    centre, beside_all = neighbours(bordered_array)
    return jnp.stack(
        [
            0.5 * (beside_all[2 * dim_index] - beside_all[2 * dim_index + 1])
            for dim_index in range(3)
        ]
    )


def divergence(bordered_array):
    centre, beside_all = neighbours(bordered_array)
    return sum(
        (
            0.5 * (beside_all[2 * dim_index][dim_index] - beside_all[2 * dim_index + 1][dim_index])
            for dim_index in range(3)
        )
    )


def restrict(field):
    leading = field.shape[:-3]
    cells_x, cells_y, cells_z = field.shape[-3:]
    blocks = field.reshape(leading + (cells_x // 2, 2, cells_y // 2, 2, cells_z // 2, 2))
    return blocks.mean(axis=(-5, -3, -1))


def prolong(field):
    return jnp.repeat(jnp.repeat(jnp.repeat(field, 2, axis=-3), 2, axis=-2), 2, axis=-1)


def evaluate_viscosity(rheology_class, class_base_stiffness):
    base = jnp.zeros(rheology_class.shape, jnp.float32)
    for layer_index in range(LAYERS):
        base = base + jnp.where(
            rheology_class == layer_index, class_base_stiffness[layer_index], 0.0
        )
    return base


def inside_mask(extent_first, extent_second, extent_vertical):
    index_x = (
        lax.axis_index("gx") * extent_first + jnp.arange(extent_first + 2, dtype=jnp.int32) - 1
    )
    index_y = (
        lax.axis_index("gy") * extent_second + jnp.arange(extent_second + 2, dtype=jnp.int32) - 1
    )
    index_z = (
        lax.axis_index("gz") * extent_vertical
        + jnp.arange(extent_vertical + 2, dtype=jnp.int32)
        - 1
    )
    inside_x = (index_x >= 0) & (index_x < extent_first * lax.axis_size("gx"))
    inside_y = (index_y >= 0) & (index_y < extent_second * lax.axis_size("gy"))
    inside_z = (index_z >= 0) & (index_z < extent_vertical * lax.axis_size("gz"))
    return inside_x[:, None, None] & inside_y[None, :, None] & inside_z[None, None, :]


def coarse_solve(coarse_res, coarse_coef, coarse_diag, pad_field):
    coarse_corr = JACOBI_WEIGHT * coarse_res / coarse_diag
    for sweep in range(COARSE_SWEEPS - 1):
        coarse_corr = (
            coarse_corr
            + JACOBI_WEIGHT
            * (coarse_res - apply_operator(coarse_coef, pad_field(coarse_corr)))
            / coarse_diag
        )
    return coarse_corr


def shards(saved_heat_state, forward_motion, dual_heat_after, rheology_class, class_base_stiffness):
    extent_first, extent_second, extent_vertical = saved_heat_state.shape
    shallower_adjacent = jnp.maximum(forward_motion, 0.0)
    deeper_adjacent = jnp.minimum(forward_motion, 0.0)
    heat_state = saved_heat_state
    for repeat_index in range(RECOMPUTE):
        heat_state = march_backward(
            finest_halo_cells(heat_state[None])[0], shallower_adjacent, deeper_adjacent
        )
    local_viscosity = evaluate_viscosity(rheology_class, class_base_stiffness) * jnp.exp(
        -ACTIVATION_ENERGY * heat_state
    )
    stacked = jnp.concatenate(
        [
            heat_state[None],
            dual_heat_after[None],
            shallower_adjacent * dual_heat_after[None],
            deeper_adjacent * dual_heat_after[None],
            local_viscosity[None],
        ],
        0,
    )
    bordered_array = finest_halo_cells(stacked)
    driving_source = motion_source(bordered_array[0], forward_motion, dual_heat_after)
    advected_result = advect_dual_heat(bordered_array[2:5], bordered_array[5:8], bordered_array[1])
    face_coef = coefficients(bordered_array[8], 1.0)
    diagonal = sum(face_coef)
    coarse_visc = restrict(local_viscosity)
    coarse_coef = coefficients(coarse_halo(coarse_visc[None])[0], 0.25)
    coarse_diag = sum(coarse_coef)
    deep_static = deep_halo(jnp.concatenate([local_viscosity[None], driving_source], 0))
    cycle_coef = coefficients(deep_static[0], 1.0)
    cycle_source = deep_static[1:4, 1:-1, 1:-1, 1:-1]
    inside = inside_mask(extent_first, extent_second, extent_vertical)
    safe_diag = jnp.where(inside, sum(cycle_coef), 1.0)
    total_cells = (
        extent_first
        * extent_second
        * extent_vertical
        * lax.axis_size("gx")
        * lax.axis_size("gy")
        * lax.axis_size("gz")
    )
    velocity = jnp.zeros(forward_motion.shape, jnp.float32)
    mean_stress = jnp.zeros(saved_heat_state.shape, jnp.float32)
    for iteration in range(SCHUR_ITERS):
        if iteration == 0:
            cycle_resid = cycle_source
        else:
            flow_press = deep_halo(jnp.concatenate([velocity, mean_stress[None]], 0))
            cycle_resid = (
                cycle_source - apply_operator(cycle_coef, flow_press[0:3]) - gradient(flow_press[3])
            )
        cycle_corr = jnp.where(inside, JACOBI_WEIGHT * cycle_resid / safe_diag, 0.0)
        residual = cycle_resid[:, 1:-1, 1:-1, 1:-1]
        correction = cycle_corr[:, 1:-1, 1:-1, 1:-1]
        residual_two = residual - apply_operator(face_coef, cycle_corr)
        coarse_res = restrict(residual_two)
        coarse_corr = coarse_solve(coarse_res, coarse_coef, coarse_diag, coarse_halo)
        correction = correction + prolong(coarse_corr)
        correction = (
            correction
            + JACOBI_WEIGHT
            * (residual - apply_operator(face_coef, finest_halo_cells(correction)))
            / diagonal
        )
        velocity = velocity + correction
        spread_flow = divergence(finest_halo_cells(velocity))
        mean_stress = mean_stress - SCHUR_WEIGHT * local_viscosity * spread_flow
        mean_stress = mean_stress - lax.psum(jnp.sum(mean_stress), ("gx", "gy", "gz")) / total_cells
    adj_temp_prev = advected_result + RAYLEIGH * velocity[2]
    return (adj_temp_prev, velocity, mean_stress)


SUB = 8
LANES = 128
FIELDS = 6
BACK = 5
EDGE = 2
PHASE = 8
HELD = 24
VMEM_LIMIT = 44 * 1024 * 1024
PACK_LIMIT = 60 * 1024 * 1024
FORWARD, ADJOINT = range(2)


def slab_plan_fits(mesh, shape):
    sizes = mesh.shape
    group = sizes["gx"] * sizes["gy"]
    block = (shape[0] // sizes["gx"], shape[1] // sizes["gy"], shape[2] // sizes["gz"])
    return (
        group == SUB
        and block[0] == SUB
        and block[0] * block[1] == LANES
        and block[1] * group == LANES
        and block[2] == LANES
        and block[2] == group * 2 * PHASE
    )


class Slabs:
    def __init__(self, mesh, shape):
        self.nx, self.ny, self.nz = mesh.shape["gx"], mesh.shape["gy"], mesh.shape["gz"]
        self.group = self.nx * self.ny
        self.width, self.breadth, self.height = shape
        self.block = (shape[0] // self.nx, shape[1] // self.ny, shape[2] // self.nz)
        self.slab = self.block[2] // self.group
        self.margin = self.slab + SUB
        self.rows = self.slab + 2 * self.margin
        self.cells = self.width * self.breadth * self.height
        self.place = []
        for ix in range(self.nx):
            for iy in range(self.ny):
                step = ix if iy % 2 == 0 else self.nx - 1 - ix
                self.place.append(iy * self.nx + step)
        self.holder = [self.place.index(j) for j in range(self.group)]

    def device(self, slab):
        return self.holder[slab % self.group] * self.nz + slab // self.group

    def shifts(self, distance):
        count = self.group * self.nz
        return [
            (self.device(p), self.device(p + distance))
            for p in range(count)
            if 0 <= p + distance < count
        ]

    def index(self):
        ix, iy = lax.axis_index("gx"), lax.axis_index("gy")
        step = jnp.where(iy % 2 == 0, ix, self.nx - 1 - ix)
        return lax.axis_index("gz") * self.group + iy * self.nx + step

    def inside(self, z, n=SUB):
        layer = self.index() * self.slab - self.margin + z
        layer = layer + lax.broadcasted_iota(jnp.int32, (n, LANES), 0)
        return (layer >= 0) & (layer < self.height)


def swap_granules(tiles, granule):
    lane = lax.broadcasted_iota(jnp.int32, (SUB, LANES), 1) // granule
    for bit in (1, 2, 4):
        low = (lane & bit) == 0
        new = list(tiles)
        for a in range(SUB):
            if a & bit:
                continue
            b = a | bit
            new[a] = jnp.where(low, tiles[a], pltpu.roll(tiles[b], granule * bit, 1))
            new[b] = jnp.where(low, pltpu.roll(tiles[a], LANES - granule * bit, 1), tiles[b])
        tiles = new
    return tiles


class Tiles:
    def __init__(self, geo):
        self.breadth = geo.breadth
        self.row = lax.broadcasted_iota(jnp.int32, (SUB, LANES), 0)
        self.lane = lax.broadcasted_iota(jnp.int32, (SUB, LANES), 1)
        self.y = self.lane % self.breadth
        self.kept = {}

    def sliding(self, ref, z, c, x):
        where = (id(ref), id(z), c)
        for key in [k for k in self.kept if k[:3] == where and abs(k[3] - x) > 1]:
            del self.kept[key]

        def load(j):
            key = (*where, j)
            if key not in self.kept:
                self.kept[key] = (ref, z, get(ref, z, c, j))
            return self.kept[key][2]

        return load

    def x(self, load, x, count, step):
        j = x + step
        if 0 <= j < count:
            return load(j)
        if step > 0:
            turned = pltpu.roll(load(0), LANES - self.breadth, 1)
            return jnp.where(self.lane < LANES - self.breadth, turned, 0.0)
        turned = pltpu.roll(load(count - 1), self.breadth, 1)
        return jnp.where(self.lane >= self.breadth, turned, 0.0)

    def ys(self, f, d):
        return pltpu.roll(f, LANES - d, 1), pltpu.roll(f, d, 1)

    def y_masks(self, d, value):
        up, down = self.y < self.breadth - d, self.y >= d
        value = jnp.float32(value)
        return jnp.where(up, value, 0.0), jnp.where(down, value, 0.0)

    def pair_sum(self, f):
        f = f + jnp.where(self.lane % 2 == 0, pltpu.roll(f, LANES - 1, 1), pltpu.roll(f, 1, 1))
        return f + jnp.where(self.row % 2 == 0, pltpu.roll(f, SUB - 1, 0), pltpu.roll(f, 1, 0))


def tree(terms):
    while len(terms) > 1:
        terms = [sum(terms[k : k + 2]) for k in range(0, len(terms), 2)]
    return terms[0]


def get(ref, z, *index):
    return ref[(*index, pl.ds(z, SUB), slice(None))]


def sweep(lo, hi, body):
    assert (hi - lo) % SUB == 0

    def step(t, _):
        late = []

        def store(ref, value, z, *index):
            ref[(*index, pl.ds(z, SUB), slice(None))] = value

        def put(*item):
            late.append(item)
            if len(late) > HELD:
                store(*late.pop(0))

        body(pl.multiple_of(t * SUB, SUB) + lo, put)
        for item in late:
            store(*item)
        return 0

    lax.fori_loop(0, (hi - lo) // SUB, step, 0)


def pack_kernel(geo, heat_in, flow_in, dual_in, kind_in, out, heat, flow, dual, kind, sems):
    b, e = geo.slab, EDGE
    pairs = ((heat_in, heat), (flow_in, flow), (dual_in, dual), (kind_in, kind))
    copies = [
        pltpu.make_async_copy(source, target, sems.at[k])
        for k, (source, target) in enumerate(pairs)
    ]
    for copy in copies:
        copy.start()
    for copy in copies:
        copy.wait()
    flat = [heat[...], flow[0], flow[1], flow[2], dual[...], kind[...].astype(jnp.float32)]
    turned = [f.reshape(LANES, LANES).T for f in flat]
    for j in range(geo.group):
        q = geo.holder[j]
        for f in range(FIELDS):
            out[q, f * b : (f + 1) * b, :] = turned[f][j * b : (j + 1) * b]
        tail = FIELDS * b
        first = jnp.concatenate([turned[f][j * b : j * b + e] for f in range(4)], 0)
        last = jnp.concatenate([turned[f][(j + 1) * b - e : (j + 1) * b] for f in range(4)], 0)
        out[q, tail : tail + SUB, :] = first
        out[q, tail + SUB : tail + 2 * SUB, :] = last


STATIC_FINE = ("s0", "s1", "s2", "visc", "w", "diag", "cxp", "cxm", "cyp", "cym", "cz")
STATIC_COARSE = ("kxp", "kxm", "kyp", "kym", "kzp", "kzm", "wc")
STATIC = STATIC_FINE + STATIC_COARSE


def iterate(geo, st, work, seqs, lo, hi, first=(), mean=None):
    v, p, res, cor, cor2, cc0, cc1 = work
    tl = Tiles(geo)
    half_up, half_down = tl.y_masks(1, 0.5)
    keep = 1.0 - JACOBI_WEIGHT
    slots = [(q, 3 * s + k) for s, q in enumerate(seqs) for k in range(3)]
    transposed = len(seqs)

    def faces(x, z):
        c = [get(st[name], z, x) for name in ("cxp", "cxm", "cyp", "cym", "cz")]
        return c + [get(st["cz"], z - 1, x)]

    def beside(ref, c, x, z):
        load = tl.sliding(ref, z, c, x)
        f = load(x)
        near = [tl.x(load, x, SUB, 1), tl.x(load, x, SUB, -1), *tl.ys(f, 1)]
        return f, near + [get(ref, z + 1, c, x), get(ref, z - 1, c, x)]

    def around(coef, ref, c, x, z):
        f, near = beside(ref, c, x, z)
        return f, tree([a * b for a, b in zip(coef, near)])

    def residual(z, put):
        for x in range(SUB):
            w = get(st["w"], z, x)
            if FORWARD in seqs and FORWARD not in first:
                coef, diag = faces(x, z), get(st["diag"], z, x)
            for s, q in enumerate(seqs):
                start = q == FORWARD and q in first
                if not start:
                    _, near = beside(p, transposed if q == ADJOINT else s, x, z)
                    slope = [
                        0.5 * (near[0] - near[1]),
                        half_up * near[2] - half_down * near[3],
                        0.5 * (near[4] - near[5]),
                    ]
                for k in range(3):
                    c = 3 * s + k
                    if q == FORWARD:
                        value = get(st["s%d" % k], z, x)
                        if not start:
                            f, total = around(coef, v, c, x, z)
                            value = value - slope[k] - (diag * f - total)
                    else:
                        value = slope[k] if q in first else get(cor, z, c, x) + slope[k]
                    put(res, value, z, c, x)
                    put(cor, w * value, z, c, x)

    sweep(lo - 8, hi + 8, residual)

    def restricted(z, put):
        for pair in range(SUB // 2):
            coefs = [faces(2 * pair + side, z) for side in range(2)]
            wc = 0.125 * get(st["wc"], z, pair)
            for _, c in slots:
                left = 0.0
                for side in range(2):
                    _, total = around(coefs[side], cor, c, 2 * pair + side, z)
                    left = left + (keep * get(res, z, c, 2 * pair + side) + total)
                put(cc0, wc * tl.pair_sum(left), z, c, pair)

    sweep(lo - 8, hi + 8, restricted)

    def coarse_step(ref, c, pair, z):
        f = get(ref, z, c, pair)
        load = lambda j: get(ref, z, c, j)
        near = [tl.x(load, pair, SUB // 2, 1), tl.x(load, pair, SUB // 2, -1), *tl.ys(f, 2)]
        near += [get(ref, z + 2, c, pair), get(ref, z - 2, c, pair)]
        terms = [get(st[name], z, pair) * b for name, b in zip(STATIC_COARSE, near)]
        return tree([get(cc0, z, c, pair), keep * f] + terms)

    def sweep_one(z, put):
        for pair in range(SUB // 2):
            for _, c in slots:
                put(cc1, coarse_step(cc0, c, pair, z), z, c, pair)

    sweep(lo - 4, hi + 4, sweep_one)

    def sweep_two(z, put):
        for pair in range(SUB // 2):
            for _, c in slots:
                value = coarse_step(cc1, c, pair, z)
                for x in (2 * pair, 2 * pair + 1):
                    put(cor2, get(cor, z, c, x) + value, z, c, x)

    sweep(lo - 4, hi + 4, sweep_two)

    def velocity(z, put):
        for x in range(SUB):
            coef, w = faces(x, z), get(st["w"], z, x)
            for q, c in slots:
                f, total = around(coef, cor2, c, x, z)
                value = get(cor, z, c, x) + keep * f + w * total
                if q == FORWARD and q not in first:
                    value = get(v, z, c, x) + value
                put(v, value, z, c, x)

    sweep(lo - 4, hi + 4, velocity)

    def pressure(z, put):
        for x in range(SUB):
            visc = SCHUR_WEIGHT * get(st["visc"], z, x)
            for s, q in enumerate(seqs):
                load = lambda j: get(v, z, 3 * s, j)
                div = 0.5 * (tl.x(load, x, SUB, 1) - tl.x(load, x, SUB, -1))
                up, down = tl.ys(get(v, z, 3 * s + 1, x), 1)
                div = div + (half_up * up - half_down * down)
                div = div + 0.5 * (get(v, z + 1, 3 * s + 2, x) - get(v, z - 1, 3 * s + 2, x))
                if q == ADJOINT:
                    value = get(p, z, s, x) + div
                    put(p, value, z, s, x)
                    put(p, visc * value, z, transposed, x)
                    coef, diag = faces(x, z), get(st["diag"], z, x)
                    for c in range(3 * s, 3 * s + 3):
                        f, total = around(coef, v, c, x, z)
                        put(cor, get(res, z, c, x) - (diag * f - total), z, c, x)
                    continue
                value = -(visc * div)
                if not (q == FORWARD and q in first):
                    value = get(p, z, s, x) + value
                if mean is not None:
                    value = value - jnp.where(geo.inside(z), mean, 0.0)
                put(p, value, z, s, x)

    sweep(lo, hi, pressure)


def whole_sum(value):
    return jnp.sum(jnp.sum(value, axis=0), axis=(0, 1), keepdims=True)


def product(left, right):
    value = 0.0
    for a, b in zip(left, right):
        value = value + a[...] * b[...]
    return whole_sum(value)


def in_lanes(values, rows):
    lane = lax.broadcasted_iota(jnp.int32, (rows, LANES), 1)
    out = jnp.zeros((rows, LANES), jnp.float32)
    for k, value in values:
        out = jnp.where(lane == k, value, out)
    return out


def setup_kernel(geo, stiffness, own, low, high, low_edge, high_edge, *refs):
    st = dict(zip(STATIC, refs))
    moved, duals, sums, raw, heat, vc, *work = refs[len(STATIC) :]
    v, p, res, cor, cor2, cc0, cc1 = work
    tl = Tiles(geo)
    b, m, n_rows = geo.slab, geo.margin, geo.rows
    granule = geo.block[1]

    def place(t, _):
        groups = []
        for source, base in ((low, m - b), (own, m), (high, m + b)):
            for u in range(0, b, SUB):
                row = pl.multiple_of(t * b, b) + u
                tiles = [source[q, pl.ds(row, SUB), :] for q in range(geo.group)]
                groups.append((base + u, tiles))
        groups = [(row, swap_granules(tiles, granule)) for row, tiles in groups]
        for row, tiles in groups:
            for x, tile in enumerate(tiles):
                raw[t, x, row : row + SUB, :] = tile
        return 0

    lax.fori_loop(0, FIELDS, place, 0)
    for source, base in ((low_edge, m - b - EDGE), (high_edge, m + 2 * b)):
        tiles = [source[q] for q in range(geo.group)]
        for x, tile in enumerate(swap_granules(tiles, granule)):
            for f in range(4):
                raw[f, x, base : base + EDGE, :] = tile[f * EDGE : (f + 1) * EDGE]

    one_up, one_down = tl.y_masks(1, 1.0)

    def beside(load, x, z):
        f = load(z, x)
        up, down = tl.ys(f, 1)
        near = [tl.x(lambda j: load(z, j), x, SUB, s) for s in (1, -1)]
        return f, near + [one_up * up, one_down * down, load(z + 1, x), load(z - 1, x)]

    def field(f):
        return lambda z, x: get(raw, z, f, x)

    def advance(old, new):
        def body(z, put):
            inside = geo.inside(z)
            for x in range(SUB):
                f, near = beside(old, x, z)
                drift = 0.0
                for k in range(3):
                    flow = get(raw, z, 1 + k, x)
                    drift = drift + jnp.maximum(flow, 0.0) * (f - near[2 * k + 1])
                    drift = drift + jnp.minimum(flow, 0.0) * (near[2 * k] - f)
                spread = sum(near) - 6.0 * f
                value = f - INCREMENT_DT * drift + INCREMENT_DT * DIFFUSIVITY * spread
                put(heat, jnp.where(inside, value, 0.0), z, new, x)

        return body

    def warm(new):
        return lambda z, x: get(heat, z, new, x)

    sweep(m - b - 4, m + 2 * b + 4, advance(field(0), 0))
    sweep(m - b, m + 2 * b, advance(warm(0), 1))

    def viscosity(z, put):
        inside = geo.inside(z)
        for pair in range(SUB // 2):
            coarse = 0.0
            for x in (2 * pair, 2 * pair + 1):
                kind = get(raw, z, 5, x)
                base = jnp.zeros(kind.shape, jnp.float32)
                for layer in range(LAYERS):
                    base = base + jnp.where(kind == float(layer), stiffness[layer], 0.0)
                value = base * jnp.exp(-ACTIVATION_ENERGY * get(heat, z, 1, x))
                value = jnp.where(inside, value, 0.0)
                put(st["visc"], value, z, x)
                coarse = coarse + value
            put(vc, 0.125 * tl.pair_sum(coarse), z, pair)

    sweep(m - b, m + 2 * b, viscosity)

    def statics(z, put):
        inside = geo.inside(z)
        for x in range(SUB):
            c, near = beside(lambda z, x: get(st["visc"], z, x), x, z)
            face = [0.5 * (c + o) for o in near]
            diag = tree(face)
            face[2], face[3] = one_up * face[2], one_down * face[3]
            for name, f in zip(("cxp", "cxm", "cyp", "cym", "cz"), face):
                put(st[name], f, z, x)
            put(st["diag"], diag, z, x)
            put(st["w"], jnp.where(inside, JACOBI_WEIGHT / diag, 0.0), z, x)
            f, near = beside(warm(1), x, z)
            dual = -INCREMENT_DT * get(raw, z, 4, x)
            for k in range(3):
                flow = get(raw, z, 1 + k, x)
                step = jnp.where(flow > 0, f - near[2 * k + 1], near[2 * k] - f)
                put(st["s%d" % k], dual * step, z, x)

    sweep(m - b, m + 2 * b, statics)

    two_up, two_down = tl.y_masks(2, 1.0)

    def coarse_statics(z, put):
        inside = geo.inside(z)
        for pair in range(SUB // 2):
            c = get(vc, z, pair)
            load = lambda j: get(vc, z, j)
            up, down = tl.ys(c, 2)
            near = [tl.x(load, pair, SUB // 2, s) for s in (1, -1)]
            near += [two_up * up, two_down * down, get(vc, z + 2, pair), get(vc, z - 2, pair)]
            face = [0.25 * (0.5 * (c + o)) for o in near]
            wc = jnp.where(inside, JACOBI_WEIGHT / sum(face), 0.0)
            face[2], face[3] = two_up * face[2], two_down * face[3]
            for name, f in zip(STATIC_COARSE, face):
                put(st[name], wc * f, z, pair)
            put(st["wc"], wc, z, pair)

    sweep(m - b, m + 2 * b, coarse_statics)

    def transport(z, put):
        for x in range(SUB):
            dual, near = beside(field(4), x, z)
            value = dual + INCREMENT_DT * DIFFUSIVITY * (sum(near) - 6.0 * dual)
            for k in range(3):
                flow, sides = beside(field(1 + k), x, z)
                a = jnp.maximum(flow, 0.0) * dual
                c = jnp.minimum(flow, 0.0) * dual
                ahead = jnp.maximum(sides[2 * k], 0.0) * near[2 * k]
                behind = jnp.minimum(sides[2 * k + 1], 0.0) * near[2 * k + 1]
                value = value - INCREMENT_DT * (a - ahead + behind - c)
            put(moved, value, z - m, x)

    sweep(m, m + b, transport)

    def unit(z, put):
        value = jnp.where(geo.inside(z), 1.0, 0.0)
        for x in range(SUB):
            put(p, value, z, 0, x)
            put(p, SCHUR_WEIGHT * get(st["visc"], z, x), z, 1, x)

    sweep(0, n_rows, unit)

    mine = slice(m, m + b)
    source = [st["s%d" % k].at[:, mine, :] for k in range(3)]
    step = [v.at[k, :, mine, :] for k in range(3)]
    iterate(geo, st, work, (ADJOINT,), m - PHASE, m + b + PHASE, (ADJOINT,))
    sums_of = [(0, product(step, source)), (1, whole_sum(p[0, :, mine, :]))]
    for k in range(4):
        duals[k] = cor[k, :, mine, :] if k < 3 else p[0, :, mine, :]
    iterate(geo, st, work, (ADJOINT,), m, m + b)
    sums_of += [(2, product(step, source))]
    for k in range(4):
        duals[4 + k] = cor[k, :, mine, :] if k < 3 else p[0, :, mine, :]
    sums[...] = in_lanes(sums_of, sums.shape[0])


def first_kernel(geo, *refs):
    st = dict(zip(STATIC, refs))
    out, *work = refs[len(STATIC) :]
    v, p = work[:2]
    rows = slice(geo.margin - PHASE, geo.margin + geo.slab + PHASE)
    iterate(geo, st, work, (FORWARD,), rows.start, rows.stop, (FORWARD,))
    for k in range(4):
        out[k] = v[k, :, rows, :] if k < 3 else p[0, :, rows, :]


def refill(geo, v, p, state, rows, shift):
    for k in range(3):
        v[k, :, rows, :] = state[k]
    if shift is None:
        p[0, :, rows, :] = state[3]
    else:
        inside = geo.inside(rows.start, rows.stop - rows.start)
        p[0, :, rows, :] = state[3] - jnp.where(inside, shift, 0.0)[None]


def second_kernel(geo, *refs):
    st = dict(zip(STATIC, refs))
    earlier, early, duals, state, sums, *work = refs[len(STATIC) :]
    v, p = work[:2]
    b, m = geo.slab, geo.margin
    m1, m2 = means(geo, early[...], None)[:2]
    refill(geo, v, p, earlier, slice(m - PHASE, m + b + PHASE), m1)
    iterate(geo, st, work, (FORWARD,), m, m + b, mean=m2)
    mine = slice(m, m + b)
    for k in range(4):
        state[k] = v[k, :, mine, :] if k < 3 else p[0, :, mine, :]
    fields = [state.at[k] for k in range(4)]
    near, far = [duals.at[k] for k in range(4)], [duals.at[4 + k] for k in range(4)]
    sums_of = [(3, product(near, fields)), (4, product(far, fields))]
    sums[...] = in_lanes(sums_of, sums.shape[0])


def means(geo, early, late):
    sums = early if late is None else early + late
    row = jnp.sum(sums, axis=0, keepdims=True) / geo.cells
    lane = lax.broadcasted_iota(jnp.int32, row.shape, 1)

    def at(k):
        return jnp.sum(jnp.where(lane == k, row, 0.0), axis=1, keepdims=True)

    c1, l1, c2, l1_x2, l2_x2 = [at(k) for k in range(5)]
    m1 = c1
    m2 = c1 + c2 - m1 * l1
    m3 = c1 + l1_x2
    m4 = c1 + c2 + l2_x2 - m3 * l1
    return m1, m2, m3, m4


def third_kernel(geo, *refs):
    st = dict(zip(STATIC, refs))
    own, low, high, out, *work = refs[len(STATIC) :]
    v, p = work[:2]
    b, m = geo.slab, geo.margin
    for source, base in ((low, m - b), (own, m), (high, m + b)):
        refill(geo, v, p, source, slice(base, base + b), None)
    rows = slice(m - PHASE, m + b + PHASE)
    iterate(geo, st, work, (FORWARD,), rows.start, rows.stop)
    for k in range(4):
        out[k] = v[k, :, rows, :] if k < 3 else p[0, :, rows, :]


def fourth_kernel(geo, *refs):
    st = dict(zip(STATIC, refs))
    state, early, late, moved, out, *work = refs[len(STATIC) :]
    v, p = work[:2]
    b, m = geo.slab, geo.margin
    m3, m4 = means(geo, early[...], late[...])[2:]
    refill(geo, v, p, state, slice(m - PHASE, m + b + PHASE), m3)
    iterate(geo, st, work, (FORWARD,), m, m + b, mean=m4)
    for u in range(0, b, SUB):
        at = slice(m + u, m + u + SUB)
        columns = range(SUB)
        fields = [[v[k, x, at, :] for x in columns] for k in range(3)]
        fields.append([p[0, x, at, :] for x in columns])
        fields.append([moved[x, u : u + SUB, :] + fields[2][x] for x in columns])
        for f, tiles in enumerate(fields):
            for q, tile in enumerate(swap_granules(tiles, geo.block[1])):
                out[q, f * b + u : f * b + u + SUB, :] = tile


def unpack_kernel(geo, chunks, heat, flow, pressure):
    b = geo.slab
    for f in range(BACK):
        rows = [chunks[geo.holder[j], f * b : (f + 1) * b, :] for j in range(geo.group)]
        block = jnp.concatenate(rows, 0).T.reshape(geo.block)
        if f < 3:
            flow[f] = block
        elif f == 3:
            pressure[...] = block
        else:
            heat[...] = block


def call(kernel, out, scratch, *args, smem=(), hbm=(), limit=VMEM_LIMIT, megabytes=2):
    f32 = jnp.float32
    cost = pl.CostEstimate(
        flops=megabytes * 1000000, bytes_accessed=megabytes * 1000000, transcendentals=0
    )
    specs = [
        pl.BlockSpec(
            memory_space=pltpu.SMEM if i in smem else pltpu.HBM if i in hbm else pltpu.VMEM
        )
        for i in range(len(args))
    ]
    return pl.pallas_call(
        kernel,
        out_shape=[jax.ShapeDtypeStruct(s, f32) for s in out],
        in_specs=specs,
        out_specs=[pl.BlockSpec(memory_space=pltpu.VMEM) for _ in out],
        scratch_shapes=[pltpu.VMEM(s, f32) if isinstance(s, tuple) else s for s in scratch],
        compiler_params=pltpu.CompilerParams(vmem_limit_bytes=limit),
        cost_estimate=cost,
    )(*args)


def slab_shards(geo, heat, flow, dual, kind, stiffness):
    b, group = geo.slab, geo.group
    rows = FIELDS * b
    inputs = (heat, flow, dual, kind)
    (chunks,) = call(
        functools.partial(pack_kernel, geo),
        [(group, rows + 2 * SUB, LANES)],
        [pltpu.VMEM(a.shape, a.dtype) for a in inputs] + [pltpu.SemaphoreType.DMA((4,))],
        *inputs,
        hbm=range(4),
        limit=PACK_LIMIT,
    )
    own = lax.all_to_all(chunks, ("gx", "gy"), 0, 0, tiled=True)
    axes = ("gx", "gy", "gz")
    low = lax.ppermute(own, axes, geo.shifts(1))
    high = lax.ppermute(own, axes, geo.shifts(-1))
    high_edge = lax.ppermute(own[:, rows : rows + SUB], axes, geo.shifts(-2))
    low_edge = lax.ppermute(own[:, rows + SUB :], axes, geo.shifts(2))

    fine, coarse = (SUB, geo.rows, LANES), (SUB // 2, geo.rows, LANES)
    slab = (SUB, b, LANES)

    def work(n, more=0):
        fields = [(3 * n, *fine), (n + more, *fine)] + [(3 * n, *fine)] * 3
        return fields + [(3 * n, *coarse)] * 2

    devices = group * geo.nz
    wide = (4, SUB, b + 2 * PHASE, LANES)
    *static, moved, duals, early = call(
        functools.partial(setup_kernel, geo),
        [fine] * len(STATIC_FINE)
        + [coarse] * len(STATIC_COARSE)
        + [slab, (8, *slab), (devices, LANES)],
        [(FIELDS, *fine), (2, *fine), coarse] + work(1, 1),
        stiffness,
        own,
        low,
        high,
        low_edge,
        high_edge,
        smem=(0,),
        megabytes=60,
    )
    early = lax.all_to_all(early, axes, 0, 0, tiled=True)
    (state,) = call(
        functools.partial(first_kernel, geo), [wide], work(1), *static, megabytes=20
    )
    state, late = call(
        functools.partial(second_kernel, geo),
        [(4, *slab), (devices, LANES)],
        work(1),
        *static,
        state,
        early,
        duals,
        megabytes=20,
    )
    low_state = lax.ppermute(state, axes, geo.shifts(1))
    high_state = lax.ppermute(state, axes, geo.shifts(-1))
    late = lax.all_to_all(late, axes, 0, 0, tiled=True)
    (state,) = call(
        functools.partial(third_kernel, geo),
        [wide],
        work(1),
        *static,
        state,
        low_state,
        high_state,
        megabytes=30,
    )
    (chunks,) = call(
        functools.partial(fourth_kernel, geo),
        [(group, BACK * b, LANES)],
        work(1),
        *static,
        state,
        early,
        late,
        moved,
        megabytes=20,
    )
    chunks = lax.all_to_all(chunks, ("gx", "gy"), 0, 0, tiled=True)
    return tuple(
        call(
            functools.partial(unpack_kernel, geo),
            [geo.block, (3, *geo.block), geo.block],
            [],
            chunks,
        )
    )


def solution(mesh):
    in_specs = (
        P("gx", "gy", "gz"),
        P(None, "gx", "gy", "gz"),
        P("gx", "gy", "gz"),
        P("gx", "gy", "gz"),
        P(),
    )
    out_specs = (P("gx", "gy", "gz"), P(None, "gx", "gy", "gz"), P("gx", "gy", "gz"))

    def program(saved_heat_state, *others):
        shape = saved_heat_state.shape
        plan = shards
        if slab_plan_fits(mesh, shape):
            plan = functools.partial(slab_shards, Slabs(mesh, shape))
        return jax.shard_map(
            plan, mesh=mesh, in_specs=in_specs, out_specs=out_specs, check_vma=False
        )(saved_heat_state, *others)

    return program
```

```python
import functools

import jax
import jax.numpy as jnp
from jax import lax
from jax.experimental import pallas as pl
from jax.experimental.pallas import tpu as pltpu
from jax.sharding import PartitionSpec as P

RECOMPUTE = 2
SCHUR_ITERS = 4
COARSE_SWEEPS = 3
LAYERS = 8


INCREMENT_DT = 0.2
DIFFUSIVITY = 0.3
ACTIVATION_ENERGY = 2.3
JACOBI_WEIGHT = 0.7
SCHUR_WEIGHT = 0.5
RAYLEIGH = 1.0


def extended(block, sides, width):
    for axis, dim in sides:
        count = lax.axis_size(axis)
        forward = [(i, i + 1) for i in range(count - 1)]
        backward = [(target, source) for source, target in forward]
        low = lax.ppermute(
            lax.slice_in_dim(block, block.shape[dim] - width, None, axis=dim), axis, forward
        )
        high = lax.ppermute(lax.slice_in_dim(block, 0, width, axis=dim), axis, backward)
        block = jnp.concatenate([low, block, high], axis=dim)
    return block


def neighbours(bordered_array):
    centre = bordered_array[..., 1:-1, 1:-1, 1:-1]
    beside_all = [
        bordered_array[..., 2:, 1:-1, 1:-1],
        bordered_array[..., :-2, 1:-1, 1:-1],
        bordered_array[..., 1:-1, 2:, 1:-1],
        bordered_array[..., 1:-1, :-2, 1:-1],
        bordered_array[..., 1:-1, 1:-1, 2:],
        bordered_array[..., 1:-1, 1:-1, :-2],
    ]
    return (centre, beside_all)


def finest_halo_cells(field):
    return extended(field, (("gx", 1), ("gy", 2), ("gz", 3)), 1)


def deep_halo(field):
    return extended(field, (("gx", 1), ("gy", 2), ("gz", 3)), 2)


def coarse_halo(field):
    return extended(field, (("gx", 1), ("gy", 2), ("gz", 3)), 1)


def march_backward(bordered_array, shallower_adjacent, deeper_adjacent):
    centre, beside_all = neighbours(bordered_array)
    drift = 0.0
    for dim_index in range(3):
        drift = (
            drift
            + shallower_adjacent[dim_index] * (centre - beside_all[2 * dim_index + 1])
            + deeper_adjacent[dim_index] * (beside_all[2 * dim_index] - centre)
        )
    spread = sum(beside_all) - 6.0 * centre
    return centre - INCREMENT_DT * drift + INCREMENT_DT * DIFFUSIVITY * spread


def motion_source(bordered_heat, forward_motion, dual_heat_after):
    centre, beside_all = neighbours(bordered_heat)
    device_pieces = [
        jnp.where(
            forward_motion[dim_index] > 0,
            centre - beside_all[2 * dim_index + 1],
            beside_all[2 * dim_index] - centre,
        )
        for dim_index in range(3)
    ]
    return -INCREMENT_DT * dual_heat_after[None] * jnp.stack(device_pieces)


def advect_dual_heat(pos_padded, neg_padded, lam_padded):
    centre, beside_all = neighbours(lam_padded)
    result = centre + INCREMENT_DT * DIFFUSIVITY * (sum(beside_all) - 6.0 * centre)
    for dim_index in range(3):
        pos_centre, pos_around = neighbours(pos_padded[dim_index])
        neg_centre, neg_around = neighbours(neg_padded[dim_index])
        result = result - INCREMENT_DT * (
            pos_centre - pos_around[2 * dim_index] + neg_around[2 * dim_index + 1] - neg_centre
        )
    return result


def coefficients(bordered_array, factor):
    centre, beside_all = neighbours(bordered_array)
    return [factor * (0.5 * (centre + other)) for other in beside_all]


def apply_operator(face_coef, bordered_array):
    centre, beside_all = neighbours(bordered_array)
    return sum((coef * (centre - other) for coef, other in zip(face_coef, beside_all)))


def gradient(bordered_array):
    centre, beside_all = neighbours(bordered_array)
    return jnp.stack(
        [
            0.5 * (beside_all[2 * dim_index] - beside_all[2 * dim_index + 1])
            for dim_index in range(3)
        ]
    )


def divergence(bordered_array):
    centre, beside_all = neighbours(bordered_array)
    return sum(
        (
            0.5 * (beside_all[2 * dim_index][dim_index] - beside_all[2 * dim_index + 1][dim_index])
            for dim_index in range(3)
        )
    )


def restrict(field):
    leading = field.shape[:-3]
    cells_x, cells_y, cells_z = field.shape[-3:]
    blocks = field.reshape(leading + (cells_x // 2, 2, cells_y // 2, 2, cells_z // 2, 2))
    return blocks.mean(axis=(-5, -3, -1))


def prolong(field):
    return jnp.repeat(jnp.repeat(jnp.repeat(field, 2, axis=-3), 2, axis=-2), 2, axis=-1)


def evaluate_viscosity(rheology_class, class_base_stiffness):
    base = jnp.zeros(rheology_class.shape, jnp.float32)
    for layer_index in range(LAYERS):
        base = base + jnp.where(
            rheology_class == layer_index, class_base_stiffness[layer_index], 0.0
        )
    return base


def inside_mask(extent_first, extent_second, extent_vertical):
    index_x = (
        lax.axis_index("gx") * extent_first + jnp.arange(extent_first + 2, dtype=jnp.int32) - 1
    )
    index_y = (
        lax.axis_index("gy") * extent_second + jnp.arange(extent_second + 2, dtype=jnp.int32) - 1
    )
    index_z = (
        lax.axis_index("gz") * extent_vertical
        + jnp.arange(extent_vertical + 2, dtype=jnp.int32)
        - 1
    )
    inside_x = (index_x >= 0) & (index_x < extent_first * lax.axis_size("gx"))
    inside_y = (index_y >= 0) & (index_y < extent_second * lax.axis_size("gy"))
    inside_z = (index_z >= 0) & (index_z < extent_vertical * lax.axis_size("gz"))
    return inside_x[:, None, None] & inside_y[None, :, None] & inside_z[None, None, :]


def coarse_solve(coarse_res, coarse_coef, coarse_diag, pad_field):
    coarse_corr = JACOBI_WEIGHT * coarse_res / coarse_diag
    for sweep in range(COARSE_SWEEPS - 1):
        coarse_corr = (
            coarse_corr
            + JACOBI_WEIGHT
            * (coarse_res - apply_operator(coarse_coef, pad_field(coarse_corr)))
            / coarse_diag
        )
    return coarse_corr


def shards(saved_heat_state, forward_motion, dual_heat_after, rheology_class, class_base_stiffness):
    extent_first, extent_second, extent_vertical = saved_heat_state.shape
    shallower_adjacent = jnp.maximum(forward_motion, 0.0)
    deeper_adjacent = jnp.minimum(forward_motion, 0.0)
    heat_state = saved_heat_state
    for repeat_index in range(RECOMPUTE):
        heat_state = march_backward(
            finest_halo_cells(heat_state[None])[0], shallower_adjacent, deeper_adjacent
        )
    local_viscosity = evaluate_viscosity(rheology_class, class_base_stiffness) * jnp.exp(
        -ACTIVATION_ENERGY * heat_state
    )
    stacked = jnp.concatenate(
        [
            heat_state[None],
            dual_heat_after[None],
            shallower_adjacent * dual_heat_after[None],
            deeper_adjacent * dual_heat_after[None],
            local_viscosity[None],
        ],
        0,
    )
    bordered_array = finest_halo_cells(stacked)
    driving_source = motion_source(bordered_array[0], forward_motion, dual_heat_after)
    advected_result = advect_dual_heat(bordered_array[2:5], bordered_array[5:8], bordered_array[1])
    face_coef = coefficients(bordered_array[8], 1.0)
    diagonal = sum(face_coef)
    coarse_visc = restrict(local_viscosity)
    coarse_coef = coefficients(coarse_halo(coarse_visc[None])[0], 0.25)
    coarse_diag = sum(coarse_coef)
    deep_static = deep_halo(jnp.concatenate([local_viscosity[None], driving_source], 0))
    cycle_coef = coefficients(deep_static[0], 1.0)
    cycle_source = deep_static[1:4, 1:-1, 1:-1, 1:-1]
    inside = inside_mask(extent_first, extent_second, extent_vertical)
    safe_diag = jnp.where(inside, sum(cycle_coef), 1.0)
    total_cells = (
        extent_first
        * extent_second
        * extent_vertical
        * lax.axis_size("gx")
        * lax.axis_size("gy")
        * lax.axis_size("gz")
    )
    velocity = jnp.zeros(forward_motion.shape, jnp.float32)
    mean_stress = jnp.zeros(saved_heat_state.shape, jnp.float32)
    for iteration in range(SCHUR_ITERS):
        if iteration == 0:
            cycle_resid = cycle_source
        else:
            flow_press = deep_halo(jnp.concatenate([velocity, mean_stress[None]], 0))
            cycle_resid = (
                cycle_source - apply_operator(cycle_coef, flow_press[0:3]) - gradient(flow_press[3])
            )
        cycle_corr = jnp.where(inside, JACOBI_WEIGHT * cycle_resid / safe_diag, 0.0)
        residual = cycle_resid[:, 1:-1, 1:-1, 1:-1]
        correction = cycle_corr[:, 1:-1, 1:-1, 1:-1]
        residual_two = residual - apply_operator(face_coef, cycle_corr)
        coarse_res = restrict(residual_two)
        coarse_corr = coarse_solve(coarse_res, coarse_coef, coarse_diag, coarse_halo)
        correction = correction + prolong(coarse_corr)
        correction = (
            correction
            + JACOBI_WEIGHT
            * (residual - apply_operator(face_coef, finest_halo_cells(correction)))
            / diagonal
        )
        velocity = velocity + correction
        spread_flow = divergence(finest_halo_cells(velocity))
        mean_stress = mean_stress - SCHUR_WEIGHT * local_viscosity * spread_flow
        mean_stress = mean_stress - lax.psum(jnp.sum(mean_stress), ("gx", "gy", "gz")) / total_cells
    adj_temp_prev = advected_result + RAYLEIGH * velocity[2]
    return (adj_temp_prev, velocity, mean_stress)


SUB = 8
LANES = 128
FIELDS = 6
BACK = 5
EDGE = 2
PHASE = 8
HELD = 64
VMEM_LIMIT = 32 * 1024 * 1024
FORWARD, ADJOINT = range(2)


def slab_plan_fits(mesh, shape):
    sizes = mesh.shape
    group = sizes["gx"] * sizes["gy"]
    block = (shape[0] // sizes["gx"], shape[1] // sizes["gy"], shape[2] // sizes["gz"])
    return (
        group == SUB
        and block[0] == SUB
        and block[0] * block[1] == LANES
        and block[1] * group == LANES
        and block[2] == LANES
        and block[2] == group * 2 * PHASE
    )


class Slabs:
    def __init__(self, mesh, shape):
        self.nx, self.ny, self.nz = mesh.shape["gx"], mesh.shape["gy"], mesh.shape["gz"]
        self.group = self.nx * self.ny
        self.width, self.breadth, self.height = shape
        self.block = (shape[0] // self.nx, shape[1] // self.ny, shape[2] // self.nz)
        self.slab = self.block[2] // self.group
        self.margin = self.slab + SUB
        self.rows = self.slab + 2 * self.margin
        self.cells = self.width * self.breadth * self.height
        self.place = []
        for ix in range(self.nx):
            for iy in range(self.ny):
                step = ix if iy % 2 == 0 else self.nx - 1 - ix
                self.place.append(iy * self.nx + step)
        self.holder = [self.place.index(j) for j in range(self.group)]

    def device(self, slab):
        return self.holder[slab % self.group] * self.nz + slab // self.group

    def shifts(self, distance):
        count = self.group * self.nz
        return [
            (self.device(p), self.device(p + distance))
            for p in range(count)
            if 0 <= p + distance < count
        ]

    def index(self):
        ix, iy = lax.axis_index("gx"), lax.axis_index("gy")
        step = jnp.where(iy % 2 == 0, ix, self.nx - 1 - ix)
        return lax.axis_index("gz") * self.group + iy * self.nx + step

    def inside(self, z, n=SUB):
        layer = self.index() * self.slab - self.margin + z
        layer = layer + lax.broadcasted_iota(jnp.int32, (n, LANES), 0)
        return (layer >= 0) & (layer < self.height)


def swap_granules(tiles, granule):
    lane = lax.broadcasted_iota(jnp.int32, (SUB, LANES), 1) // granule
    for bit in (1, 2, 4):
        low = (lane & bit) == 0
        new = list(tiles)
        for a in range(SUB):
            if a & bit:
                continue
            b = a | bit
            new[a] = jnp.where(low, tiles[a], pltpu.roll(tiles[b], granule * bit, 1))
            new[b] = jnp.where(low, pltpu.roll(tiles[a], LANES - granule * bit, 1), tiles[b])
        tiles = new
    return tiles


class Tiles:
    def __init__(self, geo):
        self.breadth = geo.breadth
        self.row = lax.broadcasted_iota(jnp.int32, (SUB, LANES), 0)
        self.lane = lax.broadcasted_iota(jnp.int32, (SUB, LANES), 1)
        self.y = self.lane % self.breadth
        self.kept = {}

    def sliding(self, ref, z, c, x):
        where = (id(ref), id(z), c)
        for key in [k for k in self.kept if k[:3] == where and abs(k[3] - x) > 1]:
            del self.kept[key]

        def load(j):
            key = (*where, j)
            if key not in self.kept:
                self.kept[key] = (ref, z, get(ref, z, c, j))
            return self.kept[key][2]

        return load

    def x(self, load, x, count, step):
        j = x + step
        if 0 <= j < count:
            return load(j)
        if step > 0:
            turned = pltpu.roll(load(0), LANES - self.breadth, 1)
            return jnp.where(self.lane < LANES - self.breadth, turned, 0.0)
        turned = pltpu.roll(load(count - 1), self.breadth, 1)
        return jnp.where(self.lane >= self.breadth, turned, 0.0)

    def ys(self, f, d):
        return pltpu.roll(f, LANES - d, 1), pltpu.roll(f, d, 1)

    def y_masks(self, d, value):
        up, down = self.y < self.breadth - d, self.y >= d
        value = jnp.float32(value)
        return jnp.where(up, value, 0.0), jnp.where(down, value, 0.0)

    def pair_sum(self, f):
        f = f + jnp.where(self.lane % 2 == 0, pltpu.roll(f, LANES - 1, 1), pltpu.roll(f, 1, 1))
        return f + jnp.where(self.row % 2 == 0, pltpu.roll(f, SUB - 1, 0), pltpu.roll(f, 1, 0))


def tree(terms):
    while len(terms) > 1:
        terms = [sum(terms[k : k + 2]) for k in range(0, len(terms), 2)]
    return terms[0]


def get(ref, z, *index):
    return ref[(*index, pl.ds(z, SUB), slice(None))]


def sweep(lo, hi, body):
    assert (hi - lo) % SUB == 0

    def step(t, _):
        late = []

        def store(ref, value, z, *index):
            ref[(*index, pl.ds(z, SUB), slice(None))] = value

        def put(*item):
            late.append(item)
            if len(late) > HELD:
                store(*late.pop(0))

        body(pl.multiple_of(t * SUB, SUB) + lo, put)
        for item in late:
            store(*item)
        return 0

    lax.fori_loop(0, (hi - lo) // SUB, step, 0)


def pack_kernel(geo, heat_in, flow_in, dual_in, kind_in, out, heat, flow, dual, kind, sems):
    b, e = geo.slab, EDGE
    pairs = ((heat_in, heat), (flow_in, flow), (dual_in, dual), (kind_in, kind))
    copies = [
        pltpu.make_async_copy(source, target, sems.at[k])
        for k, (source, target) in enumerate(pairs)
    ]
    for copy in copies:
        copy.start()
    for copy in copies:
        copy.wait()
    flat = [heat[...], flow[0], flow[1], flow[2], dual[...], kind[...].astype(jnp.float32)]
    turned = [f.reshape(LANES, LANES).T for f in flat]
    for j in range(geo.group):
        q = geo.holder[j]
        for f in range(FIELDS):
            out[q, f * b : (f + 1) * b, :] = turned[f][j * b : (j + 1) * b]
        tail = FIELDS * b
        first = jnp.concatenate([turned[f][j * b : j * b + e] for f in range(4)], 0)
        last = jnp.concatenate([turned[f][(j + 1) * b - e : (j + 1) * b] for f in range(4)], 0)
        out[q, tail : tail + SUB, :] = first
        out[q, tail + SUB : tail + 2 * SUB, :] = last


STATIC_FINE = ("s0", "s1", "s2", "visc", "w", "diag", "cxp", "cxm", "cyp", "cym", "cz")
STATIC_COARSE = ("kxp", "kxm", "kyp", "kym", "kzp", "kzm", "wc")
STATIC = STATIC_FINE + STATIC_COARSE


def iterate(geo, st, work, seqs, lo, hi, first=(), mean=None):
    v, p, res, cor, cor2, cc0, cc1 = work
    tl = Tiles(geo)
    half_up, half_down = tl.y_masks(1, 0.5)
    keep = 1.0 - JACOBI_WEIGHT
    slots = [(q, 3 * s + k) for s, q in enumerate(seqs) for k in range(3)]
    transposed = len(seqs)

    def faces(x, z):
        c = [get(st[name], z, x) for name in ("cxp", "cxm", "cyp", "cym", "cz")]
        return c + [get(st["cz"], z - 1, x)]

    def beside(ref, c, x, z):
        load = tl.sliding(ref, z, c, x)
        f = load(x)
        near = [tl.x(load, x, SUB, 1), tl.x(load, x, SUB, -1), *tl.ys(f, 1)]
        return f, near + [get(ref, z + 1, c, x), get(ref, z - 1, c, x)]

    def around(coef, ref, c, x, z):
        f, near = beside(ref, c, x, z)
        return f, tree([a * b for a, b in zip(coef, near)])

    def residual(z, put):
        for x in range(SUB):
            w = get(st["w"], z, x)
            if FORWARD in seqs and FORWARD not in first:
                coef, diag = faces(x, z), get(st["diag"], z, x)
            for s, q in enumerate(seqs):
                start = q == FORWARD and q in first
                if not start:
                    _, near = beside(p, transposed if q == ADJOINT else s, x, z)
                    slope = [
                        0.5 * (near[0] - near[1]),
                        half_up * near[2] - half_down * near[3],
                        0.5 * (near[4] - near[5]),
                    ]
                for k in range(3):
                    c = 3 * s + k
                    if q == FORWARD:
                        value = get(st["s%d" % k], z, x)
                        if not start:
                            f, total = around(coef, v, c, x, z)
                            value = value - slope[k] - (diag * f - total)
                    else:
                        value = slope[k] if q in first else get(cor, z, c, x) + slope[k]
                    put(res, value, z, c, x)
                    put(cor, w * value, z, c, x)

    sweep(lo - 8, hi + 8, residual)

    def restricted(z, put):
        for pair in range(SUB // 2):
            coefs = [faces(2 * pair + side, z) for side in range(2)]
            wc = 0.125 * get(st["wc"], z, pair)
            for _, c in slots:
                left = 0.0
                for side in range(2):
                    _, total = around(coefs[side], cor, c, 2 * pair + side, z)
                    left = left + (keep * get(res, z, c, 2 * pair + side) + total)
                put(cc0, wc * tl.pair_sum(left), z, c, pair)

    sweep(lo - 8, hi + 8, restricted)

    def coarse_step(ref, c, pair, z):
        f = get(ref, z, c, pair)
        load = lambda j: get(ref, z, c, j)
        near = [tl.x(load, pair, SUB // 2, 1), tl.x(load, pair, SUB // 2, -1), *tl.ys(f, 2)]
        near += [get(ref, z + 2, c, pair), get(ref, z - 2, c, pair)]
        terms = [get(st[name], z, pair) * b for name, b in zip(STATIC_COARSE, near)]
        return tree([get(cc0, z, c, pair), keep * f] + terms)

    def sweep_one(z, put):
        for pair in range(SUB // 2):
            for _, c in slots:
                put(cc1, coarse_step(cc0, c, pair, z), z, c, pair)

    sweep(lo - 4, hi + 4, sweep_one)

    def sweep_two(z, put):
        for pair in range(SUB // 2):
            for _, c in slots:
                value = coarse_step(cc1, c, pair, z)
                for x in (2 * pair, 2 * pair + 1):
                    put(cor2, get(cor, z, c, x) + value, z, c, x)

    sweep(lo - 4, hi + 4, sweep_two)

    def velocity(z, put):
        for x in range(SUB):
            coef, w = faces(x, z), get(st["w"], z, x)
            for q, c in slots:
                f, total = around(coef, cor2, c, x, z)
                value = get(cor, z, c, x) + keep * f + w * total
                if q == FORWARD and q not in first:
                    value = get(v, z, c, x) + value
                put(v, value, z, c, x)

    sweep(lo - 4, hi + 4, velocity)

    def pressure(z, put):
        for x in range(SUB):
            visc = SCHUR_WEIGHT * get(st["visc"], z, x)
            for s, q in enumerate(seqs):
                load = lambda j: get(v, z, 3 * s, j)
                div = 0.5 * (tl.x(load, x, SUB, 1) - tl.x(load, x, SUB, -1))
                up, down = tl.ys(get(v, z, 3 * s + 1, x), 1)
                div = div + (half_up * up - half_down * down)
                div = div + 0.5 * (get(v, z + 1, 3 * s + 2, x) - get(v, z - 1, 3 * s + 2, x))
                if q == ADJOINT:
                    value = get(p, z, s, x) + div
                    put(p, value, z, s, x)
                    put(p, visc * value, z, transposed, x)
                    coef, diag = faces(x, z), get(st["diag"], z, x)
                    for c in range(3 * s, 3 * s + 3):
                        f, total = around(coef, v, c, x, z)
                        put(cor, get(res, z, c, x) - (diag * f - total), z, c, x)
                    continue
                value = -(visc * div)
                if not (q == FORWARD and q in first):
                    value = get(p, z, s, x) + value
                if mean is not None:
                    value = value - jnp.where(geo.inside(z), mean, 0.0)
                put(p, value, z, s, x)

    sweep(lo, hi, pressure)


def whole_sum(value):
    return jnp.sum(jnp.sum(value, axis=0), axis=(0, 1), keepdims=True)


def product(left, right):
    value = 0.0
    for a, b in zip(left, right):
        value = value + a[...] * b[...]
    return whole_sum(value)


def in_lanes(values, rows):
    lane = lax.broadcasted_iota(jnp.int32, (rows, LANES), 1)
    out = jnp.zeros((rows, LANES), jnp.float32)
    for k, value in values:
        out = jnp.where(lane == k, value, out)
    return out


def setup_kernel(geo, stiffness, own, low, high, low_edge, high_edge, *refs):
    st = dict(zip(STATIC, refs))
    moved, duals, sums, raw, heat, vc, *work = refs[len(STATIC) :]
    v, p, res, cor, cor2, cc0, cc1 = work
    tl = Tiles(geo)
    b, m, n_rows = geo.slab, geo.margin, geo.rows
    granule = geo.block[1]

    def place(t, _):
        groups = []
        for source, base in ((low, m - b), (own, m), (high, m + b)):
            for u in range(0, b, SUB):
                row = pl.multiple_of(t * b, b) + u
                tiles = [source[q, pl.ds(row, SUB), :] for q in range(geo.group)]
                groups.append((base + u, tiles))
        groups = [(row, swap_granules(tiles, granule)) for row, tiles in groups]
        for row, tiles in groups:
            for x, tile in enumerate(tiles):
                raw[t, x, row : row + SUB, :] = tile
        return 0

    lax.fori_loop(0, FIELDS, place, 0)
    for source, base in ((low_edge, m - b - EDGE), (high_edge, m + 2 * b)):
        tiles = [source[q] for q in range(geo.group)]
        for x, tile in enumerate(swap_granules(tiles, granule)):
            for f in range(4):
                raw[f, x, base : base + EDGE, :] = tile[f * EDGE : (f + 1) * EDGE]

    one_up, one_down = tl.y_masks(1, 1.0)

    def beside(load, x, z):
        f = load(z, x)
        up, down = tl.ys(f, 1)
        near = [tl.x(lambda j: load(z, j), x, SUB, s) for s in (1, -1)]
        return f, near + [one_up * up, one_down * down, load(z + 1, x), load(z - 1, x)]

    def field(f):
        return lambda z, x: get(raw, z, f, x)

    def advance(old, new):
        def body(z, put):
            inside = geo.inside(z)
            for x in range(SUB):
                f, near = beside(old, x, z)
                drift = 0.0
                for k in range(3):
                    flow = get(raw, z, 1 + k, x)
                    drift = drift + jnp.maximum(flow, 0.0) * (f - near[2 * k + 1])
                    drift = drift + jnp.minimum(flow, 0.0) * (near[2 * k] - f)
                spread = sum(near) - 6.0 * f
                value = f - INCREMENT_DT * drift + INCREMENT_DT * DIFFUSIVITY * spread
                put(heat, jnp.where(inside, value, 0.0), z, new, x)

        return body

    def warm(new):
        return lambda z, x: get(heat, z, new, x)

    sweep(m - b - 4, m + 2 * b + 4, advance(field(0), 0))
    sweep(m - b, m + 2 * b, advance(warm(0), 1))

    def viscosity(z, put):
        inside = geo.inside(z)
        for pair in range(SUB // 2):
            coarse = 0.0
            for x in (2 * pair, 2 * pair + 1):
                kind = get(raw, z, 5, x)
                base = jnp.zeros(kind.shape, jnp.float32)
                for layer in range(LAYERS):
                    base = base + jnp.where(kind == float(layer), stiffness[layer], 0.0)
                value = base * jnp.exp(-ACTIVATION_ENERGY * get(heat, z, 1, x))
                value = jnp.where(inside, value, 0.0)
                put(st["visc"], value, z, x)
                coarse = coarse + value
            put(vc, 0.125 * tl.pair_sum(coarse), z, pair)

    sweep(m - b, m + 2 * b, viscosity)

    def statics(z, put):
        inside = geo.inside(z)
        for x in range(SUB):
            c, near = beside(lambda z, x: get(st["visc"], z, x), x, z)
            face = [0.5 * (c + o) for o in near]
            diag = tree(face)
            face[2], face[3] = one_up * face[2], one_down * face[3]
            for name, f in zip(("cxp", "cxm", "cyp", "cym", "cz"), face):
                put(st[name], f, z, x)
            put(st["diag"], diag, z, x)
            put(st["w"], jnp.where(inside, JACOBI_WEIGHT / diag, 0.0), z, x)
            f, near = beside(warm(1), x, z)
            dual = -INCREMENT_DT * get(raw, z, 4, x)
            for k in range(3):
                flow = get(raw, z, 1 + k, x)
                step = jnp.where(flow > 0, f - near[2 * k + 1], near[2 * k] - f)
                put(st["s%d" % k], dual * step, z, x)

    sweep(m - b, m + 2 * b, statics)

    two_up, two_down = tl.y_masks(2, 1.0)

    def coarse_statics(z, put):
        inside = geo.inside(z)
        for pair in range(SUB // 2):
            c = get(vc, z, pair)
            load = lambda j: get(vc, z, j)
            up, down = tl.ys(c, 2)
            near = [tl.x(load, pair, SUB // 2, s) for s in (1, -1)]
            near += [two_up * up, two_down * down, get(vc, z + 2, pair), get(vc, z - 2, pair)]
            face = [0.25 * (0.5 * (c + o)) for o in near]
            wc = jnp.where(inside, JACOBI_WEIGHT / sum(face), 0.0)
            face[2], face[3] = two_up * face[2], two_down * face[3]
            for name, f in zip(STATIC_COARSE, face):
                put(st[name], wc * f, z, pair)
            put(st["wc"], wc, z, pair)

    sweep(m - b, m + 2 * b, coarse_statics)

    def transport(z, put):
        for x in range(SUB):
            dual, near = beside(field(4), x, z)
            value = dual + INCREMENT_DT * DIFFUSIVITY * (sum(near) - 6.0 * dual)
            for k in range(3):
                flow, sides = beside(field(1 + k), x, z)
                a = jnp.maximum(flow, 0.0) * dual
                c = jnp.minimum(flow, 0.0) * dual
                ahead = jnp.maximum(sides[2 * k], 0.0) * near[2 * k]
                behind = jnp.minimum(sides[2 * k + 1], 0.0) * near[2 * k + 1]
                value = value - INCREMENT_DT * (a - ahead + behind - c)
            put(moved, value, z - m, x)

    sweep(m, m + b, transport)

    def unit(z, put):
        value = jnp.where(geo.inside(z), 1.0, 0.0)
        for x in range(SUB):
            put(p, value, z, 0, x)
            put(p, SCHUR_WEIGHT * get(st["visc"], z, x), z, 1, x)

    sweep(0, n_rows, unit)

    mine = slice(m, m + b)
    source = [st["s%d" % k].at[:, mine, :] for k in range(3)]
    step = [v.at[k, :, mine, :] for k in range(3)]
    iterate(geo, st, work, (ADJOINT,), m - PHASE, m + b + PHASE, (ADJOINT,))
    sums_of = [(0, product(step, source)), (1, whole_sum(p[0, :, mine, :]))]
    for k in range(4):
        duals[k] = cor[k, :, mine, :] if k < 3 else p[0, :, mine, :]
    iterate(geo, st, work, (ADJOINT,), m, m + b)
    sums_of += [(2, product(step, source))]
    for k in range(4):
        duals[4 + k] = cor[k, :, mine, :] if k < 3 else p[0, :, mine, :]
    sums[...] = in_lanes(sums_of, sums.shape[0])


def first_kernel(geo, *refs):
    st = dict(zip(STATIC, refs))
    out, *work = refs[len(STATIC) :]
    v, p = work[:2]
    rows = slice(geo.margin - PHASE, geo.margin + geo.slab + PHASE)
    iterate(geo, st, work, (FORWARD,), rows.start, rows.stop, (FORWARD,))
    for k in range(4):
        out[k] = v[k, :, rows, :] if k < 3 else p[0, :, rows, :]


def refill(geo, v, p, state, rows, shift):
    for k in range(3):
        v[k, :, rows, :] = state[k]
    if shift is None:
        p[0, :, rows, :] = state[3]
    else:
        inside = geo.inside(rows.start, rows.stop - rows.start)
        p[0, :, rows, :] = state[3] - jnp.where(inside, shift, 0.0)[None]


def second_kernel(geo, *refs):
    st = dict(zip(STATIC, refs))
    earlier, early, duals, state, sums, *work = refs[len(STATIC) :]
    v, p = work[:2]
    b, m = geo.slab, geo.margin
    m1, m2 = means(geo, early[...], None)[:2]
    refill(geo, v, p, earlier, slice(m - PHASE, m + b + PHASE), m1)
    iterate(geo, st, work, (FORWARD,), m, m + b, mean=m2)
    mine = slice(m, m + b)
    for k in range(4):
        state[k] = v[k, :, mine, :] if k < 3 else p[0, :, mine, :]
    fields = [state.at[k] for k in range(4)]
    near, far = [duals.at[k] for k in range(4)], [duals.at[4 + k] for k in range(4)]
    sums_of = [(3, product(near, fields)), (4, product(far, fields))]
    sums[...] = in_lanes(sums_of, sums.shape[0])


def means(geo, early, late):
    sums = early if late is None else early + late
    row = jnp.sum(sums, axis=0, keepdims=True) / geo.cells
    lane = lax.broadcasted_iota(jnp.int32, row.shape, 1)

    def at(k):
        return jnp.sum(jnp.where(lane == k, row, 0.0), axis=1, keepdims=True)

    c1, l1, c2, l1_x2, l2_x2 = [at(k) for k in range(5)]
    m1 = c1
    m2 = c1 + c2 - m1 * l1
    m3 = c1 + l1_x2
    m4 = c1 + c2 + l2_x2 - m3 * l1
    return m1, m2, m3, m4


def third_kernel(geo, *refs):
    st = dict(zip(STATIC, refs))
    own, low, high, out, *work = refs[len(STATIC) :]
    v, p = work[:2]
    b, m = geo.slab, geo.margin
    for source, base in ((low, m - b), (own, m), (high, m + b)):
        refill(geo, v, p, source, slice(base, base + b), None)
    rows = slice(m - PHASE, m + b + PHASE)
    iterate(geo, st, work, (FORWARD,), rows.start, rows.stop)
    for k in range(4):
        out[k] = v[k, :, rows, :] if k < 3 else p[0, :, rows, :]


def fourth_kernel(geo, *refs):
    st = dict(zip(STATIC, refs))
    state, early, late, moved, out, *work = refs[len(STATIC) :]
    v, p = work[:2]
    b, m = geo.slab, geo.margin
    m3, m4 = means(geo, early[...], late[...])[2:]
    refill(geo, v, p, state, slice(m - PHASE, m + b + PHASE), m3)
    iterate(geo, st, work, (FORWARD,), m, m + b, mean=m4)
    for u in range(0, b, SUB):
        at = slice(m + u, m + u + SUB)
        columns = range(SUB)
        fields = [[v[k, x, at, :] for x in columns] for k in range(3)]
        fields.append([p[0, x, at, :] for x in columns])
        fields.append([moved[x, u : u + SUB, :] + fields[2][x] for x in columns])
        for f, tiles in enumerate(fields):
            for q, tile in enumerate(swap_granules(tiles, geo.block[1])):
                out[q, f * b + u : f * b + u + SUB, :] = tile


def unpack_kernel(geo, chunks, heat, flow, pressure):
    b = geo.slab
    for f in range(BACK):
        rows = [chunks[geo.holder[j], f * b : (f + 1) * b, :] for j in range(geo.group)]
        block = jnp.concatenate(rows, 0).T.reshape(geo.block)
        if f < 3:
            flow[f] = block
        elif f == 3:
            pressure[...] = block
        else:
            heat[...] = block


def call(kernel, out, scratch, *args, smem=(), hbm=(), megabytes=2):
    f32 = jnp.float32
    cost = pl.CostEstimate(
        flops=megabytes * 1000000, bytes_accessed=megabytes * 1000000, transcendentals=0
    )
    specs = [
        pl.BlockSpec(
            memory_space=pltpu.SMEM if i in smem else pltpu.HBM if i in hbm else pltpu.VMEM
        )
        for i in range(len(args))
    ]
    return pl.pallas_call(
        kernel,
        out_shape=[jax.ShapeDtypeStruct(s, f32) for s in out],
        in_specs=specs,
        out_specs=[pl.BlockSpec(memory_space=pltpu.VMEM) for _ in out],
        scratch_shapes=[pltpu.VMEM(s, f32) if isinstance(s, tuple) else s for s in scratch],
        compiler_params=pltpu.CompilerParams(vmem_limit_bytes=VMEM_LIMIT),
        cost_estimate=cost,
    )(*args)


def slab_shards(geo, heat, flow, dual, kind, stiffness):
    b, group = geo.slab, geo.group
    rows = FIELDS * b
    inputs = (heat, flow, dual, kind)
    (chunks,) = call(
        functools.partial(pack_kernel, geo),
        [(group, rows + 2 * SUB, LANES)],
        [pltpu.VMEM(a.shape, a.dtype) for a in inputs] + [pltpu.SemaphoreType.DMA((4,))],
        *inputs,
        hbm=range(4),
    )
    own = lax.all_to_all(chunks, ("gx", "gy"), 0, 0, tiled=True)
    axes = ("gx", "gy", "gz")
    low = lax.ppermute(own, axes, geo.shifts(1))
    high = lax.ppermute(own, axes, geo.shifts(-1))
    high_edge = lax.ppermute(own[:, rows : rows + SUB], axes, geo.shifts(-2))
    low_edge = lax.ppermute(own[:, rows + SUB :], axes, geo.shifts(2))

    fine, coarse = (SUB, geo.rows, LANES), (SUB // 2, geo.rows, LANES)
    slab = (SUB, b, LANES)

    def work(n, more=0):
        fields = [(3 * n, *fine), (n + more, *fine)] + [(3 * n, *fine)] * 3
        return fields + [(3 * n, *coarse)] * 2

    devices = group * geo.nz
    wide = (4, SUB, b + 2 * PHASE, LANES)
    *static, moved, duals, early = call(
        functools.partial(setup_kernel, geo),
        [fine] * len(STATIC_FINE)
        + [coarse] * len(STATIC_COARSE)
        + [slab, (8, *slab), (devices, LANES)],
        [(FIELDS, *fine), (2, *fine), coarse] + work(1, 1),
        stiffness,
        own,
        low,
        high,
        low_edge,
        high_edge,
        smem=(0,),
        megabytes=60,
    )
    early = lax.all_to_all(early, axes, 0, 0, tiled=True)
    (state,) = call(
        functools.partial(first_kernel, geo), [wide], work(1), *static, megabytes=20
    )
    state, late = call(
        functools.partial(second_kernel, geo),
        [(4, *slab), (devices, LANES)],
        work(1),
        *static,
        state,
        early,
        duals,
        megabytes=20,
    )
    low_state = lax.ppermute(state, axes, geo.shifts(1))
    high_state = lax.ppermute(state, axes, geo.shifts(-1))
    late = lax.all_to_all(late, axes, 0, 0, tiled=True)
    (state,) = call(
        functools.partial(third_kernel, geo),
        [wide],
        work(1),
        *static,
        state,
        low_state,
        high_state,
        megabytes=30,
    )
    (chunks,) = call(
        functools.partial(fourth_kernel, geo),
        [(group, BACK * b, LANES)],
        work(1),
        *static,
        state,
        early,
        late,
        moved,
        megabytes=20,
    )
    chunks = lax.all_to_all(chunks, ("gx", "gy"), 0, 0, tiled=True)
    return tuple(
        call(
            functools.partial(unpack_kernel, geo),
            [geo.block, (3, *geo.block), geo.block],
            [],
            chunks,
        )
    )


def solution(mesh):
    in_specs = (
        P("gx", "gy", "gz"),
        P(None, "gx", "gy", "gz"),
        P("gx", "gy", "gz"),
        P("gx", "gy", "gz"),
        P(),
    )
    out_specs = (P("gx", "gy", "gz"), P(None, "gx", "gy", "gz"), P("gx", "gy", "gz"))

    def program(saved_heat_state, *others):
        shape = saved_heat_state.shape
        plan = shards
        if slab_plan_fits(mesh, shape):
            plan = functools.partial(slab_shards, Slabs(mesh, shape))
        return jax.shard_map(
            plan, mesh=mesh, in_specs=in_specs, out_specs=out_specs, check_vma=False
        )(saved_heat_state, *others)

    return program
```

```python
import functools

import jax
import jax.numpy as jnp
from jax import lax
from jax.experimental import pallas as pl
from jax.experimental.pallas import tpu as pltpu
from jax.sharding import PartitionSpec as P

RECOMPUTE = 2
SCHUR_ITERS = 4
COARSE_SWEEPS = 3
LAYERS = 8


INCREMENT_DT = 0.2
DIFFUSIVITY = 0.3
ACTIVATION_ENERGY = 2.3
JACOBI_WEIGHT = 0.7
SCHUR_WEIGHT = 0.5
RAYLEIGH = 1.0


def extended(block, sides, width):
    for axis, dim in sides:
        count = lax.axis_size(axis)
        forward = [(i, i + 1) for i in range(count - 1)]
        backward = [(target, source) for source, target in forward]
        low = lax.ppermute(
            lax.slice_in_dim(block, block.shape[dim] - width, None, axis=dim), axis, forward
        )
        high = lax.ppermute(lax.slice_in_dim(block, 0, width, axis=dim), axis, backward)
        block = jnp.concatenate([low, block, high], axis=dim)
    return block


def neighbours(bordered_array):
    centre = bordered_array[..., 1:-1, 1:-1, 1:-1]
    beside_all = [
        bordered_array[..., 2:, 1:-1, 1:-1],
        bordered_array[..., :-2, 1:-1, 1:-1],
        bordered_array[..., 1:-1, 2:, 1:-1],
        bordered_array[..., 1:-1, :-2, 1:-1],
        bordered_array[..., 1:-1, 1:-1, 2:],
        bordered_array[..., 1:-1, 1:-1, :-2],
    ]
    return (centre, beside_all)


def finest_halo_cells(field):
    return extended(field, (("gx", 1), ("gy", 2), ("gz", 3)), 1)


def deep_halo(field):
    return extended(field, (("gx", 1), ("gy", 2), ("gz", 3)), 2)


def coarse_halo(field):
    return extended(field, (("gx", 1), ("gy", 2), ("gz", 3)), 1)


def march_backward(bordered_array, shallower_adjacent, deeper_adjacent):
    centre, beside_all = neighbours(bordered_array)
    drift = 0.0
    for dim_index in range(3):
        drift = (
            drift
            + shallower_adjacent[dim_index] * (centre - beside_all[2 * dim_index + 1])
            + deeper_adjacent[dim_index] * (beside_all[2 * dim_index] - centre)
        )
    spread = sum(beside_all) - 6.0 * centre
    return centre - INCREMENT_DT * drift + INCREMENT_DT * DIFFUSIVITY * spread


def motion_source(bordered_heat, forward_motion, dual_heat_after):
    centre, beside_all = neighbours(bordered_heat)
    device_pieces = [
        jnp.where(
            forward_motion[dim_index] > 0,
            centre - beside_all[2 * dim_index + 1],
            beside_all[2 * dim_index] - centre,
        )
        for dim_index in range(3)
    ]
    return -INCREMENT_DT * dual_heat_after[None] * jnp.stack(device_pieces)


def advect_dual_heat(pos_padded, neg_padded, lam_padded):
    centre, beside_all = neighbours(lam_padded)
    result = centre + INCREMENT_DT * DIFFUSIVITY * (sum(beside_all) - 6.0 * centre)
    for dim_index in range(3):
        pos_centre, pos_around = neighbours(pos_padded[dim_index])
        neg_centre, neg_around = neighbours(neg_padded[dim_index])
        result = result - INCREMENT_DT * (
            pos_centre - pos_around[2 * dim_index] + neg_around[2 * dim_index + 1] - neg_centre
        )
    return result


def coefficients(bordered_array, factor):
    centre, beside_all = neighbours(bordered_array)
    return [factor * (0.5 * (centre + other)) for other in beside_all]


def apply_operator(face_coef, bordered_array):
    centre, beside_all = neighbours(bordered_array)
    return sum((coef * (centre - other) for coef, other in zip(face_coef, beside_all)))


def gradient(bordered_array):
    centre, beside_all = neighbours(bordered_array)
    return jnp.stack(
        [
            0.5 * (beside_all[2 * dim_index] - beside_all[2 * dim_index + 1])
            for dim_index in range(3)
        ]
    )


def divergence(bordered_array):
    centre, beside_all = neighbours(bordered_array)
    return sum(
        (
            0.5 * (beside_all[2 * dim_index][dim_index] - beside_all[2 * dim_index + 1][dim_index])
            for dim_index in range(3)
        )
    )


def restrict(field):
    leading = field.shape[:-3]
    cells_x, cells_y, cells_z = field.shape[-3:]
    blocks = field.reshape(leading + (cells_x // 2, 2, cells_y // 2, 2, cells_z // 2, 2))
    return blocks.mean(axis=(-5, -3, -1))


def prolong(field):
    return jnp.repeat(jnp.repeat(jnp.repeat(field, 2, axis=-3), 2, axis=-2), 2, axis=-1)


def evaluate_viscosity(rheology_class, class_base_stiffness):
    base = jnp.zeros(rheology_class.shape, jnp.float32)
    for layer_index in range(LAYERS):
        base = base + jnp.where(
            rheology_class == layer_index, class_base_stiffness[layer_index], 0.0
        )
    return base


def inside_mask(extent_first, extent_second, extent_vertical):
    index_x = (
        lax.axis_index("gx") * extent_first + jnp.arange(extent_first + 2, dtype=jnp.int32) - 1
    )
    index_y = (
        lax.axis_index("gy") * extent_second + jnp.arange(extent_second + 2, dtype=jnp.int32) - 1
    )
    index_z = (
        lax.axis_index("gz") * extent_vertical
        + jnp.arange(extent_vertical + 2, dtype=jnp.int32)
        - 1
    )
    inside_x = (index_x >= 0) & (index_x < extent_first * lax.axis_size("gx"))
    inside_y = (index_y >= 0) & (index_y < extent_second * lax.axis_size("gy"))
    inside_z = (index_z >= 0) & (index_z < extent_vertical * lax.axis_size("gz"))
    return inside_x[:, None, None] & inside_y[None, :, None] & inside_z[None, None, :]


def coarse_solve(coarse_res, coarse_coef, coarse_diag, pad_field):
    coarse_corr = JACOBI_WEIGHT * coarse_res / coarse_diag
    for sweep in range(COARSE_SWEEPS - 1):
        coarse_corr = (
            coarse_corr
            + JACOBI_WEIGHT
            * (coarse_res - apply_operator(coarse_coef, pad_field(coarse_corr)))
            / coarse_diag
        )
    return coarse_corr


def shards(saved_heat_state, forward_motion, dual_heat_after, rheology_class, class_base_stiffness):
    extent_first, extent_second, extent_vertical = saved_heat_state.shape
    shallower_adjacent = jnp.maximum(forward_motion, 0.0)
    deeper_adjacent = jnp.minimum(forward_motion, 0.0)
    heat_state = saved_heat_state
    for repeat_index in range(RECOMPUTE):
        heat_state = march_backward(
            finest_halo_cells(heat_state[None])[0], shallower_adjacent, deeper_adjacent
        )
    local_viscosity = evaluate_viscosity(rheology_class, class_base_stiffness) * jnp.exp(
        -ACTIVATION_ENERGY * heat_state
    )
    stacked = jnp.concatenate(
        [
            heat_state[None],
            dual_heat_after[None],
            shallower_adjacent * dual_heat_after[None],
            deeper_adjacent * dual_heat_after[None],
            local_viscosity[None],
        ],
        0,
    )
    bordered_array = finest_halo_cells(stacked)
    driving_source = motion_source(bordered_array[0], forward_motion, dual_heat_after)
    advected_result = advect_dual_heat(bordered_array[2:5], bordered_array[5:8], bordered_array[1])
    face_coef = coefficients(bordered_array[8], 1.0)
    diagonal = sum(face_coef)
    coarse_visc = restrict(local_viscosity)
    coarse_coef = coefficients(coarse_halo(coarse_visc[None])[0], 0.25)
    coarse_diag = sum(coarse_coef)
    deep_static = deep_halo(jnp.concatenate([local_viscosity[None], driving_source], 0))
    cycle_coef = coefficients(deep_static[0], 1.0)
    cycle_source = deep_static[1:4, 1:-1, 1:-1, 1:-1]
    inside = inside_mask(extent_first, extent_second, extent_vertical)
    safe_diag = jnp.where(inside, sum(cycle_coef), 1.0)
    total_cells = (
        extent_first
        * extent_second
        * extent_vertical
        * lax.axis_size("gx")
        * lax.axis_size("gy")
        * lax.axis_size("gz")
    )
    velocity = jnp.zeros(forward_motion.shape, jnp.float32)
    mean_stress = jnp.zeros(saved_heat_state.shape, jnp.float32)
    for iteration in range(SCHUR_ITERS):
        if iteration == 0:
            cycle_resid = cycle_source
        else:
            flow_press = deep_halo(jnp.concatenate([velocity, mean_stress[None]], 0))
            cycle_resid = (
                cycle_source - apply_operator(cycle_coef, flow_press[0:3]) - gradient(flow_press[3])
            )
        cycle_corr = jnp.where(inside, JACOBI_WEIGHT * cycle_resid / safe_diag, 0.0)
        residual = cycle_resid[:, 1:-1, 1:-1, 1:-1]
        correction = cycle_corr[:, 1:-1, 1:-1, 1:-1]
        residual_two = residual - apply_operator(face_coef, cycle_corr)
        coarse_res = restrict(residual_two)
        coarse_corr = coarse_solve(coarse_res, coarse_coef, coarse_diag, coarse_halo)
        correction = correction + prolong(coarse_corr)
        correction = (
            correction
            + JACOBI_WEIGHT
            * (residual - apply_operator(face_coef, finest_halo_cells(correction)))
            / diagonal
        )
        velocity = velocity + correction
        spread_flow = divergence(finest_halo_cells(velocity))
        mean_stress = mean_stress - SCHUR_WEIGHT * local_viscosity * spread_flow
        mean_stress = mean_stress - lax.psum(jnp.sum(mean_stress), ("gx", "gy", "gz")) / total_cells
    adj_temp_prev = advected_result + RAYLEIGH * velocity[2]
    return (adj_temp_prev, velocity, mean_stress)


SUB = 8
LANES = 128
FIELDS = 6
BACK = 5
EDGE = 2
PHASE = 8
HELD = 24
TX, TY = 4, 2
VMEM_LIMIT = 32 * 1024 * 1024
FORWARD, ADJOINT = range(2)


def slab_plan_fits(mesh, shape):
    sizes = mesh.shape
    group = sizes["gx"] * sizes["gy"]
    block = (shape[0] // sizes["gx"], shape[1] // sizes["gy"], shape[2] // sizes["gz"])
    return (
        group == SUB
        and block[0] == SUB
        and block[0] * block[1] == LANES
        and block[1] * group == LANES
        and block[2] == LANES
        and block[2] == group * 2 * PHASE
    )


class Slabs:
    def __init__(self, mesh, shape):
        self.nx, self.ny, self.nz = mesh.shape["gx"], mesh.shape["gy"], mesh.shape["gz"]
        self.group = self.nx * self.ny
        self.width, self.breadth, self.height = shape
        self.block = (shape[0] // self.nx, shape[1] // self.ny, shape[2] // self.nz)
        self.slab = self.block[2] // self.group
        self.margin = self.slab + SUB
        self.rows = self.slab + 2 * self.margin
        self.cells = self.width * self.breadth * self.height
        self.place = []
        for ix in range(self.nx):
            for iy in range(self.ny):
                step = ix if iy % 2 == 0 else self.nx - 1 - ix
                self.place.append(iy * self.nx + step)
        self.order = [
            (x + TX * part, y)
            for x in range(TX)
            for y in range(TY)
            for part in range(self.block[0] // TX)
        ]
        self.holder = [self.place.index(j) for j in range(self.group)]

    def device(self, slab):
        return self.holder[slab % self.group] * self.nz + slab // self.group

    def shifts(self, distance):
        count = self.group * self.nz
        return [
            (self.device(p), self.device(p + distance))
            for p in range(count)
            if 0 <= p + distance < count
        ]

    def index(self):
        ix, iy = lax.axis_index("gx"), lax.axis_index("gy")
        step = jnp.where(iy % 2 == 0, ix, self.nx - 1 - ix)
        return lax.axis_index("gz") * self.group + iy * self.nx + step

    def inside(self, z, n=SUB):
        layer = self.index() * self.slab - self.margin + z
        layer = layer + lax.broadcasted_iota(jnp.int32, (n, LANES), 0)
        return (layer >= 0) & (layer < self.height)


def exchange(tiles, bit, width):
    lane = lax.broadcasted_iota(jnp.int32, (SUB, LANES), 1)
    low = (lane & width) == 0
    new = list(tiles)
    for a in range(SUB):
        if not a & bit:
            b = a | bit
            new[a] = jnp.where(low, tiles[a], pltpu.roll(tiles[b], width, 1))
            new[b] = jnp.where(low, pltpu.roll(tiles[a], LANES - width, 1), tiles[b])
    return new


def gather_tiles(tiles, granule):
    for bit, width in ((1, granule // 2), (1, granule), (2, 2 * granule), (4, 4 * granule)):
        tiles = exchange(tiles, bit, width)
    return tiles


def scatter_tiles(tiles, granule):
    for bit, width in ((4, 4 * granule), (2, 2 * granule), (1, granule), (1, granule // 2)):
        tiles = exchange(tiles, bit, width)
    return tiles


class Tiles:
    def __init__(self, geo):
        self.span = geo.breadth // TY
        self.row = lax.broadcasted_iota(jnp.int32, (SUB, LANES), 0)
        self.lane = lax.broadcasted_iota(jnp.int32, (SUB, LANES), 1)
        self.y = self.lane % self.span
        self.kept = {}

    def sliding(self, ref, z, lead, t):
        where = (id(ref), id(z), lead)
        for key in [k for k in self.kept if k[:3] == where and abs(k[3] - t) > 3]:
            del self.kept[key]

        def load(j):
            key = (*where, j)
            if key not in self.kept:
                self.kept[key] = (ref, z, get(ref, z, *lead, j))
            return self.kept[key][2]

        return load

    def x(self, load, t, step, count=TX, stride=TY):
        j = t // stride + step
        if 0 <= j < count:
            return load(t + step * stride)
        if step > 0:
            turned = pltpu.roll(load(t % stride), LANES - self.span, 1)
            return jnp.where(self.lane < LANES - self.span, turned, 0.0)
        turned = pltpu.roll(load((count - 1) * stride + t % stride), self.span, 1)
        return jnp.where(self.lane >= self.span, turned, 0.0)

    def lanes(self, f, step):
        if step > 0:
            return jnp.where(self.y < self.span - 1, pltpu.roll(f, LANES - 1, 1), 0.0)
        return jnp.where(self.y > 0, pltpu.roll(f, 1, 1), 0.0)

    def y_side(self, load, t, step):
        if (t % TY == 0) == (step > 0):
            return load(t + step)
        return self.lanes(load(t - step), step)

    def beside(self, ref, z, lead, t):
        load = self.sliding(ref, z, lead, t)
        near = [self.x(load, t, 1), self.x(load, t, -1)]
        near += [self.y_side(load, t, 1), self.y_side(load, t, -1)]
        return load(t), near + [get(ref, z + 1, *lead, t), get(ref, z - 1, *lead, t)]

    def coarse_beside(self, ref, z, lead, t):
        load = lambda j: get(ref, z, *lead, j)
        f = load(t)
        near = [self.x(load, t, step, TX // 2, 1) for step in (1, -1)]
        near += [self.lanes(f, 1), self.lanes(f, -1)]
        return f, near + [get(ref, z + 2, *lead, t), get(ref, z - 2, *lead, t)]

    def pair_sum(self, f):
        return f + jnp.where(self.row % 2 == 0, pltpu.roll(f, SUB - 1, 0), pltpu.roll(f, 1, 0))


def block_of(t):
    return range(2 * TY * t, 2 * TY * (t + 1))


def tree(terms):
    while len(terms) > 1:
        terms = [sum(terms[k : k + 2]) for k in range(0, len(terms), 2)]
    return terms[0]


def get(ref, z, *index):
    return ref[(*index, pl.ds(z, SUB), slice(None))]


def sweep(lo, hi, body):
    assert (hi - lo) % SUB == 0

    def step(t, _):
        late = []

        def store(ref, value, z, *index):
            ref[(*index, pl.ds(z, SUB), slice(None))] = value

        def put(*item):
            late.append(item)
            if len(late) > HELD:
                store(*late.pop(0))

        body(pl.multiple_of(t * SUB, SUB) + lo, put)
        for item in late:
            store(*item)
        return 0

    lax.fori_loop(0, (hi - lo) // SUB, step, 0)


def pack_kernel(geo, heat_in, flow_in, dual_in, kind_in, out, heat, flow, dual, kind, sems):
    b, e = geo.slab, EDGE
    pairs = ((heat_in, heat), (flow_in, flow), (dual_in, dual), (kind_in, kind))
    copies = [
        pltpu.make_async_copy(source, target, sems.at[k])
        for k, (source, target) in enumerate(pairs)
    ]
    for copy in copies:
        copy.start()
    for copy in copies:
        copy.wait()
    fields = [heat, flow.at[0], flow.at[1], flow.at[2], dual, kind]
    turned = []
    for ref in fields:
        rows = [ref[x, pl.ds(y, SUB, stride=TY), :] for x, y in geo.order]
        turned.append(jnp.concatenate(rows, 0).astype(jnp.float32).T)
    for j in range(geo.group):
        q = geo.holder[j]
        for f in range(FIELDS):
            out[q, f * b : (f + 1) * b, :] = turned[f][j * b : (j + 1) * b]
        tail = FIELDS * b
        first = jnp.concatenate([turned[f][j * b : j * b + e] for f in range(4)], 0)
        last = jnp.concatenate([turned[f][(j + 1) * b - e : (j + 1) * b] for f in range(4)], 0)
        out[q, tail : tail + SUB, :] = first
        out[q, tail + SUB : tail + 2 * SUB, :] = last


STATIC_FINE = ("s0", "s1", "s2", "hv", "w")
STATIC_COARSE = ("kxp", "kxm", "kyp", "kym", "kzp", "kzm", "wc")
STATIC = STATIC_FINE + STATIC_COARSE


def iterate(geo, st, work, seqs, lo, hi, first=(), mean=None):
    v, p, res, cor, cor2, cc0, cc1 = work
    tl = Tiles(geo)
    keep = 1.0 - JACOBI_WEIGHT
    comps = range(3 * len(seqs))
    transposed = len(seqs)

    def faces(t, z):
        h, near = tl.beside(st["hv"], z, (), t)
        return [h + other for other in near]

    def around(face, ref, c, t, z):
        f, near = tl.beside(ref, z, (c,), t)
        return f, tree([a * b for a, b in zip(face, near)])

    def residual(z, put):
        for t in range(SUB):
            w = get(st["w"], z, t)
            if FORWARD in seqs and FORWARD not in first:
                face = faces(t, z)
                diag = tree(face)
            for s, q in enumerate(seqs):
                start = q == FORWARD and q in first
                if not start:
                    _, near = tl.beside(p, z, (transposed if q == ADJOINT else s,), t)
                    slope = [0.5 * (near[2 * k] - near[2 * k + 1]) for k in range(3)]
                for k in range(3):
                    c = 3 * s + k
                    if q == FORWARD:
                        value = get(st["s%d" % k], z, t)
                        if not start:
                            f, total = around(face, v, c, t, z)
                            value = value - slope[k] - (diag * f - total)
                    else:
                        value = slope[k] if q in first else get(cor, z, c, t) + slope[k]
                    put(res, value, z, c, t)
                    put(cor, w * value, z, c, t)

    sweep(lo - 8, hi + 8, residual)

    def restricted(z, put):
        for pair in range(TX // 2):
            left = [0.0 for _ in comps]
            for t in block_of(pair):
                face = faces(t, z)
                for c in comps:
                    _, total = around(face, cor, c, t, z)
                    left[c] = left[c] + (keep * get(res, z, c, t) + total)
            wc = 0.125 * get(st["wc"], z, pair)
            for c in comps:
                put(cc0, wc * tl.pair_sum(left[c]), z, c, pair)

    sweep(lo - 8, hi + 8, restricted)

    def coarse_step(ref, c, pair, z):
        f, near = tl.coarse_beside(ref, z, (c,), pair)
        terms = [get(st[name], z, pair) * b for name, b in zip(STATIC_COARSE, near)]
        return tree([get(cc0, z, c, pair), keep * f] + terms)

    def sweep_one(z, put):
        for pair in range(TX // 2):
            for c in comps:
                put(cc1, coarse_step(cc0, c, pair, z), z, c, pair)

    sweep(lo - 4, hi + 4, sweep_one)

    def sweep_two(z, put):
        for pair in range(TX // 2):
            for c in comps:
                value = coarse_step(cc1, c, pair, z)
                for t in block_of(pair):
                    put(cor2, get(cor, z, c, t) + value, z, c, t)

    sweep(lo - 4, hi + 4, sweep_two)

    def velocity(z, put):
        for t in range(SUB):
            face, w = faces(t, z), get(st["w"], z, t)
            for c in comps:
                f, total = around(face, cor2, c, t, z)
                value = get(cor, z, c, t) + keep * f + w * total
                if seqs[c // 3] == FORWARD and FORWARD not in first:
                    value = get(v, z, c, t) + value
                put(v, value, z, c, t)

    sweep(lo - 4, hi + 4, velocity)

    def pressure(z, put):
        for t in range(SUB):
            half = get(st["hv"], z, t)
            for s, q in enumerate(seqs):
                c = 3 * s
                if q == ADJOINT:
                    face = faces(t, z)
                    diag, div = tree(face), 0.0
                    for k in range(3):
                        f, near = tl.beside(v, z, (c + k,), t)
                        div = div + 0.5 * (near[2 * k] - near[2 * k + 1])
                        total = tree([a * b for a, b in zip(face, near)])
                        put(cor, get(res, z, c + k, t) - (diag * f - total), z, c + k, t)
                    value = get(p, z, s, t) + div
                    put(p, value, z, s, t)
                    put(p, half * value, z, transposed, t)
                    continue
                one, two = tl.sliding(v, z, (c,), t), tl.sliding(v, z, (c + 1,), t)
                div = tl.x(one, t, 1) - tl.x(one, t, -1)
                div = div + (tl.y_side(two, t, 1) - tl.y_side(two, t, -1))
                div = div + (get(v, z + 1, c + 2, t) - get(v, z - 1, c + 2, t))
                value = -(half * (0.5 * div))
                if not (q == FORWARD and q in first):
                    value = get(p, z, s, t) + value
                if mean is not None:
                    value = value - jnp.where(geo.inside(z), mean, 0.0)
                put(p, value, z, s, t)

    sweep(lo, hi, pressure)


def whole_sum(value):
    return jnp.sum(jnp.sum(value, axis=0), axis=(0, 1), keepdims=True)


def product(left, right):
    value = 0.0
    for a, b in zip(left, right):
        value = value + a[...] * b[...]
    return whole_sum(value)


def in_lanes(values, rows):
    lane = lax.broadcasted_iota(jnp.int32, (rows, LANES), 1)
    out = jnp.zeros((rows, LANES), jnp.float32)
    for k, value in values:
        out = jnp.where(lane == k, value, out)
    return out


def setup_kernel(geo, stiffness, own, low, high, low_edge, high_edge, *refs):
    st = dict(zip(STATIC, refs))
    moved, duals, sums, raw, heat, vc, *work = refs[len(STATIC) :]
    v, p, res, cor, cor2, cc0, cc1 = work
    tl = Tiles(geo)
    b, m, n_rows = geo.slab, geo.margin, geo.rows
    granule = geo.block[1]

    def place(t, _):
        groups = []
        for source, base in ((low, m - b), (own, m), (high, m + b)):
            for u in range(0, b, SUB):
                row = pl.multiple_of(t * b, b) + u
                tiles = [source[q, pl.ds(row, SUB), :] for q in range(geo.group)]
                groups.append((base + u, tiles))
        groups = [(row, gather_tiles(tiles, granule)) for row, tiles in groups]
        for row, tiles in groups:
            for x, tile in enumerate(tiles):
                raw[t, x, row : row + SUB, :] = tile
        return 0

    lax.fori_loop(0, FIELDS, place, 0)
    for source, base in ((low_edge, m - b - EDGE), (high_edge, m + 2 * b)):
        tiles = [source[q] for q in range(geo.group)]
        for x, tile in enumerate(gather_tiles(tiles, granule)):
            for f in range(4):
                raw[f, x, base : base + EDGE, :] = tile[f * EDGE : (f + 1) * EDGE]

    def advance(ref, old, new):
        def body(z, put):
            inside = geo.inside(z)
            for t in range(SUB):
                f, near = tl.beside(ref, z, (old,), t)
                drift = 0.0
                for k in range(3):
                    flow = get(raw, z, 1 + k, t)
                    drift = drift + jnp.maximum(flow, 0.0) * (f - near[2 * k + 1])
                    drift = drift + jnp.minimum(flow, 0.0) * (near[2 * k] - f)
                spread = tree(near) - 6.0 * f
                value = f - INCREMENT_DT * drift + INCREMENT_DT * DIFFUSIVITY * spread
                put(heat, jnp.where(inside, value, 0.0), z, new, t)

        return body

    sweep(m - b - 4, m + 2 * b + 4, advance(raw, 0, 0))
    sweep(m - b, m + 2 * b, advance(heat, 0, 1))

    def viscosity(z, put):
        inside = geo.inside(z)
        for pair in range(TX // 2):
            coarse = 0.0
            for t in block_of(pair):
                kind = get(raw, z, 5, t)
                base = jnp.zeros(kind.shape, jnp.float32)
                for layer in range(LAYERS):
                    base = jnp.where(kind == float(layer), stiffness[layer], base)
                value = base * jnp.exp(-ACTIVATION_ENERGY * get(heat, z, 1, t))
                value = jnp.where(inside, value, 0.0)
                put(st["hv"], 0.5 * value, z, t)
                coarse = coarse + value
            put(vc, 0.125 * tl.pair_sum(coarse), z, pair)

    sweep(m - b, m + 2 * b, viscosity)

    def statics(z, put):
        inside = geo.inside(z)
        for t in range(SUB):
            h, near = tl.beside(st["hv"], z, (), t)
            diag = tree([h + other for other in near])
            put(st["w"], jnp.where(inside, JACOBI_WEIGHT / diag, 0.0), z, t)
            f, near = tl.beside(heat, z, (1,), t)
            dual = -INCREMENT_DT * get(raw, z, 4, t)
            for k in range(3):
                flow = get(raw, z, 1 + k, t)
                step = jnp.where(flow > 0, f - near[2 * k + 1], near[2 * k] - f)
                put(st["s%d" % k], dual * step, z, t)

    sweep(m - b, m + 2 * b, statics)

    def coarse_statics(z, put):
        inside = geo.inside(z)
        for pair in range(TX // 2):
            c, near = tl.coarse_beside(vc, z, (), pair)
            face = [0.25 * (0.5 * (c + o)) for o in near]
            wc = jnp.where(inside, JACOBI_WEIGHT / tree(face), 0.0)
            for name, f in zip(STATIC_COARSE, face):
                put(st[name], wc * f, z, pair)
            put(st["wc"], wc, z, pair)

    sweep(m - b, m + 2 * b, coarse_statics)

    def transport(z, put):
        for t in range(SUB):
            dual, near = tl.beside(raw, z, (4,), t)
            value = dual + INCREMENT_DT * DIFFUSIVITY * (tree(near) - 6.0 * dual)
            for k in range(3):
                flow, sides = tl.beside(raw, z, (1 + k,), t)
                a = jnp.maximum(flow, 0.0) * dual
                c = jnp.minimum(flow, 0.0) * dual
                ahead = jnp.maximum(sides[2 * k], 0.0) * near[2 * k]
                behind = jnp.minimum(sides[2 * k + 1], 0.0) * near[2 * k + 1]
                value = value - INCREMENT_DT * (a - ahead + behind - c)
            put(moved, value, z - m, t)

    sweep(m, m + b, transport)

    def unit(z, put):
        value = jnp.where(geo.inside(z), 1.0, 0.0)
        for t in range(SUB):
            put(p, value, z, 0, t)
            put(p, get(st["hv"], z, t), z, 1, t)

    sweep(0, n_rows, unit)

    mine = slice(m, m + b)
    source = [st["s%d" % k].at[:, mine, :] for k in range(3)]
    step = [v.at[k, :, mine, :] for k in range(3)]
    iterate(geo, st, work, (ADJOINT,), m - PHASE, m + b + PHASE, (ADJOINT,))
    sums_of = [(0, product(step, source)), (1, whole_sum(p[0, :, mine, :]))]
    for k in range(4):
        duals[k] = cor[k, :, mine, :] if k < 3 else p[0, :, mine, :]
    iterate(geo, st, work, (ADJOINT,), m, m + b)
    sums_of += [(2, product(step, source))]
    for k in range(4):
        duals[4 + k] = cor[k, :, mine, :] if k < 3 else p[0, :, mine, :]
    sums[...] = in_lanes(sums_of, sums.shape[0])


def first_kernel(geo, *refs):
    st = dict(zip(STATIC, refs))
    out, *work = refs[len(STATIC) :]
    v, p = work[:2]
    rows = slice(geo.margin - PHASE, geo.margin + geo.slab + PHASE)
    iterate(geo, st, work, (FORWARD,), rows.start, rows.stop, (FORWARD,))
    for k in range(4):
        out[k] = v[k, :, rows, :] if k < 3 else p[0, :, rows, :]


def refill(geo, v, p, state, rows, shift):
    for k in range(3):
        v[k, :, rows, :] = state[k]
    if shift is None:
        p[0, :, rows, :] = state[3]
    else:
        inside = geo.inside(rows.start, rows.stop - rows.start)
        p[0, :, rows, :] = state[3] - jnp.where(inside, shift, 0.0)[None]


def second_kernel(geo, *refs):
    st = dict(zip(STATIC, refs))
    earlier, early, duals, state, sums, *work = refs[len(STATIC) :]
    v, p = work[:2]
    b, m = geo.slab, geo.margin
    m1, m2 = means(geo, early[...], None)[:2]
    refill(geo, v, p, earlier, slice(m - PHASE, m + b + PHASE), m1)
    iterate(geo, st, work, (FORWARD,), m, m + b, mean=m2)
    mine = slice(m, m + b)
    for k in range(4):
        state[k] = v[k, :, mine, :] if k < 3 else p[0, :, mine, :]
    fields = [state.at[k] for k in range(4)]
    near, far = [duals.at[k] for k in range(4)], [duals.at[4 + k] for k in range(4)]
    sums_of = [(3, product(near, fields)), (4, product(far, fields))]
    sums[...] = in_lanes(sums_of, sums.shape[0])


def means(geo, early, late):
    sums = early if late is None else early + late
    row = jnp.sum(sums, axis=0, keepdims=True) / geo.cells
    lane = lax.broadcasted_iota(jnp.int32, row.shape, 1)

    def at(k):
        return jnp.sum(jnp.where(lane == k, row, 0.0), axis=1, keepdims=True)

    c1, l1, c2, l1_x2, l2_x2 = [at(k) for k in range(5)]
    m1 = c1
    m2 = c1 + c2 - m1 * l1
    m3 = c1 + l1_x2
    m4 = c1 + c2 + l2_x2 - m3 * l1
    return m1, m2, m3, m4


def third_kernel(geo, *refs):
    st = dict(zip(STATIC, refs))
    own, low, high, out, *work = refs[len(STATIC) :]
    v, p = work[:2]
    b, m = geo.slab, geo.margin
    for source, base in ((low, m - b), (own, m), (high, m + b)):
        refill(geo, v, p, source, slice(base, base + b), None)
    rows = slice(m - PHASE, m + b + PHASE)
    iterate(geo, st, work, (FORWARD,), rows.start, rows.stop)
    for k in range(4):
        out[k] = v[k, :, rows, :] if k < 3 else p[0, :, rows, :]


def fourth_kernel(geo, *refs):
    st = dict(zip(STATIC, refs))
    state, early, late, moved, out, *work = refs[len(STATIC) :]
    v, p = work[:2]
    b, m = geo.slab, geo.margin
    m3, m4 = means(geo, early[...], late[...])[2:]
    refill(geo, v, p, state, slice(m - PHASE, m + b + PHASE), m3)
    iterate(geo, st, work, (FORWARD,), m, m + b, mean=m4)
    for u in range(0, b, SUB):
        at = slice(m + u, m + u + SUB)
        columns = range(SUB)
        fields = [[v[k, x, at, :] for x in columns] for k in range(3)]
        fields.append([p[0, x, at, :] for x in columns])
        fields.append([moved[x, u : u + SUB, :] + fields[2][x] for x in columns])
        for f, tiles in enumerate(fields):
            for q, tile in enumerate(scatter_tiles(tiles, geo.block[1])):
                out[q, f * b + u : f * b + u + SUB, :] = tile


def unpack_kernel(geo, chunks, heat, flow, pressure):
    b = geo.slab
    for f, ref in enumerate((flow.at[0], flow.at[1], flow.at[2], pressure, heat)):
        rows = [chunks[geo.holder[j], f * b : (f + 1) * b, :] for j in range(geo.group)]
        block = jnp.concatenate(rows, 0).T
        for k, (x, y) in enumerate(geo.order):
            ref[x, pl.ds(y, SUB, stride=TY), :] = block[k * SUB : (k + 1) * SUB]


def call(kernel, out, scratch, *args, smem=(), hbm=(), megabytes=2):
    f32 = jnp.float32
    cost = pl.CostEstimate(
        flops=megabytes * 1000000, bytes_accessed=megabytes * 1000000, transcendentals=0
    )
    specs = [
        pl.BlockSpec(
            memory_space=pltpu.SMEM if i in smem else pltpu.HBM if i in hbm else pltpu.VMEM
        )
        for i in range(len(args))
    ]
    return pl.pallas_call(
        kernel,
        out_shape=[jax.ShapeDtypeStruct(s, f32) for s in out],
        in_specs=specs,
        out_specs=[pl.BlockSpec(memory_space=pltpu.VMEM) for _ in out],
        scratch_shapes=[pltpu.VMEM(s, f32) if isinstance(s, tuple) else s for s in scratch],
        compiler_params=pltpu.CompilerParams(vmem_limit_bytes=VMEM_LIMIT),
        cost_estimate=cost,
    )(*args)


def slab_shards(geo, heat, flow, dual, kind, stiffness):
    b, group = geo.slab, geo.group
    rows = FIELDS * b
    inputs = (heat, flow, dual, kind)
    (chunks,) = call(
        functools.partial(pack_kernel, geo),
        [(group, rows + 2 * SUB, LANES)],
        [pltpu.VMEM(a.shape, a.dtype) for a in inputs] + [pltpu.SemaphoreType.DMA((4,))],
        *inputs,
        hbm=range(4),
    )
    own = lax.all_to_all(chunks, ("gx", "gy"), 0, 0, tiled=True)
    axes = ("gx", "gy", "gz")
    low = lax.ppermute(own, axes, geo.shifts(1))
    high = lax.ppermute(own, axes, geo.shifts(-1))
    high_edge = lax.ppermute(own[:, rows : rows + SUB], axes, geo.shifts(-2))
    low_edge = lax.ppermute(own[:, rows + SUB :], axes, geo.shifts(2))

    fine, coarse = (SUB, geo.rows, LANES), (TX // 2, geo.rows, LANES)
    slab = (SUB, b, LANES)

    def work(n, more=0):
        fields = [(3 * n, *fine), (n + more, *fine)] + [(3 * n, *fine)] * 3
        return fields + [(3 * n, *coarse)] * 2

    devices = group * geo.nz
    wide = (4, SUB, b + 2 * PHASE, LANES)
    *static, moved, duals, early = call(
        functools.partial(setup_kernel, geo),
        [fine] * len(STATIC_FINE)
        + [coarse] * len(STATIC_COARSE)
        + [slab, (8, *slab), (devices, LANES)],
        [(FIELDS, *fine), (2, *fine), coarse] + work(1, 1),
        stiffness,
        own,
        low,
        high,
        low_edge,
        high_edge,
        smem=(0,),
        megabytes=60,
    )
    early = lax.all_to_all(early, axes, 0, 0, tiled=True)
    (state,) = call(
        functools.partial(first_kernel, geo), [wide], work(1), *static, megabytes=20
    )
    state, late = call(
        functools.partial(second_kernel, geo),
        [(4, *slab), (devices, LANES)],
        work(1),
        *static,
        state,
        early,
        duals,
        megabytes=20,
    )
    low_state = lax.ppermute(state, axes, geo.shifts(1))
    high_state = lax.ppermute(state, axes, geo.shifts(-1))
    late = lax.all_to_all(late, axes, 0, 0, tiled=True)
    (state,) = call(
        functools.partial(third_kernel, geo),
        [wide],
        work(1),
        *static,
        state,
        low_state,
        high_state,
        megabytes=30,
    )
    (chunks,) = call(
        functools.partial(fourth_kernel, geo),
        [(group, BACK * b, LANES)],
        work(1),
        *static,
        state,
        early,
        late,
        moved,
        megabytes=20,
    )
    chunks = lax.all_to_all(chunks, ("gx", "gy"), 0, 0, tiled=True)
    return tuple(
        call(
            functools.partial(unpack_kernel, geo),
            [geo.block, (3, *geo.block), geo.block],
            [],
            chunks,
        )
    )


def solution(mesh):
    in_specs = (
        P("gx", "gy", "gz"),
        P(None, "gx", "gy", "gz"),
        P("gx", "gy", "gz"),
        P("gx", "gy", "gz"),
        P(),
    )
    out_specs = (P("gx", "gy", "gz"), P(None, "gx", "gy", "gz"), P("gx", "gy", "gz"))

    def program(saved_heat_state, *others):
        shape = saved_heat_state.shape
        plan = shards
        if slab_plan_fits(mesh, shape):
            plan = functools.partial(slab_shards, Slabs(mesh, shape))
        return jax.shard_map(
            plan, mesh=mesh, in_specs=in_specs, out_specs=out_specs, check_vma=False
        )(saved_heat_state, *others)

    return program
```

```python
import functools

import jax
import jax.numpy as jnp
from jax import lax
from jax.experimental import pallas as pl
from jax.experimental.pallas import tpu as pltpu
from jax.sharding import PartitionSpec as P

RECOMPUTE = 2
SCHUR_ITERS = 4
COARSE_SWEEPS = 3
LAYERS = 8


INCREMENT_DT = 0.2
DIFFUSIVITY = 0.3
ACTIVATION_ENERGY = 2.3
JACOBI_WEIGHT = 0.7
SCHUR_WEIGHT = 0.5
RAYLEIGH = 1.0


def extended(block, sides, width):
    for axis, dim in sides:
        count = lax.axis_size(axis)
        forward = [(i, i + 1) for i in range(count - 1)]
        backward = [(target, source) for source, target in forward]
        low = lax.ppermute(
            lax.slice_in_dim(block, block.shape[dim] - width, None, axis=dim), axis, forward
        )
        high = lax.ppermute(lax.slice_in_dim(block, 0, width, axis=dim), axis, backward)
        block = jnp.concatenate([low, block, high], axis=dim)
    return block


def neighbours(bordered_array):
    centre = bordered_array[..., 1:-1, 1:-1, 1:-1]
    beside_all = [
        bordered_array[..., 2:, 1:-1, 1:-1],
        bordered_array[..., :-2, 1:-1, 1:-1],
        bordered_array[..., 1:-1, 2:, 1:-1],
        bordered_array[..., 1:-1, :-2, 1:-1],
        bordered_array[..., 1:-1, 1:-1, 2:],
        bordered_array[..., 1:-1, 1:-1, :-2],
    ]
    return (centre, beside_all)


def finest_halo_cells(field):
    return extended(field, (("gx", 1), ("gy", 2), ("gz", 3)), 1)


def deep_halo(field):
    return extended(field, (("gx", 1), ("gy", 2), ("gz", 3)), 2)


def coarse_halo(field):
    return extended(field, (("gx", 1), ("gy", 2), ("gz", 3)), 1)


def march_backward(bordered_array, shallower_adjacent, deeper_adjacent):
    centre, beside_all = neighbours(bordered_array)
    drift = 0.0
    for dim_index in range(3):
        drift = (
            drift
            + shallower_adjacent[dim_index] * (centre - beside_all[2 * dim_index + 1])
            + deeper_adjacent[dim_index] * (beside_all[2 * dim_index] - centre)
        )
    spread = sum(beside_all) - 6.0 * centre
    return centre - INCREMENT_DT * drift + INCREMENT_DT * DIFFUSIVITY * spread


def motion_source(bordered_heat, forward_motion, dual_heat_after):
    centre, beside_all = neighbours(bordered_heat)
    device_pieces = [
        jnp.where(
            forward_motion[dim_index] > 0,
            centre - beside_all[2 * dim_index + 1],
            beside_all[2 * dim_index] - centre,
        )
        for dim_index in range(3)
    ]
    return -INCREMENT_DT * dual_heat_after[None] * jnp.stack(device_pieces)


def advect_dual_heat(pos_padded, neg_padded, lam_padded):
    centre, beside_all = neighbours(lam_padded)
    result = centre + INCREMENT_DT * DIFFUSIVITY * (sum(beside_all) - 6.0 * centre)
    for dim_index in range(3):
        pos_centre, pos_around = neighbours(pos_padded[dim_index])
        neg_centre, neg_around = neighbours(neg_padded[dim_index])
        result = result - INCREMENT_DT * (
            pos_centre - pos_around[2 * dim_index] + neg_around[2 * dim_index + 1] - neg_centre
        )
    return result


def coefficients(bordered_array, factor):
    centre, beside_all = neighbours(bordered_array)
    return [factor * (0.5 * (centre + other)) for other in beside_all]


def apply_operator(face_coef, bordered_array):
    centre, beside_all = neighbours(bordered_array)
    return sum((coef * (centre - other) for coef, other in zip(face_coef, beside_all)))


def gradient(bordered_array):
    centre, beside_all = neighbours(bordered_array)
    return jnp.stack(
        [
            0.5 * (beside_all[2 * dim_index] - beside_all[2 * dim_index + 1])
            for dim_index in range(3)
        ]
    )


def divergence(bordered_array):
    centre, beside_all = neighbours(bordered_array)
    return sum(
        (
            0.5 * (beside_all[2 * dim_index][dim_index] - beside_all[2 * dim_index + 1][dim_index])
            for dim_index in range(3)
        )
    )


def restrict(field):
    leading = field.shape[:-3]
    cells_x, cells_y, cells_z = field.shape[-3:]
    blocks = field.reshape(leading + (cells_x // 2, 2, cells_y // 2, 2, cells_z // 2, 2))
    return blocks.mean(axis=(-5, -3, -1))


def prolong(field):
    return jnp.repeat(jnp.repeat(jnp.repeat(field, 2, axis=-3), 2, axis=-2), 2, axis=-1)


def evaluate_viscosity(rheology_class, class_base_stiffness):
    base = jnp.zeros(rheology_class.shape, jnp.float32)
    for layer_index in range(LAYERS):
        base = base + jnp.where(
            rheology_class == layer_index, class_base_stiffness[layer_index], 0.0
        )
    return base


def inside_mask(extent_first, extent_second, extent_vertical):
    index_x = (
        lax.axis_index("gx") * extent_first + jnp.arange(extent_first + 2, dtype=jnp.int32) - 1
    )
    index_y = (
        lax.axis_index("gy") * extent_second + jnp.arange(extent_second + 2, dtype=jnp.int32) - 1
    )
    index_z = (
        lax.axis_index("gz") * extent_vertical
        + jnp.arange(extent_vertical + 2, dtype=jnp.int32)
        - 1
    )
    inside_x = (index_x >= 0) & (index_x < extent_first * lax.axis_size("gx"))
    inside_y = (index_y >= 0) & (index_y < extent_second * lax.axis_size("gy"))
    inside_z = (index_z >= 0) & (index_z < extent_vertical * lax.axis_size("gz"))
    return inside_x[:, None, None] & inside_y[None, :, None] & inside_z[None, None, :]


def coarse_solve(coarse_res, coarse_coef, coarse_diag, pad_field):
    coarse_corr = JACOBI_WEIGHT * coarse_res / coarse_diag
    for sweep in range(COARSE_SWEEPS - 1):
        coarse_corr = (
            coarse_corr
            + JACOBI_WEIGHT
            * (coarse_res - apply_operator(coarse_coef, pad_field(coarse_corr)))
            / coarse_diag
        )
    return coarse_corr


def shards(saved_heat_state, forward_motion, dual_heat_after, rheology_class, class_base_stiffness):
    extent_first, extent_second, extent_vertical = saved_heat_state.shape
    shallower_adjacent = jnp.maximum(forward_motion, 0.0)
    deeper_adjacent = jnp.minimum(forward_motion, 0.0)
    heat_state = saved_heat_state
    for repeat_index in range(RECOMPUTE):
        heat_state = march_backward(
            finest_halo_cells(heat_state[None])[0], shallower_adjacent, deeper_adjacent
        )
    local_viscosity = evaluate_viscosity(rheology_class, class_base_stiffness) * jnp.exp(
        -ACTIVATION_ENERGY * heat_state
    )
    stacked = jnp.concatenate(
        [
            heat_state[None],
            dual_heat_after[None],
            shallower_adjacent * dual_heat_after[None],
            deeper_adjacent * dual_heat_after[None],
            local_viscosity[None],
        ],
        0,
    )
    bordered_array = finest_halo_cells(stacked)
    driving_source = motion_source(bordered_array[0], forward_motion, dual_heat_after)
    advected_result = advect_dual_heat(bordered_array[2:5], bordered_array[5:8], bordered_array[1])
    face_coef = coefficients(bordered_array[8], 1.0)
    diagonal = sum(face_coef)
    coarse_visc = restrict(local_viscosity)
    coarse_coef = coefficients(coarse_halo(coarse_visc[None])[0], 0.25)
    coarse_diag = sum(coarse_coef)
    deep_static = deep_halo(jnp.concatenate([local_viscosity[None], driving_source], 0))
    cycle_coef = coefficients(deep_static[0], 1.0)
    cycle_source = deep_static[1:4, 1:-1, 1:-1, 1:-1]
    inside = inside_mask(extent_first, extent_second, extent_vertical)
    safe_diag = jnp.where(inside, sum(cycle_coef), 1.0)
    total_cells = (
        extent_first
        * extent_second
        * extent_vertical
        * lax.axis_size("gx")
        * lax.axis_size("gy")
        * lax.axis_size("gz")
    )
    velocity = jnp.zeros(forward_motion.shape, jnp.float32)
    mean_stress = jnp.zeros(saved_heat_state.shape, jnp.float32)
    for iteration in range(SCHUR_ITERS):
        if iteration == 0:
            cycle_resid = cycle_source
        else:
            flow_press = deep_halo(jnp.concatenate([velocity, mean_stress[None]], 0))
            cycle_resid = (
                cycle_source - apply_operator(cycle_coef, flow_press[0:3]) - gradient(flow_press[3])
            )
        cycle_corr = jnp.where(inside, JACOBI_WEIGHT * cycle_resid / safe_diag, 0.0)
        residual = cycle_resid[:, 1:-1, 1:-1, 1:-1]
        correction = cycle_corr[:, 1:-1, 1:-1, 1:-1]
        residual_two = residual - apply_operator(face_coef, cycle_corr)
        coarse_res = restrict(residual_two)
        coarse_corr = coarse_solve(coarse_res, coarse_coef, coarse_diag, coarse_halo)
        correction = correction + prolong(coarse_corr)
        correction = (
            correction
            + JACOBI_WEIGHT
            * (residual - apply_operator(face_coef, finest_halo_cells(correction)))
            / diagonal
        )
        velocity = velocity + correction
        spread_flow = divergence(finest_halo_cells(velocity))
        mean_stress = mean_stress - SCHUR_WEIGHT * local_viscosity * spread_flow
        mean_stress = mean_stress - lax.psum(jnp.sum(mean_stress), ("gx", "gy", "gz")) / total_cells
    adj_temp_prev = advected_result + RAYLEIGH * velocity[2]
    return (adj_temp_prev, velocity, mean_stress)


SUB = 8
LANES = 128
FIELDS = 6
BACK = 5
EDGE = 2
PHASE = 8
HELD = 24
TX, TY = 4, 2
VMEM_LIMIT = 32 * 1024 * 1024
PACK_LIMIT = 60 * 1024 * 1024
FORWARD, ADJOINT = range(2)


def slab_plan_fits(mesh, shape):
    sizes = mesh.shape
    group = sizes["gx"] * sizes["gy"]
    block = (shape[0] // sizes["gx"], shape[1] // sizes["gy"], shape[2] // sizes["gz"])
    return (
        group == SUB
        and block[0] == SUB
        and block[0] * block[1] == LANES
        and block[1] * group == LANES
        and block[2] == LANES
        and block[2] == group * 2 * PHASE
    )


class Slabs:
    def __init__(self, mesh, shape):
        self.nx, self.ny, self.nz = mesh.shape["gx"], mesh.shape["gy"], mesh.shape["gz"]
        self.group = self.nx * self.ny
        self.width, self.breadth, self.height = shape
        self.block = (shape[0] // self.nx, shape[1] // self.ny, shape[2] // self.nz)
        self.slab = self.block[2] // self.group
        self.margin = self.slab + SUB
        self.rows = self.slab + 2 * self.margin
        self.cells = self.width * self.breadth * self.height
        self.place = []
        for ix in range(self.nx):
            for iy in range(self.ny):
                step = ix if iy % 2 == 0 else self.nx - 1 - ix
                self.place.append(iy * self.nx + step)
        self.order = [
            (x + TX * part, y)
            for x in range(TX)
            for y in range(TY)
            for part in range(self.block[0] // TX)
        ]
        self.holder = [self.place.index(j) for j in range(self.group)]

    def device(self, slab):
        return self.holder[slab % self.group] * self.nz + slab // self.group

    def shifts(self, distance):
        count = self.group * self.nz
        return [
            (self.device(p), self.device(p + distance))
            for p in range(count)
            if 0 <= p + distance < count
        ]

    def index(self):
        ix, iy = lax.axis_index("gx"), lax.axis_index("gy")
        step = jnp.where(iy % 2 == 0, ix, self.nx - 1 - ix)
        return lax.axis_index("gz") * self.group + iy * self.nx + step

    def inside(self, z, n=SUB):
        layer = self.index() * self.slab - self.margin + z
        layer = layer + lax.broadcasted_iota(jnp.int32, (n, LANES), 0)
        return (layer >= 0) & (layer < self.height)


def exchange(tiles, bit, width):
    lane = lax.broadcasted_iota(jnp.int32, (SUB, LANES), 1)
    low = (lane & width) == 0
    new = list(tiles)
    for a in range(SUB):
        if not a & bit:
            b = a | bit
            new[a] = jnp.where(low, tiles[a], pltpu.roll(tiles[b], width, 1))
            new[b] = jnp.where(low, pltpu.roll(tiles[a], LANES - width, 1), tiles[b])
    return new


def gather_tiles(tiles, granule):
    for bit, width in ((1, granule // 2), (1, granule), (2, 2 * granule), (4, 4 * granule)):
        tiles = exchange(tiles, bit, width)
    return tiles


def scatter_tiles(tiles, granule):
    for bit, width in ((4, 4 * granule), (2, 2 * granule), (1, granule), (1, granule // 2)):
        tiles = exchange(tiles, bit, width)
    return tiles


class Tiles:
    def __init__(self, geo):
        self.span = geo.breadth // TY
        self.row = lax.broadcasted_iota(jnp.int32, (SUB, LANES), 0)
        self.lane = lax.broadcasted_iota(jnp.int32, (SUB, LANES), 1)
        self.y = self.lane % self.span
        self.kept, self.latest = {}, None

    def sliding(self, ref, z, lead, t):
        if self.latest is not z:
            self.latest, self.kept = z, {}
        where = (id(ref), z if isinstance(z, int) else id(z), lead)
        for key in [k for k in self.kept if k[:3] == where and abs(k[3] - t) > 3]:
            del self.kept[key]

        def load(j):
            key = (*where, j)
            if key not in self.kept:
                self.kept[key] = (ref, z, get(ref, z, *lead, j))
            return self.kept[key][2]

        return load

    def x(self, load, t, step, count=TX, stride=TY):
        j = t // stride + step
        if 0 <= j < count:
            return load(t + step * stride)
        if step > 0:
            turned = pltpu.roll(load(t % stride), LANES - self.span, 1)
            return jnp.where(self.lane < LANES - self.span, turned, 0.0)
        turned = pltpu.roll(load((count - 1) * stride + t % stride), self.span, 1)
        return jnp.where(self.lane >= self.span, turned, 0.0)

    def lanes(self, f, step):
        if step > 0:
            return jnp.where(self.y < self.span - 1, pltpu.roll(f, LANES - 1, 1), 0.0)
        return jnp.where(self.y > 0, pltpu.roll(f, 1, 1), 0.0)

    def y_side(self, load, t, step):
        if (t % TY == 0) == (step > 0):
            return load(t + step)
        return self.lanes(load(t - step), step)

    def beside(self, ref, z, lead, t):
        load = self.sliding(ref, z, lead, t)
        near = [self.x(load, t, 1), self.x(load, t, -1)]
        near += [self.y_side(load, t, 1), self.y_side(load, t, -1)]
        return load(t), near + [get(ref, z + 1, *lead, t), get(ref, z - 1, *lead, t)]

    def coarse_beside(self, ref, z, lead, t):
        load = lambda j: get(ref, z, *lead, j)
        f = load(t)
        near = [self.x(load, t, step, TX // 2, 1) for step in (1, -1)]
        near += [self.lanes(f, 1), self.lanes(f, -1)]
        return f, near + [get(ref, z + 2, *lead, t), get(ref, z - 2, *lead, t)]

    def pair_sum(self, f):
        return f + jnp.where(self.row % 2 == 0, pltpu.roll(f, SUB - 1, 0), pltpu.roll(f, 1, 0))


def block_of(t):
    return range(2 * TY * t, 2 * TY * (t + 1))


def tree(terms):
    while len(terms) > 1:
        terms = [sum(terms[k : k + 2]) for k in range(0, len(terms), 2)]
    return terms[0]


def get(ref, z, *index):
    return ref[(*index, pl.ds(z, SUB), slice(None))]


def sweep(lo, hi, body):
    count = (hi - lo) // SUB
    assert count * SUB == hi - lo
    unroll = next(u for u in (3, 2, count) if count % u == 0)

    def step(t):
        late = []

        def store(ref, value, z, *index):
            ref[(*index, pl.ds(z, SUB), slice(None))] = value

        def put(*item):
            late.append(item)
            if len(late) > HELD:
                store(*late.pop(0))

        for u in range(unroll):
            body(t + (lo + u * SUB), put)
        for item in late:
            store(*item)

    if unroll == count:
        step(0)
    else:
        span = unroll * SUB
        lax.fori_loop(0, count // unroll, lambda t, _: (step(pl.multiple_of(t * span, SUB)), 0)[1], 0)


def pack_kernel(geo, heat_in, flow_in, dual_in, kind_in, out, heat, flow, dual, kind, sems):
    b = geo.slab
    pairs = ((heat_in, heat), (flow_in, flow), (dual_in, dual), (kind_in, kind))
    copies = [
        pltpu.make_async_copy(source, target, sems.at[k])
        for k, (source, target) in enumerate(pairs)
    ]
    for copy in copies:
        copy.start()
    for copy in copies:
        copy.wait()
    fields = [heat, flow.at[0], flow.at[1], flow.at[2], dual, kind]
    turned = []
    for ref in fields:
        rows = [ref[x, pl.ds(y, SUB, stride=TY), :] for x, y in geo.order]
        turned.append(jnp.concatenate(rows, 0).astype(jnp.float32).T)
    for j in range(geo.group):
        q = geo.holder[j]
        for f in range(FIELDS):
            out[q, f * b : (f + 1) * b, :] = turned[f][j * b : (j + 1) * b]


def edge_kernel(geo, own, first, last):
    b, e = geo.slab, EDGE
    for q in range(geo.group):
        for out, at in ((first, 0), (last, b - e)):
            rows = [own[q, f * b + at : f * b + at + e, :] for f in range(4)]
            out[q] = jnp.concatenate(rows, 0)


STATIC_FINE = ("s0", "s1", "s2", "hv", "w")
STATIC_COARSE = ("kxp", "kxm", "kyp", "kym", "kzp", "kzm", "wc")
STATIC = STATIC_FINE + STATIC_COARSE


def iterate(geo, st, work, seqs, lo, hi, first=(), mean=None):
    v, p, res, cor, cor2, cc0, cc1 = work
    tl = Tiles(geo)
    keep = 1.0 - JACOBI_WEIGHT
    comps = range(3 * len(seqs))
    transposed = len(seqs)

    def faces(t, z):
        h, near = tl.beside(st["hv"], z, (), t)
        return [h + other for other in near]

    def around(face, ref, c, t, z):
        f, near = tl.beside(ref, z, (c,), t)
        return f, tree([a * b for a, b in zip(face, near)])

    def residual(z, put):
        for t in range(SUB):
            w = get(st["w"], z, t)
            if FORWARD in seqs and FORWARD not in first:
                face = faces(t, z)
                diag = tree(face)
            for s, q in enumerate(seqs):
                start = q == FORWARD and q in first
                if not start:
                    _, near = tl.beside(p, z, (transposed if q == ADJOINT else s,), t)
                    slope = [0.5 * (near[2 * k] - near[2 * k + 1]) for k in range(3)]
                for k in range(3):
                    c = 3 * s + k
                    if q == FORWARD:
                        value = get(st["s%d" % k], z, t)
                        if not start:
                            f, total = around(face, v, c, t, z)
                            value = value - slope[k] - (diag * f - total)
                    else:
                        value = slope[k] if q in first else get(cor, z, c, t) + slope[k]
                    put(res, value, z, c, t)
                    put(cor, w * value, z, c, t)

    sweep(lo - 8, hi + 8, residual)

    def restricted(z, put):
        for pair in range(TX // 2):
            left = [0.0 for _ in comps]
            for t in block_of(pair):
                face = faces(t, z)
                for c in comps:
                    _, total = around(face, cor, c, t, z)
                    left[c] = left[c] + (keep * get(res, z, c, t) + total)
            wc = 0.125 * get(st["wc"], z, pair)
            for c in comps:
                put(cc0, wc * tl.pair_sum(left[c]), z, c, pair)

    sweep(lo - 8, hi + 8, restricted)

    def coarse_step(ref, c, pair, z):
        f, near = tl.coarse_beside(ref, z, (c,), pair)
        terms = [get(st[name], z, pair) * b for name, b in zip(STATIC_COARSE, near)]
        return tree([get(cc0, z, c, pair), keep * f] + terms)

    def sweep_one(z, put):
        for pair in range(TX // 2):
            for c in comps:
                put(cc1, coarse_step(cc0, c, pair, z), z, c, pair)

    sweep(lo - 4, hi + 4, sweep_one)

    def sweep_two(z, put):
        for pair in range(TX // 2):
            for c in comps:
                value = coarse_step(cc1, c, pair, z)
                for t in block_of(pair):
                    put(cor2, get(cor, z, c, t) + value, z, c, t)

    sweep(lo - 4, hi + 4, sweep_two)

    def velocity(z, put):
        for t in range(SUB):
            face, w = faces(t, z), get(st["w"], z, t)
            for c in comps:
                f, total = around(face, cor2, c, t, z)
                value = get(cor, z, c, t) + keep * f + w * total
                if seqs[c // 3] == FORWARD and FORWARD not in first:
                    value = get(v, z, c, t) + value
                put(v, value, z, c, t)

    sweep(lo - 4, hi + 4, velocity)

    def pressure(z, put):
        for t in range(SUB):
            half = get(st["hv"], z, t)
            for s, q in enumerate(seqs):
                c = 3 * s
                if q == ADJOINT:
                    face = faces(t, z)
                    diag, div = tree(face), 0.0
                    for k in range(3):
                        f, near = tl.beside(v, z, (c + k,), t)
                        div = div + 0.5 * (near[2 * k] - near[2 * k + 1])
                        total = tree([a * b for a, b in zip(face, near)])
                        put(cor, get(res, z, c + k, t) - (diag * f - total), z, c + k, t)
                    value = get(p, z, s, t) + div
                    put(p, value, z, s, t)
                    put(p, half * value, z, transposed, t)
                    continue
                one, two = tl.sliding(v, z, (c,), t), tl.sliding(v, z, (c + 1,), t)
                div = tl.x(one, t, 1) - tl.x(one, t, -1)
                div = div + (tl.y_side(two, t, 1) - tl.y_side(two, t, -1))
                div = div + (get(v, z + 1, c + 2, t) - get(v, z - 1, c + 2, t))
                value = -(half * (0.5 * div))
                if not (q == FORWARD and q in first):
                    value = get(p, z, s, t) + value
                if mean is not None:
                    value = value - jnp.where(geo.inside(z), mean, 0.0)
                put(p, value, z, s, t)

    sweep(lo, hi, pressure)


def whole_sum(value):
    return jnp.sum(jnp.sum(value, axis=0), axis=(0, 1), keepdims=True)


def product(left, right):
    value = 0.0
    for a, b in zip(left, right):
        value = value + a[...] * b[...]
    return whole_sum(value)


def in_lanes(values, rows):
    lane = lax.broadcasted_iota(jnp.int32, (rows, LANES), 1)
    out = jnp.zeros((rows, LANES), jnp.float32)
    for k, value in values:
        out = jnp.where(lane == k, value, out)
    return out


def setup_kernel(geo, stiffness, own, low, high, low_edge, high_edge, *refs):
    st = dict(zip(STATIC, refs))
    moved, duals, sums, raw, heat, vc, *work = refs[len(STATIC) :]
    v, p, res, cor, cor2, cc0, cc1 = work
    tl = Tiles(geo)
    b, m, n_rows = geo.slab, geo.margin, geo.rows
    granule = geo.block[1]

    def place(t, _):
        groups = []
        for source, base in ((low, m - b), (own, m), (high, m + b)):
            for u in range(0, b, SUB):
                row = pl.multiple_of(t * b, b) + u
                tiles = [source[q, pl.ds(row, SUB), :] for q in range(geo.group)]
                groups.append((base + u, tiles))
        groups = [(row, gather_tiles(tiles, granule)) for row, tiles in groups]
        for row, tiles in groups:
            for x, tile in enumerate(tiles):
                raw[t, x, row : row + SUB, :] = tile
        return 0

    lax.fori_loop(0, FIELDS, place, 0)
    for source, base in ((low_edge, m - b - EDGE), (high_edge, m + 2 * b)):
        tiles = [source[q] for q in range(geo.group)]
        for x, tile in enumerate(gather_tiles(tiles, granule)):
            for f in range(4):
                raw[f, x, base : base + EDGE, :] = tile[f * EDGE : (f + 1) * EDGE]

    def advance(ref, old, new):
        def body(z, put):
            inside = geo.inside(z)
            for t in range(SUB):
                f, near = tl.beside(ref, z, (old,), t)
                drift = 0.0
                for k in range(3):
                    flow = get(raw, z, 1 + k, t)
                    drift = drift + jnp.maximum(flow, 0.0) * (f - near[2 * k + 1])
                    drift = drift + jnp.minimum(flow, 0.0) * (near[2 * k] - f)
                spread = tree(near) - 6.0 * f
                value = f - INCREMENT_DT * drift + INCREMENT_DT * DIFFUSIVITY * spread
                put(heat, jnp.where(inside, value, 0.0), z, new, t)

        return body

    sweep(m - b - 4, m + 2 * b + 4, advance(raw, 0, 0))
    sweep(m - b, m + 2 * b, advance(heat, 0, 1))

    def viscosity(z, put):
        inside = geo.inside(z)
        for pair in range(TX // 2):
            coarse = 0.0
            for t in block_of(pair):
                kind = get(raw, z, 5, t)
                base = jnp.zeros(kind.shape, jnp.float32)
                for layer in range(LAYERS):
                    base = jnp.where(kind == float(layer), stiffness[layer], base)
                value = base * jnp.exp(-ACTIVATION_ENERGY * get(heat, z, 1, t))
                value = jnp.where(inside, value, 0.0)
                put(st["hv"], 0.5 * value, z, t)
                coarse = coarse + value
            put(vc, 0.125 * tl.pair_sum(coarse), z, pair)

    sweep(m - b, m + 2 * b, viscosity)

    def statics(z, put):
        inside = geo.inside(z)
        for t in range(SUB):
            h, near = tl.beside(st["hv"], z, (), t)
            diag = tree([h + other for other in near])
            put(st["w"], jnp.where(inside, JACOBI_WEIGHT / diag, 0.0), z, t)
            f, near = tl.beside(heat, z, (1,), t)
            dual = -INCREMENT_DT * get(raw, z, 4, t)
            for k in range(3):
                flow = get(raw, z, 1 + k, t)
                step = jnp.where(flow > 0, f - near[2 * k + 1], near[2 * k] - f)
                put(st["s%d" % k], dual * step, z, t)

    sweep(m - b, m + 2 * b, statics)

    def coarse_statics(z, put):
        inside = geo.inside(z)
        for pair in range(TX // 2):
            c, near = tl.coarse_beside(vc, z, (), pair)
            face = [0.25 * (0.5 * (c + o)) for o in near]
            wc = jnp.where(inside, JACOBI_WEIGHT / tree(face), 0.0)
            for name, f in zip(STATIC_COARSE, face):
                put(st[name], wc * f, z, pair)
            put(st["wc"], wc, z, pair)

    sweep(m - b, m + 2 * b, coarse_statics)

    def transport(z, put):
        for t in range(SUB):
            dual, near = tl.beside(raw, z, (4,), t)
            value = dual + INCREMENT_DT * DIFFUSIVITY * (tree(near) - 6.0 * dual)
            for k in range(3):
                flow, sides = tl.beside(raw, z, (1 + k,), t)
                a = jnp.maximum(flow, 0.0) * dual
                c = jnp.minimum(flow, 0.0) * dual
                ahead = jnp.maximum(sides[2 * k], 0.0) * near[2 * k]
                behind = jnp.minimum(sides[2 * k + 1], 0.0) * near[2 * k + 1]
                value = value - INCREMENT_DT * (a - ahead + behind - c)
            put(moved, value, z - m, t)

    sweep(m, m + b, transport)

    def unit(z, put):
        value = jnp.where(geo.inside(z), 1.0, 0.0)
        for t in range(SUB):
            put(p, value, z, 0, t)
            put(p, get(st["hv"], z, t), z, 1, t)

    sweep(0, n_rows, unit)

    mine = slice(m, m + b)
    source = [st["s%d" % k].at[:, mine, :] for k in range(3)]
    step = [v.at[k, :, mine, :] for k in range(3)]
    iterate(geo, st, work, (ADJOINT,), m - PHASE, m + b + PHASE, (ADJOINT,))
    sums_of = [(0, product(step, source)), (1, whole_sum(p[0, :, mine, :]))]
    for k in range(4):
        duals[k] = cor[k, :, mine, :] if k < 3 else p[0, :, mine, :]
    iterate(geo, st, work, (ADJOINT,), m, m + b)
    sums_of += [(2, product(step, source))]
    for k in range(4):
        duals[4 + k] = cor[k, :, mine, :] if k < 3 else p[0, :, mine, :]
    sums[...] = in_lanes(sums_of, sums.shape[0])


def first_kernel(geo, *refs):
    st = dict(zip(STATIC, refs))
    out, *work = refs[len(STATIC) :]
    v, p = work[:2]
    rows = slice(geo.margin - PHASE, geo.margin + geo.slab + PHASE)
    iterate(geo, st, work, (FORWARD,), rows.start, rows.stop, (FORWARD,))
    for k in range(4):
        out[k] = v[k, :, rows, :] if k < 3 else p[0, :, rows, :]


def refill(geo, v, p, state, rows, shift):
    for k in range(3):
        v[k, :, rows, :] = state[k]
    if shift is None:
        p[0, :, rows, :] = state[3]
    else:
        inside = geo.inside(rows.start, rows.stop - rows.start)
        p[0, :, rows, :] = state[3] - jnp.where(inside, shift, 0.0)[None]


def second_kernel(geo, *refs):
    st = dict(zip(STATIC, refs))
    earlier, early, duals, state, sums, *work = refs[len(STATIC) :]
    v, p = work[:2]
    b, m = geo.slab, geo.margin
    m1, m2 = means(geo, early[...], None)[:2]
    refill(geo, v, p, earlier, slice(m - PHASE, m + b + PHASE), m1)
    iterate(geo, st, work, (FORWARD,), m, m + b, mean=m2)
    mine = slice(m, m + b)
    for k in range(4):
        state[k] = v[k, :, mine, :] if k < 3 else p[0, :, mine, :]
    fields = [state.at[k] for k in range(4)]
    near, far = [duals.at[k] for k in range(4)], [duals.at[4 + k] for k in range(4)]
    sums_of = [(3, product(near, fields)), (4, product(far, fields))]
    sums[...] = in_lanes(sums_of, sums.shape[0])


def means(geo, early, late):
    sums = early if late is None else early + late
    row = jnp.sum(sums, axis=0, keepdims=True) / geo.cells
    lane = lax.broadcasted_iota(jnp.int32, row.shape, 1)

    def at(k):
        return jnp.sum(jnp.where(lane == k, row, 0.0), axis=1, keepdims=True)

    c1, l1, c2, l1_x2, l2_x2 = [at(k) for k in range(5)]
    m1 = c1
    m2 = c1 + c2 - m1 * l1
    m3 = c1 + l1_x2
    m4 = c1 + c2 + l2_x2 - m3 * l1
    return m1, m2, m3, m4


def third_kernel(geo, *refs):
    st = dict(zip(STATIC, refs))
    own, low, high, out, *work = refs[len(STATIC) :]
    v, p = work[:2]
    b, m = geo.slab, geo.margin
    for source, base in ((low, m - b), (own, m), (high, m + b)):
        refill(geo, v, p, source, slice(base, base + b), None)
    rows = slice(m - PHASE, m + b + PHASE)
    iterate(geo, st, work, (FORWARD,), rows.start, rows.stop)
    for k in range(4):
        out[k] = v[k, :, rows, :] if k < 3 else p[0, :, rows, :]


def fourth_kernel(geo, *refs):
    st = dict(zip(STATIC, refs))
    state, early, late, moved, out, *work = refs[len(STATIC) :]
    v, p = work[:2]
    b, m = geo.slab, geo.margin
    m3, m4 = means(geo, early[...], late[...])[2:]
    refill(geo, v, p, state, slice(m - PHASE, m + b + PHASE), m3)
    iterate(geo, st, work, (FORWARD,), m, m + b, mean=m4)
    for u in range(0, b, SUB):
        at = slice(m + u, m + u + SUB)
        columns = range(SUB)
        fields = [[v[k, x, at, :] for x in columns] for k in range(3)]
        fields.append([p[0, x, at, :] for x in columns])
        fields.append([moved[x, u : u + SUB, :] + fields[2][x] for x in columns])
        for f, tiles in enumerate(fields):
            for q, tile in enumerate(scatter_tiles(tiles, geo.block[1])):
                out[q, f * b + u : f * b + u + SUB, :] = tile


def unpack_kernel(geo, chunks, heat, flow, pressure):
    b = geo.slab
    for f, ref in enumerate((flow.at[0], flow.at[1], flow.at[2], pressure, heat)):
        rows = [chunks[geo.holder[j], f * b : (f + 1) * b, :] for j in range(geo.group)]
        block = jnp.concatenate(rows, 0).T
        for k, (x, y) in enumerate(geo.order):
            ref[x, pl.ds(y, SUB, stride=TY), :] = block[k * SUB : (k + 1) * SUB]


def call(kernel, out, scratch, *args, smem=(), hbm=(), limit=VMEM_LIMIT, megabytes=2):
    f32 = jnp.float32
    cost = pl.CostEstimate(
        flops=megabytes * 1000000, bytes_accessed=megabytes * 1000000, transcendentals=0
    )
    specs = [
        pl.BlockSpec(
            memory_space=pltpu.SMEM if i in smem else pltpu.HBM if i in hbm else pltpu.VMEM
        )
        for i in range(len(args))
    ]
    return pl.pallas_call(
        kernel,
        out_shape=[jax.ShapeDtypeStruct(s, f32) for s in out],
        in_specs=specs,
        out_specs=[pl.BlockSpec(memory_space=pltpu.VMEM) for _ in out],
        scratch_shapes=[pltpu.VMEM(s, f32) if isinstance(s, tuple) else s for s in scratch],
        compiler_params=pltpu.CompilerParams(vmem_limit_bytes=limit),
        cost_estimate=cost,
    )(*args)


def slab_shards(geo, heat, flow, dual, kind, stiffness):
    b, group = geo.slab, geo.group
    inputs = (heat, flow, dual, kind)
    (chunks,) = call(
        functools.partial(pack_kernel, geo),
        [(group, FIELDS * b, LANES)],
        [pltpu.VMEM(a.shape, a.dtype) for a in inputs] + [pltpu.SemaphoreType.DMA((4,))],
        *inputs,
        hbm=range(4),
        limit=PACK_LIMIT,
    )
    own = lax.all_to_all(chunks, ("gx", "gy"), 0, 0, tiled=True)
    axes = ("gx", "gy", "gz")
    low = lax.ppermute(own, axes, geo.shifts(1))
    high = lax.ppermute(own, axes, geo.shifts(-1))
    edges = call(functools.partial(edge_kernel, geo), [(group, SUB, LANES)] * 2, [], own)
    high_edge = lax.ppermute(edges[0], axes, geo.shifts(-2))
    low_edge = lax.ppermute(edges[1], axes, geo.shifts(2))

    fine, coarse = (SUB, geo.rows, LANES), (TX // 2, geo.rows, LANES)
    slab = (SUB, b, LANES)

    def work(n, more=0):
        fields = [(3 * n, *fine), (n + more, *fine)] + [(3 * n, *fine)] * 3
        return fields + [(3 * n, *coarse)] * 2

    devices = group * geo.nz
    wide = (4, SUB, b + 2 * PHASE, LANES)
    *static, moved, duals, early = call(
        functools.partial(setup_kernel, geo),
        [fine] * len(STATIC_FINE)
        + [coarse] * len(STATIC_COARSE)
        + [slab, (8, *slab), (devices, LANES)],
        [(FIELDS, *fine), (2, *fine), coarse] + work(1, 1),
        stiffness,
        own,
        low,
        high,
        low_edge,
        high_edge,
        smem=(0,),
        megabytes=60,
    )
    early = lax.all_to_all(early, axes, 0, 0, tiled=True)
    (state,) = call(
        functools.partial(first_kernel, geo), [wide], work(1), *static, megabytes=20
    )
    state, late = call(
        functools.partial(second_kernel, geo),
        [(4, *slab), (devices, LANES)],
        work(1),
        *static,
        state,
        early,
        duals,
        megabytes=20,
    )
    low_state = lax.ppermute(state, axes, geo.shifts(1))
    high_state = lax.ppermute(state, axes, geo.shifts(-1))
    late = lax.all_to_all(late, axes, 0, 0, tiled=True)
    (state,) = call(
        functools.partial(third_kernel, geo),
        [wide],
        work(1),
        *static,
        state,
        low_state,
        high_state,
        megabytes=30,
    )
    (chunks,) = call(
        functools.partial(fourth_kernel, geo),
        [(group, BACK * b, LANES)],
        work(1),
        *static,
        state,
        early,
        late,
        moved,
        megabytes=20,
    )
    chunks = lax.all_to_all(chunks, ("gx", "gy"), 0, 0, tiled=True)
    return tuple(
        call(
            functools.partial(unpack_kernel, geo),
            [geo.block, (3, *geo.block), geo.block],
            [],
            chunks,
        )
    )


def solution(mesh):
    in_specs = (
        P("gx", "gy", "gz"),
        P(None, "gx", "gy", "gz"),
        P("gx", "gy", "gz"),
        P("gx", "gy", "gz"),
        P(),
    )
    out_specs = (P("gx", "gy", "gz"), P(None, "gx", "gy", "gz"), P("gx", "gy", "gz"))

    def program(saved_heat_state, *others):
        shape = saved_heat_state.shape
        plan = shards
        if slab_plan_fits(mesh, shape):
            plan = functools.partial(slab_shards, Slabs(mesh, shape))
        return jax.shard_map(
            plan, mesh=mesh, in_specs=in_specs, out_specs=out_specs, check_vma=False
        )(saved_heat_state, *others)

    return program
```

```python
import functools

import jax
import jax.numpy as jnp
from jax import lax
from jax.experimental import pallas as pl
from jax.experimental.pallas import tpu as pltpu
from jax.sharding import PartitionSpec as P

RECOMPUTE = 2
SCHUR_ITERS = 4
COARSE_SWEEPS = 3
LAYERS = 8


INCREMENT_DT = 0.2
DIFFUSIVITY = 0.3
ACTIVATION_ENERGY = 2.3
JACOBI_WEIGHT = 0.7
SCHUR_WEIGHT = 0.5
RAYLEIGH = 1.0


def extended(block, sides, width):
    for axis, dim in sides:
        count = lax.axis_size(axis)
        forward = [(i, i + 1) for i in range(count - 1)]
        backward = [(target, source) for source, target in forward]
        low = lax.ppermute(
            lax.slice_in_dim(block, block.shape[dim] - width, None, axis=dim), axis, forward
        )
        high = lax.ppermute(lax.slice_in_dim(block, 0, width, axis=dim), axis, backward)
        block = jnp.concatenate([low, block, high], axis=dim)
    return block


def neighbours(bordered_array):
    centre = bordered_array[..., 1:-1, 1:-1, 1:-1]
    beside_all = [
        bordered_array[..., 2:, 1:-1, 1:-1],
        bordered_array[..., :-2, 1:-1, 1:-1],
        bordered_array[..., 1:-1, 2:, 1:-1],
        bordered_array[..., 1:-1, :-2, 1:-1],
        bordered_array[..., 1:-1, 1:-1, 2:],
        bordered_array[..., 1:-1, 1:-1, :-2],
    ]
    return (centre, beside_all)


def finest_halo_cells(field):
    return extended(field, (("gx", 1), ("gy", 2), ("gz", 3)), 1)


def deep_halo(field):
    return extended(field, (("gx", 1), ("gy", 2), ("gz", 3)), 2)


def coarse_halo(field):
    return extended(field, (("gx", 1), ("gy", 2), ("gz", 3)), 1)


def march_backward(bordered_array, shallower_adjacent, deeper_adjacent):
    centre, beside_all = neighbours(bordered_array)
    drift = 0.0
    for dim_index in range(3):
        drift = (
            drift
            + shallower_adjacent[dim_index] * (centre - beside_all[2 * dim_index + 1])
            + deeper_adjacent[dim_index] * (beside_all[2 * dim_index] - centre)
        )
    spread = sum(beside_all) - 6.0 * centre
    return centre - INCREMENT_DT * drift + INCREMENT_DT * DIFFUSIVITY * spread


def motion_source(bordered_heat, forward_motion, dual_heat_after):
    centre, beside_all = neighbours(bordered_heat)
    device_pieces = [
        jnp.where(
            forward_motion[dim_index] > 0,
            centre - beside_all[2 * dim_index + 1],
            beside_all[2 * dim_index] - centre,
        )
        for dim_index in range(3)
    ]
    return -INCREMENT_DT * dual_heat_after[None] * jnp.stack(device_pieces)


def advect_dual_heat(pos_padded, neg_padded, lam_padded):
    centre, beside_all = neighbours(lam_padded)
    result = centre + INCREMENT_DT * DIFFUSIVITY * (sum(beside_all) - 6.0 * centre)
    for dim_index in range(3):
        pos_centre, pos_around = neighbours(pos_padded[dim_index])
        neg_centre, neg_around = neighbours(neg_padded[dim_index])
        result = result - INCREMENT_DT * (
            pos_centre - pos_around[2 * dim_index] + neg_around[2 * dim_index + 1] - neg_centre
        )
    return result


def coefficients(bordered_array, factor):
    centre, beside_all = neighbours(bordered_array)
    return [factor * (0.5 * (centre + other)) for other in beside_all]


def apply_operator(face_coef, bordered_array):
    centre, beside_all = neighbours(bordered_array)
    return sum((coef * (centre - other) for coef, other in zip(face_coef, beside_all)))


def gradient(bordered_array):
    centre, beside_all = neighbours(bordered_array)
    return jnp.stack(
        [
            0.5 * (beside_all[2 * dim_index] - beside_all[2 * dim_index + 1])
            for dim_index in range(3)
        ]
    )


def divergence(bordered_array):
    centre, beside_all = neighbours(bordered_array)
    return sum(
        (
            0.5 * (beside_all[2 * dim_index][dim_index] - beside_all[2 * dim_index + 1][dim_index])
            for dim_index in range(3)
        )
    )


def restrict(field):
    leading = field.shape[:-3]
    cells_x, cells_y, cells_z = field.shape[-3:]
    blocks = field.reshape(leading + (cells_x // 2, 2, cells_y // 2, 2, cells_z // 2, 2))
    return blocks.mean(axis=(-5, -3, -1))


def prolong(field):
    return jnp.repeat(jnp.repeat(jnp.repeat(field, 2, axis=-3), 2, axis=-2), 2, axis=-1)


def evaluate_viscosity(rheology_class, class_base_stiffness):
    base = jnp.zeros(rheology_class.shape, jnp.float32)
    for layer_index in range(LAYERS):
        base = base + jnp.where(
            rheology_class == layer_index, class_base_stiffness[layer_index], 0.0
        )
    return base


def inside_mask(extent_first, extent_second, extent_vertical):
    index_x = (
        lax.axis_index("gx") * extent_first + jnp.arange(extent_first + 2, dtype=jnp.int32) - 1
    )
    index_y = (
        lax.axis_index("gy") * extent_second + jnp.arange(extent_second + 2, dtype=jnp.int32) - 1
    )
    index_z = (
        lax.axis_index("gz") * extent_vertical
        + jnp.arange(extent_vertical + 2, dtype=jnp.int32)
        - 1
    )
    inside_x = (index_x >= 0) & (index_x < extent_first * lax.axis_size("gx"))
    inside_y = (index_y >= 0) & (index_y < extent_second * lax.axis_size("gy"))
    inside_z = (index_z >= 0) & (index_z < extent_vertical * lax.axis_size("gz"))
    return inside_x[:, None, None] & inside_y[None, :, None] & inside_z[None, None, :]


def coarse_solve(coarse_res, coarse_coef, coarse_diag, pad_field):
    coarse_corr = JACOBI_WEIGHT * coarse_res / coarse_diag
    for sweep in range(COARSE_SWEEPS - 1):
        coarse_corr = (
            coarse_corr
            + JACOBI_WEIGHT
            * (coarse_res - apply_operator(coarse_coef, pad_field(coarse_corr)))
            / coarse_diag
        )
    return coarse_corr


def shards(saved_heat_state, forward_motion, dual_heat_after, rheology_class, class_base_stiffness):
    extent_first, extent_second, extent_vertical = saved_heat_state.shape
    shallower_adjacent = jnp.maximum(forward_motion, 0.0)
    deeper_adjacent = jnp.minimum(forward_motion, 0.0)
    heat_state = saved_heat_state
    for repeat_index in range(RECOMPUTE):
        heat_state = march_backward(
            finest_halo_cells(heat_state[None])[0], shallower_adjacent, deeper_adjacent
        )
    local_viscosity = evaluate_viscosity(rheology_class, class_base_stiffness) * jnp.exp(
        -ACTIVATION_ENERGY * heat_state
    )
    stacked = jnp.concatenate(
        [
            heat_state[None],
            dual_heat_after[None],
            shallower_adjacent * dual_heat_after[None],
            deeper_adjacent * dual_heat_after[None],
            local_viscosity[None],
        ],
        0,
    )
    bordered_array = finest_halo_cells(stacked)
    driving_source = motion_source(bordered_array[0], forward_motion, dual_heat_after)
    advected_result = advect_dual_heat(bordered_array[2:5], bordered_array[5:8], bordered_array[1])
    face_coef = coefficients(bordered_array[8], 1.0)
    diagonal = sum(face_coef)
    coarse_visc = restrict(local_viscosity)
    coarse_coef = coefficients(coarse_halo(coarse_visc[None])[0], 0.25)
    coarse_diag = sum(coarse_coef)
    deep_static = deep_halo(jnp.concatenate([local_viscosity[None], driving_source], 0))
    cycle_coef = coefficients(deep_static[0], 1.0)
    cycle_source = deep_static[1:4, 1:-1, 1:-1, 1:-1]
    inside = inside_mask(extent_first, extent_second, extent_vertical)
    safe_diag = jnp.where(inside, sum(cycle_coef), 1.0)
    total_cells = (
        extent_first
        * extent_second
        * extent_vertical
        * lax.axis_size("gx")
        * lax.axis_size("gy")
        * lax.axis_size("gz")
    )
    velocity = jnp.zeros(forward_motion.shape, jnp.float32)
    mean_stress = jnp.zeros(saved_heat_state.shape, jnp.float32)
    for iteration in range(SCHUR_ITERS):
        if iteration == 0:
            cycle_resid = cycle_source
        else:
            flow_press = deep_halo(jnp.concatenate([velocity, mean_stress[None]], 0))
            cycle_resid = (
                cycle_source - apply_operator(cycle_coef, flow_press[0:3]) - gradient(flow_press[3])
            )
        cycle_corr = jnp.where(inside, JACOBI_WEIGHT * cycle_resid / safe_diag, 0.0)
        residual = cycle_resid[:, 1:-1, 1:-1, 1:-1]
        correction = cycle_corr[:, 1:-1, 1:-1, 1:-1]
        residual_two = residual - apply_operator(face_coef, cycle_corr)
        coarse_res = restrict(residual_two)
        coarse_corr = coarse_solve(coarse_res, coarse_coef, coarse_diag, coarse_halo)
        correction = correction + prolong(coarse_corr)
        correction = (
            correction
            + JACOBI_WEIGHT
            * (residual - apply_operator(face_coef, finest_halo_cells(correction)))
            / diagonal
        )
        velocity = velocity + correction
        spread_flow = divergence(finest_halo_cells(velocity))
        mean_stress = mean_stress - SCHUR_WEIGHT * local_viscosity * spread_flow
        mean_stress = mean_stress - lax.psum(jnp.sum(mean_stress), ("gx", "gy", "gz")) / total_cells
    adj_temp_prev = advected_result + RAYLEIGH * velocity[2]
    return (adj_temp_prev, velocity, mean_stress)


SUB = 8
LANES = 128
FIELDS = 6
BACK = 5
EDGE = 2
PHASE = 8
HELD = 24
TX, TY = 4, 2
VMEM_LIMIT = 32 * 1024 * 1024
PACK_LIMIT = 60 * 1024 * 1024
FORWARD, ADJOINT, RESPONSE = range(3)


def slab_plan_fits(mesh, shape):
    sizes = mesh.shape
    group = sizes["gx"] * sizes["gy"]
    block = (shape[0] // sizes["gx"], shape[1] // sizes["gy"], shape[2] // sizes["gz"])
    return (
        group == SUB
        and block[0] == SUB
        and block[0] * block[1] == LANES
        and block[1] * group == LANES
        and block[2] == LANES
        and block[2] == group * 2 * PHASE
    )


class Slabs:
    def __init__(self, mesh, shape):
        self.nx, self.ny, self.nz = mesh.shape["gx"], mesh.shape["gy"], mesh.shape["gz"]
        self.group = self.nx * self.ny
        self.width, self.breadth, self.height = shape
        self.block = (shape[0] // self.nx, shape[1] // self.ny, shape[2] // self.nz)
        self.slab = self.block[2] // self.group
        self.margin = self.slab + SUB
        self.rows = self.slab + 2 * self.margin
        self.cells = self.width * self.breadth * self.height
        self.place = []
        for ix in range(self.nx):
            for iy in range(self.ny):
                step = ix if iy % 2 == 0 else self.nx - 1 - ix
                self.place.append(iy * self.nx + step)
        self.order = [
            (x + TX * part, y)
            for x in range(TX)
            for y in range(TY)
            for part in range(self.block[0] // TX)
        ]
        self.holder = [self.place.index(j) for j in range(self.group)]

    def device(self, slab):
        return self.holder[slab % self.group] * self.nz + slab // self.group

    def shifts(self, distance):
        count = self.group * self.nz
        return [
            (self.device(p), self.device(p + distance))
            for p in range(count)
            if 0 <= p + distance < count
        ]

    def index(self):
        ix, iy = lax.axis_index("gx"), lax.axis_index("gy")
        step = jnp.where(iy % 2 == 0, ix, self.nx - 1 - ix)
        return lax.axis_index("gz") * self.group + iy * self.nx + step

    def inside(self, z, n=SUB):
        layer = self.index() * self.slab - self.margin + z
        layer = layer + lax.broadcasted_iota(jnp.int32, (n, LANES), 0)
        return (layer >= 0) & (layer < self.height)


def exchange(tiles, bit, width):
    lane = lax.broadcasted_iota(jnp.int32, (SUB, LANES), 1)
    low = (lane & width) == 0
    new = list(tiles)
    for a in range(SUB):
        if not a & bit:
            b = a | bit
            new[a] = jnp.where(low, tiles[a], pltpu.roll(tiles[b], width, 1))
            new[b] = jnp.where(low, pltpu.roll(tiles[a], LANES - width, 1), tiles[b])
    return new


def gather_tiles(tiles, granule):
    for bit, width in ((1, granule // 2), (1, granule), (2, 2 * granule), (4, 4 * granule)):
        tiles = exchange(tiles, bit, width)
    return tiles


def scatter_tiles(tiles, granule):
    for bit, width in ((4, 4 * granule), (2, 2 * granule), (1, granule), (1, granule // 2)):
        tiles = exchange(tiles, bit, width)
    return tiles


class Tiles:
    def __init__(self, geo):
        self.span = geo.breadth // TY
        self.row = lax.broadcasted_iota(jnp.int32, (SUB, LANES), 0)
        self.lane = lax.broadcasted_iota(jnp.int32, (SUB, LANES), 1)
        self.y = self.lane % self.span
        self.kept, self.latest = {}, None

    def sliding(self, ref, z, lead, t):
        if self.latest is not z:
            self.latest, self.kept = z, {}
        where = (id(ref), z if isinstance(z, int) else id(z), lead)
        for key in [k for k in self.kept if k[:3] == where and abs(k[3] - t) > 3]:
            del self.kept[key]

        def load(j):
            key = (*where, j)
            if key not in self.kept:
                self.kept[key] = (ref, z, get(ref, z, *lead, j))
            return self.kept[key][2]

        return load

    def x(self, load, t, step, count=TX, stride=TY):
        j = t // stride + step
        if 0 <= j < count:
            return load(t + step * stride)
        if step > 0:
            turned = pltpu.roll(load(t % stride), LANES - self.span, 1)
            return jnp.where(self.lane < LANES - self.span, turned, 0.0)
        turned = pltpu.roll(load((count - 1) * stride + t % stride), self.span, 1)
        return jnp.where(self.lane >= self.span, turned, 0.0)

    def lanes(self, f, step):
        if step > 0:
            return jnp.where(self.y < self.span - 1, pltpu.roll(f, LANES - 1, 1), 0.0)
        return jnp.where(self.y > 0, pltpu.roll(f, 1, 1), 0.0)

    def y_side(self, load, t, step):
        if (t % TY == 0) == (step > 0):
            return load(t + step)
        return self.lanes(load(t - step), step)

    def beside(self, ref, z, lead, t):
        load = self.sliding(ref, z, lead, t)
        near = [self.x(load, t, 1), self.x(load, t, -1)]
        near += [self.y_side(load, t, 1), self.y_side(load, t, -1)]
        return load(t), near + [get(ref, z + 1, *lead, t), get(ref, z - 1, *lead, t)]

    def coarse_beside(self, ref, z, lead, t):
        load = lambda j: get(ref, z, *lead, j)
        f = load(t)
        near = [self.x(load, t, step, TX // 2, 1) for step in (1, -1)]
        near += [self.lanes(f, 1), self.lanes(f, -1)]
        return f, near + [get(ref, z + 2, *lead, t), get(ref, z - 2, *lead, t)]

    def pair_sum(self, f):
        return f + jnp.where(self.row % 2 == 0, pltpu.roll(f, SUB - 1, 0), pltpu.roll(f, 1, 0))


def block_of(t):
    return range(2 * TY * t, 2 * TY * (t + 1))


def tree(terms):
    while len(terms) > 1:
        terms = [sum(terms[k : k + 2]) for k in range(0, len(terms), 2)]
    return terms[0]


def get(ref, z, *index):
    return ref[(*index, pl.ds(z, SUB), slice(None))]


def sweep(lo, hi, body):
    count = (hi - lo) // SUB
    assert count * SUB == hi - lo
    unroll = next(u for u in (3, 2, count) if count % u == 0)

    def step(t):
        late = []

        def store(ref, value, z, *index):
            ref[(*index, pl.ds(z, SUB), slice(None))] = value

        def put(*item):
            late.append(item)
            if len(late) > HELD:
                store(*late.pop(0))

        for u in range(unroll):
            body(t + (lo + u * SUB), put)
        for item in late:
            store(*item)

    if unroll == count:
        step(0)
    else:
        span = unroll * SUB
        lax.fori_loop(0, count // unroll, lambda t, _: (step(pl.multiple_of(t * span, SUB)), 0)[1], 0)


def pack_kernel(geo, heat_in, flow_in, dual_in, kind_in, out, heat, flow, dual, kind, sems):
    b = geo.slab
    pairs = ((heat_in, heat), (flow_in, flow), (dual_in, dual), (kind_in, kind))
    copies = [
        pltpu.make_async_copy(source, target, sems.at[k])
        for k, (source, target) in enumerate(pairs)
    ]
    for copy in copies:
        copy.start()
    for copy in copies:
        copy.wait()
    fields = [heat, flow.at[0], flow.at[1], flow.at[2], dual, kind]
    turned = []
    for ref in fields:
        rows = [ref[x, pl.ds(y, SUB, stride=TY), :] for x, y in geo.order]
        turned.append(jnp.concatenate(rows, 0).astype(jnp.float32).T)
    for j in range(geo.group):
        q = geo.holder[j]
        for f in range(FIELDS):
            out[q, f * b : (f + 1) * b, :] = turned[f][j * b : (j + 1) * b]


def edge_kernel(geo, own, first, last):
    b, e = geo.slab, EDGE
    for q in range(geo.group):
        for out, at in ((first, 0), (last, b - e)):
            rows = [own[q, f * b + at : f * b + at + e, :] for f in range(4)]
            out[q] = jnp.concatenate(rows, 0)


STATIC_FINE = ("s0", "s1", "s2", "hv", "w")
STATIC_COARSE = ("kxp", "kxm", "kyp", "kym", "kzp", "kzm", "wc")
STATIC = STATIC_FINE + STATIC_COARSE


class Static:
    def __init__(self, refs):
        self.refs = dict(zip(STATIC, refs))

    def base(self, name):
        return 0 if name == "hv" else SUB

    def get(self, name, z, *index):
        return get(self.refs[name], z - self.base(name), *index)

    def put(self, put, name, value, z, *index):
        put(self.refs[name], value, z - self.base(name), *index)


def iterate(geo, st, work, seqs, lo, hi, first=(), mean=None):
    v, p, res, cor, cor2, cc0, cc1 = work
    tl = Tiles(geo)
    keep = 1.0 - JACOBI_WEIGHT
    comps = range(3 * len(seqs))
    transposed = len(seqs)

    def faces(t, z):
        h, near = tl.beside(st.refs["hv"], z, (), t)
        return [h + other for other in near]

    def around(face, ref, c, t, z):
        f, near = tl.beside(ref, z, (c,), t)
        return f, tree([a * b for a, b in zip(face, near)])

    def residual(z, put):
        for t in range(SUB):
            w = st.get("w", z, t)
            if FORWARD in seqs and FORWARD not in first:
                face = faces(t, z)
                diag = tree(face)
            for s, q in enumerate(seqs):
                start = q == FORWARD and q in first
                if not start:
                    _, near = tl.beside(p, z, (transposed if q == ADJOINT else s,), t)
                    slope = [0.5 * (near[2 * k] - near[2 * k + 1]) for k in range(3)]
                for k in range(3):
                    c = 3 * s + k
                    if q == FORWARD:
                        value = st.get("s%d" % k, z, t)
                        if not start:
                            f, total = around(face, v, c, t, z)
                            value = value - slope[k] - (diag * f - total)
                    elif q == RESPONSE:
                        value = -slope[k]
                    else:
                        value = slope[k] if q in first else get(cor, z, c, t) + slope[k]
                    put(res, value, z, c, t)
                    put(cor, w * value, z, c, t)

    sweep(lo - 8, hi + 8, residual)

    def restricted(z, put):
        for pair in range(TX // 2):
            left = [0.0 for _ in comps]
            for t in block_of(pair):
                face = faces(t, z)
                for c in comps:
                    _, total = around(face, cor, c, t, z)
                    left[c] = left[c] + (keep * get(res, z, c, t) + total)
            wc = 0.125 * st.get("wc", z, pair)
            for c in comps:
                put(cc0, wc * tl.pair_sum(left[c]), z, c, pair)

    sweep(lo - 8, hi + 8, restricted)

    def coarse_step(ref, c, pair, z):
        f, near = tl.coarse_beside(ref, z, (c,), pair)
        terms = [st.get(name, z, pair) * b for name, b in zip(STATIC_COARSE, near)]
        return tree([get(cc0, z, c, pair), keep * f] + terms)

    def sweep_one(z, put):
        for pair in range(TX // 2):
            for c in comps:
                put(cc1, coarse_step(cc0, c, pair, z), z, c, pair)

    sweep(lo - 4, hi + 4, sweep_one)

    def sweep_two(z, put):
        for pair in range(TX // 2):
            for c in comps:
                value = coarse_step(cc1, c, pair, z)
                for t in block_of(pair):
                    put(cor2, get(cor, z, c, t) + value, z, c, t)

    sweep(lo - 4, hi + 4, sweep_two)

    def velocity(z, put):
        for t in range(SUB):
            face, w = faces(t, z), st.get("w", z, t)
            for c in comps:
                f, total = around(face, cor2, c, t, z)
                value = get(cor, z, c, t) + keep * f + w * total
                if seqs[c // 3] == FORWARD and FORWARD not in first:
                    value = get(v, z, c, t) + value
                put(v, value, z, c, t)

    sweep(lo - 4, hi + 4, velocity)

    def pressure(z, put):
        for t in range(SUB):
            half = st.get("hv", z, t)
            for s, q in enumerate(seqs):
                c = 3 * s
                if q == ADJOINT:
                    face = faces(t, z)
                    diag, div = tree(face), 0.0
                    for k in range(3):
                        f, near = tl.beside(v, z, (c + k,), t)
                        div = div + 0.5 * (near[2 * k] - near[2 * k + 1])
                        total = tree([a * b for a, b in zip(face, near)])
                        put(cor, get(res, z, c + k, t) - (diag * f - total), z, c + k, t)
                    value = get(p, z, s, t) + div
                    put(p, value, z, s, t)
                    put(p, half * value, z, transposed, t)
                    continue
                one, two = tl.sliding(v, z, (c,), t), tl.sliding(v, z, (c + 1,), t)
                div = tl.x(one, t, 1) - tl.x(one, t, -1)
                div = div + (tl.y_side(two, t, 1) - tl.y_side(two, t, -1))
                div = div + (get(v, z + 1, c + 2, t) - get(v, z - 1, c + 2, t))
                value = -(half * (0.5 * div))
                if not (q == FORWARD and q in first):
                    value = get(p, z, s, t) + value
                if mean is not None:
                    value = value - jnp.where(geo.inside(z), mean, 0.0)
                put(p, value, z, s, t)

    sweep(lo, hi, pressure)


def whole_sum(value):
    return jnp.sum(jnp.sum(value, axis=0), axis=(0, 1), keepdims=True)


def product(left, right):
    value = 0.0
    for a, b in zip(left, right):
        value = value + a[...] * b[...]
    return whole_sum(value)


def in_lanes(values, rows):
    lane = lax.broadcasted_iota(jnp.int32, (rows, LANES), 1)
    out = jnp.zeros((rows, LANES), jnp.float32)
    for k, value in values:
        out = jnp.where(lane == k, value, out)
    return out


def setup_kernel(geo, stiffness, own, low, high, low_edge, high_edge, *refs):
    st = Static(refs)
    moved, dual_out, sums, raw, heat, vc, *work = refs[len(STATIC) :]
    v, p, res, cor, cor2, cc0, cc1 = work
    tl = Tiles(geo)
    b, m, n_rows = geo.slab, geo.margin, geo.rows
    granule = geo.block[1]

    def place(t, _):
        groups = []
        for source, base in ((low, m - b), (own, m), (high, m + b)):
            for u in range(0, b, SUB):
                row = pl.multiple_of(t * b, b) + u
                tiles = [source[q, pl.ds(row, SUB), :] for q in range(geo.group)]
                groups.append((base + u, tiles))
        groups = [(row, gather_tiles(tiles, granule)) for row, tiles in groups]
        for row, tiles in groups:
            for x, tile in enumerate(tiles):
                raw[t, x, row : row + SUB, :] = tile
        return 0

    lax.fori_loop(0, FIELDS, place, 0)
    for source, base in ((low_edge, m - b - EDGE), (high_edge, m + 2 * b)):
        tiles = [source[q] for q in range(geo.group)]
        for x, tile in enumerate(gather_tiles(tiles, granule)):
            for f in range(4):
                raw[f, x, base : base + EDGE, :] = tile[f * EDGE : (f + 1) * EDGE]

    def advance(ref, old, new):
        def body(z, put):
            inside = geo.inside(z)
            for t in range(SUB):
                f, near = tl.beside(ref, z, (old,), t)
                drift = 0.0
                for k in range(3):
                    flow = get(raw, z, 1 + k, t)
                    drift = drift + jnp.maximum(flow, 0.0) * (f - near[2 * k + 1])
                    drift = drift + jnp.minimum(flow, 0.0) * (near[2 * k] - f)
                spread = tree(near) - 6.0 * f
                value = f - INCREMENT_DT * drift + INCREMENT_DT * DIFFUSIVITY * spread
                put(heat, jnp.where(inside, value, 0.0), z, new, t)

        return body

    sweep(m - b - 4, m + 2 * b + 4, advance(raw, 0, 0))
    sweep(m - b, m + 2 * b, advance(heat, 0, 1))

    def viscosity(z, put):
        inside = geo.inside(z)
        for pair in range(TX // 2):
            coarse = 0.0
            for t in block_of(pair):
                kind = get(raw, z, 5, t)
                base = jnp.zeros(kind.shape, jnp.float32)
                for layer in range(LAYERS):
                    base = jnp.where(kind == float(layer), stiffness[layer], base)
                value = base * jnp.exp(-ACTIVATION_ENERGY * get(heat, z, 1, t))
                value = jnp.where(inside, value, 0.0)
                st.put(put, "hv", 0.5 * value, z, t)
                coarse = coarse + value
            put(vc, 0.125 * tl.pair_sum(coarse), z, pair)

    sweep(m - b, m + 2 * b, viscosity)

    def statics(z, put):
        inside = geo.inside(z)
        for t in range(SUB):
            h, near = tl.beside(st.refs["hv"], z, (), t)
            diag = tree([h + other for other in near])
            st.put(put, "w", jnp.where(inside, JACOBI_WEIGHT / diag, 0.0), z, t)
            f, near = tl.beside(heat, z, (1,), t)
            dual = -INCREMENT_DT * get(raw, z, 4, t)
            for k in range(3):
                flow = get(raw, z, 1 + k, t)
                step = jnp.where(flow > 0, f - near[2 * k + 1], near[2 * k] - f)
                st.put(put, "s%d" % k, dual * step, z, t)

    sweep(m - b, m + 2 * b, statics)

    def coarse_statics(z, put):
        inside = geo.inside(z)
        for pair in range(TX // 2):
            c, near = tl.coarse_beside(vc, z, (), pair)
            face = [0.25 * (0.5 * (c + o)) for o in near]
            wc = jnp.where(inside, JACOBI_WEIGHT / tree(face), 0.0)
            for name, f in zip(STATIC_COARSE, face):
                st.put(put, name, wc * f, z, pair)
            st.put(put, "wc", wc, z, pair)

    sweep(m - b, m + 2 * b, coarse_statics)

    def transport(z, put):
        for t in range(SUB):
            dual, near = tl.beside(raw, z, (4,), t)
            value = dual + INCREMENT_DT * DIFFUSIVITY * (tree(near) - 6.0 * dual)
            for k in range(3):
                flow, sides = tl.beside(raw, z, (1 + k,), t)
                a = jnp.maximum(flow, 0.0) * dual
                c = jnp.minimum(flow, 0.0) * dual
                ahead = jnp.maximum(sides[2 * k], 0.0) * near[2 * k]
                behind = jnp.minimum(sides[2 * k + 1], 0.0) * near[2 * k + 1]
                value = value - INCREMENT_DT * (a - ahead + behind - c)
            put(moved, value, z - m, t)

    sweep(m, m + b, transport)

    def unit(z, put):
        value = jnp.where(geo.inside(z), 1.0, 0.0)
        for t in range(SUB):
            put(p, value, z, 0, t)
            put(p, st.get("hv", z, t), z, 1, t)

    sweep(0, n_rows, unit)

    mine, rows = slice(m, m + b), slice(m - PHASE, m + b + PHASE)
    iterate(geo, st, work, (ADJOINT,), rows.start, rows.stop, (ADJOINT,))
    for k in range(4):
        dual_out[k] = cor[k, :, rows, :] if k < 3 else p[0, :, rows, :]
    sums_of = [(0, source_product(geo, st, v, 0)), (1, whole_sum(p[0, :, mine, :]))]
    sums[...] = in_lanes(sums_of, sums.shape[0])


def source_product(geo, st, v, first):
    mine = slice(geo.margin, geo.margin + geo.slab)
    held = slice(geo.margin - SUB, geo.margin - SUB + geo.slab)
    left = [st.refs["s%d" % k].at[:, held, :] for k in range(3)]
    return product(left, [v.at[first + k, :, mine, :] for k in range(3)])


def first_kernel(geo, *refs):
    st = Static(refs)
    dual, state, response, later, sums, *work = refs[len(STATIC) :]
    v, p, res, cor = work[:4]
    b, m = geo.slab, geo.margin
    mine, rows = slice(m, m + b), slice(m - PHASE, m + b + PHASE)

    def unit(z, put):
        value = jnp.where(geo.inside(z), 1.0, 0.0)
        for t in range(SUB):
            put(p, value, z, 1, t)

    sweep(0, geo.rows, unit)
    both = (FORWARD, RESPONSE)
    iterate(geo, st, work, both, rows.start, rows.stop, both)
    for k in range(4):
        response[k] = v[3 + k, :, rows, :] if k < 3 else p[1, :, rows, :]
    for k in range(3):
        cor[3 + k, :, rows, :] = dual[k]
    p[1, :, rows, :] = dual[3]
    p[2, :, rows, :] = st.refs["hv"][:, rows, :] * dual[3]
    iterate(geo, st, work, (FORWARD, ADJOINT), m, m + b)
    for k in range(4):
        state[k] = v[k, :, mine, :] if k < 3 else p[0, :, mine, :]
        later[k] = cor[3 + k, :, mine, :] if k < 3 else p[1, :, mine, :]
    sums_of = [(2, source_product(geo, st, v, 3)), (3, whole_sum(p[1, :, mine, :]))]
    sums[...] = in_lanes(sums_of, 1)


def second_kernel(geo, raw, response, dual, later, early, part, state, sums):
    own = slice(PHASE, PHASE + geo.slab)
    m1 = jnp.sum(early[:, 0:1], axis=0, keepdims=True) / geo.cells
    for k in range(4):
        state[k] = raw[k] - m1 * response[k, :, own, :]
    fields = [state.at[k] for k in range(4)]
    near, far = [dual.at[k, :, own, :] for k in range(4)], [later.at[k] for k in range(4)]
    sums_of = [(4, product(near, fields)), (5, product(far, fields))]
    sums[...] = in_lanes(sums_of, sums.shape[0]) + part[...]


def means(geo, early, late):
    row = jnp.sum(early + late, axis=0, keepdims=True) / geo.cells
    c1, l1, c2, l2, l1_x2, l2_x2 = [row[:, k : k + 1] for k in range(6)]
    m2 = c1 + c2 - c1 * l1
    m3 = c1 + l1_x2 - m2 * l1
    m4 = c1 + c2 + l2_x2 - m2 * l2 - m3 * l1
    return m2, m3, m4


def third_kernel(geo, *refs):
    st = Static(refs)
    own, low, high, out, *work = refs[len(STATIC) :]
    v, p = work[:2]
    b, m = geo.slab, geo.margin
    for source, base in ((low, m - b), (own, m), (high, m + b)):
        for k in range(3):
            v[k, :, base : base + b, :] = source[k]
        p[0, :, base : base + b, :] = source[3]
    rows = slice(m - PHASE, m + b + PHASE)
    iterate(geo, st, work, (FORWARD,), rows.start, rows.stop)
    for k in range(4):
        out[k] = v[k, :, rows, :] if k < 3 else p[0, :, rows, :]


def fourth_kernel(geo, *refs):
    st = Static(refs)
    state, response, early, late, moved, out, *work = refs[len(STATIC) :]
    v, p = work[:2]
    b, m = geo.slab, geo.margin
    m2, m3, m4 = means(geo, early[...], late[...])
    rows = slice(m - PHASE, m + b + PHASE)
    for k in range(3):
        v[k, :, rows, :] = state[k] - m2 * response[k]
    shift = jnp.where(geo.inside(rows.start, rows.stop - rows.start), m3, 0.0)
    p[0, :, rows, :] = state[3] - m2 * response[3] - shift[None]
    iterate(geo, st, work, (FORWARD,), m, m + b, mean=m4)
    for u in range(0, b, SUB):
        at = slice(m + u, m + u + SUB)
        columns = range(SUB)
        fields = [[v[k, x, at, :] for x in columns] for k in range(3)]
        fields.append([p[0, x, at, :] for x in columns])
        fields.append([moved[x, u : u + SUB, :] + fields[2][x] for x in columns])
        for f, tiles in enumerate(fields):
            for q, tile in enumerate(scatter_tiles(tiles, geo.block[1])):
                out[q, f * b + u : f * b + u + SUB, :] = tile


def unpack_kernel(geo, chunks, heat, flow, pressure):
    b = geo.slab
    for f, ref in enumerate((flow.at[0], flow.at[1], flow.at[2], pressure, heat)):
        rows = [chunks[geo.holder[j], f * b : (f + 1) * b, :] for j in range(geo.group)]
        block = jnp.concatenate(rows, 0).T
        for k, (x, y) in enumerate(geo.order):
            ref[x, pl.ds(y, SUB, stride=TY), :] = block[k * SUB : (k + 1) * SUB]


def call(kernel, out, scratch, *args, smem=(), hbm=(), limit=VMEM_LIMIT, megabytes=2):
    f32 = jnp.float32
    cost = pl.CostEstimate(
        flops=megabytes * 1000000, bytes_accessed=megabytes * 1000000, transcendentals=0
    )
    specs = [
        pl.BlockSpec(
            memory_space=pltpu.SMEM if i in smem else pltpu.HBM if i in hbm else pltpu.VMEM
        )
        for i in range(len(args))
    ]
    return pl.pallas_call(
        kernel,
        out_shape=[jax.ShapeDtypeStruct(s, f32) for s in out],
        in_specs=specs,
        out_specs=[pl.BlockSpec(memory_space=pltpu.VMEM) for _ in out],
        scratch_shapes=[pltpu.VMEM(s, f32) if isinstance(s, tuple) else s for s in scratch],
        compiler_params=pltpu.CompilerParams(vmem_limit_bytes=limit),
        cost_estimate=cost,
    )(*args)


def slab_shards(geo, heat, flow, dual, kind, stiffness):
    b, group = geo.slab, geo.group
    inputs = (heat, flow, dual, kind)
    (chunks,) = call(
        functools.partial(pack_kernel, geo),
        [(group, FIELDS * b, LANES)],
        [pltpu.VMEM(a.shape, a.dtype) for a in inputs] + [pltpu.SemaphoreType.DMA((4,))],
        *inputs,
        hbm=range(4),
        limit=PACK_LIMIT,
    )
    own = lax.all_to_all(chunks, ("gx", "gy"), 0, 0, tiled=True)
    axes = ("gx", "gy", "gz")
    low = lax.ppermute(own, axes, geo.shifts(1))
    high = lax.ppermute(own, axes, geo.shifts(-1))
    edges = call(functools.partial(edge_kernel, geo), [(group, SUB, LANES)] * 2, [], own)
    high_edge = lax.ppermute(edges[0], axes, geo.shifts(-2))
    low_edge = lax.ppermute(edges[1], axes, geo.shifts(2))

    fine, coarse = (SUB, geo.rows, LANES), (TX // 2, geo.rows, LANES)
    held = geo.rows - 2 * SUB
    static_shapes = [(SUB, geo.rows if name == "hv" else held, LANES) for name in STATIC_FINE]
    static_shapes += [(TX // 2, held, LANES)] * len(STATIC_COARSE)
    slab = (SUB, b, LANES)

    def work(n, more=0):
        fields = [(3 * n, *fine), (n + more, *fine)] + [(3 * n, *fine)] * 3
        return fields + [(3 * n, *coarse)] * 2

    devices = group * geo.nz
    wide = (4, SUB, b + 2 * PHASE, LANES)
    *static, moved, dual_one, early = call(
        functools.partial(setup_kernel, geo),
        static_shapes + [slab, wide, (devices, LANES)],
        [(FIELDS, *fine), (2, *fine), coarse] + work(1, 1),
        stiffness,
        own,
        low,
        high,
        low_edge,
        high_edge,
        smem=(0,),
        megabytes=60,
    )
    early = lax.all_to_all(early, axes, 0, 0, tiled=True)
    raw, response, dual_two, part = call(
        functools.partial(first_kernel, geo),
        [(4, *slab), wide, (4, *slab), (1, LANES)],
        work(2, 1),
        *static,
        dual_one,
        megabytes=40,
    )
    state, late = call(
        functools.partial(second_kernel, geo),
        [(4, *slab), (devices, LANES)],
        [],
        raw,
        response,
        dual_one,
        dual_two,
        early,
        part,
    )
    low_state = lax.ppermute(state, axes, geo.shifts(1))
    high_state = lax.ppermute(state, axes, geo.shifts(-1))
    late = lax.all_to_all(late, axes, 0, 0, tiled=True)
    (state,) = call(
        functools.partial(third_kernel, geo),
        [wide],
        work(1),
        *static,
        state,
        low_state,
        high_state,
        megabytes=30,
    )
    (chunks,) = call(
        functools.partial(fourth_kernel, geo),
        [(group, BACK * b, LANES)],
        work(1),
        *static,
        state,
        response,
        early,
        late,
        moved,
        megabytes=20,
    )
    chunks = lax.all_to_all(chunks, ("gx", "gy"), 0, 0, tiled=True)
    return tuple(
        call(
            functools.partial(unpack_kernel, geo),
            [geo.block, (3, *geo.block), geo.block],
            [],
            chunks,
        )
    )


def solution(mesh):
    in_specs = (
        P("gx", "gy", "gz"),
        P(None, "gx", "gy", "gz"),
        P("gx", "gy", "gz"),
        P("gx", "gy", "gz"),
        P(),
    )
    out_specs = (P("gx", "gy", "gz"), P(None, "gx", "gy", "gz"), P("gx", "gy", "gz"))

    def program(saved_heat_state, *others):
        shape = saved_heat_state.shape
        plan = shards
        if slab_plan_fits(mesh, shape):
            plan = functools.partial(slab_shards, Slabs(mesh, shape))
        return jax.shard_map(
            plan, mesh=mesh, in_specs=in_specs, out_specs=out_specs, check_vma=False
        )(saved_heat_state, *others)

    return program
```

```python
import functools

import jax
import jax.numpy as jnp
from jax import lax
from jax.experimental import pallas as pl
from jax.experimental.pallas import tpu as pltpu
from jax.sharding import PartitionSpec as P

RECOMPUTE = 2
SCHUR_ITERS = 4
COARSE_SWEEPS = 3
LAYERS = 8


INCREMENT_DT = 0.2
DIFFUSIVITY = 0.3
ACTIVATION_ENERGY = 2.3
JACOBI_WEIGHT = 0.7
SCHUR_WEIGHT = 0.5
RAYLEIGH = 1.0


def extended(block, sides, width):
    for axis, dim in sides:
        count = lax.axis_size(axis)
        forward = [(i, i + 1) for i in range(count - 1)]
        backward = [(target, source) for source, target in forward]
        low = lax.ppermute(
            lax.slice_in_dim(block, block.shape[dim] - width, None, axis=dim), axis, forward
        )
        high = lax.ppermute(lax.slice_in_dim(block, 0, width, axis=dim), axis, backward)
        block = jnp.concatenate([low, block, high], axis=dim)
    return block


def neighbours(bordered_array):
    centre = bordered_array[..., 1:-1, 1:-1, 1:-1]
    beside_all = [
        bordered_array[..., 2:, 1:-1, 1:-1],
        bordered_array[..., :-2, 1:-1, 1:-1],
        bordered_array[..., 1:-1, 2:, 1:-1],
        bordered_array[..., 1:-1, :-2, 1:-1],
        bordered_array[..., 1:-1, 1:-1, 2:],
        bordered_array[..., 1:-1, 1:-1, :-2],
    ]
    return (centre, beside_all)


def finest_halo_cells(field):
    return extended(field, (("gx", 1), ("gy", 2), ("gz", 3)), 1)


def deep_halo(field):
    return extended(field, (("gx", 1), ("gy", 2), ("gz", 3)), 2)


def coarse_halo(field):
    return extended(field, (("gx", 1), ("gy", 2), ("gz", 3)), 1)


def march_backward(bordered_array, shallower_adjacent, deeper_adjacent):
    centre, beside_all = neighbours(bordered_array)
    drift = 0.0
    for dim_index in range(3):
        drift = (
            drift
            + shallower_adjacent[dim_index] * (centre - beside_all[2 * dim_index + 1])
            + deeper_adjacent[dim_index] * (beside_all[2 * dim_index] - centre)
        )
    spread = sum(beside_all) - 6.0 * centre
    return centre - INCREMENT_DT * drift + INCREMENT_DT * DIFFUSIVITY * spread


def motion_source(bordered_heat, forward_motion, dual_heat_after):
    centre, beside_all = neighbours(bordered_heat)
    device_pieces = [
        jnp.where(
            forward_motion[dim_index] > 0,
            centre - beside_all[2 * dim_index + 1],
            beside_all[2 * dim_index] - centre,
        )
        for dim_index in range(3)
    ]
    return -INCREMENT_DT * dual_heat_after[None] * jnp.stack(device_pieces)


def advect_dual_heat(pos_padded, neg_padded, lam_padded):
    centre, beside_all = neighbours(lam_padded)
    result = centre + INCREMENT_DT * DIFFUSIVITY * (sum(beside_all) - 6.0 * centre)
    for dim_index in range(3):
        pos_centre, pos_around = neighbours(pos_padded[dim_index])
        neg_centre, neg_around = neighbours(neg_padded[dim_index])
        result = result - INCREMENT_DT * (
            pos_centre - pos_around[2 * dim_index] + neg_around[2 * dim_index + 1] - neg_centre
        )
    return result


def coefficients(bordered_array, factor):
    centre, beside_all = neighbours(bordered_array)
    return [factor * (0.5 * (centre + other)) for other in beside_all]


def apply_operator(face_coef, bordered_array):
    centre, beside_all = neighbours(bordered_array)
    return sum((coef * (centre - other) for coef, other in zip(face_coef, beside_all)))


def gradient(bordered_array):
    centre, beside_all = neighbours(bordered_array)
    return jnp.stack(
        [
            0.5 * (beside_all[2 * dim_index] - beside_all[2 * dim_index + 1])
            for dim_index in range(3)
        ]
    )


def divergence(bordered_array):
    centre, beside_all = neighbours(bordered_array)
    return sum(
        (
            0.5 * (beside_all[2 * dim_index][dim_index] - beside_all[2 * dim_index + 1][dim_index])
            for dim_index in range(3)
        )
    )


def restrict(field):
    leading = field.shape[:-3]
    cells_x, cells_y, cells_z = field.shape[-3:]
    blocks = field.reshape(leading + (cells_x // 2, 2, cells_y // 2, 2, cells_z // 2, 2))
    return blocks.mean(axis=(-5, -3, -1))


def prolong(field):
    return jnp.repeat(jnp.repeat(jnp.repeat(field, 2, axis=-3), 2, axis=-2), 2, axis=-1)


def evaluate_viscosity(rheology_class, class_base_stiffness):
    base = jnp.zeros(rheology_class.shape, jnp.float32)
    for layer_index in range(LAYERS):
        base = base + jnp.where(
            rheology_class == layer_index, class_base_stiffness[layer_index], 0.0
        )
    return base


def inside_mask(extent_first, extent_second, extent_vertical):
    index_x = (
        lax.axis_index("gx") * extent_first + jnp.arange(extent_first + 2, dtype=jnp.int32) - 1
    )
    index_y = (
        lax.axis_index("gy") * extent_second + jnp.arange(extent_second + 2, dtype=jnp.int32) - 1
    )
    index_z = (
        lax.axis_index("gz") * extent_vertical
        + jnp.arange(extent_vertical + 2, dtype=jnp.int32)
        - 1
    )
    inside_x = (index_x >= 0) & (index_x < extent_first * lax.axis_size("gx"))
    inside_y = (index_y >= 0) & (index_y < extent_second * lax.axis_size("gy"))
    inside_z = (index_z >= 0) & (index_z < extent_vertical * lax.axis_size("gz"))
    return inside_x[:, None, None] & inside_y[None, :, None] & inside_z[None, None, :]


def coarse_solve(coarse_res, coarse_coef, coarse_diag, pad_field):
    coarse_corr = JACOBI_WEIGHT * coarse_res / coarse_diag
    for sweep in range(COARSE_SWEEPS - 1):
        coarse_corr = (
            coarse_corr
            + JACOBI_WEIGHT
            * (coarse_res - apply_operator(coarse_coef, pad_field(coarse_corr)))
            / coarse_diag
        )
    return coarse_corr


def shards(saved_heat_state, forward_motion, dual_heat_after, rheology_class, class_base_stiffness):
    extent_first, extent_second, extent_vertical = saved_heat_state.shape
    shallower_adjacent = jnp.maximum(forward_motion, 0.0)
    deeper_adjacent = jnp.minimum(forward_motion, 0.0)
    heat_state = saved_heat_state
    for repeat_index in range(RECOMPUTE):
        heat_state = march_backward(
            finest_halo_cells(heat_state[None])[0], shallower_adjacent, deeper_adjacent
        )
    local_viscosity = evaluate_viscosity(rheology_class, class_base_stiffness) * jnp.exp(
        -ACTIVATION_ENERGY * heat_state
    )
    stacked = jnp.concatenate(
        [
            heat_state[None],
            dual_heat_after[None],
            shallower_adjacent * dual_heat_after[None],
            deeper_adjacent * dual_heat_after[None],
            local_viscosity[None],
        ],
        0,
    )
    bordered_array = finest_halo_cells(stacked)
    driving_source = motion_source(bordered_array[0], forward_motion, dual_heat_after)
    advected_result = advect_dual_heat(bordered_array[2:5], bordered_array[5:8], bordered_array[1])
    face_coef = coefficients(bordered_array[8], 1.0)
    diagonal = sum(face_coef)
    coarse_visc = restrict(local_viscosity)
    coarse_coef = coefficients(coarse_halo(coarse_visc[None])[0], 0.25)
    coarse_diag = sum(coarse_coef)
    deep_static = deep_halo(jnp.concatenate([local_viscosity[None], driving_source], 0))
    cycle_coef = coefficients(deep_static[0], 1.0)
    cycle_source = deep_static[1:4, 1:-1, 1:-1, 1:-1]
    inside = inside_mask(extent_first, extent_second, extent_vertical)
    safe_diag = jnp.where(inside, sum(cycle_coef), 1.0)
    total_cells = (
        extent_first
        * extent_second
        * extent_vertical
        * lax.axis_size("gx")
        * lax.axis_size("gy")
        * lax.axis_size("gz")
    )
    velocity = jnp.zeros(forward_motion.shape, jnp.float32)
    mean_stress = jnp.zeros(saved_heat_state.shape, jnp.float32)
    for iteration in range(SCHUR_ITERS):
        if iteration == 0:
            cycle_resid = cycle_source
        else:
            flow_press = deep_halo(jnp.concatenate([velocity, mean_stress[None]], 0))
            cycle_resid = (
                cycle_source - apply_operator(cycle_coef, flow_press[0:3]) - gradient(flow_press[3])
            )
        cycle_corr = jnp.where(inside, JACOBI_WEIGHT * cycle_resid / safe_diag, 0.0)
        residual = cycle_resid[:, 1:-1, 1:-1, 1:-1]
        correction = cycle_corr[:, 1:-1, 1:-1, 1:-1]
        residual_two = residual - apply_operator(face_coef, cycle_corr)
        coarse_res = restrict(residual_two)
        coarse_corr = coarse_solve(coarse_res, coarse_coef, coarse_diag, coarse_halo)
        correction = correction + prolong(coarse_corr)
        correction = (
            correction
            + JACOBI_WEIGHT
            * (residual - apply_operator(face_coef, finest_halo_cells(correction)))
            / diagonal
        )
        velocity = velocity + correction
        spread_flow = divergence(finest_halo_cells(velocity))
        mean_stress = mean_stress - SCHUR_WEIGHT * local_viscosity * spread_flow
        mean_stress = mean_stress - lax.psum(jnp.sum(mean_stress), ("gx", "gy", "gz")) / total_cells
    adj_temp_prev = advected_result + RAYLEIGH * velocity[2]
    return (adj_temp_prev, velocity, mean_stress)


SUB = 8
LANES = 128
FIELDS = 6
BACK = 5
EDGE = 2
PHASE = 8
HELD = 24
TX, TY = 4, 2
VMEM_LIMIT = 32 * 1024 * 1024
PACK_LIMIT = 60 * 1024 * 1024
FORWARD, ADJOINT, RESPONSE = range(3)


def slab_plan_fits(mesh, shape):
    sizes = mesh.shape
    group = sizes["gx"] * sizes["gy"]
    block = (shape[0] // sizes["gx"], shape[1] // sizes["gy"], shape[2] // sizes["gz"])
    return (
        group == SUB
        and block[0] == SUB
        and block[0] * block[1] == LANES
        and block[1] * group == LANES
        and block[2] == LANES
        and block[2] == group * 2 * PHASE
    )


class Slabs:
    def __init__(self, mesh, shape):
        self.nx, self.ny, self.nz = mesh.shape["gx"], mesh.shape["gy"], mesh.shape["gz"]
        self.group = self.nx * self.ny
        self.width, self.breadth, self.height = shape
        self.block = (shape[0] // self.nx, shape[1] // self.ny, shape[2] // self.nz)
        self.slab = self.block[2] // self.group
        self.margin = self.slab + SUB
        self.rows = self.slab + 2 * self.margin
        self.cells = self.width * self.breadth * self.height
        self.place = []
        for ix in range(self.nx):
            for iy in range(self.ny):
                step = ix if iy % 2 == 0 else self.nx - 1 - ix
                self.place.append(iy * self.nx + step)
        self.order = [
            (x + TX * part, y)
            for x in range(TX)
            for y in range(TY)
            for part in range(self.block[0] // TX)
        ]
        self.holder = [self.place.index(j) for j in range(self.group)]

    def device(self, slab):
        return self.holder[slab % self.group] * self.nz + slab // self.group

    def shifts(self, distance):
        count = self.group * self.nz
        return [
            (self.device(p), self.device(p + distance))
            for p in range(count)
            if 0 <= p + distance < count
        ]

    def index(self):
        ix, iy = lax.axis_index("gx"), lax.axis_index("gy")
        step = jnp.where(iy % 2 == 0, ix, self.nx - 1 - ix)
        return lax.axis_index("gz") * self.group + iy * self.nx + step

    def inside(self, z, n=SUB):
        layer = self.index() * self.slab - self.margin + z
        layer = layer + lax.broadcasted_iota(jnp.int32, (n, LANES), 0)
        return (layer >= 0) & (layer < self.height)


def exchange(tiles, bit, width):
    lane = lax.broadcasted_iota(jnp.int32, (SUB, LANES), 1)
    low = (lane & width) == 0
    new = list(tiles)
    for a in range(SUB):
        if not a & bit:
            b = a | bit
            new[a] = jnp.where(low, tiles[a], pltpu.roll(tiles[b], width, 1))
            new[b] = jnp.where(low, pltpu.roll(tiles[a], LANES - width, 1), tiles[b])
    return new


def gather_tiles(tiles, granule):
    for bit, width in ((1, granule // 2), (1, granule), (2, 2 * granule), (4, 4 * granule)):
        tiles = exchange(tiles, bit, width)
    return tiles


def scatter_tiles(tiles, granule):
    for bit, width in ((4, 4 * granule), (2, 2 * granule), (1, granule), (1, granule // 2)):
        tiles = exchange(tiles, bit, width)
    return tiles


class Tiles:
    def __init__(self, geo):
        self.span = geo.breadth // TY
        self.row = lax.broadcasted_iota(jnp.int32, (SUB, LANES), 0)
        self.lane = lax.broadcasted_iota(jnp.int32, (SUB, LANES), 1)
        self.y = self.lane % self.span
        self.kept, self.latest, self.sweep = {}, None, 0

    def sliding(self, ref, z, lead, t):
        if self.latest != (self.sweep, z):
            self.latest, self.kept = (self.sweep, z), {}
        where = (id(ref), lead)
        for key in [k for k in self.kept if k[:2] == where and abs(k[2] - t) > 3]:
            del self.kept[key]

        def load(j):
            key = (*where, j)
            if key not in self.kept:
                self.kept[key] = (ref, get(ref, z, *lead, j))
            return self.kept[key][1]

        return load

    def x(self, load, t, step, count=TX, stride=TY):
        j = t // stride + step
        if 0 <= j < count:
            return load(t + step * stride)
        if step > 0:
            turned = pltpu.roll(load(t % stride), LANES - self.span, 1)
            return jnp.where(self.lane < LANES - self.span, turned, 0.0)
        turned = pltpu.roll(load((count - 1) * stride + t % stride), self.span, 1)
        return jnp.where(self.lane >= self.span, turned, 0.0)

    def lanes(self, f, step):
        if step > 0:
            return jnp.where(self.y < self.span - 1, pltpu.roll(f, LANES - 1, 1), 0.0)
        return jnp.where(self.y > 0, pltpu.roll(f, 1, 1), 0.0)

    def y_side(self, load, t, step):
        if (t % TY == 0) == (step > 0):
            return load(t + step)
        return self.lanes(load(t - step), step)

    def beside(self, ref, z, lead, t):
        load = self.sliding(ref, z, lead, t)
        near = [self.x(load, t, 1), self.x(load, t, -1)]
        near += [self.y_side(load, t, 1), self.y_side(load, t, -1)]
        return load(t), near + [get(ref, z + 1, *lead, t), get(ref, z - 1, *lead, t)]

    def coarse_beside(self, ref, z, lead, t):
        load = lambda j: get(ref, z, *lead, j)
        f = load(t)
        near = [self.x(load, t, step, TX // 2, 1) for step in (1, -1)]
        near += [self.lanes(f, 1), self.lanes(f, -1)]
        return f, near + [get(ref, z + 2, *lead, t), get(ref, z - 2, *lead, t)]

    def pair_sum(self, f):
        return f + jnp.where(self.row % 2 == 0, pltpu.roll(f, SUB - 1, 0), pltpu.roll(f, 1, 0))


def block_of(t):
    return range(2 * TY * t, 2 * TY * (t + 1))


def tree(terms):
    while len(terms) > 1:
        terms = [sum(terms[k : k + 2]) for k in range(0, len(terms), 2)]
    return terms[0]


def get(ref, z, *index):
    return ref[(*index, pl.ds(z, SUB), slice(None))]


def sweep(tl, lo, hi, body):
    tl.sweep += 1
    late = []

    def store(ref, value, z, *index):
        ref[(*index, pl.ds(z, SUB), slice(None))] = value

    def put(*item):
        late.append(item)
        if len(late) > HELD:
            store(*late.pop(0))

    for z in range(lo, hi, SUB):
        body(z, put)
    for item in late:
        store(*item)


def pack_kernel(geo, heat_in, flow_in, dual_in, kind_in, out, heat, flow, dual, kind, sems):
    b = geo.slab
    pairs = ((heat_in, heat), (flow_in, flow), (dual_in, dual), (kind_in, kind))
    copies = [
        pltpu.make_async_copy(source, target, sems.at[k])
        for k, (source, target) in enumerate(pairs)
    ]
    for copy in copies:
        copy.start()
    fields = [heat, flow.at[0], flow.at[1], flow.at[2], dual, kind]
    for f, (ref, copy) in enumerate(zip(fields, (0, 1, None, None, 2, 3))):
        if copy is not None:
            copies[copy].wait()
        rows = [ref[x, pl.ds(y, SUB, stride=TY), :] for x, y in geo.order]
        turned = jnp.concatenate(rows, 0).astype(jnp.float32).T
        for j in range(geo.group):
            out[geo.holder[j], f * b : (f + 1) * b, :] = turned[j * b : (j + 1) * b]


def edge_kernel(geo, own, first, last):
    b, e = geo.slab, EDGE
    for q in range(geo.group):
        for out, at in ((first, 0), (last, b - e)):
            rows = [own[q, f * b + at : f * b + at + e, :] for f in range(4)]
            out[q] = jnp.concatenate(rows, 0)


STATIC_FINE = ("s0", "s1", "s2", "hv", "w")
STATIC_COARSE = ("kxp", "kxm", "kyp", "kym", "kzp", "kzm", "wc")
STATIC = STATIC_FINE + STATIC_COARSE


class Static:
    def __init__(self, refs):
        self.refs = dict(zip(STATIC, refs))

    def base(self, name):
        return 0 if name == "hv" else SUB

    def get(self, name, z, *index):
        return get(self.refs[name], z - self.base(name), *index)

    def put(self, put, name, value, z, *index):
        put(self.refs[name], value, z - self.base(name), *index)


def iterate(geo, st, work, seqs, lo, hi, first=(), mean=None):
    v, p, res, cor, cor2, cc0, cc1 = work
    tl = Tiles(geo)
    keep = 1.0 - JACOBI_WEIGHT
    comps = range(3 * len(seqs))
    transposed = len(seqs)

    def faces(t, z):
        h, near = tl.beside(st.refs["hv"], z, (), t)
        return [h + other for other in near]

    def around(face, ref, c, t, z):
        f, near = tl.beside(ref, z, (c,), t)
        return f, tree([a * b for a, b in zip(face, near)])

    def residual(z, put):
        for t in range(SUB):
            w = st.get("w", z, t)
            if FORWARD in seqs and FORWARD not in first:
                face = faces(t, z)
                diag = tree(face)
            for s, q in enumerate(seqs):
                start = q == FORWARD and q in first
                if not start:
                    _, near = tl.beside(p, z, (transposed if q == ADJOINT else s,), t)
                    slope = [0.5 * (near[2 * k] - near[2 * k + 1]) for k in range(3)]
                for k in range(3):
                    c = 3 * s + k
                    if q == FORWARD:
                        value = st.get("s%d" % k, z, t)
                        if not start:
                            f, total = around(face, v, c, t, z)
                            value = value - slope[k] - (diag * f - total)
                    elif q == RESPONSE:
                        value = -slope[k]
                    else:
                        value = slope[k] if q in first else get(cor, z, c, t) + slope[k]
                    put(res, value, z, c, t)
                    put(cor, w * value, z, c, t)

    sweep(tl, lo - 8, hi + 8, residual)

    def restricted(z, put):
        for pair in range(TX // 2):
            left = [0.0 for _ in comps]
            for t in block_of(pair):
                face = faces(t, z)
                for c in comps:
                    _, total = around(face, cor, c, t, z)
                    left[c] = left[c] + (keep * get(res, z, c, t) + total)
            wc = 0.125 * st.get("wc", z, pair)
            for c in comps:
                put(cc0, wc * tl.pair_sum(left[c]), z, c, pair)

    sweep(tl, lo - 8, hi + 8, restricted)

    def coarse_step(ref, c, pair, z):
        f, near = tl.coarse_beside(ref, z, (c,), pair)
        terms = [st.get(name, z, pair) * b for name, b in zip(STATIC_COARSE, near)]
        return tree([get(cc0, z, c, pair), keep * f] + terms)

    def sweep_one(z, put):
        for pair in range(TX // 2):
            for c in comps:
                put(cc1, coarse_step(cc0, c, pair, z), z, c, pair)

    sweep(tl, lo - 4, hi + 4, sweep_one)

    def sweep_two(z, put):
        for pair in range(TX // 2):
            for c in comps:
                value = coarse_step(cc1, c, pair, z)
                for t in block_of(pair):
                    put(cor2, get(cor, z, c, t) + value, z, c, t)

    sweep(tl, lo - 4, hi + 4, sweep_two)

    def velocity(z, put):
        for t in range(SUB):
            face, w = faces(t, z), st.get("w", z, t)
            for c in comps:
                f, total = around(face, cor2, c, t, z)
                value = get(cor, z, c, t) + keep * f + w * total
                if seqs[c // 3] == FORWARD and FORWARD not in first:
                    value = get(v, z, c, t) + value
                put(v, value, z, c, t)

    sweep(tl, lo - 4, hi + 4, velocity)

    def pressure(z, put):
        for t in range(SUB):
            half = st.get("hv", z, t)
            for s, q in enumerate(seqs):
                c = 3 * s
                if q == ADJOINT:
                    face = faces(t, z)
                    diag, div = tree(face), 0.0
                    for k in range(3):
                        f, near = tl.beside(v, z, (c + k,), t)
                        div = div + 0.5 * (near[2 * k] - near[2 * k + 1])
                        total = tree([a * b for a, b in zip(face, near)])
                        put(cor, get(res, z, c + k, t) - (diag * f - total), z, c + k, t)
                    value = get(p, z, s, t) + div
                    put(p, value, z, s, t)
                    put(p, half * value, z, transposed, t)
                    continue
                one, two = tl.sliding(v, z, (c,), t), tl.sliding(v, z, (c + 1,), t)
                div = tl.x(one, t, 1) - tl.x(one, t, -1)
                div = div + (tl.y_side(two, t, 1) - tl.y_side(two, t, -1))
                div = div + (get(v, z + 1, c + 2, t) - get(v, z - 1, c + 2, t))
                value = -(half * (0.5 * div))
                if not (q == FORWARD and q in first):
                    value = get(p, z, s, t) + value
                if mean is not None:
                    value = value - jnp.where(geo.inside(z), mean, 0.0)
                put(p, value, z, s, t)

    sweep(tl, lo, hi, pressure)


def whole_sum(value):
    return jnp.sum(jnp.sum(value, axis=0), axis=(0, 1), keepdims=True)


def product(left, right):
    value = 0.0
    for a, b in zip(left, right):
        value = value + a[...] * b[...]
    return whole_sum(value)


def in_lanes(values, rows):
    lane = lax.broadcasted_iota(jnp.int32, (rows, LANES), 1)
    out = jnp.zeros((rows, LANES), jnp.float32)
    for k, value in values:
        out = jnp.where(lane == k, value, out)
    return out


def setup_kernel(geo, stiffness, own, low, high, low_edge, high_edge, *refs):
    st = Static(refs)
    moved, dual_out, sums, raw, heat, vc, *work = refs[len(STATIC) :]
    v, p, res, cor, cor2, cc0, cc1 = work
    tl = Tiles(geo)
    b, m, n_rows = geo.slab, geo.margin, geo.rows
    granule = geo.block[1]

    def place(t, _):
        groups = []
        for source, base in ((low, m - b), (own, m), (high, m + b)):
            for u in range(0, b, SUB):
                row = pl.multiple_of(t * b, b) + u
                tiles = [source[q, pl.ds(row, SUB), :] for q in range(geo.group)]
                groups.append((base + u, tiles))
        groups = [(row, gather_tiles(tiles, granule)) for row, tiles in groups]
        for row, tiles in groups:
            for x, tile in enumerate(tiles):
                raw[t, x, row : row + SUB, :] = tile
        return 0

    lax.fori_loop(0, FIELDS, place, 0)
    for source, base in ((low_edge, m - b - EDGE), (high_edge, m + 2 * b)):
        tiles = [source[q] for q in range(geo.group)]
        for x, tile in enumerate(gather_tiles(tiles, granule)):
            for f in range(4):
                raw[f, x, base : base + EDGE, :] = tile[f * EDGE : (f + 1) * EDGE]

    def advance(ref, old, new):
        def body(z, put):
            inside = geo.inside(z)
            for t in range(SUB):
                f, near = tl.beside(ref, z, (old,), t)
                drift = 0.0
                for k in range(3):
                    flow = get(raw, z, 1 + k, t)
                    drift = drift + jnp.maximum(flow, 0.0) * (f - near[2 * k + 1])
                    drift = drift + jnp.minimum(flow, 0.0) * (near[2 * k] - f)
                spread = tree(near) - 6.0 * f
                value = f - INCREMENT_DT * drift + INCREMENT_DT * DIFFUSIVITY * spread
                put(heat, jnp.where(inside, value, 0.0), z, new, t)

        return body

    sweep(tl, m - b - 4, m + 2 * b + 4, advance(raw, 0, 0))
    sweep(tl, m - b, m + 2 * b, advance(heat, 0, 1))

    def viscosity(z, put):
        inside = geo.inside(z)
        for pair in range(TX // 2):
            coarse = 0.0
            for t in block_of(pair):
                kind = get(raw, z, 5, t)
                base = jnp.zeros(kind.shape, jnp.float32)
                for layer in range(LAYERS):
                    base = jnp.where(kind == float(layer), stiffness[layer], base)
                value = base * jnp.exp(-ACTIVATION_ENERGY * get(heat, z, 1, t))
                value = jnp.where(inside, value, 0.0)
                st.put(put, "hv", 0.5 * value, z, t)
                coarse = coarse + value
            put(vc, 0.125 * tl.pair_sum(coarse), z, pair)

    sweep(tl, m - b, m + 2 * b, viscosity)

    def statics(z, put):
        inside = geo.inside(z)
        for t in range(SUB):
            h, near = tl.beside(st.refs["hv"], z, (), t)
            diag = tree([h + other for other in near])
            st.put(put, "w", jnp.where(inside, JACOBI_WEIGHT / diag, 0.0), z, t)
            f, near = tl.beside(heat, z, (1,), t)
            dual = -INCREMENT_DT * get(raw, z, 4, t)
            for k in range(3):
                flow = get(raw, z, 1 + k, t)
                step = jnp.where(flow > 0, f - near[2 * k + 1], near[2 * k] - f)
                st.put(put, "s%d" % k, dual * step, z, t)

    sweep(tl, m - b, m + 2 * b, statics)

    def coarse_statics(z, put):
        inside = geo.inside(z)
        for pair in range(TX // 2):
            c, near = tl.coarse_beside(vc, z, (), pair)
            face = [0.25 * (0.5 * (c + o)) for o in near]
            wc = jnp.where(inside, JACOBI_WEIGHT / tree(face), 0.0)
            for name, f in zip(STATIC_COARSE, face):
                st.put(put, name, wc * f, z, pair)
            st.put(put, "wc", wc, z, pair)

    sweep(tl, m - b, m + 2 * b, coarse_statics)

    def transport(z, put):
        for t in range(SUB):
            dual, near = tl.beside(raw, z, (4,), t)
            value = dual + INCREMENT_DT * DIFFUSIVITY * (tree(near) - 6.0 * dual)
            for k in range(3):
                flow, sides = tl.beside(raw, z, (1 + k,), t)
                a = jnp.maximum(flow, 0.0) * dual
                c = jnp.minimum(flow, 0.0) * dual
                ahead = jnp.maximum(sides[2 * k], 0.0) * near[2 * k]
                behind = jnp.minimum(sides[2 * k + 1], 0.0) * near[2 * k + 1]
                value = value - INCREMENT_DT * (a - ahead + behind - c)
            put(moved, value, z - m, t)

    sweep(tl, m, m + b, transport)

    def unit(z, put):
        value = jnp.where(geo.inside(z), 1.0, 0.0)
        for t in range(SUB):
            put(p, value, z, 0, t)
            put(p, st.get("hv", z, t), z, 1, t)

    sweep(tl, 0, n_rows, unit)

    mine, rows = slice(m, m + b), slice(m - PHASE, m + b + PHASE)
    iterate(geo, st, work, (ADJOINT,), rows.start, rows.stop, (ADJOINT,))
    for k in range(4):
        dual_out[k] = cor[k, :, rows, :] if k < 3 else p[0, :, rows, :]
    sums_of = [(0, source_product(geo, st, v, 0)), (1, whole_sum(p[0, :, mine, :]))]
    sums[...] = in_lanes(sums_of, sums.shape[0])


def source_product(geo, st, v, first):
    mine = slice(geo.margin, geo.margin + geo.slab)
    held = slice(geo.margin - SUB, geo.margin - SUB + geo.slab)
    left = [st.refs["s%d" % k].at[:, held, :] for k in range(3)]
    return product(left, [v.at[first + k, :, mine, :] for k in range(3)])


def first_kernel(geo, *refs):
    st = Static(refs)
    dual, state, response, sums, later, *work = refs[len(STATIC) :]
    v, p, res, cor = work[:4]
    b, m = geo.slab, geo.margin
    mine, rows = slice(m, m + b), slice(m - PHASE, m + b + PHASE)
    tl = Tiles(geo)

    def unit(z, put):
        value = jnp.where(geo.inside(z), 1.0, 0.0)
        for t in range(SUB):
            put(p, value, z, 1, t)

    sweep(tl, 0, geo.rows, unit)
    both = (FORWARD, RESPONSE)
    iterate(geo, st, work, both, rows.start, rows.stop, both)
    for k in range(4):
        response[k] = v[3 + k, :, rows, :] if k < 3 else p[1, :, rows, :]
    for k in range(3):
        cor[3 + k, :, rows, :] = dual[k]
    p[1, :, rows, :] = dual[3]
    p[2, :, rows, :] = st.refs["hv"][:, rows, :] * dual[3]
    iterate(geo, st, work, (FORWARD, ADJOINT), m, m + b)
    for k in range(4):
        state[k] = v[k, :, mine, :] if k < 3 else p[0, :, mine, :]
        later[k] = cor[3 + k, :, mine, :] if k < 3 else p[1, :, mine, :]
    own = slice(PHASE, PHASE + b)
    near, far = [dual.at[k, :, own, :] for k in range(4)], [later.at[k] for k in range(4)]
    fields, turn = [state.at[k] for k in range(4)], [response.at[k, :, own, :] for k in range(4)]
    sums_of = [(2, source_product(geo, st, v, 3)), (3, whole_sum(p[1, :, mine, :]))]
    sums_of += [(4, product(near, fields)), (5, product(far, fields)), (6, product(far, turn))]
    sums[...] = in_lanes(sums_of, sums.shape[0])


def second_kernel(geo, raw, response, early, state):
    own = slice(PHASE, PHASE + geo.slab)
    m1 = jnp.sum(early[...], axis=0, keepdims=True)[:, 0:1] / geo.cells
    for k in range(4):
        state[k] = raw[k] - m1 * response[k, :, own, :]


def means(geo, early, late):
    row = jnp.sum(early + late, axis=0, keepdims=True) / geo.cells
    c1, l1, c2, l2, l1_x2, l2_x2, l2_r1 = [row[:, k : k + 1] for k in range(7)]
    m2 = c1 + c2 - c1 * l1
    m3 = c1 + (l1_x2 - c1 * l2) - m2 * l1
    m4 = c1 + c2 + (l2_x2 - c1 * l2_r1) - m2 * l2 - m3 * l1
    return m2, m3, m4


def third_kernel(geo, *refs):
    st = Static(refs)
    own, low, high, out, *work = refs[len(STATIC) :]
    v, p = work[:2]
    b, m = geo.slab, geo.margin
    for source, base in ((low, m - b), (own, m), (high, m + b)):
        for k in range(3):
            v[k, :, base : base + b, :] = source[k]
        p[0, :, base : base + b, :] = source[3]
    rows = slice(m - PHASE, m + b + PHASE)
    iterate(geo, st, work, (FORWARD,), rows.start, rows.stop)
    for k in range(4):
        out[k] = v[k, :, rows, :] if k < 3 else p[0, :, rows, :]


def fourth_kernel(geo, *refs):
    st = Static(refs)
    state, response, early, late, moved, out, *work = refs[len(STATIC) :]
    v, p = work[:2]
    b, m = geo.slab, geo.margin
    m2, m3, m4 = means(geo, early[...], late[...])
    rows = slice(m - PHASE, m + b + PHASE)
    for k in range(3):
        v[k, :, rows, :] = state[k] - m2 * response[k]
    shift = jnp.where(geo.inside(rows.start, rows.stop - rows.start), m3, 0.0)
    p[0, :, rows, :] = state[3] - m2 * response[3] - shift[None]
    iterate(geo, st, work, (FORWARD,), m, m + b, mean=m4)
    for u in range(0, b, SUB):
        at = slice(m + u, m + u + SUB)
        columns = range(SUB)
        fields = [[v[k, x, at, :] for x in columns] for k in range(3)]
        fields.append([p[0, x, at, :] for x in columns])
        fields.append([moved[x, u : u + SUB, :] + fields[2][x] for x in columns])
        for f, tiles in enumerate(fields):
            for q, tile in enumerate(scatter_tiles(tiles, geo.block[1])):
                out[q, f * b + u : f * b + u + SUB, :] = tile


def unpack_kernel(geo, chunks, heat, flow, pressure):
    b = geo.slab
    for f, ref in enumerate((flow.at[0], flow.at[1], flow.at[2], pressure, heat)):
        rows = [chunks[geo.holder[j], f * b : (f + 1) * b, :] for j in range(geo.group)]
        block = jnp.concatenate(rows, 0).T
        for k, (x, y) in enumerate(geo.order):
            ref[x, pl.ds(y, SUB, stride=TY), :] = block[k * SUB : (k + 1) * SUB]


def call(kernel, out, scratch, *args, smem=(), hbm=(), limit=VMEM_LIMIT, megabytes=2):
    f32 = jnp.float32
    cost = pl.CostEstimate(
        flops=megabytes * 1000000, bytes_accessed=megabytes * 1000000, transcendentals=0
    )
    specs = [
        pl.BlockSpec(
            memory_space=pltpu.SMEM if i in smem else pltpu.HBM if i in hbm else pltpu.VMEM
        )
        for i in range(len(args))
    ]
    return pl.pallas_call(
        kernel,
        out_shape=[jax.ShapeDtypeStruct(s, f32) for s in out],
        in_specs=specs,
        out_specs=[pl.BlockSpec(memory_space=pltpu.VMEM) for _ in out],
        scratch_shapes=[pltpu.VMEM(s, f32) if isinstance(s, tuple) else s for s in scratch],
        compiler_params=pltpu.CompilerParams(vmem_limit_bytes=limit),
        cost_estimate=cost,
    )(*args)


def slab_shards(geo, heat, flow, dual, kind, stiffness):
    b, group = geo.slab, geo.group
    inputs = (heat, flow, dual, kind)
    (chunks,) = call(
        functools.partial(pack_kernel, geo),
        [(group, FIELDS * b, LANES)],
        [pltpu.VMEM(a.shape, a.dtype) for a in inputs] + [pltpu.SemaphoreType.DMA((4,))],
        *inputs,
        hbm=range(4),
        limit=PACK_LIMIT,
    )
    own = lax.all_to_all(chunks, ("gx", "gy"), 0, 0, tiled=True)
    axes = ("gx", "gy", "gz")
    low = lax.ppermute(own, axes, geo.shifts(1))
    high = lax.ppermute(own, axes, geo.shifts(-1))
    edges = call(functools.partial(edge_kernel, geo), [(group, SUB, LANES)] * 2, [], own)
    high_edge = lax.ppermute(edges[0], axes, geo.shifts(-2))
    low_edge = lax.ppermute(edges[1], axes, geo.shifts(2))

    fine, coarse = (SUB, geo.rows, LANES), (TX // 2, geo.rows, LANES)
    held = geo.rows - 2 * SUB
    static_shapes = [(SUB, geo.rows if name == "hv" else held, LANES) for name in STATIC_FINE]
    static_shapes += [(TX // 2, held, LANES)] * len(STATIC_COARSE)
    slab = (SUB, b, LANES)

    def work(n, more=0):
        fields = [(3 * n, *fine), (n + more, *fine)] + [(3 * n, *fine)] * 3
        return fields + [(3 * n, *coarse)] * 2

    devices = group * geo.nz
    wide = (4, SUB, b + 2 * PHASE, LANES)
    *static, moved, dual_one, early = call(
        functools.partial(setup_kernel, geo),
        static_shapes + [slab, wide, (devices, LANES)],
        [(FIELDS, *fine), (2, *fine), coarse] + work(1, 1),
        stiffness,
        own,
        low,
        high,
        low_edge,
        high_edge,
        smem=(0,),
        megabytes=60,
    )
    early = lax.all_to_all(early, axes, 0, 0, tiled=True)
    raw, response, late = call(
        functools.partial(first_kernel, geo),
        [(4, *slab), wide, (devices, LANES)],
        [(4, *slab)] + work(2, 1),
        *static,
        dual_one,
        megabytes=40,
    )
    late = lax.all_to_all(late, axes, 0, 0, tiled=True)
    (state,) = call(
        functools.partial(second_kernel, geo), [(4, *slab)], [], raw, response, early
    )
    low_state = lax.ppermute(state, axes, geo.shifts(1))
    high_state = lax.ppermute(state, axes, geo.shifts(-1))
    (state,) = call(
        functools.partial(third_kernel, geo),
        [wide],
        work(1),
        *static,
        state,
        low_state,
        high_state,
        megabytes=30,
    )
    (chunks,) = call(
        functools.partial(fourth_kernel, geo),
        [(group, BACK * b, LANES)],
        work(1),
        *static,
        state,
        response,
        early,
        late,
        moved,
        megabytes=20,
    )
    chunks = lax.all_to_all(chunks, ("gx", "gy"), 0, 0, tiled=True)
    return tuple(
        call(
            functools.partial(unpack_kernel, geo),
            [geo.block, (3, *geo.block), geo.block],
            [],
            chunks,
        )
    )


def solution(mesh):
    in_specs = (
        P("gx", "gy", "gz"),
        P(None, "gx", "gy", "gz"),
        P("gx", "gy", "gz"),
        P("gx", "gy", "gz"),
        P(),
    )
    out_specs = (P("gx", "gy", "gz"), P(None, "gx", "gy", "gz"), P("gx", "gy", "gz"))

    def program(saved_heat_state, *others):
        shape = saved_heat_state.shape
        plan = shards
        if slab_plan_fits(mesh, shape):
            plan = functools.partial(slab_shards, Slabs(mesh, shape))
        return jax.shard_map(
            plan, mesh=mesh, in_specs=in_specs, out_specs=out_specs, check_vma=False
        )(saved_heat_state, *others)

    return program
```

```python
import functools

import jax
import jax.numpy as jnp
from jax import lax
from jax.experimental import pallas as pl
from jax.experimental.pallas import tpu as pltpu
from jax.sharding import PartitionSpec as P

RECOMPUTE = 2
SCHUR_ITERS = 4
COARSE_SWEEPS = 3
LAYERS = 8


INCREMENT_DT = 0.2
DIFFUSIVITY = 0.3
ACTIVATION_ENERGY = 2.3
JACOBI_WEIGHT = 0.7
SCHUR_WEIGHT = 0.5
RAYLEIGH = 1.0


def extended(block, sides, width):
    for axis, dim in sides:
        count = lax.axis_size(axis)
        forward = [(i, i + 1) for i in range(count - 1)]
        backward = [(target, source) for source, target in forward]
        low = lax.ppermute(
            lax.slice_in_dim(block, block.shape[dim] - width, None, axis=dim), axis, forward
        )
        high = lax.ppermute(lax.slice_in_dim(block, 0, width, axis=dim), axis, backward)
        block = jnp.concatenate([low, block, high], axis=dim)
    return block


def neighbours(bordered_array):
    centre = bordered_array[..., 1:-1, 1:-1, 1:-1]
    beside_all = [
        bordered_array[..., 2:, 1:-1, 1:-1],
        bordered_array[..., :-2, 1:-1, 1:-1],
        bordered_array[..., 1:-1, 2:, 1:-1],
        bordered_array[..., 1:-1, :-2, 1:-1],
        bordered_array[..., 1:-1, 1:-1, 2:],
        bordered_array[..., 1:-1, 1:-1, :-2],
    ]
    return (centre, beside_all)


def finest_halo_cells(field):
    return extended(field, (("gx", 1), ("gy", 2), ("gz", 3)), 1)


def deep_halo(field):
    return extended(field, (("gx", 1), ("gy", 2), ("gz", 3)), 2)


def coarse_halo(field):
    return extended(field, (("gx", 1), ("gy", 2), ("gz", 3)), 1)


def march_backward(bordered_array, shallower_adjacent, deeper_adjacent):
    centre, beside_all = neighbours(bordered_array)
    drift = 0.0
    for dim_index in range(3):
        drift = (
            drift
            + shallower_adjacent[dim_index] * (centre - beside_all[2 * dim_index + 1])
            + deeper_adjacent[dim_index] * (beside_all[2 * dim_index] - centre)
        )
    spread = sum(beside_all) - 6.0 * centre
    return centre - INCREMENT_DT * drift + INCREMENT_DT * DIFFUSIVITY * spread


def motion_source(bordered_heat, forward_motion, dual_heat_after):
    centre, beside_all = neighbours(bordered_heat)
    device_pieces = [
        jnp.where(
            forward_motion[dim_index] > 0,
            centre - beside_all[2 * dim_index + 1],
            beside_all[2 * dim_index] - centre,
        )
        for dim_index in range(3)
    ]
    return -INCREMENT_DT * dual_heat_after[None] * jnp.stack(device_pieces)


def advect_dual_heat(pos_padded, neg_padded, lam_padded):
    centre, beside_all = neighbours(lam_padded)
    result = centre + INCREMENT_DT * DIFFUSIVITY * (sum(beside_all) - 6.0 * centre)
    for dim_index in range(3):
        pos_centre, pos_around = neighbours(pos_padded[dim_index])
        neg_centre, neg_around = neighbours(neg_padded[dim_index])
        result = result - INCREMENT_DT * (
            pos_centre - pos_around[2 * dim_index] + neg_around[2 * dim_index + 1] - neg_centre
        )
    return result


def coefficients(bordered_array, factor):
    centre, beside_all = neighbours(bordered_array)
    return [factor * (0.5 * (centre + other)) for other in beside_all]


def apply_operator(face_coef, bordered_array):
    centre, beside_all = neighbours(bordered_array)
    return sum((coef * (centre - other) for coef, other in zip(face_coef, beside_all)))


def gradient(bordered_array):
    centre, beside_all = neighbours(bordered_array)
    return jnp.stack(
        [
            0.5 * (beside_all[2 * dim_index] - beside_all[2 * dim_index + 1])
            for dim_index in range(3)
        ]
    )


def divergence(bordered_array):
    centre, beside_all = neighbours(bordered_array)
    return sum(
        (
            0.5 * (beside_all[2 * dim_index][dim_index] - beside_all[2 * dim_index + 1][dim_index])
            for dim_index in range(3)
        )
    )


def restrict(field):
    leading = field.shape[:-3]
    cells_x, cells_y, cells_z = field.shape[-3:]
    blocks = field.reshape(leading + (cells_x // 2, 2, cells_y // 2, 2, cells_z // 2, 2))
    return blocks.mean(axis=(-5, -3, -1))


def prolong(field):
    return jnp.repeat(jnp.repeat(jnp.repeat(field, 2, axis=-3), 2, axis=-2), 2, axis=-1)


def evaluate_viscosity(rheology_class, class_base_stiffness):
    base = jnp.zeros(rheology_class.shape, jnp.float32)
    for layer_index in range(LAYERS):
        base = base + jnp.where(
            rheology_class == layer_index, class_base_stiffness[layer_index], 0.0
        )
    return base


def inside_mask(extent_first, extent_second, extent_vertical):
    index_x = (
        lax.axis_index("gx") * extent_first + jnp.arange(extent_first + 2, dtype=jnp.int32) - 1
    )
    index_y = (
        lax.axis_index("gy") * extent_second + jnp.arange(extent_second + 2, dtype=jnp.int32) - 1
    )
    index_z = (
        lax.axis_index("gz") * extent_vertical
        + jnp.arange(extent_vertical + 2, dtype=jnp.int32)
        - 1
    )
    inside_x = (index_x >= 0) & (index_x < extent_first * lax.axis_size("gx"))
    inside_y = (index_y >= 0) & (index_y < extent_second * lax.axis_size("gy"))
    inside_z = (index_z >= 0) & (index_z < extent_vertical * lax.axis_size("gz"))
    return inside_x[:, None, None] & inside_y[None, :, None] & inside_z[None, None, :]


def coarse_solve(coarse_res, coarse_coef, coarse_diag, pad_field):
    coarse_corr = JACOBI_WEIGHT * coarse_res / coarse_diag
    for sweep in range(COARSE_SWEEPS - 1):
        coarse_corr = (
            coarse_corr
            + JACOBI_WEIGHT
            * (coarse_res - apply_operator(coarse_coef, pad_field(coarse_corr)))
            / coarse_diag
        )
    return coarse_corr


def shards(saved_heat_state, forward_motion, dual_heat_after, rheology_class, class_base_stiffness):
    extent_first, extent_second, extent_vertical = saved_heat_state.shape
    shallower_adjacent = jnp.maximum(forward_motion, 0.0)
    deeper_adjacent = jnp.minimum(forward_motion, 0.0)
    heat_state = saved_heat_state
    for repeat_index in range(RECOMPUTE):
        heat_state = march_backward(
            finest_halo_cells(heat_state[None])[0], shallower_adjacent, deeper_adjacent
        )
    local_viscosity = evaluate_viscosity(rheology_class, class_base_stiffness) * jnp.exp(
        -ACTIVATION_ENERGY * heat_state
    )
    stacked = jnp.concatenate(
        [
            heat_state[None],
            dual_heat_after[None],
            shallower_adjacent * dual_heat_after[None],
            deeper_adjacent * dual_heat_after[None],
            local_viscosity[None],
        ],
        0,
    )
    bordered_array = finest_halo_cells(stacked)
    driving_source = motion_source(bordered_array[0], forward_motion, dual_heat_after)
    advected_result = advect_dual_heat(bordered_array[2:5], bordered_array[5:8], bordered_array[1])
    face_coef = coefficients(bordered_array[8], 1.0)
    diagonal = sum(face_coef)
    coarse_visc = restrict(local_viscosity)
    coarse_coef = coefficients(coarse_halo(coarse_visc[None])[0], 0.25)
    coarse_diag = sum(coarse_coef)
    deep_static = deep_halo(jnp.concatenate([local_viscosity[None], driving_source], 0))
    cycle_coef = coefficients(deep_static[0], 1.0)
    cycle_source = deep_static[1:4, 1:-1, 1:-1, 1:-1]
    inside = inside_mask(extent_first, extent_second, extent_vertical)
    safe_diag = jnp.where(inside, sum(cycle_coef), 1.0)
    total_cells = (
        extent_first
        * extent_second
        * extent_vertical
        * lax.axis_size("gx")
        * lax.axis_size("gy")
        * lax.axis_size("gz")
    )
    velocity = jnp.zeros(forward_motion.shape, jnp.float32)
    mean_stress = jnp.zeros(saved_heat_state.shape, jnp.float32)
    for iteration in range(SCHUR_ITERS):
        if iteration == 0:
            cycle_resid = cycle_source
        else:
            flow_press = deep_halo(jnp.concatenate([velocity, mean_stress[None]], 0))
            cycle_resid = (
                cycle_source - apply_operator(cycle_coef, flow_press[0:3]) - gradient(flow_press[3])
            )
        cycle_corr = jnp.where(inside, JACOBI_WEIGHT * cycle_resid / safe_diag, 0.0)
        residual = cycle_resid[:, 1:-1, 1:-1, 1:-1]
        correction = cycle_corr[:, 1:-1, 1:-1, 1:-1]
        residual_two = residual - apply_operator(face_coef, cycle_corr)
        coarse_res = restrict(residual_two)
        coarse_corr = coarse_solve(coarse_res, coarse_coef, coarse_diag, coarse_halo)
        correction = correction + prolong(coarse_corr)
        correction = (
            correction
            + JACOBI_WEIGHT
            * (residual - apply_operator(face_coef, finest_halo_cells(correction)))
            / diagonal
        )
        velocity = velocity + correction
        spread_flow = divergence(finest_halo_cells(velocity))
        mean_stress = mean_stress - SCHUR_WEIGHT * local_viscosity * spread_flow
        mean_stress = mean_stress - lax.psum(jnp.sum(mean_stress), ("gx", "gy", "gz")) / total_cells
    adj_temp_prev = advected_result + RAYLEIGH * velocity[2]
    return (adj_temp_prev, velocity, mean_stress)


SUB = 8
LANES = 128
FIELDS = 6
BACK = 5
EDGE = 2
PHASE = 8
HELD = 24
TX, TY = 4, 2
VMEM_LIMIT = 32 * 1024 * 1024
PACK_LIMIT = 60 * 1024 * 1024
FORWARD, ADJOINT, RESPONSE = range(3)


def slab_plan_fits(mesh, shape):
    sizes = mesh.shape
    group = sizes["gx"] * sizes["gy"]
    block = (shape[0] // sizes["gx"], shape[1] // sizes["gy"], shape[2] // sizes["gz"])
    return (
        group == SUB
        and block[0] == SUB
        and block[0] * block[1] == LANES
        and block[1] * group == LANES
        and block[2] == LANES
        and block[2] == group * 2 * PHASE
    )


class Slabs:
    def __init__(self, mesh, shape):
        self.nx, self.ny, self.nz = mesh.shape["gx"], mesh.shape["gy"], mesh.shape["gz"]
        self.group = self.nx * self.ny
        self.width, self.breadth, self.height = shape
        self.block = (shape[0] // self.nx, shape[1] // self.ny, shape[2] // self.nz)
        self.slab = self.block[2] // self.group
        self.margin = self.slab + SUB
        self.rows = self.slab + 2 * self.margin
        self.cells = self.width * self.breadth * self.height
        self.place = []
        for ix in range(self.nx):
            for iy in range(self.ny):
                step = ix if iy % 2 == 0 else self.nx - 1 - ix
                self.place.append(iy * self.nx + step)
        self.order = [
            (x + TX * part, y)
            for x in range(TX)
            for y in range(TY)
            for part in range(self.block[0] // TX)
        ]
        self.holder = [self.place.index(j) for j in range(self.group)]

    def device(self, slab):
        return self.holder[slab % self.group] * self.nz + slab // self.group

    def shifts(self, distance):
        count = self.group * self.nz
        return [
            (self.device(p), self.device(p + distance))
            for p in range(count)
            if 0 <= p + distance < count
        ]

    def index(self):
        ix, iy = lax.axis_index("gx"), lax.axis_index("gy")
        step = jnp.where(iy % 2 == 0, ix, self.nx - 1 - ix)
        return lax.axis_index("gz") * self.group + iy * self.nx + step

    def inside(self, z, n=SUB):
        layer = self.index() * self.slab - self.margin + z
        layer = layer + lax.broadcasted_iota(jnp.int32, (n, LANES), 0)
        return (layer >= 0) & (layer < self.height)


def exchange(tiles, bit, width):
    lane = lax.broadcasted_iota(jnp.int32, (SUB, LANES), 1)
    low = (lane & width) == 0
    new = list(tiles)
    for a in range(SUB):
        if not a & bit:
            b = a | bit
            new[a] = jnp.where(low, tiles[a], pltpu.roll(tiles[b], width, 1))
            new[b] = jnp.where(low, pltpu.roll(tiles[a], LANES - width, 1), tiles[b])
    return new


def gather_tiles(tiles, granule):
    for bit, width in ((1, granule // 2), (1, granule), (2, 2 * granule), (4, 4 * granule)):
        tiles = exchange(tiles, bit, width)
    return tiles


def scatter_tiles(tiles, granule):
    for bit, width in ((4, 4 * granule), (2, 2 * granule), (1, granule), (1, granule // 2)):
        tiles = exchange(tiles, bit, width)
    return tiles


class Tiles:
    def __init__(self, geo):
        self.span = geo.breadth // TY
        self.row = lax.broadcasted_iota(jnp.int32, (SUB, LANES), 0)
        self.lane = lax.broadcasted_iota(jnp.int32, (SUB, LANES), 1)
        self.y = self.lane % self.span
        self.kept, self.latest, self.sweep = {}, None, 0

    def sliding(self, ref, z, lead, t, shift=0):
        if self.latest != (self.sweep, z):
            self.latest, self.kept = (self.sweep, z), {}
        where = (id(ref), lead)
        for key in [k for k in self.kept if k[:2] == where and abs(k[2] - t) > 3]:
            del self.kept[key]

        def load(j):
            key = (*where, j)
            if key not in self.kept:
                self.kept[key] = (ref, get(ref, z - shift, *lead, j))
            return self.kept[key][1]

        return load

    def x(self, load, t, step, count=TX, stride=TY):
        j = t // stride + step
        if 0 <= j < count:
            return load(t + step * stride)
        if step > 0:
            turned = pltpu.roll(load(t % stride), LANES - self.span, 1)
            return jnp.where(self.lane < LANES - self.span, turned, 0.0)
        turned = pltpu.roll(load((count - 1) * stride + t % stride), self.span, 1)
        return jnp.where(self.lane >= self.span, turned, 0.0)

    def lanes(self, f, step):
        if step > 0:
            return jnp.where(self.y < self.span - 1, pltpu.roll(f, LANES - 1, 1), 0.0)
        return jnp.where(self.y > 0, pltpu.roll(f, 1, 1), 0.0)

    def y_side(self, load, t, step):
        if (t % TY == 0) == (step > 0):
            return load(t + step)
        return self.lanes(load(t - step), step)

    def beside(self, ref, z, lead, t, shift=0):
        load = self.sliding(ref, z, lead, t, shift)
        near = [self.x(load, t, 1), self.x(load, t, -1)]
        near += [self.y_side(load, t, 1), self.y_side(load, t, -1)]
        z = z - shift
        return load(t), near + [get(ref, z + 1, *lead, t), get(ref, z - 1, *lead, t)]

    def coarse_beside(self, ref, z, lead, t):
        load = lambda j: get(ref, z, *lead, j)
        f = load(t)
        near = [self.x(load, t, step, TX // 2, 1) for step in (1, -1)]
        near += [self.lanes(f, 1), self.lanes(f, -1)]
        return f, near + [get(ref, z + 2, *lead, t), get(ref, z - 2, *lead, t)]

    def pair_sum(self, f):
        return f + jnp.where(self.row % 2 == 0, pltpu.roll(f, SUB - 1, 0), pltpu.roll(f, 1, 0))


def block_of(t):
    return range(2 * TY * t, 2 * TY * (t + 1))


def tree(terms):
    while len(terms) > 1:
        terms = [sum(terms[k : k + 2]) for k in range(0, len(terms), 2)]
    return terms[0]


def get(ref, z, *index):
    return ref[(*index, pl.ds(z, SUB), slice(None))]


def sweep(tl, lo, hi, body):
    tl.sweep += 1
    late = []

    def store(ref, value, z, *index):
        ref[(*index, pl.ds(z, SUB), slice(None))] = value

    def put(*item):
        late.append(item)
        if len(late) > HELD:
            store(*late.pop(0))

    for z in range(lo, hi, SUB):
        body(z, put)
    for item in late:
        store(*item)


def pack_kernel(geo, heat_in, flow_in, dual_in, kind_in, out, heat, flow, dual, kind, sems):
    b = geo.slab
    pairs = ((heat_in, heat), (flow_in, flow), (dual_in, dual), (kind_in, kind))
    copies = [
        pltpu.make_async_copy(source, target, sems.at[k])
        for k, (source, target) in enumerate(pairs)
    ]
    for copy in copies:
        copy.start()
    fields = [heat, flow.at[0], flow.at[1], flow.at[2], dual, kind]
    for f, (ref, copy) in enumerate(zip(fields, (0, 1, None, None, 2, 3))):
        if copy is not None:
            copies[copy].wait()
        rows = [ref[x, pl.ds(y, SUB, stride=TY), :] for x, y in geo.order]
        turned = jnp.concatenate(rows, 0).astype(jnp.float32).T
        for j in range(geo.group):
            out[geo.holder[j], f * b : (f + 1) * b, :] = turned[j * b : (j + 1) * b]


def edge_kernel(geo, own, first, last):
    b, e = geo.slab, EDGE
    for q in range(geo.group):
        for out, at in ((first, 0), (last, b - e)):
            rows = [own[q, f * b + at : f * b + at + e, :] for f in range(4)]
            out[q] = jnp.concatenate(rows, 0)


STATIC_FINE = ("s0", "s1", "s2", "w", "hv")
STATIC_COARSE = ("wc", "vh")
STATIC = STATIC_FINE + STATIC_COARSE
CUT = {name: SUB // 2 if name in ("hv", "vh") else SUB for name in STATIC}


class Static:
    def __init__(self, refs):
        self.refs = dict(zip(STATIC, refs))

    def get(self, name, z, *index):
        return get(self.refs[name], z - CUT[name], *index)

    def put(self, put, name, value, z, *index):
        put(self.refs[name], value, z - CUT[name], *index)

    def faces(self, tl, z, t):
        h, near = tl.beside(self.refs["hv"], z, (), t, CUT["hv"])
        return [h + other for other in near]

    def coarse_faces(self, tl, z, pair):
        h, near = tl.coarse_beside(self.refs["vh"], z - CUT["vh"], (), pair)
        return [h + other for other in near]


def iterate(geo, st, work, seqs, lo, hi, first=()):
    v, p, res, cor, cor2, cc0, cc1 = work
    tl = Tiles(geo)
    keep = 1.0 - JACOBI_WEIGHT
    comps = range(3 * len(seqs))
    transposed = len(seqs)

    def faces(t, z):
        return st.faces(tl, z, t)

    def around(face, ref, c, t, z):
        f, near = tl.beside(ref, z, (c,), t)
        return f, tree([a * b for a, b in zip(face, near)])

    def residual(z, put):
        for t in range(SUB):
            w = st.get("w", z, t)
            if any(q != ADJOINT and q not in first for q in seqs):
                face = faces(t, z)
                diag = tree(face)
            for s, q in enumerate(seqs):
                if not (q == FORWARD and q in first):
                    _, near = tl.beside(p, z, (transposed if q == ADJOINT else s,), t)
                    slope = [0.5 * (near[2 * k] - near[2 * k + 1]) for k in range(3)]
                for k in range(3):
                    c = 3 * s + k
                    if q == ADJOINT:
                        value = slope[k] if q in first else get(cor, z, c, t) + slope[k]
                    else:
                        if q == FORWARD:
                            value = st.get("s%d" % k, z, t)
                            value = value if q in first else value - slope[k]
                        else:
                            value = -slope[k]
                        if q not in first:
                            f, total = around(face, v, c, t, z)
                            value = value - (diag * f - total)
                    put(res, value, z, c, t)
                    put(cor, w * value, z, c, t)

    sweep(tl, lo - 8, hi + 8, residual)

    def restricted(z, put):
        for pair in range(TX // 2):
            left = [0.0 for _ in comps]
            for t in block_of(pair):
                face = faces(t, z)
                for c in comps:
                    _, total = around(face, cor, c, t, z)
                    left[c] = left[c] + (keep * get(res, z, c, t) + total)
            wc = 0.125 * st.get("wc", z, pair)
            for c in comps:
                put(cc0, wc * tl.pair_sum(left[c]), z, c, pair)

    sweep(tl, lo - 8, hi + 8, restricted)

    def coarse_step(face, wc, ref, c, pair, z):
        f, near = tl.coarse_beside(ref, z, (c,), pair)
        total = tree([a * b for a, b in zip(face, near)])
        return get(cc0, z, c, pair) + keep * f + wc * total

    def sweep_one(z, put):
        for pair in range(TX // 2):
            face, wc = st.coarse_faces(tl, z, pair), st.get("wc", z, pair)
            for c in comps:
                put(cc1, coarse_step(face, wc, cc0, c, pair, z), z, c, pair)

    sweep(tl, lo - 4, hi + 4, sweep_one)

    def sweep_two(z, put):
        for pair in range(TX // 2):
            face, wc = st.coarse_faces(tl, z, pair), st.get("wc", z, pair)
            for c in comps:
                value = coarse_step(face, wc, cc1, c, pair, z)
                for t in block_of(pair):
                    put(cor2, get(cor, z, c, t) + value, z, c, t)

    sweep(tl, lo - 4, hi + 4, sweep_two)

    def velocity(z, put):
        for t in range(SUB):
            face, w = faces(t, z), st.get("w", z, t)
            for c in comps:
                f, total = around(face, cor2, c, t, z)
                value = get(cor, z, c, t) + keep * f + w * total
                if seqs[c // 3] != ADJOINT and seqs[c // 3] not in first:
                    value = get(v, z, c, t) + value
                put(v, value, z, c, t)

    sweep(tl, lo - 4, hi + 4, velocity)

    def pressure(z, put):
        for t in range(SUB):
            half = st.get("hv", z, t)
            for s, q in enumerate(seqs):
                c = 3 * s
                if q == ADJOINT:
                    face = faces(t, z)
                    diag, div = tree(face), 0.0
                    for k in range(3):
                        f, near = tl.beside(v, z, (c + k,), t)
                        div = div + 0.5 * (near[2 * k] - near[2 * k + 1])
                        total = tree([a * b for a, b in zip(face, near)])
                        put(cor, get(res, z, c + k, t) - (diag * f - total), z, c + k, t)
                    value = get(p, z, s, t) + div
                    put(p, value, z, s, t)
                    put(p, half * value, z, transposed, t)
                    continue
                one, two = tl.sliding(v, z, (c,), t), tl.sliding(v, z, (c + 1,), t)
                div = tl.x(one, t, 1) - tl.x(one, t, -1)
                div = div + (tl.y_side(two, t, 1) - tl.y_side(two, t, -1))
                div = div + (get(v, z + 1, c + 2, t) - get(v, z - 1, c + 2, t))
                value = -(half * (0.5 * div))
                if not (q == FORWARD and q in first):
                    value = get(p, z, s, t) + value
                put(p, value, z, s, t)

    sweep(tl, lo, hi, pressure)


def whole_sum(value):
    return jnp.sum(jnp.sum(value, axis=0), axis=(0, 1), keepdims=True)


def product(left, right):
    value = 0.0
    for a, b in zip(left, right):
        value = value + a[...] * b[...]
    return whole_sum(value)


def in_lanes(values, rows):
    lane = lax.broadcasted_iota(jnp.int32, (rows, LANES), 1)
    out = jnp.zeros((rows, LANES), jnp.float32)
    for k, value in values:
        out = jnp.where(lane == k, value, out)
    return out


def setup_kernel(geo, stiffness, own, low, high, low_edge, high_edge, *refs):
    st = Static(refs)
    moved, response, down, up, sums, raw, heat, vc, one, *work = refs[len(STATIC) :]
    v, p, res, cor, cor2, cc0, cc1 = work
    tl = Tiles(geo)
    b, m, n_rows = geo.slab, geo.margin, geo.rows
    granule = geo.block[1]

    for f in range(FIELDS):
        groups = []
        for source, base in ((low, m - b), (own, m), (high, m + b)):
            for u in range(0, b, SUB):
                row = f * b + u
                tiles = [source[q, row : row + SUB, :] for q in range(geo.group)]
                groups.append((base + u, tiles))
        for row, tiles in groups:
            for x, tile in enumerate(gather_tiles(tiles, granule)):
                raw[f, x, row : row + SUB, :] = tile
    for source, base in ((low_edge, m - b - EDGE), (high_edge, m + 2 * b)):
        tiles = [source[q] for q in range(geo.group)]
        for x, tile in enumerate(gather_tiles(tiles, granule)):
            for f in range(4):
                raw[f, x, base : base + EDGE, :] = tile[f * EDGE : (f + 1) * EDGE]

    def advance(ref, old, new):
        def body(z, put):
            inside = geo.inside(z)
            for t in range(SUB):
                f, near = tl.beside(ref, z, (old,), t)
                drift = 0.0
                for k in range(3):
                    flow = get(raw, z, 1 + k, t)
                    drift = drift + jnp.maximum(flow, 0.0) * (f - near[2 * k + 1])
                    drift = drift + jnp.minimum(flow, 0.0) * (near[2 * k] - f)
                spread = tree(near) - 6.0 * f
                value = f - INCREMENT_DT * drift + INCREMENT_DT * DIFFUSIVITY * spread
                put(heat, jnp.where(inside, value, 0.0), z, new, t)

        return body

    sweep(tl, m - b - 4, m + 2 * b + 4, advance(raw, 0, 0))
    sweep(tl, m - b, m + 2 * b, advance(heat, 0, 1))

    def viscosity(z, put):
        inside = geo.inside(z)
        for pair in range(TX // 2):
            coarse = 0.0
            for t in block_of(pair):
                kind = get(raw, z, 5, t)
                base = jnp.zeros(kind.shape, jnp.float32)
                for layer in range(LAYERS):
                    base = jnp.where(kind == float(layer), stiffness[layer], base)
                value = base * jnp.exp(-ACTIVATION_ENERGY * get(heat, z, 1, t))
                value = jnp.where(inside, value, 0.0)
                st.put(put, "hv", 0.5 * value, z, t)
                coarse = coarse + value
            put(vc, 0.125 * tl.pair_sum(coarse), z, pair)

    sweep(tl, m - b, m + 2 * b, viscosity)

    def statics(z, put):
        inside = geo.inside(z)
        for t in range(SUB):
            diag = tree(st.faces(tl, z, t))
            st.put(put, "w", jnp.where(inside, JACOBI_WEIGHT / diag, 0.0), z, t)
            f, near = tl.beside(heat, z, (1,), t)
            dual = -INCREMENT_DT * get(raw, z, 4, t)
            for k in range(3):
                flow = get(raw, z, 1 + k, t)
                step = jnp.where(flow > 0, f - near[2 * k + 1], near[2 * k] - f)
                st.put(put, "s%d" % k, dual * step, z, t)

    sweep(tl, m - b, m + 2 * b, statics)

    def coarse_statics(z, put):
        inside = geo.inside(z)
        for pair in range(TX // 2):
            c, near = tl.coarse_beside(vc, z, (), pair)
            face = [0.25 * (0.5 * (c + o)) for o in near]
            st.put(put, "wc", jnp.where(inside, JACOBI_WEIGHT / tree(face), 0.0), z, pair)
            st.put(put, "vh", 0.125 * c, z, pair)

    sweep(tl, m - b, m + 2 * b, coarse_statics)

    def transport(z, put):
        for t in range(SUB):
            dual, near = tl.beside(raw, z, (4,), t)
            value = dual + INCREMENT_DT * DIFFUSIVITY * (tree(near) - 6.0 * dual)
            for k in range(3):
                flow, sides = tl.beside(raw, z, (1 + k,), t)
                a = jnp.maximum(flow, 0.0) * dual
                c = jnp.minimum(flow, 0.0) * dual
                ahead = jnp.maximum(sides[2 * k], 0.0) * near[2 * k]
                behind = jnp.minimum(sides[2 * k + 1], 0.0) * near[2 * k + 1]
                value = value - INCREMENT_DT * (a - ahead + behind - c)
            put(moved, value, z - m, t)

    sweep(tl, m, m + b, transport)

    def unit(z, put):
        value = jnp.where(geo.inside(z), 1.0, 0.0)
        for t in range(SUB):
            put(p, value, z, 1, t)
            put(p, value, z, 2, t)
            put(p, st.get("hv", z, t), z, 3, t)

    sweep(tl, m - b, m + 2 * b, unit)

    mine = slice(m, m + b)

    def fields(s, three=v):
        return [three.at[3 * s + k, :, mine, :] for k in range(3)] + [p.at[s, :, mine, :]]

    every = (FORWARD, ADJOINT, RESPONSE)
    iterate(geo, st, work, every, m - PHASE, m + b + PHASE, every)
    for k, (a, r) in enumerate(zip(fields(1, cor), fields(2))):
        one[k] = a[...]
        response[k] = r[...]
    sums_of = [(0, source_product(geo, st, v, 3)), (1, whole_sum(one[3]))]
    iterate(geo, st, work, every, m, m + b)
    near, far, turn = [one.at[k] for k in range(4)], fields(1, cor), [response.at[k] for k in range(4)]
    sums_of += [(2, source_product(geo, st, v, 3)), (3, whole_sum(p[1, :, mine, :]))]
    sums_of += [(4, product(near, fields(0))), (5, product(far, fields(0))), (6, product(far, turn))]
    sums[...] = in_lanes(sums_of, sums.shape[0])
    for k, (x, r) in enumerate(zip(fields(0), fields(2))):
        state, turned = x[...], r[...]
        for out, part in ((down, turned[:, :PHASE]), (up, turned[:, b - PHASE :])):
            out[:, k * b : (k + 1) * b, :] = state
            out[:, 4 * b + k * PHASE : 4 * b + (k + 1) * PHASE, :] = part


def source_product(geo, st, v, first):
    mine = slice(geo.margin, geo.margin + geo.slab)
    held = slice(geo.margin - CUT["s0"], geo.margin - CUT["s0"] + geo.slab)
    left = [st.refs["s%d" % k].at[:, held, :] for k in range(3)]
    return product(left, [v.at[first + k, :, mine, :] for k in range(3)])


def second_kernel(geo, *refs):
    st = Static(refs)
    down, up, low, high, final, *work = refs[len(STATIC) :]
    v, p = work[:2]
    b, m = geo.slab, geo.margin
    for k in range(4):
        rows, part = slice(k * b, (k + 1) * b), slice(4 * b + k * PHASE, 4 * b + (k + 1) * PHASE)
        state, turned = (v.at[k], v.at[3 + k]) if k < 3 else (p.at[0], p.at[1])
        for source, base in ((low, m - b), (down, m), (high, m + b)):
            state[:, base : base + b, :] = source[:, rows, :]
        for source, base in ((low, m - PHASE), (down, m), (up, m + b - PHASE), (high, m + b)):
            turned[:, base : base + PHASE, :] = source[:, part, :]
    iterate(geo, st, work, (FORWARD,), m - PHASE, m + b + PHASE)
    iterate(geo, st, work, (FORWARD, RESPONSE), m, m + b)
    mine = slice(m, m + b)
    for s in range(2):
        for k in range(4):
            final[4 * s + k] = v[3 * s + k, :, mine, :] if k < 3 else p[s, :, mine, :]


def means(geo, sums):
    row = jnp.sum(sums, axis=0, keepdims=True) / geo.cells
    c1, l1, c2, l2, l1_x2, l2_x2, l2_r1 = [row[:, k : k + 1] for k in range(7)]
    m1 = c1
    m2 = c1 + c2 - m1 * l1
    m3 = c1 + (l1_x2 - m1 * l2) - m2 * l1
    m4 = c1 + c2 + (l2_x2 - m1 * l2_r1) - m2 * l2 - m3 * l1
    return m1, m2, m3, m4


def combine_kernel(geo, sums, final, down, up, response, moved, out):
    b = geo.slab
    means_of = [jnp.broadcast_to(value, (SUB, LANES)) for value in means(geo, sums[...])]
    m1, m2, m3, m4 = means_of
    for u in range(0, b, SUB):
        rows = slice(u, u + SUB)
        fields = []
        for k in range(4):
            turned = down if u < PHASE else up
            at = 4 * b + k * PHASE + (u if u < PHASE else u - (b - PHASE))
            tiles = []
            for t in range(SUB):
                value = final[k, t, rows, :] - m1 * final[4 + k, t, rows, :]
                value = value - m2 * turned[t, at : at + SUB, :] - m3 * response[k, t, rows, :]
                tiles.append(value - m4 if k == 3 else value)
            fields.append(tiles)
        fields.append([moved[t, rows, :] + fields[2][t] for t in range(SUB)])
        for f, tiles in enumerate(fields):
            for q, tile in enumerate(scatter_tiles(tiles, geo.block[1])):
                out[q, f * b + u : f * b + u + SUB, :] = tile


def unpack_kernel(geo, chunks, heat, flow, pressure):
    b = geo.slab
    for f, ref in enumerate((flow.at[0], flow.at[1], flow.at[2], pressure, heat)):
        rows = [chunks[geo.holder[j], f * b : (f + 1) * b, :] for j in range(geo.group)]
        block = jnp.concatenate(rows, 0).T
        for k, (x, y) in enumerate(geo.order):
            ref[x, pl.ds(y, SUB, stride=TY), :] = block[k * SUB : (k + 1) * SUB]


def call(kernel, out, scratch, *args, smem=(), hbm=(), limit=VMEM_LIMIT, megabytes=2):
    f32 = jnp.float32
    cost = pl.CostEstimate(
        flops=megabytes * 1000000, bytes_accessed=megabytes * 1000000, transcendentals=0
    )
    specs = [
        pl.BlockSpec(
            memory_space=pltpu.SMEM if i in smem else pltpu.HBM if i in hbm else pltpu.VMEM
        )
        for i in range(len(args))
    ]
    return pl.pallas_call(
        kernel,
        out_shape=[jax.ShapeDtypeStruct(s, f32) for s in out],
        in_specs=specs,
        out_specs=[pl.BlockSpec(memory_space=pltpu.VMEM) for _ in out],
        scratch_shapes=[pltpu.VMEM(s, f32) if isinstance(s, tuple) else s for s in scratch],
        compiler_params=pltpu.CompilerParams(vmem_limit_bytes=limit),
        cost_estimate=cost,
    )(*args)


def slab_shards(geo, heat, flow, dual, kind, stiffness):
    b, group = geo.slab, geo.group
    inputs = (heat, flow, dual, kind)
    (chunks,) = call(
        functools.partial(pack_kernel, geo),
        [(group, FIELDS * b, LANES)],
        [pltpu.VMEM(a.shape, a.dtype) for a in inputs] + [pltpu.SemaphoreType.DMA((4,))],
        *inputs,
        hbm=range(4),
        limit=PACK_LIMIT,
    )
    own = lax.all_to_all(chunks, ("gx", "gy"), 0, 0, tiled=True)
    axes = ("gx", "gy", "gz")
    low = lax.ppermute(own, axes, geo.shifts(1))
    high = lax.ppermute(own, axes, geo.shifts(-1))
    edges = call(functools.partial(edge_kernel, geo), [(group, SUB, LANES)] * 2, [], own)
    high_edge = lax.ppermute(edges[0], axes, geo.shifts(-2))
    low_edge = lax.ppermute(edges[1], axes, geo.shifts(2))

    fine, coarse = (SUB, geo.rows, LANES), (TX // 2, geo.rows, LANES)
    static_shapes = [
        (SUB if name in STATIC_FINE else TX // 2, geo.rows - 2 * CUT[name], LANES)
        for name in STATIC
    ]
    slab = (SUB, b, LANES)

    def work(n, more=0):
        fields = [(3 * n, *fine), (n + more, *fine)] + [(3 * n, *fine)] * 3
        return fields + [(3 * n, *coarse)] * 2

    devices = group * geo.nz
    message = (SUB, 4 * b + 4 * PHASE, LANES)
    *static, moved, response, down, up, sums = call(
        functools.partial(setup_kernel, geo),
        static_shapes + [slab, (4, *slab), message, message, (devices, LANES)],
        [(FIELDS, *fine), (2, *fine), coarse, (4, *slab)] + work(3, 1),
        stiffness,
        own,
        low,
        high,
        low_edge,
        high_edge,
        smem=(0,),
        megabytes=60,
    )
    from_low = lax.ppermute(up, axes, geo.shifts(1))
    from_high = lax.ppermute(down, axes, geo.shifts(-1))
    sums = lax.all_to_all(sums, axes, 0, 0, tiled=True)
    (final,) = call(
        functools.partial(second_kernel, geo),
        [(8, *slab)],
        work(2),
        *static,
        down,
        up,
        from_low,
        from_high,
        megabytes=30,
    )
    (chunks,) = call(
        functools.partial(combine_kernel, geo),
        [(group, BACK * b, LANES)],
        [],
        sums,
        final,
        down,
        up,
        response,
        moved,
    )
    chunks = lax.all_to_all(chunks, ("gx", "gy"), 0, 0, tiled=True)
    return tuple(
        call(
            functools.partial(unpack_kernel, geo),
            [geo.block, (3, *geo.block), geo.block],
            [],
            chunks,
        )
    )


def solution(mesh):
    in_specs = (
        P("gx", "gy", "gz"),
        P(None, "gx", "gy", "gz"),
        P("gx", "gy", "gz"),
        P("gx", "gy", "gz"),
        P(),
    )
    out_specs = (P("gx", "gy", "gz"), P(None, "gx", "gy", "gz"), P("gx", "gy", "gz"))

    def program(saved_heat_state, *others):
        shape = saved_heat_state.shape
        plan = shards
        if slab_plan_fits(mesh, shape):
            plan = functools.partial(slab_shards, Slabs(mesh, shape))
        return jax.shard_map(
            plan, mesh=mesh, in_specs=in_specs, out_specs=out_specs, check_vma=False
        )(saved_heat_state, *others)

    return program
```

```python
import functools

import jax
import jax.numpy as jnp
from jax import lax
from jax.experimental import pallas as pl
from jax.experimental.pallas import tpu as pltpu
from jax.sharding import PartitionSpec as P

RECOMPUTE = 2
SCHUR_ITERS = 4
COARSE_SWEEPS = 3
LAYERS = 8


INCREMENT_DT = 0.2
DIFFUSIVITY = 0.3
ACTIVATION_ENERGY = 2.3
JACOBI_WEIGHT = 0.7
SCHUR_WEIGHT = 0.5
RAYLEIGH = 1.0


def extended(block, sides, width):
    for axis, dim in sides:
        count = lax.axis_size(axis)
        forward = [(i, i + 1) for i in range(count - 1)]
        backward = [(target, source) for source, target in forward]
        low = lax.ppermute(
            lax.slice_in_dim(block, block.shape[dim] - width, None, axis=dim), axis, forward
        )
        high = lax.ppermute(lax.slice_in_dim(block, 0, width, axis=dim), axis, backward)
        block = jnp.concatenate([low, block, high], axis=dim)
    return block


def neighbours(bordered_array):
    centre = bordered_array[..., 1:-1, 1:-1, 1:-1]
    beside_all = [
        bordered_array[..., 2:, 1:-1, 1:-1],
        bordered_array[..., :-2, 1:-1, 1:-1],
        bordered_array[..., 1:-1, 2:, 1:-1],
        bordered_array[..., 1:-1, :-2, 1:-1],
        bordered_array[..., 1:-1, 1:-1, 2:],
        bordered_array[..., 1:-1, 1:-1, :-2],
    ]
    return (centre, beside_all)


def finest_halo_cells(field):
    return extended(field, (("gx", 1), ("gy", 2), ("gz", 3)), 1)


def deep_halo(field):
    return extended(field, (("gx", 1), ("gy", 2), ("gz", 3)), 2)


def coarse_halo(field):
    return extended(field, (("gx", 1), ("gy", 2), ("gz", 3)), 1)


def march_backward(bordered_array, shallower_adjacent, deeper_adjacent):
    centre, beside_all = neighbours(bordered_array)
    drift = 0.0
    for dim_index in range(3):
        drift = (
            drift
            + shallower_adjacent[dim_index] * (centre - beside_all[2 * dim_index + 1])
            + deeper_adjacent[dim_index] * (beside_all[2 * dim_index] - centre)
        )
    spread = sum(beside_all) - 6.0 * centre
    return centre - INCREMENT_DT * drift + INCREMENT_DT * DIFFUSIVITY * spread


def motion_source(bordered_heat, forward_motion, dual_heat_after):
    centre, beside_all = neighbours(bordered_heat)
    device_pieces = [
        jnp.where(
            forward_motion[dim_index] > 0,
            centre - beside_all[2 * dim_index + 1],
            beside_all[2 * dim_index] - centre,
        )
        for dim_index in range(3)
    ]
    return -INCREMENT_DT * dual_heat_after[None] * jnp.stack(device_pieces)


def advect_dual_heat(pos_padded, neg_padded, lam_padded):
    centre, beside_all = neighbours(lam_padded)
    result = centre + INCREMENT_DT * DIFFUSIVITY * (sum(beside_all) - 6.0 * centre)
    for dim_index in range(3):
        pos_centre, pos_around = neighbours(pos_padded[dim_index])
        neg_centre, neg_around = neighbours(neg_padded[dim_index])
        result = result - INCREMENT_DT * (
            pos_centre - pos_around[2 * dim_index] + neg_around[2 * dim_index + 1] - neg_centre
        )
    return result


def coefficients(bordered_array, factor):
    centre, beside_all = neighbours(bordered_array)
    return [factor * (0.5 * (centre + other)) for other in beside_all]


def apply_operator(face_coef, bordered_array):
    centre, beside_all = neighbours(bordered_array)
    return sum((coef * (centre - other) for coef, other in zip(face_coef, beside_all)))


def gradient(bordered_array):
    centre, beside_all = neighbours(bordered_array)
    return jnp.stack(
        [
            0.5 * (beside_all[2 * dim_index] - beside_all[2 * dim_index + 1])
            for dim_index in range(3)
        ]
    )


def divergence(bordered_array):
    centre, beside_all = neighbours(bordered_array)
    return sum(
        (
            0.5 * (beside_all[2 * dim_index][dim_index] - beside_all[2 * dim_index + 1][dim_index])
            for dim_index in range(3)
        )
    )


def restrict(field):
    leading = field.shape[:-3]
    cells_x, cells_y, cells_z = field.shape[-3:]
    blocks = field.reshape(leading + (cells_x // 2, 2, cells_y // 2, 2, cells_z // 2, 2))
    return blocks.mean(axis=(-5, -3, -1))


def prolong(field):
    return jnp.repeat(jnp.repeat(jnp.repeat(field, 2, axis=-3), 2, axis=-2), 2, axis=-1)


def evaluate_viscosity(rheology_class, class_base_stiffness):
    base = jnp.zeros(rheology_class.shape, jnp.float32)
    for layer_index in range(LAYERS):
        base = base + jnp.where(
            rheology_class == layer_index, class_base_stiffness[layer_index], 0.0
        )
    return base


def inside_mask(extent_first, extent_second, extent_vertical):
    index_x = (
        lax.axis_index("gx") * extent_first + jnp.arange(extent_first + 2, dtype=jnp.int32) - 1
    )
    index_y = (
        lax.axis_index("gy") * extent_second + jnp.arange(extent_second + 2, dtype=jnp.int32) - 1
    )
    index_z = (
        lax.axis_index("gz") * extent_vertical
        + jnp.arange(extent_vertical + 2, dtype=jnp.int32)
        - 1
    )
    inside_x = (index_x >= 0) & (index_x < extent_first * lax.axis_size("gx"))
    inside_y = (index_y >= 0) & (index_y < extent_second * lax.axis_size("gy"))
    inside_z = (index_z >= 0) & (index_z < extent_vertical * lax.axis_size("gz"))
    return inside_x[:, None, None] & inside_y[None, :, None] & inside_z[None, None, :]


def coarse_solve(coarse_res, coarse_coef, coarse_diag, pad_field):
    coarse_corr = JACOBI_WEIGHT * coarse_res / coarse_diag
    for sweep in range(COARSE_SWEEPS - 1):
        coarse_corr = (
            coarse_corr
            + JACOBI_WEIGHT
            * (coarse_res - apply_operator(coarse_coef, pad_field(coarse_corr)))
            / coarse_diag
        )
    return coarse_corr


def shards(saved_heat_state, forward_motion, dual_heat_after, rheology_class, class_base_stiffness):
    extent_first, extent_second, extent_vertical = saved_heat_state.shape
    shallower_adjacent = jnp.maximum(forward_motion, 0.0)
    deeper_adjacent = jnp.minimum(forward_motion, 0.0)
    heat_state = saved_heat_state
    for repeat_index in range(RECOMPUTE):
        heat_state = march_backward(
            finest_halo_cells(heat_state[None])[0], shallower_adjacent, deeper_adjacent
        )
    local_viscosity = evaluate_viscosity(rheology_class, class_base_stiffness) * jnp.exp(
        -ACTIVATION_ENERGY * heat_state
    )
    stacked = jnp.concatenate(
        [
            heat_state[None],
            dual_heat_after[None],
            shallower_adjacent * dual_heat_after[None],
            deeper_adjacent * dual_heat_after[None],
            local_viscosity[None],
        ],
        0,
    )
    bordered_array = finest_halo_cells(stacked)
    driving_source = motion_source(bordered_array[0], forward_motion, dual_heat_after)
    advected_result = advect_dual_heat(bordered_array[2:5], bordered_array[5:8], bordered_array[1])
    face_coef = coefficients(bordered_array[8], 1.0)
    diagonal = sum(face_coef)
    coarse_visc = restrict(local_viscosity)
    coarse_coef = coefficients(coarse_halo(coarse_visc[None])[0], 0.25)
    coarse_diag = sum(coarse_coef)
    deep_static = deep_halo(jnp.concatenate([local_viscosity[None], driving_source], 0))
    cycle_coef = coefficients(deep_static[0], 1.0)
    cycle_source = deep_static[1:4, 1:-1, 1:-1, 1:-1]
    inside = inside_mask(extent_first, extent_second, extent_vertical)
    safe_diag = jnp.where(inside, sum(cycle_coef), 1.0)
    total_cells = (
        extent_first
        * extent_second
        * extent_vertical
        * lax.axis_size("gx")
        * lax.axis_size("gy")
        * lax.axis_size("gz")
    )
    velocity = jnp.zeros(forward_motion.shape, jnp.float32)
    mean_stress = jnp.zeros(saved_heat_state.shape, jnp.float32)
    for iteration in range(SCHUR_ITERS):
        if iteration == 0:
            cycle_resid = cycle_source
        else:
            flow_press = deep_halo(jnp.concatenate([velocity, mean_stress[None]], 0))
            cycle_resid = (
                cycle_source - apply_operator(cycle_coef, flow_press[0:3]) - gradient(flow_press[3])
            )
        cycle_corr = jnp.where(inside, JACOBI_WEIGHT * cycle_resid / safe_diag, 0.0)
        residual = cycle_resid[:, 1:-1, 1:-1, 1:-1]
        correction = cycle_corr[:, 1:-1, 1:-1, 1:-1]
        residual_two = residual - apply_operator(face_coef, cycle_corr)
        coarse_res = restrict(residual_two)
        coarse_corr = coarse_solve(coarse_res, coarse_coef, coarse_diag, coarse_halo)
        correction = correction + prolong(coarse_corr)
        correction = (
            correction
            + JACOBI_WEIGHT
            * (residual - apply_operator(face_coef, finest_halo_cells(correction)))
            / diagonal
        )
        velocity = velocity + correction
        spread_flow = divergence(finest_halo_cells(velocity))
        mean_stress = mean_stress - SCHUR_WEIGHT * local_viscosity * spread_flow
        mean_stress = mean_stress - lax.psum(jnp.sum(mean_stress), ("gx", "gy", "gz")) / total_cells
    adj_temp_prev = advected_result + RAYLEIGH * velocity[2]
    return (adj_temp_prev, velocity, mean_stress)


SUB = 8
LANES = 128
FIELDS = 6
BACK = 5
EDGE = 2
PHASE = 8
HELD = 24
TX, TY = 4, 2
VMEM_LIMIT = 32 * 1024 * 1024
PACK_LIMIT = 60 * 1024 * 1024
FORWARD, ADJOINT, RESPONSE = range(3)
TURNED = 3


def slab_plan_fits(mesh, shape):
    sizes = mesh.shape
    group = sizes["gx"] * sizes["gy"]
    block = (shape[0] // sizes["gx"], shape[1] // sizes["gy"], shape[2] // sizes["gz"])
    return (
        group == SUB
        and block[0] == SUB
        and block[0] * block[1] == LANES
        and block[1] * group == LANES
        and block[2] == LANES
        and block[2] == group * 2 * PHASE
    )


class Slabs:
    def __init__(self, mesh, shape):
        self.nx, self.ny, self.nz = mesh.shape["gx"], mesh.shape["gy"], mesh.shape["gz"]
        self.group = self.nx * self.ny
        self.width, self.breadth, self.height = shape
        self.block = (shape[0] // self.nx, shape[1] // self.ny, shape[2] // self.nz)
        self.slab = self.block[2] // self.group
        self.margin = self.slab + SUB
        self.rows = self.slab + 2 * self.margin
        self.cells = self.width * self.breadth * self.height
        self.place = []
        for ix in range(self.nx):
            for iy in range(self.ny):
                step = ix if iy % 2 == 0 else self.nx - 1 - ix
                self.place.append(iy * self.nx + step)
        self.order = [
            (x + TX * part, y)
            for x in range(TX)
            for y in range(TY)
            for part in range(self.block[0] // TX)
        ]
        self.holder = [self.place.index(j) for j in range(self.group)]

    def device(self, slab):
        return self.holder[slab % self.group] * self.nz + slab // self.group

    def shifts(self, distance):
        count = self.group * self.nz
        return [
            (self.device(p), self.device(p + distance))
            for p in range(count)
            if 0 <= p + distance < count
        ]

    def index(self):
        ix, iy = lax.axis_index("gx"), lax.axis_index("gy")
        step = jnp.where(iy % 2 == 0, ix, self.nx - 1 - ix)
        return lax.axis_index("gz") * self.group + iy * self.nx + step

    def inside(self, z, n=SUB):
        layer = self.index() * self.slab - self.margin + z
        layer = layer + lax.broadcasted_iota(jnp.int32, (n, LANES), 0)
        return (layer >= 0) & (layer < self.height)


def exchange(tiles, bit, width):
    lane = lax.broadcasted_iota(jnp.int32, (SUB, LANES), 1)
    low = (lane & width) == 0
    new = list(tiles)
    for a in range(SUB):
        if not a & bit:
            b = a | bit
            new[a] = jnp.where(low, tiles[a], pltpu.roll(tiles[b], width, 1))
            new[b] = jnp.where(low, pltpu.roll(tiles[a], LANES - width, 1), tiles[b])
    return new


def gather_tiles(tiles, granule):
    for bit, width in ((1, granule // 2), (1, granule), (2, 2 * granule), (4, 4 * granule)):
        tiles = exchange(tiles, bit, width)
    return tiles


def scatter_tiles(tiles, granule):
    for bit, width in ((4, 4 * granule), (2, 2 * granule), (1, granule), (1, granule // 2)):
        tiles = exchange(tiles, bit, width)
    return tiles


class Tiles:
    def __init__(self, geo):
        self.span = geo.breadth // TY
        self.row = lax.broadcasted_iota(jnp.int32, (SUB, LANES), 0)
        self.lane = lax.broadcasted_iota(jnp.int32, (SUB, LANES), 1)
        self.y = self.lane % self.span
        self.kept, self.latest, self.sweep = {}, None, 0

    def sliding(self, ref, z, lead, t, shift=0):
        if self.latest != (self.sweep, z):
            self.latest, self.kept = (self.sweep, z), {}
        where = (id(ref), lead)
        for key in [k for k in self.kept if k[:2] == where and abs(k[2] - t) > 3]:
            del self.kept[key]

        def load(j):
            key = (*where, j)
            if key not in self.kept:
                self.kept[key] = (ref, get(ref, z - shift, *lead, j))
            return self.kept[key][1]

        return load

    def x(self, load, t, step, count=TX, stride=TY):
        j = t // stride + step
        if 0 <= j < count:
            return load(t + step * stride)
        if step > 0:
            turned = pltpu.roll(load(t % stride), LANES - self.span, 1)
            return jnp.where(self.lane < LANES - self.span, turned, 0.0)
        turned = pltpu.roll(load((count - 1) * stride + t % stride), self.span, 1)
        return jnp.where(self.lane >= self.span, turned, 0.0)

    def lanes(self, f, step):
        if step > 0:
            return jnp.where(self.y < self.span - 1, pltpu.roll(f, LANES - 1, 1), 0.0)
        return jnp.where(self.y > 0, pltpu.roll(f, 1, 1), 0.0)

    def y_side(self, load, t, step):
        if (t % TY == 0) == (step > 0):
            return load(t + step)
        return self.lanes(load(t - step), step)

    def beside(self, ref, z, lead, t, shift=0):
        load = self.sliding(ref, z, lead, t, shift)
        near = [self.x(load, t, 1), self.x(load, t, -1)]
        near += [self.y_side(load, t, 1), self.y_side(load, t, -1)]
        z = z - shift
        return load(t), near + [get(ref, z + 1, *lead, t), get(ref, z - 1, *lead, t)]

    def coarse_beside(self, ref, z, lead, t):
        load = lambda j: get(ref, z, *lead, j)
        f = load(t)
        near = [self.x(load, t, step, TX // 2, 1) for step in (1, -1)]
        near += [self.lanes(f, 1), self.lanes(f, -1)]
        return f, near + [get(ref, z + 2, *lead, t), get(ref, z - 2, *lead, t)]

    def pair_sum(self, f):
        return f + jnp.where(self.row % 2 == 0, pltpu.roll(f, SUB - 1, 0), pltpu.roll(f, 1, 0))


def block_of(t):
    return range(2 * TY * t, 2 * TY * (t + 1))


def tree(terms):
    while len(terms) > 1:
        terms = [sum(terms[k : k + 2]) for k in range(0, len(terms), 2)]
    return terms[0]


def get(ref, z, *index):
    return ref[(*index, pl.ds(z, SUB), slice(None))]


def sweep(tl, lo, hi, body):
    tl.sweep += 1
    late = []

    def store(ref, value, z, *index):
        ref[(*index, pl.ds(z, SUB), slice(None))] = value

    def put(*item):
        late.append(item)
        if len(late) > HELD:
            store(*late.pop(0))

    for z in range(lo, hi, SUB):
        body(z, put)
    for item in late:
        store(*item)


def pack_kernel(geo, heat_in, flow_in, dual_in, kind_in, out, heat, flow, dual, kind, sems):
    b = geo.slab
    pairs = ((heat_in, heat), (flow_in, flow), (dual_in, dual), (kind_in, kind))
    copies = [
        pltpu.make_async_copy(source, target, sems.at[k])
        for k, (source, target) in enumerate(pairs)
    ]
    for copy in copies:
        copy.start()
    fields = [heat, flow.at[0], flow.at[1], flow.at[2], dual, kind]
    for f, (ref, copy) in enumerate(zip(fields, (0, 1, None, None, 2, 3))):
        if copy is not None:
            copies[copy].wait()
        rows = [ref[x, pl.ds(y, SUB, stride=TY), :] for x, y in geo.order]
        turned = jnp.concatenate(rows, 0).astype(jnp.float32).T
        for j in range(geo.group):
            out[geo.holder[j], f * b : (f + 1) * b, :] = turned[j * b : (j + 1) * b]


def edge_kernel(geo, own, first, last):
    b, e = geo.slab, EDGE
    for q in range(geo.group):
        for out, at in ((first, 0), (last, b - e)):
            rows = [own[q, f * b + at : f * b + at + e, :] for f in range(4)]
            out[q] = jnp.concatenate(rows, 0)


STATIC_FINE = ("s0", "s1", "s2", "w", "hv")
STATIC_COARSE = ("vh",)
STATIC = STATIC_FINE + STATIC_COARSE
CUT = {name: SUB // 2 if name in ("hv", "vh") else SUB for name in STATIC}


class Static:
    def __init__(self, refs):
        self.refs = dict(zip(STATIC, refs))

    def get(self, name, z, *index):
        return get(self.refs[name], z - CUT[name], *index)

    def put(self, put, name, value, z, *index):
        put(self.refs[name], value, z - CUT[name], *index)

    def faces(self, tl, z, t):
        h, near = tl.beside(self.refs["hv"], z, (), t, CUT["hv"])
        return [h + other for other in near]

    def coarse_faces(self, tl, z, pair):
        h, near = tl.coarse_beside(self.refs["vh"], z - CUT["vh"], (), pair)
        return [h + other for other in near]

    def coarse_weight(self, geo, face, z):
        return jnp.where(geo.inside(z), JACOBI_WEIGHT / tree(face), 0.0)


def iterate(geo, st, work, seqs, lo, hi, first=()):
    v, p, res, cor, cor2, cc0, cc1 = work
    tl = Tiles(geo)
    keep = 1.0 - JACOBI_WEIGHT
    kinds = {3 * s + k: q for q, s in seqs.items() for k in range(3)}
    comps = list(kinds)

    def faces(t, z):
        return st.faces(tl, z, t)

    def around(face, ref, c, t, z):
        f, near = tl.beside(ref, z, (c,), t)
        return f, tree([a * b for a, b in zip(face, near)])

    def residual(z, put):
        for t in range(SUB):
            w = st.get("w", z, t)
            if any(q != ADJOINT and q not in first for q in seqs):
                face = faces(t, z)
                diag = tree(face)
            for q, s in seqs.items():
                if not (q == FORWARD and q in first):
                    _, near = tl.beside(p, z, (TURNED if q == ADJOINT else s,), t)
                    slope = [0.5 * (near[2 * k] - near[2 * k + 1]) for k in range(3)]
                for k in range(3):
                    c = 3 * s + k
                    if q == ADJOINT:
                        value = slope[k] if q in first else get(cor, z, c, t) + slope[k]
                    else:
                        if q == FORWARD:
                            value = st.get("s%d" % k, z, t)
                            value = value if q in first else value - slope[k]
                        else:
                            value = -slope[k]
                        if q not in first:
                            f, total = around(face, v, c, t, z)
                            value = value - (diag * f - total)
                    put(res, value, z, c, t)
                    put(cor, w * value, z, c, t)

    sweep(tl, lo - 8, hi + 8, residual)

    def restricted(z, put):
        for pair in range(TX // 2):
            left = dict.fromkeys(comps, 0.0)
            for t in block_of(pair):
                face = faces(t, z)
                for c in comps:
                    _, total = around(face, cor, c, t, z)
                    left[c] = left[c] + (keep * get(res, z, c, t) + total)
            wc = 0.125 * st.coarse_weight(geo, st.coarse_faces(tl, z, pair), z)
            for c in comps:
                put(cc0, wc * tl.pair_sum(left[c]), z, c, pair)

    sweep(tl, lo - 8, hi + 8, restricted)

    def coarse_step(face, wc, ref, c, pair, z):
        f, near = tl.coarse_beside(ref, z, (c,), pair)
        total = tree([a * b for a, b in zip(face, near)])
        return get(cc0, z, c, pair) + keep * f + wc * total

    def sweep_one(z, put):
        for pair in range(TX // 2):
            face = st.coarse_faces(tl, z, pair)
            wc = st.coarse_weight(geo, face, z)
            for c in comps:
                put(cc1, coarse_step(face, wc, cc0, c, pair, z), z, c, pair)

    sweep(tl, lo - 4, hi + 4, sweep_one)

    def sweep_two(z, put):
        for pair in range(TX // 2):
            face = st.coarse_faces(tl, z, pair)
            wc = st.coarse_weight(geo, face, z)
            for c in comps:
                value = coarse_step(face, wc, cc1, c, pair, z)
                for t in block_of(pair):
                    put(cor2, get(cor, z, c, t) + value, z, c, t)

    sweep(tl, lo - 4, hi + 4, sweep_two)

    def velocity(z, put):
        for t in range(SUB):
            face, w = faces(t, z), st.get("w", z, t)
            for c in comps:
                f, total = around(face, cor2, c, t, z)
                value = get(cor, z, c, t) + keep * f + w * total
                if kinds[c] != ADJOINT and kinds[c] not in first:
                    value = get(v, z, c, t) + value
                put(v, value, z, c, t)

    sweep(tl, lo - 4, hi + 4, velocity)

    def pressure(z, put):
        for t in range(SUB):
            half = st.get("hv", z, t)
            for q, s in seqs.items():
                c = 3 * s
                if q == ADJOINT:
                    face = faces(t, z)
                    diag, div = tree(face), 0.0
                    for k in range(3):
                        f, near = tl.beside(v, z, (c + k,), t)
                        div = div + 0.5 * (near[2 * k] - near[2 * k + 1])
                        total = tree([a * b for a, b in zip(face, near)])
                        put(cor, get(res, z, c + k, t) - (diag * f - total), z, c + k, t)
                    value = get(p, z, s, t) + div
                    put(p, value, z, s, t)
                    put(p, half * value, z, TURNED, t)
                    continue
                one, two = tl.sliding(v, z, (c,), t), tl.sliding(v, z, (c + 1,), t)
                div = tl.x(one, t, 1) - tl.x(one, t, -1)
                div = div + (tl.y_side(two, t, 1) - tl.y_side(two, t, -1))
                div = div + (get(v, z + 1, c + 2, t) - get(v, z - 1, c + 2, t))
                value = -(half * (0.5 * div))
                if not (q == FORWARD and q in first):
                    value = get(p, z, s, t) + value
                put(p, value, z, s, t)

    sweep(tl, lo, hi, pressure)


def whole_sum(value):
    return jnp.sum(jnp.sum(value, axis=0), axis=(0, 1), keepdims=True)


def product(left, right):
    value = 0.0
    for a, b in zip(left, right):
        value = value + a[...] * b[...]
    return whole_sum(value)


def in_lanes(values, rows):
    lane = lax.broadcasted_iota(jnp.int32, (rows, LANES), 1)
    out = jnp.zeros((rows, LANES), jnp.float32)
    for k, value in values:
        out = jnp.where(lane == k, value, out)
    return out


def setup_kernel(geo, stiffness, own, low, high, low_edge, high_edge, *refs):
    st = Static(refs)
    moved, response, down, up, sums, raw, heat, one, *work = refs[len(STATIC) :]
    v, p, res, cor, cor2, cc0, cc1 = work
    tl = Tiles(geo)
    b, m, n_rows = geo.slab, geo.margin, geo.rows
    granule = geo.block[1]

    for f in range(FIELDS):
        groups = []
        for source, base in ((low, m - b), (own, m), (high, m + b)):
            for u in range(0, b, SUB):
                row = f * b + u
                tiles = [source[q, row : row + SUB, :] for q in range(geo.group)]
                groups.append((base + u, tiles))
        for row, tiles in groups:
            for x, tile in enumerate(gather_tiles(tiles, granule)):
                raw[f, x, row : row + SUB, :] = tile
    for source, base in ((low_edge, m - b - EDGE), (high_edge, m + 2 * b)):
        tiles = [source[q] for q in range(geo.group)]
        for x, tile in enumerate(gather_tiles(tiles, granule)):
            for f in range(4):
                raw[f, x, base : base + EDGE, :] = tile[f * EDGE : (f + 1) * EDGE]

    def advance(ref, old, new):
        def body(z, put):
            inside = geo.inside(z)
            for t in range(SUB):
                f, near = tl.beside(ref, z, (old,), t)
                drift = 0.0
                for k in range(3):
                    flow = get(raw, z, 1 + k, t)
                    drift = drift + jnp.maximum(flow, 0.0) * (f - near[2 * k + 1])
                    drift = drift + jnp.minimum(flow, 0.0) * (near[2 * k] - f)
                spread = tree(near) - 6.0 * f
                value = f - INCREMENT_DT * drift + INCREMENT_DT * DIFFUSIVITY * spread
                put(heat, jnp.where(inside, value, 0.0), z, new, t)

        return body

    sweep(tl, m - b - 4, m + 2 * b + 4, advance(raw, 0, 0))
    sweep(tl, m - b, m + 2 * b, advance(heat, 0, 1))

    def viscosity(z, put):
        inside = geo.inside(z)
        for pair in range(TX // 2):
            coarse = 0.0
            for t in block_of(pair):
                kind = get(raw, z, 5, t)
                base = jnp.zeros(kind.shape, jnp.float32)
                for layer in range(LAYERS):
                    base = jnp.where(kind == float(layer), stiffness[layer], base)
                value = base * jnp.exp(-ACTIVATION_ENERGY * get(heat, z, 1, t))
                value = jnp.where(inside, value, 0.0)
                st.put(put, "hv", 0.5 * value, z, t)
                coarse = coarse + value
            st.put(put, "vh", 0.125 * 0.125 * tl.pair_sum(coarse), z, pair)

    sweep(tl, m - b, m + 2 * b, viscosity)

    def statics(z, put):
        inside = geo.inside(z)
        for t in range(SUB):
            diag = tree(st.faces(tl, z, t))
            st.put(put, "w", jnp.where(inside, JACOBI_WEIGHT / diag, 0.0), z, t)
            f, near = tl.beside(heat, z, (1,), t)
            dual = -INCREMENT_DT * get(raw, z, 4, t)
            for k in range(3):
                flow = get(raw, z, 1 + k, t)
                step = jnp.where(flow > 0, f - near[2 * k + 1], near[2 * k] - f)
                st.put(put, "s%d" % k, dual * step, z, t)

    sweep(tl, m - b, m + 2 * b, statics)

    def transport(z, put):
        for t in range(SUB):
            dual, near = tl.beside(raw, z, (4,), t)
            value = dual + INCREMENT_DT * DIFFUSIVITY * (tree(near) - 6.0 * dual)
            for k in range(3):
                flow, sides = tl.beside(raw, z, (1 + k,), t)
                a = jnp.maximum(flow, 0.0) * dual
                c = jnp.minimum(flow, 0.0) * dual
                ahead = jnp.maximum(sides[2 * k], 0.0) * near[2 * k]
                behind = jnp.minimum(sides[2 * k + 1], 0.0) * near[2 * k + 1]
                value = value - INCREMENT_DT * (a - ahead + behind - c)
            put(moved, value, z - m, t)

    sweep(tl, m, m + b, transport)

    def unit(z, put):
        value = jnp.where(geo.inside(z), 1.0, 0.0)
        for t in range(SUB):
            put(p, value, z, 1, t)
            put(p, value, z, 2, t)
            put(p, st.get("hv", z, t), z, 3, t)

    sweep(tl, m - b, m + 2 * b, unit)

    mine = slice(m, m + b)

    def fields(s, three=v):
        return [three.at[3 * s + k, :, mine, :] for k in range(3)] + [p.at[s, :, mine, :]]

    pair, dual = {FORWARD: 0, RESPONSE: 2}, {ADJOINT: 1}
    iterate(geo, st, work, dual, m - PHASE, m + b + PHASE, dual)
    iterate(geo, st, work, pair, m - PHASE, m + b + PHASE, pair)
    for k, (a, r) in enumerate(zip(fields(1, cor), fields(2))):
        one[k] = a[...]
        response[k] = r[...]
    sums_of = [(0, source_product(geo, st, v, 3)), (1, whole_sum(one[3]))]
    iterate(geo, st, work, dual, m, m + b)
    iterate(geo, st, work, pair, m, m + b)
    near, far, turn = [one.at[k] for k in range(4)], fields(1, cor), [response.at[k] for k in range(4)]
    sums_of += [(2, source_product(geo, st, v, 3)), (3, whole_sum(p[1, :, mine, :]))]
    sums_of += [(4, product(near, fields(0))), (5, product(far, fields(0))), (6, product(far, turn))]
    sums[...] = in_lanes(sums_of, sums.shape[0])
    for k, (x, r) in enumerate(zip(fields(0), fields(2))):
        state, turned = x[...], r[...]
        for out, part in ((down, turned[:, :PHASE]), (up, turned[:, b - PHASE :])):
            out[:, k * b : (k + 1) * b, :] = state
            out[:, 4 * b + k * PHASE : 4 * b + (k + 1) * PHASE, :] = part


def source_product(geo, st, v, first):
    mine = slice(geo.margin, geo.margin + geo.slab)
    held = slice(geo.margin - CUT["s0"], geo.margin - CUT["s0"] + geo.slab)
    left = [st.refs["s%d" % k].at[:, held, :] for k in range(3)]
    return product(left, [v.at[first + k, :, mine, :] for k in range(3)])


def second_kernel(geo, *refs):
    st = Static(refs)
    down, up, low, high, final, *work = refs[len(STATIC) :]
    v, p = work[:2]
    b, m = geo.slab, geo.margin
    for k in range(4):
        rows, part = slice(k * b, (k + 1) * b), slice(4 * b + k * PHASE, 4 * b + (k + 1) * PHASE)
        state, turned = (v.at[k], v.at[3 + k]) if k < 3 else (p.at[0], p.at[1])
        for source, base in ((low, m - b), (down, m), (high, m + b)):
            state[:, base : base + b, :] = source[:, rows, :]
        for source, base in ((low, m - PHASE), (down, m), (up, m + b - PHASE), (high, m + b)):
            turned[:, base : base + PHASE, :] = source[:, part, :]
    iterate(geo, st, work, {FORWARD: 0}, m - PHASE, m + b + PHASE)
    iterate(geo, st, work, {FORWARD: 0, RESPONSE: 1}, m, m + b)
    mine = slice(m, m + b)
    for s in range(2):
        for k in range(4):
            final[4 * s + k] = v[3 * s + k, :, mine, :] if k < 3 else p[s, :, mine, :]


def means(geo, sums):
    row = jnp.sum(sums, axis=0, keepdims=True) / geo.cells
    c1, l1, c2, l2, l1_x2, l2_x2, l2_r1 = [row[:, k : k + 1] for k in range(7)]
    m1 = c1
    m2 = c1 + c2 - m1 * l1
    m3 = c1 + (l1_x2 - m1 * l2) - m2 * l1
    m4 = c1 + c2 + (l2_x2 - m1 * l2_r1) - m2 * l2 - m3 * l1
    return m1, m2, m3, m4


def combine_kernel(geo, sums, final, down, up, response, moved, out):
    b = geo.slab
    means_of = [jnp.broadcast_to(value, (SUB, LANES)) for value in means(geo, sums[...])]
    m1, m2, m3, m4 = means_of
    for u in range(0, b, SUB):
        rows = slice(u, u + SUB)
        fields = []
        for k in range(4):
            turned = down if u < PHASE else up
            at = 4 * b + k * PHASE + (u if u < PHASE else u - (b - PHASE))
            tiles = []
            for t in range(SUB):
                value = final[k, t, rows, :] - m1 * final[4 + k, t, rows, :]
                value = value - m2 * turned[t, at : at + SUB, :] - m3 * response[k, t, rows, :]
                tiles.append(value - m4 if k == 3 else value)
            fields.append(tiles)
        fields.append([moved[t, rows, :] + fields[2][t] for t in range(SUB)])
        for f, tiles in enumerate(fields):
            for q, tile in enumerate(scatter_tiles(tiles, geo.block[1])):
                out[q, f * b + u : f * b + u + SUB, :] = tile


def unpack_kernel(geo, chunks, heat, flow, pressure):
    b = geo.slab
    for f, ref in enumerate((flow.at[0], flow.at[1], flow.at[2], pressure, heat)):
        rows = [chunks[geo.holder[j], f * b : (f + 1) * b, :] for j in range(geo.group)]
        block = jnp.concatenate(rows, 0).T
        for k, (x, y) in enumerate(geo.order):
            ref[x, pl.ds(y, SUB, stride=TY), :] = block[k * SUB : (k + 1) * SUB]


def call(kernel, out, scratch, *args, smem=(), hbm=(), limit=VMEM_LIMIT, megabytes=2):
    f32 = jnp.float32
    cost = pl.CostEstimate(
        flops=megabytes * 1000000, bytes_accessed=megabytes * 1000000, transcendentals=0
    )
    specs = [
        pl.BlockSpec(
            memory_space=pltpu.SMEM if i in smem else pltpu.HBM if i in hbm else pltpu.VMEM
        )
        for i in range(len(args))
    ]
    return pl.pallas_call(
        kernel,
        out_shape=[jax.ShapeDtypeStruct(s, f32) for s in out],
        in_specs=specs,
        out_specs=[pl.BlockSpec(memory_space=pltpu.VMEM) for _ in out],
        scratch_shapes=[pltpu.VMEM(s, f32) if isinstance(s, tuple) else s for s in scratch],
        compiler_params=pltpu.CompilerParams(vmem_limit_bytes=limit),
        cost_estimate=cost,
    )(*args)


def slab_shards(geo, heat, flow, dual, kind, stiffness):
    b, group = geo.slab, geo.group
    inputs = (heat, flow, dual, kind)
    (chunks,) = call(
        functools.partial(pack_kernel, geo),
        [(group, FIELDS * b, LANES)],
        [pltpu.VMEM(a.shape, a.dtype) for a in inputs] + [pltpu.SemaphoreType.DMA((4,))],
        *inputs,
        hbm=range(4),
        limit=PACK_LIMIT,
    )
    own = lax.all_to_all(chunks, ("gx", "gy"), 0, 0, tiled=True)
    axes = ("gx", "gy", "gz")
    low = lax.ppermute(own, axes, geo.shifts(1))
    high = lax.ppermute(own, axes, geo.shifts(-1))
    edges = call(functools.partial(edge_kernel, geo), [(group, SUB, LANES)] * 2, [], own)
    high_edge = lax.ppermute(edges[0], axes, geo.shifts(-2))
    low_edge = lax.ppermute(edges[1], axes, geo.shifts(2))

    fine, coarse = (SUB, geo.rows, LANES), (TX // 2, geo.rows, LANES)
    static_shapes = [
        (SUB if name in STATIC_FINE else TX // 2, geo.rows - 2 * CUT[name], LANES)
        for name in STATIC
    ]
    slab = (SUB, b, LANES)

    def work(n, more=0):
        fields = [(3 * n, *fine), (n + more, *fine)] + [(3 * n, *fine)] * 3
        return fields + [(3 * n, *coarse)] * 2

    devices = group * geo.nz
    message = (SUB, 4 * b + 4 * PHASE, LANES)
    *static, moved, response, down, up, sums = call(
        functools.partial(setup_kernel, geo),
        static_shapes + [slab, (4, *slab), message, message, (devices, LANES)],
        [(FIELDS, *fine), (2, *fine), (4, *slab)] + work(3, 1),
        stiffness,
        own,
        low,
        high,
        low_edge,
        high_edge,
        smem=(0,),
        megabytes=60,
    )
    from_low = lax.ppermute(up, axes, geo.shifts(1))
    from_high = lax.ppermute(down, axes, geo.shifts(-1))
    sums = lax.all_to_all(sums, axes, 0, 0, tiled=True)
    (final,) = call(
        functools.partial(second_kernel, geo),
        [(8, *slab)],
        work(2),
        *static,
        down,
        up,
        from_low,
        from_high,
        megabytes=30,
    )
    (chunks,) = call(
        functools.partial(combine_kernel, geo),
        [(group, BACK * b, LANES)],
        [],
        sums,
        final,
        down,
        up,
        response,
        moved,
    )
    chunks = lax.all_to_all(chunks, ("gx", "gy"), 0, 0, tiled=True)
    return tuple(
        call(
            functools.partial(unpack_kernel, geo),
            [geo.block, (3, *geo.block), geo.block],
            [],
            chunks,
        )
    )


def solution(mesh):
    in_specs = (
        P("gx", "gy", "gz"),
        P(None, "gx", "gy", "gz"),
        P("gx", "gy", "gz"),
        P("gx", "gy", "gz"),
        P(),
    )
    out_specs = (P("gx", "gy", "gz"), P(None, "gx", "gy", "gz"), P("gx", "gy", "gz"))

    def program(saved_heat_state, *others):
        shape = saved_heat_state.shape
        plan = shards
        if slab_plan_fits(mesh, shape):
            plan = functools.partial(slab_shards, Slabs(mesh, shape))
        return jax.shard_map(
            plan, mesh=mesh, in_specs=in_specs, out_specs=out_specs, check_vma=False
        )(saved_heat_state, *others)

    return program
```

```python
import functools

import jax
import jax.numpy as jnp
from jax import lax
from jax.experimental import pallas as pl
from jax.experimental.pallas import tpu as pltpu
from jax.sharding import PartitionSpec as P

RECOMPUTE = 2
SCHUR_ITERS = 4
COARSE_SWEEPS = 3
LAYERS = 8


INCREMENT_DT = 0.2
DIFFUSIVITY = 0.3
ACTIVATION_ENERGY = 2.3
JACOBI_WEIGHT = 0.7
SCHUR_WEIGHT = 0.5
RAYLEIGH = 1.0


def extended(block, sides, width):
    for axis, dim in sides:
        count = lax.axis_size(axis)
        forward = [(i, i + 1) for i in range(count - 1)]
        backward = [(target, source) for source, target in forward]
        low = lax.ppermute(
            lax.slice_in_dim(block, block.shape[dim] - width, None, axis=dim), axis, forward
        )
        high = lax.ppermute(lax.slice_in_dim(block, 0, width, axis=dim), axis, backward)
        block = jnp.concatenate([low, block, high], axis=dim)
    return block


def neighbours(bordered_array):
    centre = bordered_array[..., 1:-1, 1:-1, 1:-1]
    beside_all = [
        bordered_array[..., 2:, 1:-1, 1:-1],
        bordered_array[..., :-2, 1:-1, 1:-1],
        bordered_array[..., 1:-1, 2:, 1:-1],
        bordered_array[..., 1:-1, :-2, 1:-1],
        bordered_array[..., 1:-1, 1:-1, 2:],
        bordered_array[..., 1:-1, 1:-1, :-2],
    ]
    return (centre, beside_all)


def finest_halo_cells(field):
    return extended(field, (("gx", 1), ("gy", 2), ("gz", 3)), 1)


def deep_halo(field):
    return extended(field, (("gx", 1), ("gy", 2), ("gz", 3)), 2)


def coarse_halo(field):
    return extended(field, (("gx", 1), ("gy", 2), ("gz", 3)), 1)


def march_backward(bordered_array, shallower_adjacent, deeper_adjacent):
    centre, beside_all = neighbours(bordered_array)
    drift = 0.0
    for dim_index in range(3):
        drift = (
            drift
            + shallower_adjacent[dim_index] * (centre - beside_all[2 * dim_index + 1])
            + deeper_adjacent[dim_index] * (beside_all[2 * dim_index] - centre)
        )
    spread = sum(beside_all) - 6.0 * centre
    return centre - INCREMENT_DT * drift + INCREMENT_DT * DIFFUSIVITY * spread


def motion_source(bordered_heat, forward_motion, dual_heat_after):
    centre, beside_all = neighbours(bordered_heat)
    device_pieces = [
        jnp.where(
            forward_motion[dim_index] > 0,
            centre - beside_all[2 * dim_index + 1],
            beside_all[2 * dim_index] - centre,
        )
        for dim_index in range(3)
    ]
    return -INCREMENT_DT * dual_heat_after[None] * jnp.stack(device_pieces)


def advect_dual_heat(pos_padded, neg_padded, lam_padded):
    centre, beside_all = neighbours(lam_padded)
    result = centre + INCREMENT_DT * DIFFUSIVITY * (sum(beside_all) - 6.0 * centre)
    for dim_index in range(3):
        pos_centre, pos_around = neighbours(pos_padded[dim_index])
        neg_centre, neg_around = neighbours(neg_padded[dim_index])
        result = result - INCREMENT_DT * (
            pos_centre - pos_around[2 * dim_index] + neg_around[2 * dim_index + 1] - neg_centre
        )
    return result


def coefficients(bordered_array, factor):
    centre, beside_all = neighbours(bordered_array)
    return [factor * (0.5 * (centre + other)) for other in beside_all]


def apply_operator(face_coef, bordered_array):
    centre, beside_all = neighbours(bordered_array)
    return sum((coef * (centre - other) for coef, other in zip(face_coef, beside_all)))


def gradient(bordered_array):
    centre, beside_all = neighbours(bordered_array)
    return jnp.stack(
        [
            0.5 * (beside_all[2 * dim_index] - beside_all[2 * dim_index + 1])
            for dim_index in range(3)
        ]
    )


def divergence(bordered_array):
    centre, beside_all = neighbours(bordered_array)
    return sum(
        (
            0.5 * (beside_all[2 * dim_index][dim_index] - beside_all[2 * dim_index + 1][dim_index])
            for dim_index in range(3)
        )
    )


def restrict(field):
    leading = field.shape[:-3]
    cells_x, cells_y, cells_z = field.shape[-3:]
    blocks = field.reshape(leading + (cells_x // 2, 2, cells_y // 2, 2, cells_z // 2, 2))
    return blocks.mean(axis=(-5, -3, -1))


def prolong(field):
    return jnp.repeat(jnp.repeat(jnp.repeat(field, 2, axis=-3), 2, axis=-2), 2, axis=-1)


def evaluate_viscosity(rheology_class, class_base_stiffness):
    base = jnp.zeros(rheology_class.shape, jnp.float32)
    for layer_index in range(LAYERS):
        base = base + jnp.where(
            rheology_class == layer_index, class_base_stiffness[layer_index], 0.0
        )
    return base


def inside_mask(extent_first, extent_second, extent_vertical):
    index_x = (
        lax.axis_index("gx") * extent_first + jnp.arange(extent_first + 2, dtype=jnp.int32) - 1
    )
    index_y = (
        lax.axis_index("gy") * extent_second + jnp.arange(extent_second + 2, dtype=jnp.int32) - 1
    )
    index_z = (
        lax.axis_index("gz") * extent_vertical
        + jnp.arange(extent_vertical + 2, dtype=jnp.int32)
        - 1
    )
    inside_x = (index_x >= 0) & (index_x < extent_first * lax.axis_size("gx"))
    inside_y = (index_y >= 0) & (index_y < extent_second * lax.axis_size("gy"))
    inside_z = (index_z >= 0) & (index_z < extent_vertical * lax.axis_size("gz"))
    return inside_x[:, None, None] & inside_y[None, :, None] & inside_z[None, None, :]


def coarse_solve(coarse_res, coarse_coef, coarse_diag, pad_field):
    coarse_corr = JACOBI_WEIGHT * coarse_res / coarse_diag
    for sweep in range(COARSE_SWEEPS - 1):
        coarse_corr = (
            coarse_corr
            + JACOBI_WEIGHT
            * (coarse_res - apply_operator(coarse_coef, pad_field(coarse_corr)))
            / coarse_diag
        )
    return coarse_corr


def shards(saved_heat_state, forward_motion, dual_heat_after, rheology_class, class_base_stiffness):
    extent_first, extent_second, extent_vertical = saved_heat_state.shape
    shallower_adjacent = jnp.maximum(forward_motion, 0.0)
    deeper_adjacent = jnp.minimum(forward_motion, 0.0)
    heat_state = saved_heat_state
    for repeat_index in range(RECOMPUTE):
        heat_state = march_backward(
            finest_halo_cells(heat_state[None])[0], shallower_adjacent, deeper_adjacent
        )
    local_viscosity = evaluate_viscosity(rheology_class, class_base_stiffness) * jnp.exp(
        -ACTIVATION_ENERGY * heat_state
    )
    stacked = jnp.concatenate(
        [
            heat_state[None],
            dual_heat_after[None],
            shallower_adjacent * dual_heat_after[None],
            deeper_adjacent * dual_heat_after[None],
            local_viscosity[None],
        ],
        0,
    )
    bordered_array = finest_halo_cells(stacked)
    driving_source = motion_source(bordered_array[0], forward_motion, dual_heat_after)
    advected_result = advect_dual_heat(bordered_array[2:5], bordered_array[5:8], bordered_array[1])
    face_coef = coefficients(bordered_array[8], 1.0)
    diagonal = sum(face_coef)
    coarse_visc = restrict(local_viscosity)
    coarse_coef = coefficients(coarse_halo(coarse_visc[None])[0], 0.25)
    coarse_diag = sum(coarse_coef)
    deep_static = deep_halo(jnp.concatenate([local_viscosity[None], driving_source], 0))
    cycle_coef = coefficients(deep_static[0], 1.0)
    cycle_source = deep_static[1:4, 1:-1, 1:-1, 1:-1]
    inside = inside_mask(extent_first, extent_second, extent_vertical)
    safe_diag = jnp.where(inside, sum(cycle_coef), 1.0)
    total_cells = (
        extent_first
        * extent_second
        * extent_vertical
        * lax.axis_size("gx")
        * lax.axis_size("gy")
        * lax.axis_size("gz")
    )
    velocity = jnp.zeros(forward_motion.shape, jnp.float32)
    mean_stress = jnp.zeros(saved_heat_state.shape, jnp.float32)
    for iteration in range(SCHUR_ITERS):
        if iteration == 0:
            cycle_resid = cycle_source
        else:
            flow_press = deep_halo(jnp.concatenate([velocity, mean_stress[None]], 0))
            cycle_resid = (
                cycle_source - apply_operator(cycle_coef, flow_press[0:3]) - gradient(flow_press[3])
            )
        cycle_corr = jnp.where(inside, JACOBI_WEIGHT * cycle_resid / safe_diag, 0.0)
        residual = cycle_resid[:, 1:-1, 1:-1, 1:-1]
        correction = cycle_corr[:, 1:-1, 1:-1, 1:-1]
        residual_two = residual - apply_operator(face_coef, cycle_corr)
        coarse_res = restrict(residual_two)
        coarse_corr = coarse_solve(coarse_res, coarse_coef, coarse_diag, coarse_halo)
        correction = correction + prolong(coarse_corr)
        correction = (
            correction
            + JACOBI_WEIGHT
            * (residual - apply_operator(face_coef, finest_halo_cells(correction)))
            / diagonal
        )
        velocity = velocity + correction
        spread_flow = divergence(finest_halo_cells(velocity))
        mean_stress = mean_stress - SCHUR_WEIGHT * local_viscosity * spread_flow
        mean_stress = mean_stress - lax.psum(jnp.sum(mean_stress), ("gx", "gy", "gz")) / total_cells
    adj_temp_prev = advected_result + RAYLEIGH * velocity[2]
    return (adj_temp_prev, velocity, mean_stress)


SUB = 8
LANES = 128
FIELDS = 6
BACK = 5
EDGE = 2
PHASE = 8
HELD = 24
TX, TY = 4, 2
VMEM_LIMIT = 32 * 1024 * 1024
PACK_LIMIT = 60 * 1024 * 1024
FORWARD, ADJOINT, RESPONSE = range(3)
TURNED = 2


def slab_plan_fits(mesh, shape):
    sizes = mesh.shape
    group = sizes["gx"] * sizes["gy"]
    block = (shape[0] // sizes["gx"], shape[1] // sizes["gy"], shape[2] // sizes["gz"])
    return (
        group == SUB
        and block[0] == SUB
        and block[0] * block[1] == LANES
        and block[1] * group == LANES
        and block[2] == LANES
        and block[2] == group * 2 * PHASE
    )


class Slabs:
    def __init__(self, mesh, shape):
        self.nx, self.ny, self.nz = mesh.shape["gx"], mesh.shape["gy"], mesh.shape["gz"]
        self.group = self.nx * self.ny
        self.width, self.breadth, self.height = shape
        self.block = (shape[0] // self.nx, shape[1] // self.ny, shape[2] // self.nz)
        self.slab = self.block[2] // self.group
        self.margin = self.slab + SUB
        self.rows = self.slab + 2 * self.margin
        self.cells = self.width * self.breadth * self.height
        self.place = []
        for ix in range(self.nx):
            for iy in range(self.ny):
                step = ix if iy % 2 == 0 else self.nx - 1 - ix
                self.place.append(iy * self.nx + step)
        self.order = [
            (x + TX * part, y)
            for x in range(TX)
            for y in range(TY)
            for part in range(self.block[0] // TX)
        ]
        self.holder = [self.place.index(j) for j in range(self.group)]

    def device(self, slab):
        return self.holder[slab % self.group] * self.nz + slab // self.group

    def shifts(self, distance):
        count = self.group * self.nz
        return [
            (self.device(p), self.device(p + distance))
            for p in range(count)
            if 0 <= p + distance < count
        ]

    def index(self):
        ix, iy = lax.axis_index("gx"), lax.axis_index("gy")
        step = jnp.where(iy % 2 == 0, ix, self.nx - 1 - ix)
        return lax.axis_index("gz") * self.group + iy * self.nx + step

    def inside(self, z, n=SUB):
        layer = self.index() * self.slab - self.margin + z
        layer = layer + lax.broadcasted_iota(jnp.int32, (n, LANES), 0)
        return (layer >= 0) & (layer < self.height)


def exchange(tiles, bit, width):
    lane = lax.broadcasted_iota(jnp.int32, (SUB, LANES), 1)
    low = (lane & width) == 0
    new = list(tiles)
    for a in range(SUB):
        if not a & bit:
            b = a | bit
            new[a] = jnp.where(low, tiles[a], pltpu.roll(tiles[b], width, 1))
            new[b] = jnp.where(low, pltpu.roll(tiles[a], LANES - width, 1), tiles[b])
    return new


def gather_tiles(tiles, granule):
    for bit, width in ((1, granule // 2), (1, granule), (2, 2 * granule), (4, 4 * granule)):
        tiles = exchange(tiles, bit, width)
    return tiles


def scatter_tiles(tiles, granule):
    for bit, width in ((4, 4 * granule), (2, 2 * granule), (1, granule), (1, granule // 2)):
        tiles = exchange(tiles, bit, width)
    return tiles


class Tiles:
    def __init__(self, geo):
        self.span = geo.breadth // TY
        self.row = lax.broadcasted_iota(jnp.int32, (SUB, LANES), 0)
        self.lane = lax.broadcasted_iota(jnp.int32, (SUB, LANES), 1)
        self.y = self.lane % self.span
        self.kept, self.latest, self.sweep = {}, None, 0

    def sliding(self, ref, z, lead, t, shift=0):
        if self.latest != (self.sweep, z):
            self.latest, self.kept = (self.sweep, z), {}
        where = (id(ref), lead)
        for key in [k for k in self.kept if k[:2] == where and abs(k[2] - t) > 3]:
            del self.kept[key]

        def load(j):
            key = (*where, j)
            if key not in self.kept:
                self.kept[key] = (ref, get(ref, z - shift, *lead, j))
            return self.kept[key][1]

        return load

    def x(self, load, t, step, count=TX, stride=TY):
        j = t // stride + step
        if 0 <= j < count:
            return load(t + step * stride)
        if step > 0:
            turned = pltpu.roll(load(t % stride), LANES - self.span, 1)
            return jnp.where(self.lane < LANES - self.span, turned, 0.0)
        turned = pltpu.roll(load((count - 1) * stride + t % stride), self.span, 1)
        return jnp.where(self.lane >= self.span, turned, 0.0)

    def lanes(self, f, step):
        if step > 0:
            return jnp.where(self.y < self.span - 1, pltpu.roll(f, LANES - 1, 1), 0.0)
        return jnp.where(self.y > 0, pltpu.roll(f, 1, 1), 0.0)

    def y_side(self, load, t, step):
        if (t % TY == 0) == (step > 0):
            return load(t + step)
        return self.lanes(load(t - step), step)

    def beside(self, ref, z, lead, t, shift=0):
        load = self.sliding(ref, z, lead, t, shift)
        near = [self.x(load, t, 1), self.x(load, t, -1)]
        near += [self.y_side(load, t, 1), self.y_side(load, t, -1)]
        z = z - shift
        return load(t), near + [get(ref, z + 1, *lead, t), get(ref, z - 1, *lead, t)]

    def coarse_beside(self, ref, z, lead, t):
        load = lambda j: get(ref, z, *lead, j)
        f = load(t)
        near = [self.x(load, t, step, TX // 2, 1) for step in (1, -1)]
        near += [self.lanes(f, 1), self.lanes(f, -1)]
        return f, near + [get(ref, z + 2, *lead, t), get(ref, z - 2, *lead, t)]

    def pair_sum(self, f):
        return f + jnp.where(self.row % 2 == 0, pltpu.roll(f, SUB - 1, 0), pltpu.roll(f, 1, 0))


def block_of(t):
    return range(2 * TY * t, 2 * TY * (t + 1))


def tree(terms):
    while len(terms) > 1:
        terms = [sum(terms[k : k + 2]) for k in range(0, len(terms), 2)]
    return terms[0]


def get(ref, z, *index):
    return ref[(*index, pl.ds(z, SUB), slice(None))]


def sweep(tl, lo, hi, body):
    tl.sweep += 1
    late = []

    def store(ref, value, z, *index):
        ref[(*index, pl.ds(z, SUB), slice(None))] = value

    def put(*item):
        late.append(item)
        if len(late) > HELD:
            store(*late.pop(0))

    for z in range(lo, hi, SUB):
        body(z, put)
    for item in late:
        store(*item)


def pack_kernel(geo, heat_in, flow_in, dual_in, kind_in, out, heat, flow, dual, kind, sems):
    b = geo.slab
    pairs = ((heat_in, heat), (flow_in, flow), (dual_in, dual), (kind_in, kind))
    copies = [
        pltpu.make_async_copy(source, target, sems.at[k])
        for k, (source, target) in enumerate(pairs)
    ]
    for copy in copies:
        copy.start()
    fields = [heat, flow.at[0], flow.at[1], flow.at[2], dual, kind]
    for f, (ref, copy) in enumerate(zip(fields, (0, 1, None, None, 2, 3))):
        if copy is not None:
            copies[copy].wait()
        rows = [ref[x, pl.ds(y, SUB, stride=TY), :] for x, y in geo.order]
        turned = jnp.concatenate(rows, 0).astype(jnp.float32).T
        for j in range(geo.group):
            out[geo.holder[j], f * b : (f + 1) * b, :] = turned[j * b : (j + 1) * b]


def edge_kernel(geo, own, first, last):
    b, e = geo.slab, EDGE
    for q in range(geo.group):
        for out, at in ((first, 0), (last, b - e)):
            rows = [own[q, f * b + at : f * b + at + e, :] for f in range(4)]
            out[q] = jnp.concatenate(rows, 0)


STATIC_FINE = ("s0", "s1", "s2", "w", "hv")
STATIC_COARSE = ("vh",)
STATIC = STATIC_FINE + STATIC_COARSE
CUT = {name: SUB // 2 if name in ("hv", "vh") else SUB for name in STATIC}


class Static:
    def __init__(self, refs):
        self.refs = dict(zip(STATIC, refs))

    def get(self, name, z, *index):
        return get(self.refs[name], z - CUT[name], *index)

    def put(self, put, name, value, z, *index):
        put(self.refs[name], value, z - CUT[name], *index)

    def faces(self, tl, z, t):
        h, near = tl.beside(self.refs["hv"], z, (), t, CUT["hv"])
        return [h + other for other in near]

    def coarse_faces(self, tl, z, pair):
        h, near = tl.coarse_beside(self.refs["vh"], z - CUT["vh"], (), pair)
        return [h + other for other in near]

    def coarse_weight(self, geo, face, z):
        return jnp.where(geo.inside(z), JACOBI_WEIGHT / tree(face), 0.0)


def iterate(geo, st, work, seqs, lo, hi, first=()):
    v, p, res, cor, cor2, cc0, cc1 = work
    tl = Tiles(geo)
    keep = 1.0 - JACOBI_WEIGHT
    kinds = {3 * s + k: q for q, s in seqs.items() for k in range(3)}
    comps = list(kinds)

    def faces(t, z):
        return st.faces(tl, z, t)

    def around(face, ref, c, t, z):
        f, near = tl.beside(ref, z, (c,), t)
        return f, tree([a * b for a, b in zip(face, near)])

    def residual(z, put):
        for t in range(SUB):
            w = st.get("w", z, t)
            if any(q != ADJOINT and q not in first for q in seqs):
                face = faces(t, z)
                diag = tree(face)
            for q, s in seqs.items():
                if not (q == FORWARD and q in first):
                    _, near = tl.beside(p, z, (TURNED if q == ADJOINT else s,), t)
                    slope = [0.5 * (near[2 * k] - near[2 * k + 1]) for k in range(3)]
                for k in range(3):
                    c = 3 * s + k
                    if q == ADJOINT:
                        value = slope[k] if q in first else get(cor, z, c, t) + slope[k]
                    else:
                        if q == FORWARD:
                            value = st.get("s%d" % k, z, t)
                            value = value if q in first else value - slope[k]
                        else:
                            value = -slope[k]
                        if q not in first:
                            f, total = around(face, v, c, t, z)
                            value = value - (diag * f - total)
                    put(res, value, z, c, t)
                    put(cor, w * value, z, c, t)

    sweep(tl, lo - 8, hi + 8, residual)

    def restricted(z, put):
        for pair in range(TX // 2):
            left = dict.fromkeys(comps, 0.0)
            for t in block_of(pair):
                face = faces(t, z)
                for c in comps:
                    _, total = around(face, cor, c, t, z)
                    left[c] = left[c] + (keep * get(res, z, c, t) + total)
            wc = 0.125 * st.coarse_weight(geo, st.coarse_faces(tl, z, pair), z)
            for c in comps:
                put(cc0, wc * tl.pair_sum(left[c]), z, c, pair)

    sweep(tl, lo - 8, hi + 8, restricted)

    def coarse_step(face, wc, ref, c, pair, z):
        f, near = tl.coarse_beside(ref, z, (c,), pair)
        total = tree([a * b for a, b in zip(face, near)])
        return get(cc0, z, c, pair) + keep * f + wc * total

    def sweep_one(z, put):
        for pair in range(TX // 2):
            face = st.coarse_faces(tl, z, pair)
            wc = st.coarse_weight(geo, face, z)
            for c in comps:
                put(cc1, coarse_step(face, wc, cc0, c, pair, z), z, c, pair)

    sweep(tl, lo - 4, hi + 4, sweep_one)

    def sweep_two(z, put):
        for pair in range(TX // 2):
            face = st.coarse_faces(tl, z, pair)
            wc = st.coarse_weight(geo, face, z)
            for c in comps:
                value = coarse_step(face, wc, cc1, c, pair, z)
                for t in block_of(pair):
                    put(cor2, get(cor, z, c, t) + value, z, c, t)

    sweep(tl, lo - 4, hi + 4, sweep_two)

    def velocity(z, put):
        for t in range(SUB):
            face, w = faces(t, z), st.get("w", z, t)
            for c in comps:
                f, total = around(face, cor2, c, t, z)
                value = get(cor, z, c, t) + keep * f + w * total
                if kinds[c] != ADJOINT and kinds[c] not in first:
                    value = get(v, z, c, t) + value
                put(v, value, z, c, t)

    sweep(tl, lo - 4, hi + 4, velocity)

    def pressure(z, put):
        for t in range(SUB):
            half = st.get("hv", z, t)
            for q, s in seqs.items():
                c = 3 * s
                if q == ADJOINT:
                    face = faces(t, z)
                    diag, div = tree(face), 0.0
                    for k in range(3):
                        f, near = tl.beside(v, z, (c + k,), t)
                        div = div + 0.5 * (near[2 * k] - near[2 * k + 1])
                        total = tree([a * b for a, b in zip(face, near)])
                        put(cor, get(res, z, c + k, t) - (diag * f - total), z, c + k, t)
                    value = get(p, z, s, t) + div
                    put(p, value, z, s, t)
                    put(p, half * value, z, TURNED, t)
                    continue
                one, two = tl.sliding(v, z, (c,), t), tl.sliding(v, z, (c + 1,), t)
                div = tl.x(one, t, 1) - tl.x(one, t, -1)
                div = div + (tl.y_side(two, t, 1) - tl.y_side(two, t, -1))
                div = div + (get(v, z + 1, c + 2, t) - get(v, z - 1, c + 2, t))
                value = -(half * (0.5 * div))
                if not (q == FORWARD and q in first):
                    value = get(p, z, s, t) + value
                put(p, value, z, s, t)

    sweep(tl, lo, hi, pressure)


def whole_sum(value):
    return jnp.sum(jnp.sum(value, axis=0), axis=(0, 1), keepdims=True)


def product(left, right):
    value = 0.0
    for a, b in zip(left, right):
        value = value + a[...] * b[...]
    return whole_sum(value)


def in_lanes(values, rows):
    lane = lax.broadcasted_iota(jnp.int32, (rows, LANES), 1)
    out = jnp.zeros((rows, LANES), jnp.float32)
    for k, value in values:
        out = jnp.where(lane == k, value, out)
    return out


def setup_kernel(geo, stiffness, own, low, high, low_edge, high_edge, *refs):
    st = Static(refs)
    moved, dual_out, sums, raw, heat, *work = refs[len(STATIC) :]
    v, p, res, cor, cor2, cc0, cc1 = work
    tl = Tiles(geo)
    b, m, n_rows = geo.slab, geo.margin, geo.rows
    granule = geo.block[1]

    for f in range(FIELDS):
        groups = []
        for source, base in ((low, m - b), (own, m), (high, m + b)):
            for u in range(0, b, SUB):
                row = f * b + u
                tiles = [source[q, row : row + SUB, :] for q in range(geo.group)]
                groups.append((base + u, tiles))
        for row, tiles in groups:
            for x, tile in enumerate(gather_tiles(tiles, granule)):
                raw[f, x, row : row + SUB, :] = tile
    for source, base in ((low_edge, m - b - EDGE), (high_edge, m + 2 * b)):
        tiles = [source[q] for q in range(geo.group)]
        for x, tile in enumerate(gather_tiles(tiles, granule)):
            for f in range(4):
                raw[f, x, base : base + EDGE, :] = tile[f * EDGE : (f + 1) * EDGE]

    def advance(ref, old, new):
        def body(z, put):
            inside = geo.inside(z)
            for t in range(SUB):
                f, near = tl.beside(ref, z, (old,), t)
                drift = 0.0
                for k in range(3):
                    flow = get(raw, z, 1 + k, t)
                    drift = drift + jnp.maximum(flow, 0.0) * (f - near[2 * k + 1])
                    drift = drift + jnp.minimum(flow, 0.0) * (near[2 * k] - f)
                spread = tree(near) - 6.0 * f
                value = f - INCREMENT_DT * drift + INCREMENT_DT * DIFFUSIVITY * spread
                put(heat, jnp.where(inside, value, 0.0), z, new, t)

        return body

    sweep(tl, m - b - 4, m + 2 * b + 4, advance(raw, 0, 0))
    sweep(tl, m - b, m + 2 * b, advance(heat, 0, 1))

    def viscosity(z, put):
        inside = geo.inside(z)
        for pair in range(TX // 2):
            coarse = 0.0
            for t in block_of(pair):
                kind = get(raw, z, 5, t)
                base = jnp.zeros(kind.shape, jnp.float32)
                for layer in range(LAYERS):
                    base = jnp.where(kind == float(layer), stiffness[layer], base)
                value = base * jnp.exp(-ACTIVATION_ENERGY * get(heat, z, 1, t))
                value = jnp.where(inside, value, 0.0)
                st.put(put, "hv", 0.5 * value, z, t)
                coarse = coarse + value
            st.put(put, "vh", 0.125 * 0.125 * tl.pair_sum(coarse), z, pair)

    sweep(tl, m - b, m + 2 * b, viscosity)

    def statics(z, put):
        inside = geo.inside(z)
        for t in range(SUB):
            diag = tree(st.faces(tl, z, t))
            st.put(put, "w", jnp.where(inside, JACOBI_WEIGHT / diag, 0.0), z, t)
            f, near = tl.beside(heat, z, (1,), t)
            dual = -INCREMENT_DT * get(raw, z, 4, t)
            for k in range(3):
                flow = get(raw, z, 1 + k, t)
                step = jnp.where(flow > 0, f - near[2 * k + 1], near[2 * k] - f)
                st.put(put, "s%d" % k, dual * step, z, t)

    sweep(tl, m - b, m + 2 * b, statics)

    def transport(z, put):
        for t in range(SUB):
            dual, near = tl.beside(raw, z, (4,), t)
            value = dual + INCREMENT_DT * DIFFUSIVITY * (tree(near) - 6.0 * dual)
            for k in range(3):
                flow, sides = tl.beside(raw, z, (1 + k,), t)
                a = jnp.maximum(flow, 0.0) * dual
                c = jnp.minimum(flow, 0.0) * dual
                ahead = jnp.maximum(sides[2 * k], 0.0) * near[2 * k]
                behind = jnp.minimum(sides[2 * k + 1], 0.0) * near[2 * k + 1]
                value = value - INCREMENT_DT * (a - ahead + behind - c)
            put(moved, value, z - m, t)

    sweep(tl, m, m + b, transport)

    def unit(z, put):
        value = jnp.where(geo.inside(z), 1.0, 0.0)
        for t in range(SUB):
            put(p, value, z, 0, t)
            put(p, st.get("hv", z, t), z, TURNED, t)

    sweep(tl, m - b, m + 2 * b, unit)

    mine, rows = slice(m, m + b), slice(m - PHASE, m + b + PHASE)
    dual = {ADJOINT: 0}
    iterate(geo, st, work, dual, rows.start, rows.stop, dual)
    for k in range(4):
        dual_out[k] = cor[k, :, rows, :] if k < 3 else p[0, :, rows, :]
    sums_of = [(0, source_product(geo, st, v, 0)), (1, whole_sum(p[0, :, mine, :]))]
    sums[...] = in_lanes(sums_of, sums.shape[0])


def source_product(geo, st, v, first):
    mine = slice(geo.margin, geo.margin + geo.slab)
    held = slice(geo.margin - CUT["s0"], geo.margin - CUT["s0"] + geo.slab)
    left = [st.refs["s%d" % k].at[:, held, :] for k in range(3)]
    return product(left, [v.at[first + k, :, mine, :] for k in range(3)])


def first_kernel(geo, *refs):
    st = Static(refs)
    dual, state, response, second, sums, *work = refs[len(STATIC) :]
    v, p, res, cor = work[:4]
    b, m = geo.slab, geo.margin
    mine, rows = slice(m, m + b), slice(m - PHASE, m + b + PHASE)
    tl = Tiles(geo)

    def unit(z, put):
        value = jnp.where(geo.inside(z), 1.0, 0.0)
        for t in range(SUB):
            put(p, value, z, 1, t)

    def fields(s, three=v):
        return [three.at[3 * s + k, :, mine, :] for k in range(3)] + [p.at[s, :, mine, :]]

    sweep(tl, m - b, m + 2 * b, unit)
    pair = {FORWARD: 0, RESPONSE: 1}
    iterate(geo, st, work, pair, rows.start, rows.stop, pair)
    for k, ref in enumerate(fields(1)):
        response[k] = ref[...]
    iterate(geo, st, work, pair, m, m + b)
    for k, (x, r) in enumerate(zip(fields(0), fields(1))):
        state[k], second[k] = x[...], r[...]
    for k in range(3):
        cor[k, :, rows, :] = dual[k]
    p[0, :, rows, :] = dual[3]
    held = slice(rows.start - CUT["hv"], rows.stop - CUT["hv"])
    p[TURNED, :, rows, :] = st.refs["hv"][:, held, :] * dual[3]
    iterate(geo, st, work, {ADJOINT: 0}, m, m + b)
    own = slice(PHASE, PHASE + b)
    near, far = [dual.at[k, :, own, :] for k in range(4)], fields(0, cor)
    last, turn = [state.at[k] for k in range(4)], [response.at[k] for k in range(4)]
    sums_of = [(2, source_product(geo, st, v, 0)), (3, whole_sum(p[0, :, mine, :]))]
    sums_of += [(4, product(near, last)), (5, product(far, last)), (6, product(far, turn))]
    sums[...] = in_lanes(sums_of, sums.shape[0])


def second_kernel(geo, raw, response, early, state):
    m1 = jnp.sum(early[...], axis=0, keepdims=True)[:, 0:1] / geo.cells
    for k in range(4):
        state[k] = raw[k] - m1 * response[k]


def third_kernel(geo, *refs):
    st = Static(refs)
    own, low, high, final, *work = refs[len(STATIC) :]
    v, p = work[:2]
    b, m = geo.slab, geo.margin
    for k in range(4):
        state = v.at[k] if k < 3 else p.at[0]
        for source, base in ((low, m - b), (own, m), (high, m + b)):
            state[:, base : base + b, :] = source[k]
    iterate(geo, st, work, {FORWARD: 0}, m - PHASE, m + b + PHASE)
    iterate(geo, st, work, {FORWARD: 0}, m, m + b)
    for k in range(4):
        final[k] = v[k, :, m : m + b, :] if k < 3 else p[0, :, m : m + b, :]


def means(geo, sums):
    row = jnp.sum(sums, axis=0, keepdims=True) / geo.cells
    c1, l1, c2, l2, l1_x2, l2_x2, l2_r1 = [row[:, k : k + 1] for k in range(7)]
    m1 = c1
    m2 = c1 + c2 - m1 * l1
    m3 = c1 + (l1_x2 - m1 * l2) - m2 * l1
    m4 = c1 + c2 + (l2_x2 - m1 * l2_r1) - m2 * l2 - m3 * l1
    return m2, m3, m4


def combine_kernel(geo, early, late, final, second, response, moved, out):
    b = geo.slab
    values = means(geo, early[...] + late[...])
    m2, m3, m4 = [jnp.broadcast_to(value, (SUB, LANES)) for value in values]
    for u in range(0, b, SUB):
        rows = slice(u, u + SUB)
        fields = []
        for k in range(4):
            tiles = []
            for t in range(SUB):
                value = final[k, t, rows, :] - m2 * second[k, t, rows, :]
                value = value - m3 * response[k, t, rows, :]
                tiles.append(value - m4 if k == 3 else value)
            fields.append(tiles)
        fields.append([moved[t, rows, :] + fields[2][t] for t in range(SUB)])
        for f, tiles in enumerate(fields):
            for q, tile in enumerate(scatter_tiles(tiles, geo.block[1])):
                out[q, f * b + u : f * b + u + SUB, :] = tile


def unpack_kernel(geo, chunks, heat, flow, pressure):
    b = geo.slab
    for f, ref in enumerate((flow.at[0], flow.at[1], flow.at[2], pressure, heat)):
        rows = [chunks[geo.holder[j], f * b : (f + 1) * b, :] for j in range(geo.group)]
        block = jnp.concatenate(rows, 0).T
        for k, (x, y) in enumerate(geo.order):
            ref[x, pl.ds(y, SUB, stride=TY), :] = block[k * SUB : (k + 1) * SUB]


def call(kernel, out, scratch, *args, smem=(), hbm=(), limit=VMEM_LIMIT, megabytes=2):
    f32 = jnp.float32
    cost = pl.CostEstimate(
        flops=megabytes * 1000000, bytes_accessed=megabytes * 1000000, transcendentals=0
    )
    specs = [
        pl.BlockSpec(
            memory_space=pltpu.SMEM if i in smem else pltpu.HBM if i in hbm else pltpu.VMEM
        )
        for i in range(len(args))
    ]
    return pl.pallas_call(
        kernel,
        out_shape=[jax.ShapeDtypeStruct(s, f32) for s in out],
        in_specs=specs,
        out_specs=[pl.BlockSpec(memory_space=pltpu.VMEM) for _ in out],
        scratch_shapes=[pltpu.VMEM(s, f32) if isinstance(s, tuple) else s for s in scratch],
        compiler_params=pltpu.CompilerParams(vmem_limit_bytes=limit),
        cost_estimate=cost,
    )(*args)


def slab_shards(geo, heat, flow, dual, kind, stiffness):
    b, group = geo.slab, geo.group
    inputs = (heat, flow, dual, kind)
    (chunks,) = call(
        functools.partial(pack_kernel, geo),
        [(group, FIELDS * b, LANES)],
        [pltpu.VMEM(a.shape, a.dtype) for a in inputs] + [pltpu.SemaphoreType.DMA((4,))],
        *inputs,
        hbm=range(4),
        limit=PACK_LIMIT,
    )
    own = lax.all_to_all(chunks, ("gx", "gy"), 0, 0, tiled=True)
    axes = ("gx", "gy", "gz")
    low = lax.ppermute(own, axes, geo.shifts(1))
    high = lax.ppermute(own, axes, geo.shifts(-1))
    edges = call(functools.partial(edge_kernel, geo), [(group, SUB, LANES)] * 2, [], own)
    high_edge = lax.ppermute(edges[0], axes, geo.shifts(-2))
    low_edge = lax.ppermute(edges[1], axes, geo.shifts(2))

    fine, coarse = (SUB, geo.rows, LANES), (TX // 2, geo.rows, LANES)
    static_shapes = [
        (SUB if name in STATIC_FINE else TX // 2, geo.rows - 2 * CUT[name], LANES)
        for name in STATIC
    ]
    slab = (SUB, b, LANES)

    def work(n):
        fields = [(3 * n, *fine), (TURNED + 1, *fine)] + [(3 * n, *fine)] * 3
        return fields + [(3 * n, *coarse)] * 2

    devices = group * geo.nz
    wide, state = (4, SUB, b + 2 * PHASE, LANES), (4, *slab)
    *static, moved, dual_one, early = call(
        functools.partial(setup_kernel, geo),
        static_shapes + [slab, wide, (devices, LANES)],
        [(FIELDS, *fine), (2, *fine)] + work(1),
        stiffness,
        own,
        low,
        high,
        low_edge,
        high_edge,
        smem=(0,),
        megabytes=60,
    )
    early = lax.all_to_all(early, axes, 0, 0, tiled=True)
    raw, response, second, late = call(
        functools.partial(first_kernel, geo),
        [state, state, state, (devices, LANES)],
        work(2),
        *static,
        dual_one,
        megabytes=40,
    )
    late = lax.all_to_all(late, axes, 0, 0, tiled=True)
    (mine,) = call(functools.partial(second_kernel, geo), [state], [], raw, response, early)
    low_state = lax.ppermute(mine, axes, geo.shifts(1))
    high_state = lax.ppermute(mine, axes, geo.shifts(-1))
    (final,) = call(
        functools.partial(third_kernel, geo),
        [state],
        work(1),
        *static,
        mine,
        low_state,
        high_state,
        megabytes=30,
    )
    (chunks,) = call(
        functools.partial(combine_kernel, geo),
        [(group, BACK * b, LANES)],
        [],
        early,
        late,
        final,
        second,
        response,
        moved,
    )
    chunks = lax.all_to_all(chunks, ("gx", "gy"), 0, 0, tiled=True)
    return tuple(
        call(
            functools.partial(unpack_kernel, geo),
            [geo.block, (3, *geo.block), geo.block],
            [],
            chunks,
        )
    )


def solution(mesh):
    in_specs = (
        P("gx", "gy", "gz"),
        P(None, "gx", "gy", "gz"),
        P("gx", "gy", "gz"),
        P("gx", "gy", "gz"),
        P(),
    )
    out_specs = (P("gx", "gy", "gz"), P(None, "gx", "gy", "gz"), P("gx", "gy", "gz"))

    def program(saved_heat_state, *others):
        shape = saved_heat_state.shape
        plan = shards
        if slab_plan_fits(mesh, shape):
            plan = functools.partial(slab_shards, Slabs(mesh, shape))
        return jax.shard_map(
            plan, mesh=mesh, in_specs=in_specs, out_specs=out_specs, check_vma=False
        )(saved_heat_state, *others)

    return program
```

```python
import functools

import jax
import jax.numpy as jnp
from jax import lax
from jax.experimental import pallas as pl
from jax.experimental.pallas import tpu as pltpu
from jax.sharding import PartitionSpec as P

RECOMPUTE = 2
SCHUR_ITERS = 4
COARSE_SWEEPS = 3
LAYERS = 8


INCREMENT_DT = 0.2
DIFFUSIVITY = 0.3
ACTIVATION_ENERGY = 2.3
JACOBI_WEIGHT = 0.7
SCHUR_WEIGHT = 0.5
RAYLEIGH = 1.0


def extended(block, sides, width):
    for axis, dim in sides:
        count = lax.axis_size(axis)
        forward = [(i, i + 1) for i in range(count - 1)]
        backward = [(target, source) for source, target in forward]
        low = lax.ppermute(
            lax.slice_in_dim(block, block.shape[dim] - width, None, axis=dim), axis, forward
        )
        high = lax.ppermute(lax.slice_in_dim(block, 0, width, axis=dim), axis, backward)
        block = jnp.concatenate([low, block, high], axis=dim)
    return block


def neighbours(bordered_array):
    centre = bordered_array[..., 1:-1, 1:-1, 1:-1]
    beside_all = [
        bordered_array[..., 2:, 1:-1, 1:-1],
        bordered_array[..., :-2, 1:-1, 1:-1],
        bordered_array[..., 1:-1, 2:, 1:-1],
        bordered_array[..., 1:-1, :-2, 1:-1],
        bordered_array[..., 1:-1, 1:-1, 2:],
        bordered_array[..., 1:-1, 1:-1, :-2],
    ]
    return (centre, beside_all)


def finest_halo_cells(field):
    return extended(field, (("gx", 1), ("gy", 2), ("gz", 3)), 1)


def deep_halo(field):
    return extended(field, (("gx", 1), ("gy", 2), ("gz", 3)), 2)


def coarse_halo(field):
    return extended(field, (("gx", 1), ("gy", 2), ("gz", 3)), 1)


def march_backward(bordered_array, shallower_adjacent, deeper_adjacent):
    centre, beside_all = neighbours(bordered_array)
    drift = 0.0
    for dim_index in range(3):
        drift = (
            drift
            + shallower_adjacent[dim_index] * (centre - beside_all[2 * dim_index + 1])
            + deeper_adjacent[dim_index] * (beside_all[2 * dim_index] - centre)
        )
    spread = sum(beside_all) - 6.0 * centre
    return centre - INCREMENT_DT * drift + INCREMENT_DT * DIFFUSIVITY * spread


def motion_source(bordered_heat, forward_motion, dual_heat_after):
    centre, beside_all = neighbours(bordered_heat)
    device_pieces = [
        jnp.where(
            forward_motion[dim_index] > 0,
            centre - beside_all[2 * dim_index + 1],
            beside_all[2 * dim_index] - centre,
        )
        for dim_index in range(3)
    ]
    return -INCREMENT_DT * dual_heat_after[None] * jnp.stack(device_pieces)


def advect_dual_heat(pos_padded, neg_padded, lam_padded):
    centre, beside_all = neighbours(lam_padded)
    result = centre + INCREMENT_DT * DIFFUSIVITY * (sum(beside_all) - 6.0 * centre)
    for dim_index in range(3):
        pos_centre, pos_around = neighbours(pos_padded[dim_index])
        neg_centre, neg_around = neighbours(neg_padded[dim_index])
        result = result - INCREMENT_DT * (
            pos_centre - pos_around[2 * dim_index] + neg_around[2 * dim_index + 1] - neg_centre
        )
    return result


def coefficients(bordered_array, factor):
    centre, beside_all = neighbours(bordered_array)
    return [factor * (0.5 * (centre + other)) for other in beside_all]


def apply_operator(face_coef, bordered_array):
    centre, beside_all = neighbours(bordered_array)
    return sum((coef * (centre - other) for coef, other in zip(face_coef, beside_all)))


def gradient(bordered_array):
    centre, beside_all = neighbours(bordered_array)
    return jnp.stack(
        [
            0.5 * (beside_all[2 * dim_index] - beside_all[2 * dim_index + 1])
            for dim_index in range(3)
        ]
    )


def divergence(bordered_array):
    centre, beside_all = neighbours(bordered_array)
    return sum(
        (
            0.5 * (beside_all[2 * dim_index][dim_index] - beside_all[2 * dim_index + 1][dim_index])
            for dim_index in range(3)
        )
    )


def restrict(field):
    leading = field.shape[:-3]
    cells_x, cells_y, cells_z = field.shape[-3:]
    blocks = field.reshape(leading + (cells_x // 2, 2, cells_y // 2, 2, cells_z // 2, 2))
    return blocks.mean(axis=(-5, -3, -1))


def prolong(field):
    return jnp.repeat(jnp.repeat(jnp.repeat(field, 2, axis=-3), 2, axis=-2), 2, axis=-1)


def evaluate_viscosity(rheology_class, class_base_stiffness):
    base = jnp.zeros(rheology_class.shape, jnp.float32)
    for layer_index in range(LAYERS):
        base = base + jnp.where(
            rheology_class == layer_index, class_base_stiffness[layer_index], 0.0
        )
    return base


def inside_mask(extent_first, extent_second, extent_vertical):
    index_x = (
        lax.axis_index("gx") * extent_first + jnp.arange(extent_first + 2, dtype=jnp.int32) - 1
    )
    index_y = (
        lax.axis_index("gy") * extent_second + jnp.arange(extent_second + 2, dtype=jnp.int32) - 1
    )
    index_z = (
        lax.axis_index("gz") * extent_vertical
        + jnp.arange(extent_vertical + 2, dtype=jnp.int32)
        - 1
    )
    inside_x = (index_x >= 0) & (index_x < extent_first * lax.axis_size("gx"))
    inside_y = (index_y >= 0) & (index_y < extent_second * lax.axis_size("gy"))
    inside_z = (index_z >= 0) & (index_z < extent_vertical * lax.axis_size("gz"))
    return inside_x[:, None, None] & inside_y[None, :, None] & inside_z[None, None, :]


def coarse_solve(coarse_res, coarse_coef, coarse_diag, pad_field):
    coarse_corr = JACOBI_WEIGHT * coarse_res / coarse_diag
    for sweep in range(COARSE_SWEEPS - 1):
        coarse_corr = (
            coarse_corr
            + JACOBI_WEIGHT
            * (coarse_res - apply_operator(coarse_coef, pad_field(coarse_corr)))
            / coarse_diag
        )
    return coarse_corr


def shards(saved_heat_state, forward_motion, dual_heat_after, rheology_class, class_base_stiffness):
    extent_first, extent_second, extent_vertical = saved_heat_state.shape
    shallower_adjacent = jnp.maximum(forward_motion, 0.0)
    deeper_adjacent = jnp.minimum(forward_motion, 0.0)
    heat_state = saved_heat_state
    for repeat_index in range(RECOMPUTE):
        heat_state = march_backward(
            finest_halo_cells(heat_state[None])[0], shallower_adjacent, deeper_adjacent
        )
    local_viscosity = evaluate_viscosity(rheology_class, class_base_stiffness) * jnp.exp(
        -ACTIVATION_ENERGY * heat_state
    )
    stacked = jnp.concatenate(
        [
            heat_state[None],
            dual_heat_after[None],
            shallower_adjacent * dual_heat_after[None],
            deeper_adjacent * dual_heat_after[None],
            local_viscosity[None],
        ],
        0,
    )
    bordered_array = finest_halo_cells(stacked)
    driving_source = motion_source(bordered_array[0], forward_motion, dual_heat_after)
    advected_result = advect_dual_heat(bordered_array[2:5], bordered_array[5:8], bordered_array[1])
    face_coef = coefficients(bordered_array[8], 1.0)
    diagonal = sum(face_coef)
    coarse_visc = restrict(local_viscosity)
    coarse_coef = coefficients(coarse_halo(coarse_visc[None])[0], 0.25)
    coarse_diag = sum(coarse_coef)
    deep_static = deep_halo(jnp.concatenate([local_viscosity[None], driving_source], 0))
    cycle_coef = coefficients(deep_static[0], 1.0)
    cycle_source = deep_static[1:4, 1:-1, 1:-1, 1:-1]
    inside = inside_mask(extent_first, extent_second, extent_vertical)
    safe_diag = jnp.where(inside, sum(cycle_coef), 1.0)
    total_cells = (
        extent_first
        * extent_second
        * extent_vertical
        * lax.axis_size("gx")
        * lax.axis_size("gy")
        * lax.axis_size("gz")
    )
    velocity = jnp.zeros(forward_motion.shape, jnp.float32)
    mean_stress = jnp.zeros(saved_heat_state.shape, jnp.float32)
    for iteration in range(SCHUR_ITERS):
        if iteration == 0:
            cycle_resid = cycle_source
        else:
            flow_press = deep_halo(jnp.concatenate([velocity, mean_stress[None]], 0))
            cycle_resid = (
                cycle_source - apply_operator(cycle_coef, flow_press[0:3]) - gradient(flow_press[3])
            )
        cycle_corr = jnp.where(inside, JACOBI_WEIGHT * cycle_resid / safe_diag, 0.0)
        residual = cycle_resid[:, 1:-1, 1:-1, 1:-1]
        correction = cycle_corr[:, 1:-1, 1:-1, 1:-1]
        residual_two = residual - apply_operator(face_coef, cycle_corr)
        coarse_res = restrict(residual_two)
        coarse_corr = coarse_solve(coarse_res, coarse_coef, coarse_diag, coarse_halo)
        correction = correction + prolong(coarse_corr)
        correction = (
            correction
            + JACOBI_WEIGHT
            * (residual - apply_operator(face_coef, finest_halo_cells(correction)))
            / diagonal
        )
        velocity = velocity + correction
        spread_flow = divergence(finest_halo_cells(velocity))
        mean_stress = mean_stress - SCHUR_WEIGHT * local_viscosity * spread_flow
        mean_stress = mean_stress - lax.psum(jnp.sum(mean_stress), ("gx", "gy", "gz")) / total_cells
    adj_temp_prev = advected_result + RAYLEIGH * velocity[2]
    return (adj_temp_prev, velocity, mean_stress)


SUB = 8
LANES = 128
FIELDS = 6
BACK = 5
EDGE = 2
PHASE = 8
HELD = 24
TX, TY = 4, 2
VMEM_LIMIT = 32 * 1024 * 1024
PACK_LIMIT = 60 * 1024 * 1024
FORWARD, ADJOINT, RESPONSE = range(3)
TURNED = 3


def slab_plan_fits(mesh, shape):
    sizes = mesh.shape
    group = sizes["gx"] * sizes["gy"]
    block = (shape[0] // sizes["gx"], shape[1] // sizes["gy"], shape[2] // sizes["gz"])
    return (
        group == SUB
        and block[0] == SUB
        and block[0] * block[1] == LANES
        and block[1] * group == LANES
        and block[2] == LANES
        and block[2] == group * 2 * PHASE
    )


class Slabs:
    def __init__(self, mesh, shape):
        self.nx, self.ny, self.nz = mesh.shape["gx"], mesh.shape["gy"], mesh.shape["gz"]
        self.group = self.nx * self.ny
        self.width, self.breadth, self.height = shape
        self.block = (shape[0] // self.nx, shape[1] // self.ny, shape[2] // self.nz)
        self.slab = self.block[2] // self.group
        self.margin = self.slab + SUB
        self.rows = self.slab + 2 * self.margin
        self.cells = self.width * self.breadth * self.height
        self.place = []
        for ix in range(self.nx):
            for iy in range(self.ny):
                step = ix if iy % 2 == 0 else self.nx - 1 - ix
                self.place.append(iy * self.nx + step)
        self.order = [
            (x + TX * part, y)
            for x in range(TX)
            for y in range(TY)
            for part in range(self.block[0] // TX)
        ]
        self.holder = [self.place.index(j) for j in range(self.group)]

    def device(self, slab):
        return self.holder[slab % self.group] * self.nz + slab // self.group

    def shifts(self, distance):
        count = self.group * self.nz
        return [
            (self.device(p), self.device(p + distance))
            for p in range(count)
            if 0 <= p + distance < count
        ]

    def index(self):
        ix, iy = lax.axis_index("gx"), lax.axis_index("gy")
        step = jnp.where(iy % 2 == 0, ix, self.nx - 1 - ix)
        return lax.axis_index("gz") * self.group + iy * self.nx + step

    def inside(self, z, n=SUB):
        layer = self.index() * self.slab - self.margin + z
        layer = layer + lax.broadcasted_iota(jnp.int32, (n, LANES), 0)
        return (layer >= 0) & (layer < self.height)


def exchange(tiles, bit, width):
    lane = lax.broadcasted_iota(jnp.int32, (SUB, LANES), 1)
    low = (lane & width) == 0
    new = list(tiles)
    for a in range(SUB):
        if not a & bit:
            b = a | bit
            new[a] = jnp.where(low, tiles[a], pltpu.roll(tiles[b], width, 1))
            new[b] = jnp.where(low, pltpu.roll(tiles[a], LANES - width, 1), tiles[b])
    return new


def gather_tiles(tiles, granule):
    for bit, width in ((1, granule // 2), (1, granule), (2, 2 * granule), (4, 4 * granule)):
        tiles = exchange(tiles, bit, width)
    return tiles


def scatter_tiles(tiles, granule):
    for bit, width in ((4, 4 * granule), (2, 2 * granule), (1, granule), (1, granule // 2)):
        tiles = exchange(tiles, bit, width)
    return tiles


class Tiles:
    def __init__(self, geo):
        self.span = geo.breadth // TY
        self.row = lax.broadcasted_iota(jnp.int32, (SUB, LANES), 0)
        self.lane = lax.broadcasted_iota(jnp.int32, (SUB, LANES), 1)
        self.y = self.lane % self.span
        self.kept, self.latest, self.sweep = {}, None, 0

    def sliding(self, ref, z, lead, t, shift=0):
        if self.latest != (self.sweep, z):
            self.latest, self.kept = (self.sweep, z), {}
        where = (id(ref), lead)
        for key in [k for k in self.kept if k[:2] == where and abs(k[2] - t) > 3]:
            del self.kept[key]

        def load(j):
            key = (*where, j)
            if key not in self.kept:
                self.kept[key] = (ref, get(ref, z - shift, *lead, j))
            return self.kept[key][1]

        return load

    def x(self, load, t, step, count=TX, stride=TY):
        j = t // stride + step
        if 0 <= j < count:
            return load(t + step * stride)
        if step > 0:
            turned = pltpu.roll(load(t % stride), LANES - self.span, 1)
            return jnp.where(self.lane < LANES - self.span, turned, 0.0)
        turned = pltpu.roll(load((count - 1) * stride + t % stride), self.span, 1)
        return jnp.where(self.lane >= self.span, turned, 0.0)

    def lanes(self, f, step):
        if step > 0:
            return jnp.where(self.y < self.span - 1, pltpu.roll(f, LANES - 1, 1), 0.0)
        return jnp.where(self.y > 0, pltpu.roll(f, 1, 1), 0.0)

    def y_side(self, load, t, step):
        if (t % TY == 0) == (step > 0):
            return load(t + step)
        return self.lanes(load(t - step), step)

    def beside(self, ref, z, lead, t, shift=0):
        load = self.sliding(ref, z, lead, t, shift)
        near = [self.x(load, t, 1), self.x(load, t, -1)]
        near += [self.y_side(load, t, 1), self.y_side(load, t, -1)]
        z = z - shift
        return load(t), near + [get(ref, z + 1, *lead, t), get(ref, z - 1, *lead, t)]

    def coarse_beside(self, ref, z, lead, t):
        load = lambda j: get(ref, z, *lead, j)
        f = load(t)
        near = [self.x(load, t, step, TX // 2, 1) for step in (1, -1)]
        near += [self.lanes(f, 1), self.lanes(f, -1)]
        return f, near + [get(ref, z + 2, *lead, t), get(ref, z - 2, *lead, t)]

    def pair_sum(self, f):
        return f + jnp.where(self.row % 2 == 0, pltpu.roll(f, SUB - 1, 0), pltpu.roll(f, 1, 0))


def block_of(t):
    return range(2 * TY * t, 2 * TY * (t + 1))


def tree(terms):
    while len(terms) > 1:
        terms = [sum(terms[k : k + 2]) for k in range(0, len(terms), 2)]
    return terms[0]


def get(ref, z, *index):
    return ref[(*index, pl.ds(z, SUB), slice(None))]


def sweep(tl, lo, hi, body):
    tl.sweep += 1
    late = []

    def store(ref, value, z, *index):
        ref[(*index, pl.ds(z, SUB), slice(None))] = value

    def put(*item):
        late.append(item)
        if len(late) > HELD:
            store(*late.pop(0))

    for z in range(lo, hi, SUB):
        body(z, put)
    for item in late:
        store(*item)


def pack_kernel(geo, heat_in, flow_in, dual_in, kind_in, out, heat, flow, dual, kind, sems):
    b = geo.slab
    pairs = ((heat_in, heat), (flow_in, flow), (dual_in, dual), (kind_in, kind))
    copies = [
        pltpu.make_async_copy(source, target, sems.at[k])
        for k, (source, target) in enumerate(pairs)
    ]
    for copy in copies:
        copy.start()
    fields = [heat, flow.at[0], flow.at[1], flow.at[2], dual, kind]
    for f, (ref, copy) in enumerate(zip(fields, (0, 1, None, None, 2, 3))):
        if copy is not None:
            copies[copy].wait()
        rows = [ref[x, pl.ds(y, SUB, stride=TY), :] for x, y in geo.order]
        turned = jnp.concatenate(rows, 0).astype(jnp.float32).T
        for j in range(geo.group):
            out[geo.holder[j], f * b : (f + 1) * b, :] = turned[j * b : (j + 1) * b]


def edge_kernel(geo, own, first, last):
    b, e = geo.slab, EDGE
    for q in range(geo.group):
        for out, at in ((first, 0), (last, b - e)):
            rows = [own[q, f * b + at : f * b + at + e, :] for f in range(4)]
            out[q] = jnp.concatenate(rows, 0)


STATIC_FINE = ("s0", "s1", "s2", "w", "hv")
STATIC_COARSE = ("vh",)
STATIC = STATIC_FINE + STATIC_COARSE
CUT = {name: SUB // 2 if name in ("hv", "vh") else SUB for name in STATIC}


class Static:
    def __init__(self, refs):
        self.refs = dict(zip(STATIC, refs))

    def get(self, name, z, *index):
        return get(self.refs[name], z - CUT[name], *index)

    def put(self, put, name, value, z, *index):
        put(self.refs[name], value, z - CUT[name], *index)

    def faces(self, tl, z, t):
        h, near = tl.beside(self.refs["hv"], z, (), t, CUT["hv"])
        return [h + other for other in near]

    def coarse_faces(self, tl, z, pair):
        h, near = tl.coarse_beside(self.refs["vh"], z - CUT["vh"], (), pair)
        return [h + other for other in near]

    def coarse_weight(self, geo, face, z):
        return jnp.where(geo.inside(z), JACOBI_WEIGHT / tree(face), 0.0)


def iterate(geo, st, work, seqs, lo, hi, first=()):
    v, p, res, cor, cor2, cc0, cc1 = work
    tl = Tiles(geo)
    keep = 1.0 - JACOBI_WEIGHT
    kinds = {3 * s + k: q for q, s in seqs.items() for k in range(3)}
    comps = list(kinds)

    def faces(t, z):
        return st.faces(tl, z, t)

    def around(face, ref, c, t, z):
        f, near = tl.beside(ref, z, (c,), t)
        return f, tree([a * b for a, b in zip(face, near)])

    def residual(z, put):
        for t in range(SUB):
            w = st.get("w", z, t)
            if any(q != ADJOINT and q not in first for q in seqs):
                face = faces(t, z)
                diag = tree(face)
            for q, s in seqs.items():
                if not (q == FORWARD and q in first):
                    _, near = tl.beside(p, z, (TURNED if q == ADJOINT else s,), t)
                    slope = [0.5 * (near[2 * k] - near[2 * k + 1]) for k in range(3)]
                for k in range(3):
                    c = 3 * s + k
                    if q == ADJOINT:
                        value = slope[k] if q in first else get(cor, z, c, t) + slope[k]
                    else:
                        if q == FORWARD:
                            value = st.get("s%d" % k, z, t)
                            value = value if q in first else value - slope[k]
                        else:
                            value = -slope[k]
                        if q not in first:
                            f, total = around(face, v, c, t, z)
                            value = value - (diag * f - total)
                    put(res, value, z, c, t)
                    put(cor, w * value, z, c, t)

    sweep(tl, lo - 8, hi + 8, residual)

    def restricted(z, put):
        for pair in range(TX // 2):
            left = dict.fromkeys(comps, 0.0)
            for t in block_of(pair):
                face = faces(t, z)
                for c in comps:
                    _, total = around(face, cor, c, t, z)
                    left[c] = left[c] + (keep * get(res, z, c, t) + total)
            wc = 0.125 * st.coarse_weight(geo, st.coarse_faces(tl, z, pair), z)
            for c in comps:
                put(cc0, wc * tl.pair_sum(left[c]), z, c, pair)

    sweep(tl, lo - 8, hi + 8, restricted)

    def coarse_step(face, wc, ref, c, pair, z):
        f, near = tl.coarse_beside(ref, z, (c,), pair)
        total = tree([a * b for a, b in zip(face, near)])
        return get(cc0, z, c, pair) + keep * f + wc * total

    def sweep_one(z, put):
        for pair in range(TX // 2):
            face = st.coarse_faces(tl, z, pair)
            wc = st.coarse_weight(geo, face, z)
            for c in comps:
                put(cc1, coarse_step(face, wc, cc0, c, pair, z), z, c, pair)

    sweep(tl, lo - 4, hi + 4, sweep_one)

    def sweep_two(z, put):
        for pair in range(TX // 2):
            face = st.coarse_faces(tl, z, pair)
            wc = st.coarse_weight(geo, face, z)
            for c in comps:
                value = coarse_step(face, wc, cc1, c, pair, z)
                for t in block_of(pair):
                    put(cor2, get(cor, z, c, t) + value, z, c, t)

    sweep(tl, lo - 4, hi + 4, sweep_two)

    def velocity(z, put):
        for t in range(SUB):
            face, w = faces(t, z), st.get("w", z, t)
            for c in comps:
                f, total = around(face, cor2, c, t, z)
                value = get(cor, z, c, t) + keep * f + w * total
                if kinds[c] != ADJOINT and kinds[c] not in first:
                    value = get(v, z, c, t) + value
                put(v, value, z, c, t)

    sweep(tl, lo - 4, hi + 4, velocity)

    def pressure(z, put):
        for t in range(SUB):
            half = st.get("hv", z, t)
            for q, s in seqs.items():
                c = 3 * s
                if q == ADJOINT:
                    face = faces(t, z)
                    diag, div = tree(face), 0.0
                    for k in range(3):
                        f, near = tl.beside(v, z, (c + k,), t)
                        div = div + 0.5 * (near[2 * k] - near[2 * k + 1])
                        total = tree([a * b for a, b in zip(face, near)])
                        put(cor, get(res, z, c + k, t) - (diag * f - total), z, c + k, t)
                    value = get(p, z, s, t) + div
                    put(p, value, z, s, t)
                    put(p, half * value, z, TURNED, t)
                    continue
                one, two = tl.sliding(v, z, (c,), t), tl.sliding(v, z, (c + 1,), t)
                div = tl.x(one, t, 1) - tl.x(one, t, -1)
                div = div + (tl.y_side(two, t, 1) - tl.y_side(two, t, -1))
                div = div + (get(v, z + 1, c + 2, t) - get(v, z - 1, c + 2, t))
                value = -(half * (0.5 * div))
                if not (q == FORWARD and q in first):
                    value = get(p, z, s, t) + value
                put(p, value, z, s, t)

    sweep(tl, lo, hi, pressure)


def whole_sum(value):
    return jnp.sum(jnp.sum(value, axis=0), axis=(0, 1), keepdims=True)


def product(left, right):
    value = 0.0
    for a, b in zip(left, right):
        value = value + a[...] * b[...]
    return whole_sum(value)


def in_lanes(values, rows):
    lane = lax.broadcasted_iota(jnp.int32, (rows, LANES), 1)
    out = jnp.zeros((rows, LANES), jnp.float32)
    for k, value in values:
        out = jnp.where(lane == k, value, out)
    return out


def setup_kernel(geo, stiffness, own, low, high, low_edge, high_edge, *refs):
    st = Static(refs)
    moved, response, down, up, sums, raw, heat, one, *work = refs[len(STATIC) :]
    v, p, res, cor, cor2, cc0, cc1 = work
    tl = Tiles(geo)
    b, m, n_rows = geo.slab, geo.margin, geo.rows
    granule = geo.block[1]

    def place(f, _):
        groups = []
        for source, base in ((low, m - b), (own, m), (high, m + b)):
            for u in range(0, b, SUB):
                row = pl.multiple_of(f * b, b) + u
                tiles = [source[q, pl.ds(row, SUB), :] for q in range(geo.group)]
                groups.append((base + u, tiles))
        groups = [(row, gather_tiles(tiles, granule)) for row, tiles in groups]
        for row, tiles in groups:
            for x, tile in enumerate(tiles):
                raw[f, x, row : row + SUB, :] = tile
        return 0

    lax.fori_loop(0, FIELDS, place, 0)
    for source, base in ((low_edge, m - b - EDGE), (high_edge, m + 2 * b)):
        tiles = [source[q] for q in range(geo.group)]
        for x, tile in enumerate(gather_tiles(tiles, granule)):
            for f in range(4):
                raw[f, x, base : base + EDGE, :] = tile[f * EDGE : (f + 1) * EDGE]

    def advance(ref, old, new):
        def body(z, put):
            inside = geo.inside(z)
            for t in range(SUB):
                f, near = tl.beside(ref, z, (old,), t)
                drift = 0.0
                for k in range(3):
                    flow = get(raw, z, 1 + k, t)
                    drift = drift + jnp.maximum(flow, 0.0) * (f - near[2 * k + 1])
                    drift = drift + jnp.minimum(flow, 0.0) * (near[2 * k] - f)
                spread = tree(near) - 6.0 * f
                value = f - INCREMENT_DT * drift + INCREMENT_DT * DIFFUSIVITY * spread
                put(heat, jnp.where(inside, value, 0.0), z, new, t)

        return body

    sweep(tl, m - b - 4, m + 2 * b + 4, advance(raw, 0, 0))
    sweep(tl, m - b, m + 2 * b, advance(heat, 0, 1))

    def viscosity(z, put):
        inside = geo.inside(z)
        for pair in range(TX // 2):
            coarse = 0.0
            for t in block_of(pair):
                kind = get(raw, z, 5, t)
                base = jnp.zeros(kind.shape, jnp.float32)
                for layer in range(LAYERS):
                    base = jnp.where(kind == float(layer), stiffness[layer], base)
                value = base * jnp.exp(-ACTIVATION_ENERGY * get(heat, z, 1, t))
                value = jnp.where(inside, value, 0.0)
                st.put(put, "hv", 0.5 * value, z, t)
                coarse = coarse + value
            st.put(put, "vh", 0.125 * 0.125 * tl.pair_sum(coarse), z, pair)

    sweep(tl, m - b, m + 2 * b, viscosity)

    def statics(z, put):
        inside = geo.inside(z)
        for t in range(SUB):
            diag = tree(st.faces(tl, z, t))
            st.put(put, "w", jnp.where(inside, JACOBI_WEIGHT / diag, 0.0), z, t)
            f, near = tl.beside(heat, z, (1,), t)
            dual = -INCREMENT_DT * get(raw, z, 4, t)
            for k in range(3):
                flow = get(raw, z, 1 + k, t)
                step = jnp.where(flow > 0, f - near[2 * k + 1], near[2 * k] - f)
                st.put(put, "s%d" % k, dual * step, z, t)

    sweep(tl, m - b, m + 2 * b, statics)

    def transport(z, put):
        for t in range(SUB):
            dual, near = tl.beside(raw, z, (4,), t)
            value = dual + INCREMENT_DT * DIFFUSIVITY * (tree(near) - 6.0 * dual)
            for k in range(3):
                flow, sides = tl.beside(raw, z, (1 + k,), t)
                a = jnp.maximum(flow, 0.0) * dual
                c = jnp.minimum(flow, 0.0) * dual
                ahead = jnp.maximum(sides[2 * k], 0.0) * near[2 * k]
                behind = jnp.minimum(sides[2 * k + 1], 0.0) * near[2 * k + 1]
                value = value - INCREMENT_DT * (a - ahead + behind - c)
            put(moved, value, z - m, t)

    sweep(tl, m, m + b, transport)

    def unit(z, put):
        value = jnp.where(geo.inside(z), 1.0, 0.0)
        for t in range(SUB):
            put(p, value, z, 1, t)
            put(p, value, z, 2, t)
            put(p, st.get("hv", z, t), z, 3, t)

    sweep(tl, m - b, m + 2 * b, unit)

    mine = slice(m, m + b)

    def fields(s, three=v):
        return [three.at[3 * s + k, :, mine, :] for k in range(3)] + [p.at[s, :, mine, :]]

    pair, dual = {FORWARD: 0, RESPONSE: 2}, {ADJOINT: 1}
    iterate(geo, st, work, dual, m - PHASE, m + b + PHASE, dual)
    iterate(geo, st, work, pair, m - PHASE, m + b + PHASE, pair)
    for k, (a, r) in enumerate(zip(fields(1, cor), fields(2))):
        one[k] = a[...]
        response[k] = r[...]
    sums_of = [(0, source_product(geo, st, v, 3)), (1, whole_sum(one[3]))]
    iterate(geo, st, work, dual, m, m + b)
    iterate(geo, st, work, pair, m, m + b)
    near, far, turn = [one.at[k] for k in range(4)], fields(1, cor), [response.at[k] for k in range(4)]
    sums_of += [(2, source_product(geo, st, v, 3)), (3, whole_sum(p[1, :, mine, :]))]
    sums_of += [(4, product(near, fields(0))), (5, product(far, fields(0))), (6, product(far, turn))]
    sums[...] = in_lanes(sums_of, sums.shape[0])
    for k, (x, r) in enumerate(zip(fields(0), fields(2))):
        state, turned = x[...], r[...]
        for out, part in ((down, turned[:, :PHASE]), (up, turned[:, b - PHASE :])):
            out[:, k * b : (k + 1) * b, :] = state
            out[:, 4 * b + k * PHASE : 4 * b + (k + 1) * PHASE, :] = part


def source_product(geo, st, v, first):
    mine = slice(geo.margin, geo.margin + geo.slab)
    held = slice(geo.margin - CUT["s0"], geo.margin - CUT["s0"] + geo.slab)
    left = [st.refs["s%d" % k].at[:, held, :] for k in range(3)]
    return product(left, [v.at[first + k, :, mine, :] for k in range(3)])


def second_kernel(geo, *refs):
    st = Static(refs)
    down, up, low, high, final, *work = refs[len(STATIC) :]
    v, p = work[:2]
    b, m = geo.slab, geo.margin
    for k in range(4):
        rows, part = slice(k * b, (k + 1) * b), slice(4 * b + k * PHASE, 4 * b + (k + 1) * PHASE)
        state, turned = (v.at[k], v.at[3 + k]) if k < 3 else (p.at[0], p.at[1])
        for source, base in ((low, m - b), (down, m), (high, m + b)):
            state[:, base : base + b, :] = source[:, rows, :]
        for source, base in ((low, m - PHASE), (down, m), (up, m + b - PHASE), (high, m + b)):
            turned[:, base : base + PHASE, :] = source[:, part, :]
    iterate(geo, st, work, {FORWARD: 0}, m - PHASE, m + b + PHASE)
    iterate(geo, st, work, {FORWARD: 0, RESPONSE: 1}, m, m + b)
    mine = slice(m, m + b)
    for s in range(2):
        for k in range(4):
            final[4 * s + k] = v[3 * s + k, :, mine, :] if k < 3 else p[s, :, mine, :]


def means(geo, sums):
    row = jnp.sum(sums, axis=0, keepdims=True) / geo.cells
    c1, l1, c2, l2, l1_x2, l2_x2, l2_r1 = [row[:, k : k + 1] for k in range(7)]
    m1 = c1
    m2 = c1 + c2 - m1 * l1
    m3 = c1 + (l1_x2 - m1 * l2) - m2 * l1
    m4 = c1 + c2 + (l2_x2 - m1 * l2_r1) - m2 * l2 - m3 * l1
    return m1, m2, m3, m4


def combine_kernel(geo, sums, final, down, up, response, moved, out):
    b = geo.slab
    means_of = [jnp.broadcast_to(value, (SUB, LANES)) for value in means(geo, sums[...])]
    m1, m2, m3, m4 = means_of
    for u in range(0, b, SUB):
        rows = slice(u, u + SUB)
        fields = []
        for k in range(4):
            turned = down if u < PHASE else up
            at = 4 * b + k * PHASE + (u if u < PHASE else u - (b - PHASE))
            tiles = []
            for t in range(SUB):
                value = final[k, t, rows, :] - m1 * final[4 + k, t, rows, :]
                value = value - m2 * turned[t, at : at + SUB, :] - m3 * response[k, t, rows, :]
                tiles.append(value - m4 if k == 3 else value)
            fields.append(tiles)
        fields.append([moved[t, rows, :] + fields[2][t] for t in range(SUB)])
        for f, tiles in enumerate(fields):
            for q, tile in enumerate(scatter_tiles(tiles, geo.block[1])):
                out[q, f * b + u : f * b + u + SUB, :] = tile


def unpack_kernel(geo, chunks, heat, flow, pressure):
    b = geo.slab
    for f, ref in enumerate((flow.at[0], flow.at[1], flow.at[2], pressure, heat)):
        rows = [chunks[geo.holder[j], f * b : (f + 1) * b, :] for j in range(geo.group)]
        block = jnp.concatenate(rows, 0).T
        for k, (x, y) in enumerate(geo.order):
            ref[x, pl.ds(y, SUB, stride=TY), :] = block[k * SUB : (k + 1) * SUB]


def call(kernel, out, scratch, *args, smem=(), hbm=(), limit=VMEM_LIMIT, megabytes=2):
    f32 = jnp.float32
    cost = pl.CostEstimate(
        flops=megabytes * 1000000, bytes_accessed=megabytes * 1000000, transcendentals=0
    )
    specs = [
        pl.BlockSpec(
            memory_space=pltpu.SMEM if i in smem else pltpu.HBM if i in hbm else pltpu.VMEM
        )
        for i in range(len(args))
    ]
    return pl.pallas_call(
        kernel,
        out_shape=[jax.ShapeDtypeStruct(s, f32) for s in out],
        in_specs=specs,
        out_specs=[pl.BlockSpec(memory_space=pltpu.VMEM) for _ in out],
        scratch_shapes=[pltpu.VMEM(s, f32) if isinstance(s, tuple) else s for s in scratch],
        compiler_params=pltpu.CompilerParams(vmem_limit_bytes=limit),
        cost_estimate=cost,
    )(*args)


def slab_shards(geo, heat, flow, dual, kind, stiffness):
    b, group = geo.slab, geo.group
    inputs = (heat, flow, dual, kind)
    (chunks,) = call(
        functools.partial(pack_kernel, geo),
        [(group, FIELDS * b, LANES)],
        [pltpu.VMEM(a.shape, a.dtype) for a in inputs] + [pltpu.SemaphoreType.DMA((4,))],
        *inputs,
        hbm=range(4),
        limit=PACK_LIMIT,
    )
    own = lax.all_to_all(chunks, ("gx", "gy"), 0, 0, tiled=True)
    axes = ("gx", "gy", "gz")
    low = lax.ppermute(own, axes, geo.shifts(1))
    high = lax.ppermute(own, axes, geo.shifts(-1))
    edges = call(functools.partial(edge_kernel, geo), [(group, SUB, LANES)] * 2, [], own)
    high_edge = lax.ppermute(edges[0], axes, geo.shifts(-2))
    low_edge = lax.ppermute(edges[1], axes, geo.shifts(2))

    fine, coarse = (SUB, geo.rows, LANES), (TX // 2, geo.rows, LANES)
    static_shapes = [
        (SUB if name in STATIC_FINE else TX // 2, geo.rows - 2 * CUT[name], LANES)
        for name in STATIC
    ]
    slab = (SUB, b, LANES)

    def work(n, more=0):
        fields = [(3 * n, *fine), (n + more, *fine)] + [(3 * n, *fine)] * 3
        return fields + [(3 * n, *coarse)] * 2

    devices = group * geo.nz
    message = (SUB, 4 * b + 4 * PHASE, LANES)
    *static, moved, response, down, up, sums = call(
        functools.partial(setup_kernel, geo),
        static_shapes + [slab, (4, *slab), message, message, (devices, LANES)],
        [(FIELDS, *fine), (2, *fine), (4, *slab)] + work(3, 1),
        stiffness,
        own,
        low,
        high,
        low_edge,
        high_edge,
        smem=(0,),
        megabytes=60,
    )
    from_low = lax.ppermute(up, axes, geo.shifts(1))
    from_high = lax.ppermute(down, axes, geo.shifts(-1))
    sums = lax.all_to_all(sums, axes, 0, 0, tiled=True)
    (final,) = call(
        functools.partial(second_kernel, geo),
        [(8, *slab)],
        work(2),
        *static,
        down,
        up,
        from_low,
        from_high,
        megabytes=30,
    )
    (chunks,) = call(
        functools.partial(combine_kernel, geo),
        [(group, BACK * b, LANES)],
        [],
        sums,
        final,
        down,
        up,
        response,
        moved,
    )
    chunks = lax.all_to_all(chunks, ("gx", "gy"), 0, 0, tiled=True)
    return tuple(
        call(
            functools.partial(unpack_kernel, geo),
            [geo.block, (3, *geo.block), geo.block],
            [],
            chunks,
        )
    )


def solution(mesh):
    in_specs = (
        P("gx", "gy", "gz"),
        P(None, "gx", "gy", "gz"),
        P("gx", "gy", "gz"),
        P("gx", "gy", "gz"),
        P(),
    )
    out_specs = (P("gx", "gy", "gz"), P(None, "gx", "gy", "gz"), P("gx", "gy", "gz"))

    def program(saved_heat_state, *others):
        shape = saved_heat_state.shape
        plan = shards
        if slab_plan_fits(mesh, shape):
            plan = functools.partial(slab_shards, Slabs(mesh, shape))
        return jax.shard_map(
            plan, mesh=mesh, in_specs=in_specs, out_specs=out_specs, check_vma=False
        )(saved_heat_state, *others)

    return program
```

```python
import functools

import jax
import jax.numpy as jnp
from jax import lax
from jax.experimental import pallas as pl
from jax.experimental.pallas import tpu as pltpu
from jax.sharding import PartitionSpec as P

RECOMPUTE = 2
SCHUR_ITERS = 4
COARSE_SWEEPS = 3
LAYERS = 8


INCREMENT_DT = 0.2
DIFFUSIVITY = 0.3
ACTIVATION_ENERGY = 2.3
JACOBI_WEIGHT = 0.7
SCHUR_WEIGHT = 0.5
RAYLEIGH = 1.0


def extended(block, sides, width):
    for axis, dim in sides:
        count = lax.axis_size(axis)
        forward = [(i, i + 1) for i in range(count - 1)]
        backward = [(target, source) for source, target in forward]
        low = lax.ppermute(
            lax.slice_in_dim(block, block.shape[dim] - width, None, axis=dim), axis, forward
        )
        high = lax.ppermute(lax.slice_in_dim(block, 0, width, axis=dim), axis, backward)
        block = jnp.concatenate([low, block, high], axis=dim)
    return block


def neighbours(bordered_array):
    centre = bordered_array[..., 1:-1, 1:-1, 1:-1]
    beside_all = [
        bordered_array[..., 2:, 1:-1, 1:-1],
        bordered_array[..., :-2, 1:-1, 1:-1],
        bordered_array[..., 1:-1, 2:, 1:-1],
        bordered_array[..., 1:-1, :-2, 1:-1],
        bordered_array[..., 1:-1, 1:-1, 2:],
        bordered_array[..., 1:-1, 1:-1, :-2],
    ]
    return (centre, beside_all)


def finest_halo_cells(field):
    return extended(field, (("gx", 1), ("gy", 2), ("gz", 3)), 1)


def deep_halo(field):
    return extended(field, (("gx", 1), ("gy", 2), ("gz", 3)), 2)


def coarse_halo(field):
    return extended(field, (("gx", 1), ("gy", 2), ("gz", 3)), 1)


def march_backward(bordered_array, shallower_adjacent, deeper_adjacent):
    centre, beside_all = neighbours(bordered_array)
    drift = 0.0
    for dim_index in range(3):
        drift = (
            drift
            + shallower_adjacent[dim_index] * (centre - beside_all[2 * dim_index + 1])
            + deeper_adjacent[dim_index] * (beside_all[2 * dim_index] - centre)
        )
    spread = sum(beside_all) - 6.0 * centre
    return centre - INCREMENT_DT * drift + INCREMENT_DT * DIFFUSIVITY * spread


def motion_source(bordered_heat, forward_motion, dual_heat_after):
    centre, beside_all = neighbours(bordered_heat)
    device_pieces = [
        jnp.where(
            forward_motion[dim_index] > 0,
            centre - beside_all[2 * dim_index + 1],
            beside_all[2 * dim_index] - centre,
        )
        for dim_index in range(3)
    ]
    return -INCREMENT_DT * dual_heat_after[None] * jnp.stack(device_pieces)


def advect_dual_heat(pos_padded, neg_padded, lam_padded):
    centre, beside_all = neighbours(lam_padded)
    result = centre + INCREMENT_DT * DIFFUSIVITY * (sum(beside_all) - 6.0 * centre)
    for dim_index in range(3):
        pos_centre, pos_around = neighbours(pos_padded[dim_index])
        neg_centre, neg_around = neighbours(neg_padded[dim_index])
        result = result - INCREMENT_DT * (
            pos_centre - pos_around[2 * dim_index] + neg_around[2 * dim_index + 1] - neg_centre
        )
    return result


def coefficients(bordered_array, factor):
    centre, beside_all = neighbours(bordered_array)
    return [factor * (0.5 * (centre + other)) for other in beside_all]


def apply_operator(face_coef, bordered_array):
    centre, beside_all = neighbours(bordered_array)
    return sum((coef * (centre - other) for coef, other in zip(face_coef, beside_all)))


def gradient(bordered_array):
    centre, beside_all = neighbours(bordered_array)
    return jnp.stack(
        [
            0.5 * (beside_all[2 * dim_index] - beside_all[2 * dim_index + 1])
            for dim_index in range(3)
        ]
    )


def divergence(bordered_array):
    centre, beside_all = neighbours(bordered_array)
    return sum(
        (
            0.5 * (beside_all[2 * dim_index][dim_index] - beside_all[2 * dim_index + 1][dim_index])
            for dim_index in range(3)
        )
    )


def restrict(field):
    leading = field.shape[:-3]
    cells_x, cells_y, cells_z = field.shape[-3:]
    blocks = field.reshape(leading + (cells_x // 2, 2, cells_y // 2, 2, cells_z // 2, 2))
    return blocks.mean(axis=(-5, -3, -1))


def prolong(field):
    return jnp.repeat(jnp.repeat(jnp.repeat(field, 2, axis=-3), 2, axis=-2), 2, axis=-1)


def evaluate_viscosity(rheology_class, class_base_stiffness):
    base = jnp.zeros(rheology_class.shape, jnp.float32)
    for layer_index in range(LAYERS):
        base = base + jnp.where(
            rheology_class == layer_index, class_base_stiffness[layer_index], 0.0
        )
    return base


def inside_mask(extent_first, extent_second, extent_vertical):
    index_x = (
        lax.axis_index("gx") * extent_first + jnp.arange(extent_first + 2, dtype=jnp.int32) - 1
    )
    index_y = (
        lax.axis_index("gy") * extent_second + jnp.arange(extent_second + 2, dtype=jnp.int32) - 1
    )
    index_z = (
        lax.axis_index("gz") * extent_vertical
        + jnp.arange(extent_vertical + 2, dtype=jnp.int32)
        - 1
    )
    inside_x = (index_x >= 0) & (index_x < extent_first * lax.axis_size("gx"))
    inside_y = (index_y >= 0) & (index_y < extent_second * lax.axis_size("gy"))
    inside_z = (index_z >= 0) & (index_z < extent_vertical * lax.axis_size("gz"))
    return inside_x[:, None, None] & inside_y[None, :, None] & inside_z[None, None, :]


def coarse_solve(coarse_res, coarse_coef, coarse_diag, pad_field):
    coarse_corr = JACOBI_WEIGHT * coarse_res / coarse_diag
    for sweep in range(COARSE_SWEEPS - 1):
        coarse_corr = (
            coarse_corr
            + JACOBI_WEIGHT
            * (coarse_res - apply_operator(coarse_coef, pad_field(coarse_corr)))
            / coarse_diag
        )
    return coarse_corr


def shards(saved_heat_state, forward_motion, dual_heat_after, rheology_class, class_base_stiffness):
    extent_first, extent_second, extent_vertical = saved_heat_state.shape
    shallower_adjacent = jnp.maximum(forward_motion, 0.0)
    deeper_adjacent = jnp.minimum(forward_motion, 0.0)
    heat_state = saved_heat_state
    for repeat_index in range(RECOMPUTE):
        heat_state = march_backward(
            finest_halo_cells(heat_state[None])[0], shallower_adjacent, deeper_adjacent
        )
    local_viscosity = evaluate_viscosity(rheology_class, class_base_stiffness) * jnp.exp(
        -ACTIVATION_ENERGY * heat_state
    )
    stacked = jnp.concatenate(
        [
            heat_state[None],
            dual_heat_after[None],
            shallower_adjacent * dual_heat_after[None],
            deeper_adjacent * dual_heat_after[None],
            local_viscosity[None],
        ],
        0,
    )
    bordered_array = finest_halo_cells(stacked)
    driving_source = motion_source(bordered_array[0], forward_motion, dual_heat_after)
    advected_result = advect_dual_heat(bordered_array[2:5], bordered_array[5:8], bordered_array[1])
    face_coef = coefficients(bordered_array[8], 1.0)
    diagonal = sum(face_coef)
    coarse_visc = restrict(local_viscosity)
    coarse_coef = coefficients(coarse_halo(coarse_visc[None])[0], 0.25)
    coarse_diag = sum(coarse_coef)
    deep_static = deep_halo(jnp.concatenate([local_viscosity[None], driving_source], 0))
    cycle_coef = coefficients(deep_static[0], 1.0)
    cycle_source = deep_static[1:4, 1:-1, 1:-1, 1:-1]
    inside = inside_mask(extent_first, extent_second, extent_vertical)
    safe_diag = jnp.where(inside, sum(cycle_coef), 1.0)
    total_cells = (
        extent_first
        * extent_second
        * extent_vertical
        * lax.axis_size("gx")
        * lax.axis_size("gy")
        * lax.axis_size("gz")
    )
    velocity = jnp.zeros(forward_motion.shape, jnp.float32)
    mean_stress = jnp.zeros(saved_heat_state.shape, jnp.float32)
    for iteration in range(SCHUR_ITERS):
        if iteration == 0:
            cycle_resid = cycle_source
        else:
            flow_press = deep_halo(jnp.concatenate([velocity, mean_stress[None]], 0))
            cycle_resid = (
                cycle_source - apply_operator(cycle_coef, flow_press[0:3]) - gradient(flow_press[3])
            )
        cycle_corr = jnp.where(inside, JACOBI_WEIGHT * cycle_resid / safe_diag, 0.0)
        residual = cycle_resid[:, 1:-1, 1:-1, 1:-1]
        correction = cycle_corr[:, 1:-1, 1:-1, 1:-1]
        residual_two = residual - apply_operator(face_coef, cycle_corr)
        coarse_res = restrict(residual_two)
        coarse_corr = coarse_solve(coarse_res, coarse_coef, coarse_diag, coarse_halo)
        correction = correction + prolong(coarse_corr)
        correction = (
            correction
            + JACOBI_WEIGHT
            * (residual - apply_operator(face_coef, finest_halo_cells(correction)))
            / diagonal
        )
        velocity = velocity + correction
        spread_flow = divergence(finest_halo_cells(velocity))
        mean_stress = mean_stress - SCHUR_WEIGHT * local_viscosity * spread_flow
        mean_stress = mean_stress - lax.psum(jnp.sum(mean_stress), ("gx", "gy", "gz")) / total_cells
    adj_temp_prev = advected_result + RAYLEIGH * velocity[2]
    return (adj_temp_prev, velocity, mean_stress)


SUB = 8
LANES = 128
FIELDS = 6
BACK = 5
EDGE = 2
PHASE = 8
HELD = 24
TX, TY = 4, 2
VMEM_LIMIT = 32 * 1024 * 1024
PACK_LIMIT = 60 * 1024 * 1024
FORWARD, ADJOINT, RESPONSE = range(3)
TURNED = 3


def slab_plan_fits(mesh, shape):
    sizes = mesh.shape
    group = sizes["gx"] * sizes["gy"]
    block = (shape[0] // sizes["gx"], shape[1] // sizes["gy"], shape[2] // sizes["gz"])
    return (
        group == SUB
        and block[0] == SUB
        and block[0] * block[1] == LANES
        and block[1] * group == LANES
        and block[2] == LANES
        and block[2] == group * 2 * PHASE
    )


class Slabs:
    def __init__(self, mesh, shape):
        self.nx, self.ny, self.nz = mesh.shape["gx"], mesh.shape["gy"], mesh.shape["gz"]
        self.group = self.nx * self.ny
        self.width, self.breadth, self.height = shape
        self.block = (shape[0] // self.nx, shape[1] // self.ny, shape[2] // self.nz)
        self.slab = self.block[2] // self.group
        self.margin = self.slab + SUB
        self.rows = self.slab + 2 * self.margin
        self.cells = self.width * self.breadth * self.height
        self.place = []
        for ix in range(self.nx):
            for iy in range(self.ny):
                step = ix if iy % 2 == 0 else self.nx - 1 - ix
                self.place.append(iy * self.nx + step)
        self.order = [
            (x + TX * part, y)
            for x in range(TX)
            for y in range(TY)
            for part in range(self.block[0] // TX)
        ]
        self.holder = [self.place.index(j) for j in range(self.group)]

    def device(self, slab):
        return self.holder[slab % self.group] * self.nz + slab // self.group

    def shifts(self, distance):
        count = self.group * self.nz
        return [
            (self.device(p), self.device(p + distance))
            for p in range(count)
            if 0 <= p + distance < count
        ]

    def index(self):
        ix, iy = lax.axis_index("gx"), lax.axis_index("gy")
        step = jnp.where(iy % 2 == 0, ix, self.nx - 1 - ix)
        return lax.axis_index("gz") * self.group + iy * self.nx + step

    def inside(self, z, n=SUB):
        layer = self.index() * self.slab - self.margin + z
        layer = layer + lax.broadcasted_iota(jnp.int32, (n, LANES), 0)
        return (layer >= 0) & (layer < self.height)


def exchange(tiles, bit, width):
    lane = lax.broadcasted_iota(jnp.int32, (SUB, LANES), 1)
    low = (lane & width) == 0
    new = list(tiles)
    for a in range(SUB):
        if not a & bit:
            b = a | bit
            new[a] = jnp.where(low, tiles[a], pltpu.roll(tiles[b], width, 1))
            new[b] = jnp.where(low, pltpu.roll(tiles[a], LANES - width, 1), tiles[b])
    return new


def gather_tiles(tiles, granule):
    for bit, width in ((1, granule // 2), (1, granule), (2, 2 * granule), (4, 4 * granule)):
        tiles = exchange(tiles, bit, width)
    return tiles


def scatter_tiles(tiles, granule):
    for bit, width in ((4, 4 * granule), (2, 2 * granule), (1, granule), (1, granule // 2)):
        tiles = exchange(tiles, bit, width)
    return tiles


class Tiles:
    def __init__(self, geo):
        self.span = geo.breadth // TY
        self.row = lax.broadcasted_iota(jnp.int32, (SUB, LANES), 0)
        self.lane = lax.broadcasted_iota(jnp.int32, (SUB, LANES), 1)
        self.y = self.lane % self.span
        self.kept, self.latest, self.sweep = {}, None, 0
        self.masked, self.done, self.trimmed = True, None, None

    def sliding(self, ref, z, lead, t, shift=0):
        if self.latest != (self.sweep, z):
            self.latest, self.kept = (self.sweep, z), {}
        where = (id(ref), lead)
        for key in [k for k in self.kept if k[:2] == where and abs(k[2] - t) > 3]:
            del self.kept[key]

        def load(j):
            key = (*where, j)
            if key not in self.kept:
                self.kept[key] = (ref, get(ref, z - shift, *lead, j))
            return self.kept[key][1]

        return load

    def x(self, load, t, step, count=TX, stride=TY):
        j = t // stride + step
        if 0 <= j < count:
            return load(t + step * stride)
        if step > 0:
            turned = pltpu.roll(load(t % stride), LANES - self.span, 1)
            return self.keep(self.lane < LANES - self.span, turned)
        turned = pltpu.roll(load((count - 1) * stride + t % stride), self.span, 1)
        return self.keep(self.lane >= self.span, turned)

    def lanes(self, f, step):
        if step > 0:
            return self.keep(self.y < self.span - 1, pltpu.roll(f, LANES - 1, 1))
        return self.keep(self.y > 0, pltpu.roll(f, 1, 1))

    def keep(self, inside, f):
        return jnp.where(inside, f, 0.0) if self.masked else f

    def cut(self, face, t):
        if self.done is not face:
            a, b, c, d, e, f = face
            a = jnp.where(self.lane < LANES - self.span, a, 0.0) if t // TY == TX - 1 else a
            b = jnp.where(self.lane >= self.span, b, 0.0) if t // TY == 0 else b
            c = jnp.where(self.y < self.span - 1, c, 0.0) if t % TY else c
            d = d if t % TY else jnp.where(self.y > 0, d, 0.0)
            self.done, self.trimmed = face, [a, b, c, d, e, f]
        return self.trimmed

    def y_side(self, load, t, step):
        if (t % TY == 0) == (step > 0):
            return load(t + step)
        return self.lanes(load(t - step), step)

    def beside(self, ref, z, lead, t, shift=0):
        load = self.sliding(ref, z, lead, t, shift)
        near = [self.x(load, t, 1), self.x(load, t, -1)]
        near += [self.y_side(load, t, 1), self.y_side(load, t, -1)]
        z = z - shift
        return load(t), near + [get(ref, z + 1, *lead, t), get(ref, z - 1, *lead, t)]

    def coarse_beside(self, ref, z, lead, t):
        load = lambda j: get(ref, z, *lead, j)
        f = load(t)
        near = [self.x(load, t, step, TX // 2, 1) for step in (1, -1)]
        near += [self.lanes(f, 1), self.lanes(f, -1)]
        return f, near + [get(ref, z + 2, *lead, t), get(ref, z - 2, *lead, t)]

    def pair_sum(self, f):
        return f + jnp.where(self.row % 2 == 0, pltpu.roll(f, SUB - 1, 0), pltpu.roll(f, 1, 0))


def block_of(t):
    return range(2 * TY * t, 2 * TY * (t + 1))


def tree(terms):
    while len(terms) > 1:
        terms = [sum(terms[k : k + 2]) for k in range(0, len(terms), 2)]
    return terms[0]


def get(ref, z, *index):
    return ref[(*index, pl.ds(z, SUB), slice(None))]


def sweep(tl, lo, hi, body):
    tl.sweep += 1
    late = []

    def store(ref, value, z, *index):
        ref[(*index, pl.ds(z, SUB), slice(None))] = value

    def put(*item):
        late.append(item)
        if len(late) > HELD:
            store(*late.pop(0))

    for z in range(lo, hi, SUB):
        body(z, put)
    for item in late:
        store(*item)


def pack_kernel(geo, heat_in, flow_in, dual_in, kind_in, out, heat, flow, dual, kind, sems):
    b = geo.slab
    pairs = ((heat_in, heat), (flow_in, flow), (dual_in, dual), (kind_in, kind))
    copies = [
        pltpu.make_async_copy(source, target, sems.at[k])
        for k, (source, target) in enumerate(pairs)
    ]
    for copy in copies:
        copy.start()
    fields = [heat, flow.at[0], flow.at[1], flow.at[2], dual, kind]
    for f, (ref, copy) in enumerate(zip(fields, (0, 1, None, None, 2, 3))):
        if copy is not None:
            copies[copy].wait()
        rows = [ref[x, pl.ds(y, SUB, stride=TY), :] for x, y in geo.order]
        turned = jnp.concatenate(rows, 0).astype(jnp.float32).T
        for j in range(geo.group):
            out[geo.holder[j], f * b : (f + 1) * b, :] = turned[j * b : (j + 1) * b]


def edge_kernel(geo, own, first, last):
    b, e = geo.slab, EDGE
    for q in range(geo.group):
        for out, at in ((first, 0), (last, b - e)):
            rows = [own[q, f * b + at : f * b + at + e, :] for f in range(4)]
            out[q] = jnp.concatenate(rows, 0)


STATIC_FINE = ("s0", "s1", "s2", "w", "hv")
STATIC_COARSE = ("vh",)
STATIC = STATIC_FINE + STATIC_COARSE
CUT = {name: SUB // 2 if name in ("hv", "vh") else SUB for name in STATIC}


class Static:
    def __init__(self, refs):
        self.refs = dict(zip(STATIC, refs))

    def get(self, name, z, *index):
        return get(self.refs[name], z - CUT[name], *index)

    def put(self, put, name, value, z, *index):
        put(self.refs[name], value, z - CUT[name], *index)

    def faces(self, tl, z, t):
        h, near = tl.beside(self.refs["hv"], z, (), t, CUT["hv"])
        return [h + other for other in near]

    def coarse_faces(self, tl, z, pair):
        h, near = tl.coarse_beside(self.refs["vh"], z - CUT["vh"], (), pair)
        return [h + other for other in near]

    def coarse_weight(self, geo, face, z):
        return jnp.where(geo.inside(z), JACOBI_WEIGHT / tree(face), 0.0)


def iterate(geo, st, work, seqs, lo, hi, first=()):
    v, p, res, cor, cor2, cc0, cc1 = work
    tl = Tiles(geo)
    keep = 1.0 - JACOBI_WEIGHT
    kinds = {3 * s + k: q for q, s in seqs.items() for k in range(3)}
    comps = list(kinds)

    def faces(t, z):
        return st.faces(tl, z, t)

    def around(face, ref, c, t, z):
        tl.masked = False
        f, near = tl.beside(ref, z, (c,), t)
        tl.masked = True
        return f, tree([a * b for a, b in zip(tl.cut(face, t), near)])

    def residual(z, put):
        for t in range(SUB):
            w = st.get("w", z, t)
            if any(q != ADJOINT and q not in first for q in seqs):
                face = faces(t, z)
                diag = tree(face)
            for q, s in seqs.items():
                if not (q == FORWARD and q in first):
                    _, near = tl.beside(p, z, (TURNED if q == ADJOINT else s,), t)
                    slope = [0.5 * (near[2 * k] - near[2 * k + 1]) for k in range(3)]
                for k in range(3):
                    c = 3 * s + k
                    if q == ADJOINT:
                        value = slope[k] if q in first else get(cor, z, c, t) + slope[k]
                    else:
                        if q == FORWARD:
                            value = st.get("s%d" % k, z, t)
                            value = value if q in first else value - slope[k]
                        else:
                            value = -slope[k]
                        if q not in first:
                            f, total = around(face, v, c, t, z)
                            value = value - (diag * f - total)
                    put(res, value, z, c, t)
                    put(cor, w * value, z, c, t)

    sweep(tl, lo - 8, hi + 8, residual)

    def restricted(z, put):
        for pair in range(TX // 2):
            left = dict.fromkeys(comps, 0.0)
            for t in block_of(pair):
                face = faces(t, z)
                for c in comps:
                    _, total = around(face, cor, c, t, z)
                    left[c] = left[c] + (keep * get(res, z, c, t) + total)
            wc = 0.125 * st.coarse_weight(geo, st.coarse_faces(tl, z, pair), z)
            for c in comps:
                put(cc0, wc * tl.pair_sum(left[c]), z, c, pair)

    sweep(tl, lo - 8, hi + 8, restricted)

    def coarse_step(face, wc, ref, c, pair, z):
        f, near = tl.coarse_beside(ref, z, (c,), pair)
        total = tree([a * b for a, b in zip(face, near)])
        return get(cc0, z, c, pair) + keep * f + wc * total

    def sweep_one(z, put):
        for pair in range(TX // 2):
            face = st.coarse_faces(tl, z, pair)
            wc = st.coarse_weight(geo, face, z)
            for c in comps:
                put(cc1, coarse_step(face, wc, cc0, c, pair, z), z, c, pair)

    sweep(tl, lo - 4, hi + 4, sweep_one)

    def sweep_two(z, put):
        for pair in range(TX // 2):
            face = st.coarse_faces(tl, z, pair)
            wc = st.coarse_weight(geo, face, z)
            for c in comps:
                value = coarse_step(face, wc, cc1, c, pair, z)
                for t in block_of(pair):
                    put(cor2, get(cor, z, c, t) + value, z, c, t)

    sweep(tl, lo - 4, hi + 4, sweep_two)

    def velocity(z, put):
        for t in range(SUB):
            face, w = faces(t, z), st.get("w", z, t)
            for c in comps:
                f, total = around(face, cor2, c, t, z)
                value = get(cor, z, c, t) + keep * f + w * total
                if kinds[c] != ADJOINT and kinds[c] not in first:
                    value = get(v, z, c, t) + value
                put(v, value, z, c, t)

    sweep(tl, lo - 4, hi + 4, velocity)

    def pressure(z, put):
        for t in range(SUB):
            half = st.get("hv", z, t)
            for q, s in seqs.items():
                c = 3 * s
                if q == ADJOINT:
                    face = faces(t, z)
                    diag, div = tree(face), 0.0
                    for k in range(3):
                        f, near = tl.beside(v, z, (c + k,), t)
                        div = div + 0.5 * (near[2 * k] - near[2 * k + 1])
                        total = tree([a * b for a, b in zip(face, near)])
                        put(cor, get(res, z, c + k, t) - (diag * f - total), z, c + k, t)
                    value = get(p, z, s, t) + div
                    put(p, value, z, s, t)
                    put(p, half * value, z, TURNED, t)
                    continue
                one, two = tl.sliding(v, z, (c,), t), tl.sliding(v, z, (c + 1,), t)
                div = tl.x(one, t, 1) - tl.x(one, t, -1)
                div = div + (tl.y_side(two, t, 1) - tl.y_side(two, t, -1))
                div = div + (get(v, z + 1, c + 2, t) - get(v, z - 1, c + 2, t))
                value = -(half * (0.5 * div))
                if not (q == FORWARD and q in first):
                    value = get(p, z, s, t) + value
                put(p, value, z, s, t)

    sweep(tl, lo, hi, pressure)


def whole_sum(value):
    return jnp.sum(jnp.sum(value, axis=0), axis=(0, 1), keepdims=True)


def product(left, right):
    value = 0.0
    for a, b in zip(left, right):
        value = value + a[...] * b[...]
    return whole_sum(value)


def in_lanes(values, rows):
    lane = lax.broadcasted_iota(jnp.int32, (rows, LANES), 1)
    out = jnp.zeros((rows, LANES), jnp.float32)
    for k, value in values:
        out = jnp.where(lane == k, value, out)
    return out


def setup_kernel(geo, stiffness, own, low, high, low_edge, high_edge, *refs):
    st = Static(refs)
    moved, response, down, up, sums, raw, heat, one, *work = refs[len(STATIC) :]
    v, p, res, cor, cor2, cc0, cc1 = work
    tl = Tiles(geo)
    b, m, n_rows = geo.slab, geo.margin, geo.rows
    granule = geo.block[1]

    def place(f, _):
        groups = []
        for source, base in ((low, m - b), (own, m), (high, m + b)):
            for u in range(0, b, SUB):
                row = pl.multiple_of(f * b, b) + u
                tiles = [source[q, pl.ds(row, SUB), :] for q in range(geo.group)]
                groups.append((base + u, tiles))
        groups = [(row, gather_tiles(tiles, granule)) for row, tiles in groups]
        for row, tiles in groups:
            for x, tile in enumerate(tiles):
                raw[f, x, row : row + SUB, :] = tile
        return 0

    lax.fori_loop(0, FIELDS, place, 0)
    for source, base in ((low_edge, m - b - EDGE), (high_edge, m + 2 * b)):
        tiles = [source[q] for q in range(geo.group)]
        for x, tile in enumerate(gather_tiles(tiles, granule)):
            for f in range(4):
                raw[f, x, base : base + EDGE, :] = tile[f * EDGE : (f + 1) * EDGE]

    def advance(ref, old, new):
        def body(z, put):
            inside = geo.inside(z)
            for t in range(SUB):
                f, near = tl.beside(ref, z, (old,), t)
                drift = 0.0
                for k in range(3):
                    flow = get(raw, z, 1 + k, t)
                    drift = drift + jnp.maximum(flow, 0.0) * (f - near[2 * k + 1])
                    drift = drift + jnp.minimum(flow, 0.0) * (near[2 * k] - f)
                spread = tree(near) - 6.0 * f
                value = f - INCREMENT_DT * drift + INCREMENT_DT * DIFFUSIVITY * spread
                put(heat, jnp.where(inside, value, 0.0), z, new, t)

        return body

    sweep(tl, m - b - 4, m + 2 * b + 4, advance(raw, 0, 0))
    sweep(tl, m - b, m + 2 * b, advance(heat, 0, 1))

    def viscosity(z, put):
        inside = geo.inside(z)
        for pair in range(TX // 2):
            coarse = 0.0
            for t in block_of(pair):
                kind = get(raw, z, 5, t)
                base = jnp.zeros(kind.shape, jnp.float32)
                for layer in range(LAYERS):
                    base = jnp.where(kind == float(layer), stiffness[layer], base)
                value = base * jnp.exp(-ACTIVATION_ENERGY * get(heat, z, 1, t))
                value = jnp.where(inside, value, 0.0)
                st.put(put, "hv", 0.5 * value, z, t)
                coarse = coarse + value
            st.put(put, "vh", 0.125 * 0.125 * tl.pair_sum(coarse), z, pair)

    sweep(tl, m - b, m + 2 * b, viscosity)

    def statics(z, put):
        inside = geo.inside(z)
        for t in range(SUB):
            diag = tree(st.faces(tl, z, t))
            st.put(put, "w", jnp.where(inside, JACOBI_WEIGHT / diag, 0.0), z, t)
            f, near = tl.beside(heat, z, (1,), t)
            dual = -INCREMENT_DT * get(raw, z, 4, t)
            for k in range(3):
                flow = get(raw, z, 1 + k, t)
                step = jnp.where(flow > 0, f - near[2 * k + 1], near[2 * k] - f)
                st.put(put, "s%d" % k, dual * step, z, t)

    sweep(tl, m - b, m + 2 * b, statics)

    def transport(z, put):
        for t in range(SUB):
            dual, near = tl.beside(raw, z, (4,), t)
            value = dual + INCREMENT_DT * DIFFUSIVITY * (tree(near) - 6.0 * dual)
            for k in range(3):
                flow, sides = tl.beside(raw, z, (1 + k,), t)
                a = jnp.maximum(flow, 0.0) * dual
                c = jnp.minimum(flow, 0.0) * dual
                ahead = jnp.maximum(sides[2 * k], 0.0) * near[2 * k]
                behind = jnp.minimum(sides[2 * k + 1], 0.0) * near[2 * k + 1]
                value = value - INCREMENT_DT * (a - ahead + behind - c)
            put(moved, value, z - m, t)

    sweep(tl, m, m + b, transport)

    def unit(z, put):
        value = jnp.where(geo.inside(z), 1.0, 0.0)
        for t in range(SUB):
            put(p, value, z, 1, t)
            put(p, value, z, 2, t)
            put(p, st.get("hv", z, t), z, 3, t)

    sweep(tl, m - b, m + 2 * b, unit)

    mine = slice(m, m + b)

    def fields(s, three=v):
        return [three.at[3 * s + k, :, mine, :] for k in range(3)] + [p.at[s, :, mine, :]]

    pair, dual = {FORWARD: 0, RESPONSE: 2}, {ADJOINT: 1}
    iterate(geo, st, work, dual, m - PHASE, m + b + PHASE, dual)
    iterate(geo, st, work, pair, m - PHASE, m + b + PHASE, pair)
    for k, (a, r) in enumerate(zip(fields(1, cor), fields(2))):
        one[k] = a[...]
        response[k] = r[...]
    sums_of = [(0, source_product(geo, st, v, 3)), (1, whole_sum(one[3]))]
    iterate(geo, st, work, dual, m, m + b)
    iterate(geo, st, work, pair, m, m + b)
    near, far, turn = [one.at[k] for k in range(4)], fields(1, cor), [response.at[k] for k in range(4)]
    sums_of += [(2, source_product(geo, st, v, 3)), (3, whole_sum(p[1, :, mine, :]))]
    sums_of += [(4, product(near, fields(0))), (5, product(far, fields(0))), (6, product(far, turn))]
    sums[...] = in_lanes(sums_of, sums.shape[0])
    for k, (x, r) in enumerate(zip(fields(0), fields(2))):
        state, turned = x[...], r[...]
        for out, part in ((down, turned[:, :PHASE]), (up, turned[:, b - PHASE :])):
            out[:, k * b : (k + 1) * b, :] = state
            out[:, 4 * b + k * PHASE : 4 * b + (k + 1) * PHASE, :] = part


def source_product(geo, st, v, first):
    mine = slice(geo.margin, geo.margin + geo.slab)
    held = slice(geo.margin - CUT["s0"], geo.margin - CUT["s0"] + geo.slab)
    left = [st.refs["s%d" % k].at[:, held, :] for k in range(3)]
    return product(left, [v.at[first + k, :, mine, :] for k in range(3)])


def second_kernel(geo, *refs):
    st = Static(refs)
    down, up, low, high, final, *work = refs[len(STATIC) :]
    v, p = work[:2]
    b, m = geo.slab, geo.margin
    for k in range(4):
        rows, part = slice(k * b, (k + 1) * b), slice(4 * b + k * PHASE, 4 * b + (k + 1) * PHASE)
        state, turned = (v.at[k], v.at[3 + k]) if k < 3 else (p.at[0], p.at[1])
        for source, base in ((low, m - b), (down, m), (high, m + b)):
            state[:, base : base + b, :] = source[:, rows, :]
        for source, base in ((low, m - PHASE), (down, m), (up, m + b - PHASE), (high, m + b)):
            turned[:, base : base + PHASE, :] = source[:, part, :]
    iterate(geo, st, work, {FORWARD: 0}, m - PHASE, m + b + PHASE)
    iterate(geo, st, work, {FORWARD: 0, RESPONSE: 1}, m, m + b)
    mine = slice(m, m + b)
    for s in range(2):
        for k in range(4):
            final[4 * s + k] = v[3 * s + k, :, mine, :] if k < 3 else p[s, :, mine, :]


def means(geo, sums):
    row = jnp.sum(sums, axis=0, keepdims=True) / geo.cells
    c1, l1, c2, l2, l1_x2, l2_x2, l2_r1 = [row[:, k : k + 1] for k in range(7)]
    m1 = c1
    m2 = c1 + c2 - m1 * l1
    m3 = c1 + (l1_x2 - m1 * l2) - m2 * l1
    m4 = c1 + c2 + (l2_x2 - m1 * l2_r1) - m2 * l2 - m3 * l1
    return m1, m2, m3, m4


def combine_kernel(geo, sums, final, down, up, response, moved, out):
    b = geo.slab
    means_of = [jnp.broadcast_to(value, (SUB, LANES)) for value in means(geo, sums[...])]
    m1, m2, m3, m4 = means_of
    for u in range(0, b, SUB):
        rows = slice(u, u + SUB)
        fields = []
        for k in range(4):
            turned = down if u < PHASE else up
            at = 4 * b + k * PHASE + (u if u < PHASE else u - (b - PHASE))
            tiles = []
            for t in range(SUB):
                value = final[k, t, rows, :] - m1 * final[4 + k, t, rows, :]
                value = value - m2 * turned[t, at : at + SUB, :] - m3 * response[k, t, rows, :]
                tiles.append(value - m4 if k == 3 else value)
            fields.append(tiles)
        fields.append([moved[t, rows, :] + fields[2][t] for t in range(SUB)])
        for f, tiles in enumerate(fields):
            for q, tile in enumerate(scatter_tiles(tiles, geo.block[1])):
                out[q, f * b + u : f * b + u + SUB, :] = tile


def unpack_kernel(geo, chunks, heat, flow, pressure):
    b = geo.slab
    for f, ref in enumerate((flow.at[0], flow.at[1], flow.at[2], pressure, heat)):
        rows = [chunks[geo.holder[j], f * b : (f + 1) * b, :] for j in range(geo.group)]
        block = jnp.concatenate(rows, 0).T
        for k, (x, y) in enumerate(geo.order):
            ref[x, pl.ds(y, SUB, stride=TY), :] = block[k * SUB : (k + 1) * SUB]


def call(kernel, out, scratch, *args, smem=(), hbm=(), limit=VMEM_LIMIT, megabytes=2):
    f32 = jnp.float32
    cost = pl.CostEstimate(
        flops=megabytes * 1000000, bytes_accessed=megabytes * 1000000, transcendentals=0
    )
    specs = [
        pl.BlockSpec(
            memory_space=pltpu.SMEM if i in smem else pltpu.HBM if i in hbm else pltpu.VMEM
        )
        for i in range(len(args))
    ]
    return pl.pallas_call(
        kernel,
        out_shape=[jax.ShapeDtypeStruct(s, f32) for s in out],
        in_specs=specs,
        out_specs=[pl.BlockSpec(memory_space=pltpu.VMEM) for _ in out],
        scratch_shapes=[pltpu.VMEM(s, f32) if isinstance(s, tuple) else s for s in scratch],
        compiler_params=pltpu.CompilerParams(vmem_limit_bytes=limit),
        cost_estimate=cost,
    )(*args)


def slab_shards(geo, heat, flow, dual, kind, stiffness):
    b, group = geo.slab, geo.group
    inputs = (heat, flow, dual, kind)
    (chunks,) = call(
        functools.partial(pack_kernel, geo),
        [(group, FIELDS * b, LANES)],
        [pltpu.VMEM(a.shape, a.dtype) for a in inputs] + [pltpu.SemaphoreType.DMA((4,))],
        *inputs,
        hbm=range(4),
        limit=PACK_LIMIT,
    )
    own = lax.all_to_all(chunks, ("gx", "gy"), 0, 0, tiled=True)
    axes = ("gx", "gy", "gz")
    low = lax.ppermute(own, axes, geo.shifts(1))
    high = lax.ppermute(own, axes, geo.shifts(-1))
    edges = call(functools.partial(edge_kernel, geo), [(group, SUB, LANES)] * 2, [], own)
    high_edge = lax.ppermute(edges[0], axes, geo.shifts(-2))
    low_edge = lax.ppermute(edges[1], axes, geo.shifts(2))

    fine, coarse = (SUB, geo.rows, LANES), (TX // 2, geo.rows, LANES)
    static_shapes = [
        (SUB if name in STATIC_FINE else TX // 2, geo.rows - 2 * CUT[name], LANES)
        for name in STATIC
    ]
    slab = (SUB, b, LANES)

    def work(n, more=0):
        fields = [(3 * n, *fine), (n + more, *fine)] + [(3 * n, *fine)] * 3
        return fields + [(3 * n, *coarse)] * 2

    devices = group * geo.nz
    message = (SUB, 4 * b + 4 * PHASE, LANES)
    *static, moved, response, down, up, sums = call(
        functools.partial(setup_kernel, geo),
        static_shapes + [slab, (4, *slab), message, message, (devices, LANES)],
        [(FIELDS, *fine), (2, *fine), (4, *slab)] + work(3, 1),
        stiffness,
        own,
        low,
        high,
        low_edge,
        high_edge,
        smem=(0,),
        megabytes=60,
    )
    from_low = lax.ppermute(up, axes, geo.shifts(1))
    from_high = lax.ppermute(down, axes, geo.shifts(-1))
    sums = lax.all_to_all(sums, axes, 0, 0, tiled=True)
    (final,) = call(
        functools.partial(second_kernel, geo),
        [(8, *slab)],
        work(2),
        *static,
        down,
        up,
        from_low,
        from_high,
        megabytes=30,
    )
    (chunks,) = call(
        functools.partial(combine_kernel, geo),
        [(group, BACK * b, LANES)],
        [],
        sums,
        final,
        down,
        up,
        response,
        moved,
    )
    chunks = lax.all_to_all(chunks, ("gx", "gy"), 0, 0, tiled=True)
    return tuple(
        call(
            functools.partial(unpack_kernel, geo),
            [geo.block, (3, *geo.block), geo.block],
            [],
            chunks,
        )
    )


def solution(mesh):
    in_specs = (
        P("gx", "gy", "gz"),
        P(None, "gx", "gy", "gz"),
        P("gx", "gy", "gz"),
        P("gx", "gy", "gz"),
        P(),
    )
    out_specs = (P("gx", "gy", "gz"), P(None, "gx", "gy", "gz"), P("gx", "gy", "gz"))

    def program(saved_heat_state, *others):
        shape = saved_heat_state.shape
        plan = shards
        if slab_plan_fits(mesh, shape):
            plan = functools.partial(slab_shards, Slabs(mesh, shape))
        return jax.shard_map(
            plan, mesh=mesh, in_specs=in_specs, out_specs=out_specs, check_vma=False
        )(saved_heat_state, *others)

    return program
```
